32 devices in a mesh: dp: 4 (over y, x), shard: 8 (over z, core).
Axes of the slice: x: 2, y: 2, z: 4, core: 2. Of those that a mesh axis runs over, the one named last changes fastest.
Arguments:
- tokens: bfloat16 [10240, 2048], P(('dp', 'shard')), may hold values from -6 to 6
- cotangent: bfloat16 [10240, 2048], P(('dp', 'shard')), may hold values from -27 to 27
- segments: int32 [10240], P(('dp', 'shard')), may hold values from 0 to 10239, as said below
- positions: int32 [10240], P(('dp', 'shard')), may hold values from 0 to 4095, as said below
- attn_master: float32 [2048, 8192], P(('dp', 'shard')), may hold values from -0.53033009 to 0.53033009
- mlp_master: float32 [2048, 16896], P(('dp', 'shard')), may hold values from -0.125 to 0.125
- norm_master: float32 [7, 2048], P(None, ('dp', 'shard')), may hold values from -0.6 to 2.7
- attn_first: float32 [2048, 8192], P(('dp', 'shard')), may hold values from -0.00024414062 to 0.00024414062
- mlp_first: float32 [2048, 16896], P(('dp', 'shard')), may hold values from -0.00024414062 to 0.00024414062
- norm_first: float32 [7, 2048], P(None, ('dp', 'shard')), may hold values from -0.0012207031 to 0.0012207031
- attn_second: float32 [2048, 8192], P(('dp', 'shard')), may hold values from 1.0234547e-09 to 4.0860355e-09
- mlp_second: float32 [2048, 16896], P(('dp', 'shard')), may hold values from 1.0234547e-09 to 4.0860355e-09
- norm_second: float32 [7, 2048], P(None, ('dp', 'shard')), may hold values from 2.5683653e-08 to 1.0234546e-07
Outputs:
- block_out: bfloat16 [10240, 2048], P(('dp', 'shard'))
- input_grad: float32 [10240, 2048], P(('dp', 'shard'))
- grad_norm: float32 [], replicated
- attn_master_new: float32 [2048, 8192], P(('dp', 'shard'))
- mlp_master_new: float32 [2048, 16896], P(('dp', 'shard'))
- norm_master_new: float32 [7, 2048], P(None, ('dp', 'shard'))
- attn_first_new: float32 [2048, 8192], P(('dp', 'shard'))
- mlp_first_new: float32 [2048, 16896], P(('dp', 'shard'))
- norm_first_new: float32 [7, 2048], P(None, ('dp', 'shard'))
- attn_second_new: float32 [2048, 8192], P(('dp', 'shard'))
- mlp_second_new: float32 [2048, 16896], P(('dp', 'shard'))
- norm_second_new: float32 [7, 2048], P(None, ('dp', 'shard'))
The draws below stay inside these ranges and needn't reach their ends.
Inputs may be any that keep to these rules, and one draw needn't show every extreme that they name: `segments`: A token's segment number is the place of its document's first token; numbers never fall along the tokens, and a new one begins at the first token of every 320-token sequence. Within one segment the positions rise by one from token to token.
All inputs are finite; a program needn't handle non-finite values.
Results may differ from the reference program's by a relative error of at most 0.013.
The reference program's roundings to bfloat16 on the way count: a program that leaves them out, or rounds other values in their place, can miss the bound.
Values may be sent and summed in bfloat16 or wider, within the bound.
A program may use at most 832 MiB of HBM per device.

```python
import math
import jax
import jax.numpy as jnp
from jax import lax

D = 2048
HEADS = 32
HEAD = 64
FF = 5632
ROT = 16
TOK_DEV = 320
STEP = 10
TOKENS = 10240
N_DP = 4
N_SHARD = 8


def doc_layout(key):
    total_rows = TOK_DEV * N_DP * N_SHARD
    places = jnp.arange(total_rows, dtype=jnp.int32)
    starts = jax.random.randint(jax.random.fold_in(key, 101), (total_rows,), 0, 24) == 0
    starts = starts | (places % TOK_DEV == 0) | (places == total_rows - 1)
    doc_ids = jnp.cumsum(starts.astype(jnp.int32)) - 1
    begins = lax.cummax(jnp.where(starts, places, 0), axis=0)
    offsets = jax.random.randint(jax.random.fold_in(key, 102), (total_rows,), 0, 4096 - TOK_DEV + 1)
    doc_places = jnp.arange(total_rows, dtype=jnp.int32)
    offsets = jnp.where(doc_places == 0, 0, offsets)
    offsets = jnp.where(doc_places == doc_ids[total_rows - 1], 4095, offsets)
    return (begins.astype(jnp.int32), (places - begins + offsets[doc_ids]).astype(jnp.int32))


def draw_segments(key, part):
    doc_begins, position_ids = doc_layout(key)
    return doc_begins


def draw_positions(key, part):
    doc_begins, position_ids = doc_layout(key)
    return position_ids


def draw_attn_master(key, part):
    key = jax.random.fold_in(key, 7)
    noise = jnp.clip(jax.random.normal(key, (D, 4 * D), jnp.float32), -6.0, 6.0)
    columns = jnp.arange(4 * D)
    column_scale = jnp.where(columns < 3 * D, 1.0, 4.0) / jnp.sqrt(jnp.float32(D))
    return noise * column_scale[None, :]


def draw_norm_master(key, part):
    key = jax.random.fold_in(key, 8)
    key_gain, key_shift = jax.random.split(key)
    lift = jnp.arange(D, dtype=jnp.float32) / (D - 1)
    gain_noise = jnp.clip(jax.random.normal(key_gain, (7, D), jnp.float32), -2.0, 2.0)
    shift_noise = jnp.clip(jax.random.normal(key_shift, (7, D), jnp.float32), -2.0, 2.0)
    rising = 0.6 * jnp.exp(lift * jnp.log(3.0))
    gains = rising[None, :] * (1.0 + 0.1 * gain_noise)
    shifts = 0.3 * shift_noise
    row_ids = jnp.arange(7)[:, None]
    return jnp.where((row_ids == 0) | (row_ids == 5), gains, shifts)


def draw_cotangent(key, part):
    key = jax.random.fold_in(key, 9)
    key_noise, key_perm = jax.random.split(key)
    device_count = N_DP * N_SHARD
    total_rows = TOK_DEV * device_count
    lift = jnp.arange(D, dtype=jnp.float32) / (D - 1)
    noise = jnp.clip(jax.random.normal(key_noise, (total_rows, D), jnp.float32), -4.0, 4.0)
    rising = 0.6 * jnp.exp(lift * jnp.log(3.0))
    pairing = jax.random.permutation(key_perm, device_count)
    owner = pairing[jnp.arange(total_rows) // TOK_DEV]
    column_block = jnp.arange(D) // (D // device_count)
    spike = jnp.where(owner[:, None] == column_block[None, :], 3.0, 1.0)
    return (noise * rising[None, :] * spike).astype(jnp.bfloat16)


def shard_levels(key, shape, cuts, least, largest):
    gain = 1.0
    for position, parts in cuts:
        steps = jax.random.uniform(jax.random.fold_in(jax.random.fold_in(key, 6), position), (parts,), jnp.float32, least / len(cuts), largest / len(cuts))
        gain = gain * jnp.repeat(jnp.exp(steps), shape[position] // parts).reshape((-1,) + (1,) * (len(shape) - 1 - position))
    return gain


def gaussian(rng, shape, scale, limit, cuts=(), held_as=jnp.bfloat16):
    drawn = scale * jax.random.normal(rng, shape, jnp.float32)
    if cuts:
        drawn = drawn * shard_levels(rng, shape, cuts, -0.22, 0.18)
    return jnp.clip(drawn, -limit, limit).astype(held_as)


def setup_inputs(seed: int = 0) -> dict:
    streams_of = jax.random.split(jax.random.key(seed), 14)
    tokens = gaussian(streams_of[0], (TOKENS, D), 1.0, 6.0, ((0, 32),))
    cotangent = draw_cotangent(jax.random.fold_in(streams_of[13], 71), 0)
    segments = draw_segments(jax.random.fold_in(streams_of[13], 71), 0)
    positions = draw_positions(jax.random.fold_in(streams_of[13], 71), 0)
    attn_master = draw_attn_master(jax.random.fold_in(streams_of[13], 71), 0)
    mlp_master = gaussian(streams_of[5], (D, 3 * FF), D ** -0.5, 0.125, ((0, 32),), jnp.float32)
    norm_master = draw_norm_master(jax.random.fold_in(streams_of[13], 71), 0)
    attn_first = gaussian(streams_of[7], (D, 4 * D), (0.111 / (D * (4 * D + 3 * FF + 7)) ** 0.5), 0.00024414062, ((0, 32),), jnp.float32)
    mlp_first = gaussian(streams_of[8], (D, 3 * FF), (0.111 / (D * (4 * D + 3 * FF + 7)) ** 0.5), 0.00024414062, ((0, 32),), jnp.float32)
    norm_first = gaussian(streams_of[9], (7, D), (0.555 / (D * (4 * D + 3 * FF + 7)) ** 0.5), 0.0012207031, ((1, 32),), jnp.float32)
    attn_second = jnp.clip(jnp.exp(math.log(4.086035509942576e-09) - 1.3843913663428595 * jax.random.uniform(streams_of[10], (D, 4 * D), jnp.float32) ** shard_levels(streams_of[10], (D, 4 * D), ((0, 32),), -0.2, 0.2)), 1.023454654358602e-09, 4.086035509942576e-09)
    mlp_second = jnp.clip(jnp.exp(math.log(4.086035509942576e-09) - 1.3843913663428595 * jax.random.uniform(streams_of[11], (D, 3 * FF), jnp.float32) ** shard_levels(streams_of[11], (D, 3 * FF), ((0, 32),), -0.2, 0.2)), 1.023454654358602e-09, 4.086035509942576e-09)
    norm_second = jnp.clip(jnp.exp(math.log(1.0234546010678969e-07) - 1.38249925 * jax.random.uniform(streams_of[12], (7, D), jnp.float32) ** shard_levels(streams_of[12], (7, D), ((1, 32),), -0.2, 0.2)), 2.5683652538077695e-08, 1.0234546010678969e-07)
    return dict(tokens=tokens, cotangent=cotangent, segments=segments, positions=positions, attn_master=attn_master, mlp_master=mlp_master, norm_master=norm_master, attn_first=attn_first, mlp_first=mlp_first, norm_first=norm_first, attn_second=attn_second, mlp_second=mlp_second, norm_second=norm_second)


@jax.custom_vjp
def low(v):
    return lax.optimization_barrier(v.astype(jnp.bfloat16)).astype(jnp.float32)

@jax.custom_vjp
def low_back(v):
    return v

def low_keep(v):
    return (low(v), None)

def low_pass(kept, grad):
    return (grad,)

def back_keep(v):
    return (v, None)

def back_low(kept, grad):
    return (low(grad),)
low.defvjp(low_keep, low_pass)
low_back.defvjp(back_keep, back_low)
PRECISE = lax.Precision.HIGHEST
NORM_EPS = 1e-05
NEG_FILL = -1e+30
ROPE_BASE = 10000.0
CLIP_NORM = 1.0
BETA_ONE = 0.9
BETA_TWO = 0.95
ADAM_EPS = 1e-08
RATE_MATRIX = 0.02
RATE_VECTOR = 0.2
DECAY_MATRIX = 0.1

def layer_norm(values_in, gain_vec, shift_vec):
    average = lax.optimization_barrier(jnp.mean(values_in, axis=-1, keepdims=True))
    centered = values_in - average
    variance = lax.optimization_barrier(jnp.mean(centered * centered, axis=-1, keepdims=True))
    return centered * lax.rsqrt(variance + NORM_EPS) * gain_vec + shift_vec

def rotary_tables(position_ids):
    half_rot = ROT // 2
    inverse_freq = ROPE_BASE ** (-(jnp.arange(half_rot, dtype=jnp.float32) * 2.0 / ROT))
    angles = position_ids.astype(jnp.float32)[:, None] * inverse_freq[None, :]
    return (jnp.cos(angles)[:, None, :], jnp.sin(angles)[:, None, :])

def rotate(heads_in, cos_table, sin_table):
    half_rot = ROT // 2
    first_half = heads_in[..., :half_rot]
    second_half = heads_in[..., half_rot:ROT]
    rest_part = heads_in[..., ROT:]
    turned_one = first_half * cos_table - second_half * sin_table
    turned_two = second_half * cos_table + first_half * sin_table
    return jnp.concatenate([turned_one, turned_two, rest_part], -1)

def forward(attn_w, mlp_w, norm_w, inputs, seg_ids, position_ids):
    attn_w = low(attn_w)
    mlp_w = low(mlp_w)
    norm_w = low(norm_w)
    row_count = inputs.shape[0]
    seq_count = row_count // TOK_DEV
    normed1 = low(layer_norm(inputs, norm_w[0], norm_w[1]))
    qkv = low_back(jnp.dot(normed1, attn_w[:, :3 * D], precision=PRECISE) + norm_w[2:5].reshape(3 * D))
    cos_table, sin_table = rotary_tables(position_ids)
    queries = low(rotate(qkv[:, :D].reshape(row_count, HEADS, HEAD), cos_table, sin_table))
    key_rows = low(rotate(qkv[:, D:2 * D].reshape(row_count, HEADS, HEAD), cos_table, sin_table))
    values = low(qkv[:, 2 * D:].reshape(row_count, HEADS, HEAD))
    q_four = queries.reshape(seq_count, TOK_DEV, HEADS, HEAD)
    k_four = key_rows.reshape(seq_count, TOK_DEV, HEADS, HEAD)
    v_four = values.reshape(seq_count, TOK_DEV, HEADS, HEAD)
    scores = low_back(jnp.einsum('gshd,gthd->ghst', q_four, k_four, precision=PRECISE) * HEAD ** (-0.5))
    seg_grid = seg_ids.reshape(seq_count, TOK_DEV)
    places = jnp.arange(TOK_DEV)
    allowed = (seg_grid[:, :, None] == seg_grid[:, None, :]) & (places[:, None] >= places[None, :])[None]
    scores = jnp.where(allowed[:, None], scores, NEG_FILL)
    attend_low = low(jax.nn.softmax(scores, axis=-1))
    mixture = jnp.einsum('ghst,gthd->gshd', attend_low, v_four, precision=PRECISE).reshape(row_count, D)
    mixture = low(low_back(mixture))
    attention = low_back(jnp.dot(mixture, attn_w[:, 3 * D:], precision=PRECISE))
    resid = inputs + attention
    normed2 = low(layer_norm(resid, norm_w[5], norm_w[6]))
    gate_up = low_back(jnp.dot(normed2, mlp_w[:, :2 * FF], precision=PRECISE))
    hidden = low(jax.nn.silu(gate_up[:, :FF]) * gate_up[:, FF:])
    return resid + jnp.dot(hidden, mlp_w[:, 2 * FF:].T, precision=PRECISE)

def adam_update(master, first, second, grads, factor, rate, decay):
    clipped = grads * factor
    first_new = BETA_ONE * first + (1.0 - BETA_ONE) * clipped
    second_new = BETA_TWO * second + (1.0 - BETA_TWO) * clipped * clipped
    first_hat = first_new / (1.0 - BETA_ONE ** STEP)
    second_hat = second_new / (1.0 - BETA_TWO ** STEP)
    master_new = master - rate * (first_hat / (jnp.sqrt(second_hat) + ADAM_EPS) + decay * master)
    return (master_new, first_new, second_new)

def reference(tokens, cotangent, segments, positions, attn_master, mlp_master, norm_master, attn_first, mlp_first, norm_first, attn_second, mlp_second, norm_second):
    device_count = N_DP * N_SHARD
    per_group = 1
    for candidate in range(1, device_count + 1):
        if device_count % candidate == 0 and candidate * TOK_DEV <= 4096:
            per_group = candidate
    group_rows = per_group * TOK_DEV
    group_count = tokens.shape[0] // group_rows
    token_groups = tokens.astype(jnp.float32).reshape(group_count, group_rows, D)
    cot_groups = cotangent.astype(jnp.float32).reshape(group_count, group_rows, D)
    seg_groups = segments.reshape(group_count, group_rows)
    pos_groups = positions.reshape(group_count, group_rows)

    def accumulate(carried, slices):
        token_part, cot_part, seg_part, pos_part = slices

        def apply_block(attn_in, mlp_in, norm_in, token_in):
            return forward(attn_in, mlp_in, norm_in, token_in, seg_part, pos_part)
        result, pull_back = jax.vjp(apply_block, attn_master, mlp_master, norm_master, token_part)
        grad_attn, grad_mlp, grad_normp, grad_input = pull_back(cot_part)
        carried = (carried[0] + grad_attn, carried[1] + grad_mlp, carried[2] + grad_normp)
        return (carried, (result.astype(jnp.bfloat16), grad_input))
    zeros_init = (jnp.zeros_like(attn_master), jnp.zeros_like(mlp_master), jnp.zeros_like(norm_master))
    (grad_attn, grad_mlp, grad_normp), (out_groups, grad_groups) = lax.scan(accumulate, zeros_init, (token_groups, cot_groups, seg_groups, pos_groups))
    block_out = out_groups.reshape(tokens.shape[0], D)
    input_grad = grad_groups.reshape(tokens.shape[0], D)
    squares = jnp.sum(grad_attn * grad_attn) + jnp.sum(grad_mlp * grad_mlp) + jnp.sum(grad_normp * grad_normp)
    grad_norm = jnp.sqrt(squares)
    factor = CLIP_NORM / jnp.maximum(grad_norm, CLIP_NORM)
    attn_new, attn_first_new, attn_second_new = adam_update(attn_master, attn_first, attn_second, grad_attn, factor, RATE_MATRIX, DECAY_MATRIX)
    mlp_new, mlp_first_new, mlp_second_new = adam_update(mlp_master, mlp_first, mlp_second, grad_mlp, factor, RATE_MATRIX, DECAY_MATRIX)
    norm_new, norm_first_new, norm_second_new = adam_update(norm_master, norm_first, norm_second, grad_normp, factor, RATE_VECTOR, 0.0)
    return (block_out, input_grad, grad_norm, attn_new, mlp_new, norm_new, attn_first_new, mlp_first_new, norm_first_new, attn_second_new, mlp_second_new, norm_second_new)
```

```python
import jax
import jax.numpy as jnp
from jax import lax
from jax.sharding import PartitionSpec as P

D = 2048
HEADS = 32
HEAD = 64
FF = 5632
ROT = 16
STEP = 10


NORM_EPS = 1e-05
NEG_FILL = -1e30
ROPE_BASE = 10000.0
CLIP_NORM = 1.0
BETA_ONE = 0.9
BETA_TWO = 0.95
ADAM_EPS = 1e-08
RATE_MATRIX = 0.02
RATE_VECTOR = 0.2
DECAY_MATRIX = 0.1
LEAD_DIMS = (((0,), (0,)), ((), ()))
LAST_DIMS = (((1,), (1,)), ((), ()))


def layer_norm(values_in, gain_vec, shift_vec):
    average = jnp.mean(values_in, axis=-1, keepdims=True)
    centered = values_in - average
    variance = jnp.mean(centered * centered, axis=-1, keepdims=True)
    return centered * lax.rsqrt(variance + NORM_EPS) * gain_vec + shift_vec


def rotary_tables(position_ids):
    half_rot = ROT // 2
    inverse_freq = ROPE_BASE ** (-(jnp.arange(half_rot, dtype=jnp.float32) * 2.0 / ROT))
    angles = position_ids.astype(jnp.float32)[:, None] * inverse_freq[None, :]
    return (jnp.cos(angles)[:, None, :], jnp.sin(angles)[:, None, :])


def rotate(heads_in, cos_table, sin_table):
    half_rot = ROT // 2
    first_half = heads_in[..., :half_rot]
    second_half = heads_in[..., half_rot:ROT]
    rest_part = heads_in[..., ROT:]
    turned_one = first_half * cos_table - second_half * sin_table
    turned_two = second_half * cos_table + first_half * sin_table
    return jnp.concatenate([turned_one, turned_two, rest_part], -1)


def pad_last(array, size):
    missing = size - array.shape[-1]
    if missing == 0:
        return array
    return jnp.pad(array, [(0, 0)] * (array.ndim - 1) + [(0, missing)])


def activate(gate_part, up_part):
    return jax.nn.silu(gate_part) * up_part


def adam_update(master, first, second, grads, factor, rate, decay):
    clipped = grads * factor
    first_new = BETA_ONE * first + (1.0 - BETA_ONE) * clipped
    second_new = BETA_TWO * second + (1.0 - BETA_TWO) * clipped * clipped
    first_hat = first_new / (1.0 - BETA_ONE**STEP)
    second_hat = second_new / (1.0 - BETA_TWO**STEP)
    master_new = master - rate * (first_hat / (jnp.sqrt(second_hat) + ADAM_EPS) + decay * master)
    return (master_new, first_new, second_new)


def exchange_dp(blocks):
    return lax.all_to_all(blocks, "dp", 0, 0, tiled=True)


def gather_dp(rows):
    return lax.all_gather(rows, "dp", axis=0, tiled=True)


def scatter_sum_dp(parts):
    return lax.psum_scatter(parts, "dp", scatter_dimension=0, tiled=True)


def gather_shard(block):
    return lax.all_gather(block, "shard", axis=1)


def scatter_sum_shard(parts):
    return lax.psum_scatter(parts, "shard", scatter_dimension=1)


def layer_stats(values_in):
    average = jnp.mean(values_in, axis=-1, keepdims=True)
    centered = values_in - average
    variance = jnp.mean(centered * centered, axis=-1, keepdims=True)
    inverse = lax.rsqrt(variance + NORM_EPS)
    return centered * inverse, inverse


def layer_back(grads, gain_vec, unit, inverse):
    scaled = grads * gain_vec
    mean_one = jnp.mean(scaled, axis=-1, keepdims=True)
    mean_two = jnp.mean(scaled * unit, axis=-1, keepdims=True)
    return inverse * (scaled - mean_one - unit * mean_two)


def per_device(
    tokens,
    cotangent,
    segments,
    positions,
    attn_master,
    mlp_master,
    norm_master,
    attn_first,
    mlp_first,
    norm_first,
    attn_second,
    mlp_second,
    norm_second,
):
    low = jnp.bfloat16
    full = jnp.float32
    n_dp = lax.axis_size("dp")
    n_sh = lax.axis_size("shard")
    seq = tokens.shape[0]
    rows = attn_master.shape[0]
    heads = HEADS // n_dp
    width = D // n_dp
    ff_width = -(-FF // (128 * n_dp)) * 128
    ff_pad = ff_width * n_dp
    scale = HEAD ** (-0.5)

    qkv_send = attn_master[:, : 3 * D].astype(low).reshape(rows, 3, n_dp, width)
    qkv_send = qkv_send.transpose(2, 0, 1, 3).reshape(n_dp, rows, 3 * width)
    mlp_send = pad_last(mlp_master.astype(low).reshape(rows, 3, FF), ff_pad)
    mlp_send = mlp_send.reshape(rows, 3, n_dp, ff_width)
    mlp_send = mlp_send.transpose(2, 0, 1, 3).reshape(n_dp, rows, 3 * ff_width)
    norm_full = lax.all_gather(norm_master.astype(low), ("dp", "shard"), axis=1, tiled=True)
    norm_vals = norm_full.astype(full)
    w_qkv = gather_shard(exchange_dp(qkv_send)).reshape(D, 3 * width)
    w_out = gather_shard(attn_master[None, :, 3 * D :].astype(low)).reshape(width, D)
    tokens_all = gather_dp(tokens)
    places_all = gather_dp(jnp.stack([segments, positions], 0)[None])
    cot_all = gather_dp(cotangent)
    w_mlp = gather_shard(exchange_dp(mlp_send)).reshape(D, 3 * ff_width)
    w_gu = w_mlp[:, : 2 * ff_width]
    w_down = w_mlp[:, 2 * ff_width :]
    seg_all, pos_all = places_all[:, 0], places_all[:, 1]

    inputs_all = tokens_all.astype(full)
    unit1, _ = layer_stats(inputs_all)
    normed1 = (unit1 * norm_vals[0] + norm_vals[1]).astype(low)
    my_dp = lax.axis_index("dp")
    bias = lax.dynamic_slice(norm_vals[2:5], (0, my_dp * width), (3, width)).reshape(3 * width)
    qkv = jnp.dot(normed1, w_qkv, preferred_element_type=full) + bias
    qkv = qkv.reshape(n_dp * seq, 3 * heads, HEAD)
    cos_table, sin_table = rotary_tables(pos_all.reshape(-1))

    def split(array):
        return array.reshape(n_dp, seq, heads, HEAD)

    queries = split(rotate(qkv[:, :heads], cos_table, sin_table).astype(low))
    key_rows = split(rotate(qkv[:, heads : 2 * heads], cos_table, sin_table).astype(low))
    values = split(qkv[:, 2 * heads :].astype(low))
    places = jnp.arange(seq)
    allowed = (seg_all[:, :, None] == seg_all[:, None, :]) & (
        places[:, None] >= places[None, :]
    )[None]
    scores = (
        jnp.einsum("gshd,gthd->ghst", queries, key_rows, preferred_element_type=full) * scale
    )
    scores = jnp.where(allowed[:, None], scores, NEG_FILL)
    attend = jax.nn.softmax(scores, axis=-1)
    attend_low = attend.astype(low)
    mixture = (
        jnp.einsum("ghst,gthd->gshd", attend_low, values, preferred_element_type=full)
        .reshape(n_dp * seq, width)
        .astype(low)
    )
    attn_part = jnp.dot(mixture, w_out, preferred_element_type=full).astype(low)
    resid = tokens.astype(full) + scatter_sum_dp(attn_part).astype(full)
    unit2, inverse2 = layer_stats(resid)
    normed2 = gather_dp((unit2 * norm_vals[5] + norm_vals[6]).astype(low))
    gate_up = jnp.dot(normed2, w_gu, preferred_element_type=full)
    hidden_f, act_pull = jax.vjp(activate, gate_up[:, :ff_width], gate_up[:, ff_width:])
    hidden = hidden_f.astype(low)
    grad_hidden = jnp.dot(cot_all, w_down, preferred_element_type=full)
    grad_gate, grad_up = act_pull(grad_hidden)
    grad_gu = jnp.concatenate([grad_gate, grad_up], 1).astype(low)
    norm2_part = lax.dot_general(grad_gu, w_gu, LAST_DIMS, preferred_element_type=full)
    grad_norm2 = scatter_sum_dp(norm2_part.astype(low)).astype(full)
    out_part = lax.dot_general(hidden, w_down, LAST_DIMS, preferred_element_type=full)
    block_out = (resid + scatter_sum_dp(out_part.astype(low)).astype(full)).astype(low)
    part_gu = lax.dot_general(normed2, grad_gu, LEAD_DIMS, preferred_element_type=full)
    part_down = lax.dot_general(cot_all, hidden, LEAD_DIMS, preferred_element_type=full)
    part_mlp = jnp.concatenate([part_gu.astype(low), part_down.astype(low)], 1)
    mlp_sum = scatter_sum_shard(part_mlp.reshape(n_dp, n_sh, rows, 3 * ff_width))

    grad_gain2 = jnp.sum(grad_norm2 * unit2, axis=0)
    grad_shift2 = jnp.sum(grad_norm2, axis=0)
    grad_resid = cotangent.astype(full) + layer_back(grad_norm2, norm_vals[5], unit2, inverse2)
    grad_attn_out = gather_dp(grad_resid.astype(low))
    grad_mixture = lax.dot_general(grad_attn_out, w_out, LAST_DIMS, preferred_element_type=full)
    grad_mixture = split(grad_mixture.astype(low))
    grad_attend = jnp.einsum("gshd,gthd->ghst", grad_mixture, values, preferred_element_type=full)
    grad_values = jnp.einsum(
        "ghst,gshd->gthd", attend_low, grad_mixture, preferred_element_type=full
    )
    grad_scores = (
        attend * (grad_attend - jnp.sum(attend * grad_attend, axis=-1, keepdims=True))
    ).astype(low)
    grad_queries = (
        jnp.einsum("ghst,gthd->gshd", grad_scores, key_rows, preferred_element_type=full) * scale
    )
    grad_keys = (
        jnp.einsum("ghst,gshd->gthd", grad_scores, queries, preferred_element_type=full) * scale
    )

    def turn_back(grads):
        grads = grads.reshape(n_dp * seq, heads, HEAD)
        return rotate(grads, cos_table, -sin_table).reshape(n_dp * seq, width)

    grad_qkv = jnp.concatenate(
        [
            turn_back(grad_queries),
            turn_back(grad_keys),
            grad_values.reshape(n_dp * seq, width),
        ],
        1,
    ).astype(low)
    part_qkv = lax.dot_general(normed1, grad_qkv, LEAD_DIMS, preferred_element_type=full)
    part_out = lax.dot_general(mixture, grad_attn_out, LEAD_DIMS, preferred_element_type=full)
    qkv_sum = scatter_sum_shard(part_qkv.astype(low).reshape(n_dp, n_sh, rows, 3 * width))
    out_sum = scatter_sum_shard(part_out.astype(low).reshape(1, n_sh, rows, D))[0].astype(full)

    norm1_part = lax.dot_general(grad_qkv, w_qkv, LAST_DIMS, preferred_element_type=full)
    grad_gain1 = jnp.sum(norm1_part * unit1, axis=0)
    grad_shift1 = jnp.sum(norm1_part, axis=0)
    grad_bias = jnp.sum(grad_qkv, axis=0, dtype=full).reshape(3, width)
    grad_norm1 = scatter_sum_dp(norm1_part.astype(low)).astype(full)
    own_unit1, own_inverse1 = layer_stats(tokens.astype(full))
    input_grad = grad_resid + layer_back(grad_norm1, norm_vals[0], own_unit1, own_inverse1)
    norm_term = lax.dynamic_update_slice(
        jnp.zeros((3, D), full), grad_bias, (0, my_dp * width)
    )
    norm_term = jnp.concatenate(
        [grad_gain1[None], grad_shift1[None], norm_term, grad_gain2[None], grad_shift2[None]], 0
    )
    norm_grad = lax.psum_scatter(norm_term, ("dp", "shard"), scatter_dimension=1, tiled=True)

    def columns_back(summed, parts, part_width, keep):
        back = exchange_dp(summed).reshape(n_dp, rows, parts, part_width)
        back = back.transpose(1, 2, 0, 3).reshape(rows, parts, n_dp * part_width)
        return back[:, :, :keep].reshape(rows, parts * keep).astype(full)

    mlp_grad = columns_back(mlp_sum, 3, ff_width, FF)
    attn_grad = jnp.concatenate([columns_back(qkv_sum, 3, width, D), out_sum], 1)
    squares = (
        jnp.sum(attn_grad * attn_grad)
        + jnp.sum(mlp_grad * mlp_grad)
        + jnp.sum(norm_grad * norm_grad)
    )
    overall = lax.psum(squares, ("dp", "shard"))
    grad_size = jnp.sqrt(overall)
    factor = CLIP_NORM / jnp.maximum(grad_size, CLIP_NORM)
    attn_new, attn_first_new, attn_second_new = adam_update(
        attn_master, attn_first, attn_second, attn_grad, factor, RATE_MATRIX, DECAY_MATRIX
    )
    mlp_new, mlp_first_new, mlp_second_new = adam_update(
        mlp_master, mlp_first, mlp_second, mlp_grad, factor, RATE_MATRIX, DECAY_MATRIX
    )
    norm_new, norm_first_new, norm_second_new = adam_update(
        norm_master, norm_first, norm_second, norm_grad, factor, RATE_VECTOR, 0.0
    )
    return (
        block_out,
        input_grad,
        grad_size,
        attn_new,
        mlp_new,
        norm_new,
        attn_first_new,
        mlp_first_new,
        norm_first_new,
        attn_second_new,
        mlp_second_new,
        norm_second_new,
    )


def solution(mesh):
    in_specs = (
        P(("dp", "shard"), None),
        P(("dp", "shard"), None),
        P(("dp", "shard")),
        P(("dp", "shard")),
        P(("dp", "shard"), None),
        P(("dp", "shard"), None),
        P(None, ("dp", "shard")),
        P(("dp", "shard"), None),
        P(("dp", "shard"), None),
        P(None, ("dp", "shard")),
        P(("dp", "shard"), None),
        P(("dp", "shard"), None),
        P(None, ("dp", "shard")),
    )
    out_specs = (
        P(("dp", "shard"), None),
        P(("dp", "shard"), None),
        P(),
        P(("dp", "shard"), None),
        P(("dp", "shard"), None),
        P(None, ("dp", "shard")),
        P(("dp", "shard"), None),
        P(("dp", "shard"), None),
        P(None, ("dp", "shard")),
        P(("dp", "shard"), None),
        P(("dp", "shard"), None),
        P(None, ("dp", "shard")),
    )
    return jax.shard_map(
        per_device, mesh=mesh, in_specs=in_specs, out_specs=out_specs, check_vma=False
    )
```

```python
import functools

import numpy as np
import jax
import jax.numpy as jnp
from jax import lax
from jax.experimental import pallas as pl
from jax.experimental.pallas import tpu as pltpu
from jax.sharding import PartitionSpec as P

D = 2048
HEADS = 32
HEAD = 64
FF = 5632
ROT = 16
STEP = 10


NORM_EPS = 1e-05
NEG_FILL = -1e30
ROPE_BASE = 10000.0
CLIP_NORM = 1.0
BETA_ONE = 0.9
BETA_TWO = 0.95
ADAM_EPS = 1e-08
RATE_MATRIX = 0.02
RATE_VECTOR = 0.2
DECAY_MATRIX = 0.1
LEAD_DIMS = (((0,), (0,)), ((), ()))
LAST_DIMS = (((1,), (1,)), ((), ()))


def layer_norm(values_in, gain_vec, shift_vec):
    average = jnp.mean(values_in, axis=-1, keepdims=True)
    centered = values_in - average
    variance = jnp.mean(centered * centered, axis=-1, keepdims=True)
    return centered * lax.rsqrt(variance + NORM_EPS) * gain_vec + shift_vec


def rotary_tables(position_ids):
    half_rot = ROT // 2
    inverse_freq = ROPE_BASE ** (-(jnp.arange(half_rot, dtype=jnp.float32) * 2.0 / ROT))
    angles = position_ids.astype(jnp.float32)[:, None] * inverse_freq[None, :]
    return (jnp.cos(angles)[:, None, :], jnp.sin(angles)[:, None, :])


def rotate(heads_in, cos_table, sin_table):
    half_rot = ROT // 2
    first_half = heads_in[..., :half_rot]
    second_half = heads_in[..., half_rot:ROT]
    rest_part = heads_in[..., ROT:]
    turned_one = first_half * cos_table - second_half * sin_table
    turned_two = second_half * cos_table + first_half * sin_table
    return jnp.concatenate([turned_one, turned_two, rest_part], -1)


def pad_last(array, size):
    missing = size - array.shape[-1]
    if missing == 0:
        return array
    return jnp.pad(array, [(0, 0)] * (array.ndim - 1) + [(0, missing)])


def activate(gate_part, up_part):
    return jax.nn.silu(gate_part) * up_part


def adam_update(master, first, second, grads, factor, rate, decay):
    clipped = grads * factor
    first_new = BETA_ONE * first + (1.0 - BETA_ONE) * clipped
    second_new = BETA_TWO * second + (1.0 - BETA_TWO) * clipped * clipped
    first_hat = first_new / (1.0 - BETA_ONE**STEP)
    second_hat = second_new / (1.0 - BETA_TWO**STEP)
    master_new = master - rate * (first_hat / (jnp.sqrt(second_hat) + ADAM_EPS) + decay * master)
    return (master_new, first_new, second_new)


def exchange_dp(blocks):
    return lax.all_to_all(blocks, "dp", 0, 0, tiled=True)


def gather_dp(rows):
    return lax.all_gather(rows, "dp", axis=0, tiled=True)


def scatter_sum_dp(parts):
    return lax.psum_scatter(parts, "dp", scatter_dimension=0, tiled=True)


def gather_shard(block):
    return lax.all_gather(block, "shard", axis=1)


def scatter_sum_shard(parts):
    return lax.psum_scatter(parts, "shard", scatter_dimension=1)


def layer_stats(values_in):
    average = jnp.mean(values_in, axis=-1, keepdims=True)
    centered = values_in - average
    variance = jnp.mean(centered * centered, axis=-1, keepdims=True)
    inverse = lax.rsqrt(variance + NORM_EPS)
    return centered * inverse, inverse


def layer_back(grads, gain_vec, unit, inverse):
    scaled = grads * gain_vec
    mean_one = jnp.mean(scaled, axis=-1, keepdims=True)
    mean_two = jnp.mean(scaled * unit, axis=-1, keepdims=True)
    return inverse * (scaled - mean_one - unit * mean_two)


def per_device_any(
    tokens,
    cotangent,
    segments,
    positions,
    attn_master,
    mlp_master,
    norm_master,
    attn_first,
    mlp_first,
    norm_first,
    attn_second,
    mlp_second,
    norm_second,
):
    low = jnp.bfloat16
    full = jnp.float32
    n_dp = lax.axis_size("dp")
    n_sh = lax.axis_size("shard")
    seq = tokens.shape[0]
    rows = attn_master.shape[0]
    heads = HEADS // n_dp
    width = D // n_dp
    ff_width = -(-FF // (128 * n_dp)) * 128
    ff_pad = ff_width * n_dp
    scale = HEAD ** (-0.5)

    qkv_send = attn_master[:, : 3 * D].astype(low).reshape(rows, 3, n_dp, width)
    qkv_send = qkv_send.transpose(2, 0, 1, 3).reshape(n_dp, rows, 3 * width)
    mlp_send = pad_last(mlp_master.astype(low).reshape(rows, 3, FF), ff_pad)
    mlp_send = mlp_send.reshape(rows, 3, n_dp, ff_width)
    mlp_send = mlp_send.transpose(2, 0, 1, 3).reshape(n_dp, rows, 3 * ff_width)
    norm_full = lax.all_gather(norm_master.astype(low), ("dp", "shard"), axis=1, tiled=True)
    norm_vals = norm_full.astype(full)
    w_qkv = gather_shard(exchange_dp(qkv_send)).reshape(D, 3 * width)
    w_out = gather_shard(attn_master[None, :, 3 * D :].astype(low)).reshape(width, D)
    tokens_all = gather_dp(tokens)
    places_all = gather_dp(jnp.stack([segments, positions], 0)[None])
    cot_all = gather_dp(cotangent)
    w_mlp = gather_shard(exchange_dp(mlp_send)).reshape(D, 3 * ff_width)
    w_gu = w_mlp[:, : 2 * ff_width]
    w_down = w_mlp[:, 2 * ff_width :]
    seg_all, pos_all = places_all[:, 0], places_all[:, 1]

    inputs_all = tokens_all.astype(full)
    unit1, _ = layer_stats(inputs_all)
    normed1 = (unit1 * norm_vals[0] + norm_vals[1]).astype(low)
    my_dp = lax.axis_index("dp")
    bias = lax.dynamic_slice(norm_vals[2:5], (0, my_dp * width), (3, width)).reshape(3 * width)
    qkv = jnp.dot(normed1, w_qkv, preferred_element_type=full) + bias
    qkv = qkv.reshape(n_dp * seq, 3 * heads, HEAD)
    cos_table, sin_table = rotary_tables(pos_all.reshape(-1))

    def split(array):
        return array.reshape(n_dp, seq, heads, HEAD)

    queries = split(rotate(qkv[:, :heads], cos_table, sin_table).astype(low))
    key_rows = split(rotate(qkv[:, heads : 2 * heads], cos_table, sin_table).astype(low))
    values = split(qkv[:, 2 * heads :].astype(low))
    places = jnp.arange(seq)
    allowed = (seg_all[:, :, None] == seg_all[:, None, :]) & (
        places[:, None] >= places[None, :]
    )[None]
    scores = (
        jnp.einsum("gshd,gthd->ghst", queries, key_rows, preferred_element_type=full) * scale
    )
    scores = jnp.where(allowed[:, None], scores, NEG_FILL)
    attend = jax.nn.softmax(scores, axis=-1)
    attend_low = attend.astype(low)
    mixture = (
        jnp.einsum("ghst,gthd->gshd", attend_low, values, preferred_element_type=full)
        .reshape(n_dp * seq, width)
        .astype(low)
    )
    attn_part = jnp.dot(mixture, w_out, preferred_element_type=full).astype(low)
    resid = tokens.astype(full) + scatter_sum_dp(attn_part).astype(full)
    unit2, inverse2 = layer_stats(resid)
    normed2 = gather_dp((unit2 * norm_vals[5] + norm_vals[6]).astype(low))
    gate_up = jnp.dot(normed2, w_gu, preferred_element_type=full)
    hidden_f, act_pull = jax.vjp(activate, gate_up[:, :ff_width], gate_up[:, ff_width:])
    hidden = hidden_f.astype(low)
    grad_hidden = jnp.dot(cot_all, w_down, preferred_element_type=full)
    grad_gate, grad_up = act_pull(grad_hidden)
    grad_gu = jnp.concatenate([grad_gate, grad_up], 1).astype(low)
    norm2_part = lax.dot_general(grad_gu, w_gu, LAST_DIMS, preferred_element_type=full)
    grad_norm2 = scatter_sum_dp(norm2_part.astype(low)).astype(full)
    out_part = lax.dot_general(hidden, w_down, LAST_DIMS, preferred_element_type=full)
    block_out = (resid + scatter_sum_dp(out_part.astype(low)).astype(full)).astype(low)
    part_gu = lax.dot_general(normed2, grad_gu, LEAD_DIMS, preferred_element_type=full)
    part_down = lax.dot_general(cot_all, hidden, LEAD_DIMS, preferred_element_type=full)
    part_mlp = jnp.concatenate([part_gu.astype(low), part_down.astype(low)], 1)
    mlp_sum = scatter_sum_shard(part_mlp.reshape(n_dp, n_sh, rows, 3 * ff_width))

    grad_gain2 = jnp.sum(grad_norm2 * unit2, axis=0)
    grad_shift2 = jnp.sum(grad_norm2, axis=0)
    grad_resid = cotangent.astype(full) + layer_back(grad_norm2, norm_vals[5], unit2, inverse2)
    grad_attn_out = gather_dp(grad_resid.astype(low))
    grad_mixture = lax.dot_general(grad_attn_out, w_out, LAST_DIMS, preferred_element_type=full)
    grad_mixture = split(grad_mixture.astype(low))
    grad_attend = jnp.einsum("gshd,gthd->ghst", grad_mixture, values, preferred_element_type=full)
    grad_values = jnp.einsum(
        "ghst,gshd->gthd", attend_low, grad_mixture, preferred_element_type=full
    )
    grad_scores = (
        attend * (grad_attend - jnp.sum(attend * grad_attend, axis=-1, keepdims=True))
    ).astype(low)
    grad_queries = (
        jnp.einsum("ghst,gthd->gshd", grad_scores, key_rows, preferred_element_type=full) * scale
    )
    grad_keys = (
        jnp.einsum("ghst,gshd->gthd", grad_scores, queries, preferred_element_type=full) * scale
    )

    def turn_back(grads):
        grads = grads.reshape(n_dp * seq, heads, HEAD)
        return rotate(grads, cos_table, -sin_table).reshape(n_dp * seq, width)

    grad_qkv = jnp.concatenate(
        [
            turn_back(grad_queries),
            turn_back(grad_keys),
            grad_values.reshape(n_dp * seq, width),
        ],
        1,
    ).astype(low)
    part_qkv = lax.dot_general(normed1, grad_qkv, LEAD_DIMS, preferred_element_type=full)
    part_out = lax.dot_general(mixture, grad_attn_out, LEAD_DIMS, preferred_element_type=full)
    qkv_sum = scatter_sum_shard(part_qkv.astype(low).reshape(n_dp, n_sh, rows, 3 * width))
    out_sum = scatter_sum_shard(part_out.astype(low).reshape(1, n_sh, rows, D))[0].astype(full)

    norm1_part = lax.dot_general(grad_qkv, w_qkv, LAST_DIMS, preferred_element_type=full)
    grad_gain1 = jnp.sum(norm1_part * unit1, axis=0)
    grad_shift1 = jnp.sum(norm1_part, axis=0)
    grad_bias = jnp.sum(grad_qkv, axis=0, dtype=full).reshape(3, width)
    grad_norm1 = scatter_sum_dp(norm1_part.astype(low)).astype(full)
    own_unit1, own_inverse1 = layer_stats(tokens.astype(full))
    input_grad = grad_resid + layer_back(grad_norm1, norm_vals[0], own_unit1, own_inverse1)
    norm_term = lax.dynamic_update_slice(
        jnp.zeros((3, D), full), grad_bias, (0, my_dp * width)
    )
    norm_term = jnp.concatenate(
        [grad_gain1[None], grad_shift1[None], norm_term, grad_gain2[None], grad_shift2[None]], 0
    )
    norm_grad = lax.psum_scatter(norm_term, ("dp", "shard"), scatter_dimension=1, tiled=True)

    def columns_back(summed, parts, part_width, keep):
        back = exchange_dp(summed).reshape(n_dp, rows, parts, part_width)
        back = back.transpose(1, 2, 0, 3).reshape(rows, parts, n_dp * part_width)
        return back[:, :, :keep].reshape(rows, parts * keep).astype(full)

    mlp_grad = columns_back(mlp_sum, 3, ff_width, FF)
    attn_grad = jnp.concatenate([columns_back(qkv_sum, 3, width, D), out_sum], 1)
    squares = (
        jnp.sum(attn_grad * attn_grad)
        + jnp.sum(mlp_grad * mlp_grad)
        + jnp.sum(norm_grad * norm_grad)
    )
    overall = lax.psum(squares, ("dp", "shard"))
    grad_size = jnp.sqrt(overall)
    factor = CLIP_NORM / jnp.maximum(grad_size, CLIP_NORM)
    attn_new, attn_first_new, attn_second_new = adam_update(
        attn_master, attn_first, attn_second, attn_grad, factor, RATE_MATRIX, DECAY_MATRIX
    )
    mlp_new, mlp_first_new, mlp_second_new = adam_update(
        mlp_master, mlp_first, mlp_second, mlp_grad, factor, RATE_MATRIX, DECAY_MATRIX
    )
    norm_new, norm_first_new, norm_second_new = adam_update(
        norm_master, norm_first, norm_second, norm_grad, factor, RATE_VECTOR, 0.0
    )
    return (
        block_out,
        input_grad,
        grad_size,
        attn_new,
        mlp_new,
        norm_new,
        attn_first_new,
        mlp_first_new,
        norm_first_new,
        attn_second_new,
        mlp_second_new,
        norm_second_new,
    )


MESH = pl.DeviceIdType.MESH
ANY = pl.BlockSpec(memory_space=pl.ANY)
VMEM = pl.BlockSpec(memory_space=pltpu.VMEM)
LOW = jnp.bfloat16
FULL = jnp.float32
N_DP = 4
N_SH = 8
BIG_VMEM = 56 * 1024 * 1024


def dp_peer(step):
    mine = lax.axis_index("dp")
    if step == 1:
        return mine + 1 - 2 * (mine % 2)
    if step == 2:
        return (mine + 2) % 4
    return 3 - mine


def to_dp(step):
    return (dp_peer(step), lax.axis_index("shard"))


def to_shard(step):
    return (lax.axis_index("dp"), (lax.axis_index("shard") + step) % N_SH)


def greet(peers):
    barrier = pltpu.get_barrier_semaphore()
    for peer in peers:
        pl.semaphore_signal(barrier, inc=1, device_id=peer, device_id_type=MESH)
    pl.semaphore_wait(barrier, len(peers))


def remote(source, target, sems, index, peer):
    return pltpu.make_async_remote_copy(
        src_ref=source,
        dst_ref=target,
        send_sem=sems[0].at[index],
        recv_sem=sems[1].at[index],
        device_id=peer,
        device_id_type=MESH,
    )


def sems(count):
    return [pltpu.SemaphoreType.DMA((count,)), pltpu.SemaphoreType.DMA((count,))]


def comm_params(number):
    return pltpu.CompilerParams(
        collective_id=number, has_side_effects=True, vmem_limit_bytes=BIG_VMEM
    )


def sum_small_kernel(x_ref, out_ref, near, far, part, send_a, recv_a, send_b, recv_b):
    greet([to_dp(k) for k in (1, 2, 3)] + [to_shard(j) for j in range(1, N_SH)])
    copies = [
        remote(x_ref, near.at[k - 1], (send_a, recv_a), k - 1, to_dp(k)) for k in (1, 2, 3)
    ]
    for copy in copies:
        copy.start()
    for copy in copies:
        copy.wait()
    part[...] = x_ref[...] + near[0] + near[1] + near[2]
    copies = [
        remote(part, far.at[j - 1], (send_b, recv_b), j - 1, to_shard(j)) for j in range(1, N_SH)
    ]
    for copy in copies:
        copy.start()
    for copy in copies:
        copy.wait()
    total = part[...]
    for j in range(N_SH - 1):
        total = total + far[j]
    out_ref[...] = total


def sum_small(value, number):
    shape = value.shape
    return pl.pallas_call(
        sum_small_kernel,
        out_shape=jax.ShapeDtypeStruct(shape, FULL),
        in_specs=[VMEM],
        out_specs=VMEM,
        scratch_shapes=[
            pltpu.VMEM((N_DP - 1,) + shape, FULL),
            pltpu.VMEM((N_SH - 1,) + shape, FULL),
            pltpu.VMEM(shape, FULL),
        ]
        + sems(N_DP - 1)
        + sems(N_SH - 1),
        compiler_params=comm_params(number),
        name="sum_small",
    )(value)


def exchange_kernel(count, *refs):
    ins, outs, (send, recv, local) = refs[:count], refs[count : 2 * count], refs[2 * count :]
    mine = lax.axis_index("dp")
    greet([to_dp(k) for k in (1, 2, 3)])
    copies = []
    for n in range(count):
        for k in (3, 1, 2):
            copies.append(
                remote(
                    ins[n].at[dp_peer(k)],
                    outs[n].at[mine],
                    (send, recv),
                    3 * n + k - 1,
                    to_dp(k),
                )
            )
    own = [
        pltpu.make_async_copy(ins[n].at[mine], outs[n].at[mine], local.at[n])
        for n in range(count)
    ]
    for copy in copies + own:
        copy.start()
    for copy in copies + own:
        copy.wait()


def exchange(arrays, number):
    count = len(arrays)
    return pl.pallas_call(
        functools.partial(exchange_kernel, count),
        out_shape=[jax.ShapeDtypeStruct(a.shape, a.dtype) for a in arrays],
        in_specs=[ANY] * count,
        out_specs=[ANY] * count,
        scratch_shapes=sems(3 * count) + [pltpu.SemaphoreType.DMA((count,))],
        compiler_params=comm_params(number),
        name="exchange",
    )(*arrays)


def spread(own, result, sem_pair, base, relays):
    half = own.shape[0] // 2
    top, bottom = pl.ds(0, half), pl.ds(half, half)
    sent = [
        remote(own.at[top], result.at[1, top], sem_pair, base + 0, to_dp(1)),
        remote(own.at[bottom], result.at[2, bottom], sem_pair, base + 1, to_dp(2)),
        remote(own.at[bottom], result.at[1, bottom], sem_pair, base + 2, to_dp(1)),
        remote(own.at[top], result.at[2, top], sem_pair, base + 3, to_dp(2)),
    ]
    passed = [
        remote(result.at[1, top], result.at[3, top], sem_pair, base + 4, to_dp(2)),
        remote(result.at[2, bottom], result.at[3, bottom], sem_pair, base + 5, to_dp(1)),
    ]
    for copy in sent:
        copy.start()
    return sent, passed


def pass_on(sent, passed):
    sent[0].wait_recv()
    passed[0].start()
    sent[1].wait_recv()
    passed[1].start()


def spread_end(sent, passed):
    sent[2].wait_recv()
    sent[3].wait_recv()
    passed[0].wait_recv()
    passed[1].wait_recv()
    for copy in sent + passed:
        copy.wait_send()


def start_kernel(
    tok_ref, cot_ref, place_ref, mlp_ref, tok_all, cot_all, place_all, mlp_out, send, recv, local
):
    mine = lax.axis_index("dp")
    greet([to_dp(k) for k in (1, 2, 3)])
    pair = (send, recv)
    places = [
        remote(place_ref, place_all.at[k], pair, 12 + k - 1, to_dp(k)) for k in (1, 2, 3)
    ]
    blocks = [
        remote(mlp_ref.at[dp_peer(k)], mlp_out.at[mine], pair, 15 + k - 1, to_dp(k))
        for k in (3, 1, 2)
    ]
    own = [
        pltpu.make_async_copy(tok_ref, tok_all.at[0], local.at[0]),
        pltpu.make_async_copy(cot_ref, cot_all.at[0], local.at[1]),
        pltpu.make_async_copy(place_ref, place_all.at[0], local.at[2]),
        pltpu.make_async_copy(mlp_ref.at[mine], mlp_out.at[mine], local.at[3]),
    ]
    tok = spread(tok_ref, tok_all, pair, 0, True)
    for copy in places + own:
        copy.start()
    pass_on(*tok)
    for copy in blocks:
        copy.start()
    cot = spread(cot_ref, cot_all, pair, 6, True)
    pass_on(*cot)
    spread_end(*tok)
    spread_end(*cot)
    for copy in places + own + blocks:
        copy.wait()


def start(tokens, cotangent, places, mlp_send, number):
    group = jax.ShapeDtypeStruct((N_DP,) + tokens.shape, tokens.dtype)
    return pl.pallas_call(
        start_kernel,
        out_shape=[
            group,
            group,
            jax.ShapeDtypeStruct((N_DP,) + places.shape, places.dtype),
            jax.ShapeDtypeStruct(mlp_send.shape, mlp_send.dtype),
        ],
        in_specs=[ANY] * 4,
        out_specs=[ANY] * 4,
        scratch_shapes=sems(18) + [pltpu.SemaphoreType.DMA((4,))],
        compiler_params=comm_params(number),
        name="start",
    )(tokens, cotangent, places, mlp_send)


def unit_rows(values):
    average = jnp.mean(values, axis=-1, keepdims=True)
    centered = values - average
    variance = jnp.mean(centered * centered, axis=-1, keepdims=True)
    inverse = lax.rsqrt(variance + NORM_EPS)
    return centered * inverse, inverse


def turn(value, cos_ref, up_ref, down_ref, sign):
    left = pltpu.roll(value, 128 - ROT // 2, 1)
    right = pltpu.roll(value, ROT // 2, 1)
    return value * cos_ref[...] + sign * (left * up_ref[...] + right * down_ref[...])


def head_masks():
    lane = lax.broadcasted_iota(jnp.int32, (1, 128), 1)
    return [lane < HEAD, lane >= HEAD]


def softmax_rows(queries, keys, bias):
    scores = lax.dot_general(queries, keys, LAST_DIMS, preferred_element_type=FULL)
    scores = scores * (HEAD ** (-0.5)) + bias
    top = jnp.max(scores, axis=-1, keepdims=True)
    weights = jnp.exp(scores - top)
    return weights / jnp.sum(weights, axis=-1, keepdims=True)


def attn_forward_kernel(
    tok_ref, norm_ref, w_ref, b_ref, mask_ref, cos_ref, up_ref, down_ref,
    normed_ref, q_ref, k_ref, v_ref, mix_ref, qkv_ref,
):
    width = q_ref.shape[-1]
    unit, _ = unit_rows(tok_ref[0].astype(FULL))
    normed_ref[0] = (unit * norm_ref[0:1, :] + norm_ref[1:2, :]).astype(LOW)
    qkv_ref[...] = jnp.dot(normed_ref[0], w_ref[...], preferred_element_type=FULL) + b_ref[...]
    masks = head_masks()
    for pair in range(width // 128):
        here = slice(pair * 128, pair * 128 + 128)
        queries = turn(qkv_ref[:, here], cos_ref, up_ref, down_ref, 1.0).astype(LOW)
        there = slice(width + pair * 128, width + pair * 128 + 128)
        keys = turn(qkv_ref[:, there], cos_ref, up_ref, down_ref, 1.0).astype(LOW)
        there = slice(2 * width + pair * 128, 2 * width + pair * 128 + 128)
        values = qkv_ref[:, there].astype(LOW)
        q_ref[0, :, here] = queries
        k_ref[0, :, here] = keys
        v_ref[0, :, here] = values
        total = None
        for mask in masks:
            attend = softmax_rows(queries, jnp.where(mask, keys, 0), mask_ref[0])
            part = jnp.dot(
                attend.astype(LOW), jnp.where(mask, values, 0), preferred_element_type=FULL
            )
            total = part if total is None else total + part
        mix_ref[0, :, here] = total.astype(LOW)


def group_spec(array):
    return pl.BlockSpec((1,) + array.shape[1:], lambda g: (g, 0, 0))


def whole_spec(array):
    return pl.BlockSpec(array.shape, lambda g: (0,) * len(array.shape))


def attn_forward(tokens, norm_vals, w_qkv, bias, mask, tables):
    groups, seq, _ = tokens.shape
    width = w_qkv.shape[1] // 3
    row_spec = pl.BlockSpec((seq, 128), lambda g: (g, 0))
    part = jax.ShapeDtypeStruct((groups, seq, width), LOW)
    normed = jax.ShapeDtypeStruct(tokens.shape, LOW)
    return pl.pallas_call(
        attn_forward_kernel,
        grid=(groups,),
        out_shape=[normed, part, part, part, part],
        in_specs=[
            group_spec(tokens),
            whole_spec(norm_vals),
            whole_spec(w_qkv),
            whole_spec(bias),
            group_spec(mask),
            row_spec,
            row_spec,
            row_spec,
        ],
        out_specs=[group_spec(normed)] + [group_spec(part)] * 4,
        scratch_shapes=[pltpu.VMEM((seq, 3 * width), FULL)],
        compiler_params=pltpu.CompilerParams(vmem_limit_bytes=BIG_VMEM),
        cost_estimate=pl.CostEstimate(
            flops=2 * groups * seq * (D * 3 * width + 2 * seq * width * 2),
            bytes_accessed=2 * (w_qkv.size + 3 * tokens.size),
            transcendentals=groups * seq * seq * (width // HEAD),
        ),
        name="attn_forward",
    )(tokens, norm_vals, w_qkv, bias, mask, *tables)


def attn_backward_kernel(
    gao_ref, w_ref, q_ref, k_ref, v_ref, mask_ref, cos_ref, up_ref, down_ref,
    grad_ref, sum_ref, gm_ref,
):
    width = q_ref.shape[-1]
    scale = HEAD ** (-0.5)
    gm_ref[...] = lax.dot_general(
        gao_ref[0], w_ref[...], LAST_DIMS, preferred_element_type=FULL
    ).astype(LOW)
    masks = head_masks()
    for pair in range(width // 128):
        here = slice(pair * 128, pair * 128 + 128)
        queries, keys, values = q_ref[0, :, here], k_ref[0, :, here], v_ref[0, :, here]
        grads = gm_ref[:, here]
        grad_q = grad_k = grad_v = 0.0
        for mask in masks:
            keys_one = jnp.where(mask, keys, 0)
            attend = softmax_rows(queries, keys_one, mask_ref[0])
            grad_attend = lax.dot_general(
                grads, jnp.where(mask, values, 0), LAST_DIMS, preferred_element_type=FULL
            )
            grad_v += lax.dot_general(
                attend.astype(LOW),
                jnp.where(mask, grads, 0),
                LEAD_DIMS,
                preferred_element_type=FULL,
            )
            mean = jnp.sum(attend * grad_attend, axis=-1, keepdims=True)
            grad_scores = (attend * (grad_attend - mean)).astype(LOW)
            grad_q += jnp.dot(grad_scores, keys_one, preferred_element_type=FULL)
            grad_k += lax.dot_general(
                grad_scores, jnp.where(mask, queries, 0), LEAD_DIMS, preferred_element_type=FULL
            )
        grad_q = turn(grad_q * scale, cos_ref, up_ref, down_ref, -1.0)
        grad_k = turn(grad_k * scale, cos_ref, up_ref, down_ref, -1.0)
        for n, grad in enumerate((grad_q, grad_k, grad_v)):
            start = n * width + pair * 128
            grad_ref[0, :, start : start + 128] = grad.astype(LOW)

    @pl.when(pl.program_id(0) == 0)
    def _():
        sum_ref[...] = jnp.zeros_like(sum_ref)

    sum_ref[0:1, :] += jnp.sum(grad_ref[0].astype(FULL), axis=0, keepdims=True)


def attn_backward(gao, w_out, queries, keys, values, mask, tables):
    groups, seq, _ = gao.shape
    width = queries.shape[-1]
    row_spec = pl.BlockSpec((seq, 128), lambda g: (g, 0))
    grad = jax.ShapeDtypeStruct((groups, seq, 3 * width), LOW)
    sums = jax.ShapeDtypeStruct((8, 3 * width), FULL)
    return pl.pallas_call(
        attn_backward_kernel,
        grid=(groups,),
        out_shape=[grad, sums],
        in_specs=[
            group_spec(gao),
            whole_spec(w_out),
            group_spec(queries),
            group_spec(keys),
            group_spec(values),
            group_spec(mask),
            row_spec,
            row_spec,
            row_spec,
        ],
        out_specs=[group_spec(grad), whole_spec(sums)],
        scratch_shapes=[pltpu.VMEM((seq, width), LOW)],
        compiler_params=pltpu.CompilerParams(vmem_limit_bytes=BIG_VMEM),
        cost_estimate=pl.CostEstimate(
            flops=2 * groups * seq * (D * width + 5 * seq * width * 2),
            bytes_accessed=2 * (gao.size + 6 * queries.size),
            transcendentals=groups * seq * seq * (width // HEAD),
        ),
        name="attn_backward",
    )(gao, w_out, queries, keys, values, mask, *tables)


class RowSum:
    scratch = 3

    def __init__(self, parts, scratch, pair, base):
        self.parts = parts
        self.out, self.diag, self.full = scratch
        self.half = parts.shape[1] // 2
        self.top, self.bottom = pl.ds(0, self.half), pl.ds(self.half, self.half)
        top, bottom = self.top, self.bottom
        self.first = [
            remote(parts.at[3, top], self.diag.at[0], pair, base + 0, to_dp(1)),
            remote(parts.at[3, bottom], self.diag.at[1], pair, base + 1, to_dp(2)),
            remote(parts.at[1, top], self.full.at[0, top], pair, base + 2, to_dp(1)),
            remote(parts.at[2, bottom], self.full.at[1, bottom], pair, base + 3, to_dp(2)),
        ]
        self.second = [
            remote(self.out.at[0], self.full.at[0, bottom], pair, base + 4, to_dp(1)),
            remote(self.out.at[1], self.full.at[1, top], pair, base + 5, to_dp(2)),
        ]

    def start(self):
        for copy in self.first:
            copy.start()

    def relay(self):
        self.first[1].wait_recv()
        self.out[0] = (
            self.parts[1, self.bottom].astype(FULL) + self.diag[1].astype(FULL)
        ).astype(LOW)
        self.second[0].start()
        self.first[0].wait_recv()
        self.out[1] = (self.parts[2, self.top].astype(FULL) + self.diag[0].astype(FULL)).astype(
            LOW
        )
        self.second[1].start()

    def finish(self):
        self.first[2].wait_recv()
        self.first[3].wait_recv()
        self.second[0].wait_recv()
        self.second[1].wait_recv()
        for copy in self.first + self.second:
            copy.wait_send()

    def rows(self, part):
        return (
            self.parts[0, part].astype(FULL)
            + self.full[0, part].astype(FULL)
            + self.full[1, part].astype(FULL)
        )


def row_sum_scratch(rows, cols):
    return [
        pltpu.VMEM((2, rows // 2, cols), LOW),
        pltpu.VMEM((2, rows // 2, cols), LOW),
        pltpu.VMEM((2, rows, cols), LOW),
    ]


CHUNK = 32


def in_chunks(rows, body):
    def step(index, carry):
        body(pl.ds(pl.multiple_of(index * CHUNK, CHUNK), CHUNK))
        return carry

    lax.fori_loop(0, rows // CHUNK, step, 0)


def mid_forward_kernel(
    part_ref, tok_ref, norm_ref, resid_ref, normed_all, out, diag, full, own, send, recv, local
):
    rows = tok_ref.shape[0]
    greet([to_dp(1), to_dp(2)])
    total = RowSum(part_ref, (out, diag, full), (send, recv), 0)
    total.start()
    total.relay()
    total.finish()

    def body(here):
        resid = tok_ref[here].astype(FULL) + total.rows(here)
        resid_ref[here] = resid
        unit, _ = unit_rows(resid)
        own[here] = (unit * norm_ref[5:6, :] + norm_ref[6:7, :]).astype(LOW)

    in_chunks(rows, body)
    keep = pltpu.make_async_copy(own, normed_all.at[0], local.at[0])
    sent = spread(own, normed_all, (send, recv), 6, True)
    keep.start()
    pass_on(*sent)
    spread_end(*sent)
    keep.wait()


def mid_forward(part, tokens, norm_vals, number):
    rows, cols = tokens.shape
    return pl.pallas_call(
        mid_forward_kernel,
        out_shape=[
            jax.ShapeDtypeStruct(tokens.shape, FULL),
            jax.ShapeDtypeStruct(part.shape, LOW),
        ],
        in_specs=[VMEM, VMEM, VMEM],
        out_specs=[VMEM, ANY],
        scratch_shapes=row_sum_scratch(rows, cols)
        + [pltpu.VMEM((rows, cols), LOW)]
        + sems(12)
        + [pltpu.SemaphoreType.DMA((1,))],
        compiler_params=comm_params(number),
        name="mid_forward",
    )(part, tokens, norm_vals)


def mid_backward_kernel(
    part_ref, resid_ref, cot_ref, norm_ref,
    grad_ref, gao_all, sum_ref, out, diag, full, own, send, recv, local,
):
    rows = resid_ref.shape[0]
    greet([to_dp(1), to_dp(2)])
    total = RowSum(part_ref, (out, diag, full), (send, recv), 0)
    total.start()
    sum_ref[...] = jnp.zeros_like(sum_ref)
    total.relay()
    total.finish()

    def body(here):
        grads = total.rows(here)
        unit, inverse = unit_rows(resid_ref[here])
        sum_ref[0:1, :] += jnp.sum(grads * unit, axis=0, keepdims=True)
        sum_ref[1:2, :] += jnp.sum(grads, axis=0, keepdims=True)
        grad = cot_ref[here].astype(FULL) + layer_back(grads, norm_ref[5:6, :], unit, inverse)
        grad_ref[here] = grad
        own[here] = grad.astype(LOW)

    in_chunks(rows, body)
    keep = pltpu.make_async_copy(own, gao_all.at[0], local.at[0])
    sent = spread(own, gao_all, (send, recv), 6, True)
    keep.start()
    pass_on(*sent)
    spread_end(*sent)
    keep.wait()


def mid_backward(part, resid, cotangent, norm_vals, number):
    rows, cols = resid.shape
    return pl.pallas_call(
        mid_backward_kernel,
        out_shape=[
            jax.ShapeDtypeStruct(resid.shape, FULL),
            jax.ShapeDtypeStruct(part.shape, LOW),
            jax.ShapeDtypeStruct((8, cols), FULL),
        ],
        in_specs=[VMEM] * 4,
        out_specs=[VMEM, ANY, VMEM],
        scratch_shapes=row_sum_scratch(rows, cols)
        + [pltpu.VMEM((rows, cols), LOW)]
        + sems(12)
        + [pltpu.SemaphoreType.DMA((1,))],
        compiler_params=comm_params(number),
        name="mid_backward",
    )(part, resid, cotangent, norm_vals)


def last_rows_kernel(
    norm1_ref, down_ref, tok_ref, resid_ref, grad_ref, norm_ref,
    input_ref, block_ref, sum_ref, out_a, diag_a, full_a, out_b, diag_b, full_b, send, recv,
):
    rows = tok_ref.shape[0]
    greet([to_dp(1), to_dp(2)])
    first = RowSum(norm1_ref, (out_a, diag_a, full_a), (send, recv), 0)
    second = RowSum(down_ref, (out_b, diag_b, full_b), (send, recv), 6)
    first.start()
    second.start()
    sum_ref[...] = jnp.zeros_like(sum_ref)
    first.relay()
    second.relay()
    first.finish()

    def body_one(here):
        grads = first.rows(here)
        unit, inverse = unit_rows(tok_ref[here].astype(FULL))
        sum_ref[0:1, :] += jnp.sum(grads * unit, axis=0, keepdims=True)
        sum_ref[1:2, :] += jnp.sum(grads, axis=0, keepdims=True)
        input_ref[here] = grad_ref[here] + layer_back(grads, norm_ref[0:1, :], unit, inverse)

    in_chunks(rows, body_one)
    second.finish()

    def body_two(here):
        block_ref[here] = (resid_ref[here] + second.rows(here)).astype(LOW)

    in_chunks(rows, body_two)


def last_rows(norm1_part, down_part, tokens, resid, grad_resid, norm_vals, number):
    rows, cols = tokens.shape
    return pl.pallas_call(
        last_rows_kernel,
        out_shape=[
            jax.ShapeDtypeStruct(tokens.shape, FULL),
            jax.ShapeDtypeStruct(tokens.shape, LOW),
            jax.ShapeDtypeStruct((8, cols), FULL),
        ],
        in_specs=[VMEM] * 6,
        out_specs=[VMEM] * 3,
        scratch_shapes=row_sum_scratch(rows, cols) * 2 + sems(12),
        compiler_params=comm_params(number),
        name="last_rows",
    )(norm1_part, down_part, tokens, resid, grad_resid, norm_vals)


def adam_kernel(parts, factor_ref, *refs):
    grad_refs = refs[:-6]
    master_ref, first_ref, second_ref, master_out, first_out, second_out = refs[-6:]

    def update(grads):
        outs = adam_update(
            master_ref[...],
            first_ref[...],
            second_ref[...],
            grads.astype(FULL),
            factor_ref[0, 0],
            RATE_MATRIX,
            DECAY_MATRIX,
        )
        master_out[...], first_out[...], second_out[...] = outs

    if len(grad_refs) == 1:
        update(grad_refs[0][0])
    else:
        step = pl.program_id(0)

        @pl.when(step < parts * N_DP)
        def _():
            update(grad_refs[0][0])

        @pl.when(step >= parts * N_DP)
        def _():
            update(grad_refs[1][...])


def adam_apply(factor, blocks, extra, master, first, second, parts):
    rows, cols = master.shape
    width = blocks.shape[-1] // parts
    steps = parts * N_DP
    column = pl.BlockSpec((rows, width), lambda j: (0, j))
    last = steps - 1
    in_specs = [
        pl.BlockSpec(memory_space=pltpu.SMEM),
        pl.BlockSpec(
            (1, rows, width),
            lambda j: (jnp.minimum(j, last) % N_DP, 0, jnp.minimum(j, last) // N_DP),
        ),
    ]
    grads = [blocks]
    if extra is not None:
        in_specs.append(pl.BlockSpec((rows, width), lambda j: (0, jnp.maximum(j - steps, 0))))
        grads.append(extra)
    return pl.pallas_call(
        functools.partial(adam_kernel, parts),
        grid=(cols // width,),
        out_shape=[jax.ShapeDtypeStruct(master.shape, FULL)] * 3,
        in_specs=in_specs + [column] * 3,
        out_specs=[column] * 3,
        compiler_params=pltpu.CompilerParams(vmem_limit_bytes=BIG_VMEM),
        cost_estimate=pl.CostEstimate(
            flops=20 * master.size, bytes_accessed=26 * master.size, transcendentals=master.size
        ),
        name="adam",
    )(factor, *grads, master, first, second)


def per_device_fast(
    tokens,
    cotangent,
    segments,
    positions,
    attn_master,
    mlp_master,
    norm_master,
    attn_first,
    mlp_first,
    norm_first,
    attn_second,
    mlp_second,
    norm_second,
):
    seq = tokens.shape[0]
    rows = attn_master.shape[0]
    width = D // N_DP
    ff_width = FF // N_DP
    my_dp = lax.axis_index("dp")
    my_shard = lax.axis_index("shard")
    my_cols = (my_dp * N_SH + my_shard) * rows

    qkv_send = attn_master[:, : 3 * D].astype(LOW).reshape(rows, 3, N_DP, width)
    qkv_send = qkv_send.transpose(2, 0, 1, 3).reshape(N_DP, rows, 3 * width)
    (qkv_blocks,) = exchange([qkv_send], 0)
    w_qkv = lax.all_gather(qkv_blocks, "shard", axis=1).reshape(D, 3 * width)
    w_out = lax.all_gather(attn_master[:, 3 * D :].astype(LOW), "shard", axis=0, tiled=True)
    norm_place = lax.dynamic_update_slice(
        jnp.zeros((8, D), FULL), norm_master.astype(LOW).astype(FULL), (0, my_cols)
    )
    norm_vals = sum_small(norm_place, 1)
    mlp_send = mlp_master.astype(LOW).reshape(rows, 3, N_DP, ff_width)
    mlp_send = mlp_send.transpose(2, 0, 1, 3).reshape(N_DP, rows, 3 * ff_width)
    places = jnp.stack([segments, positions], 0)
    tok_all, cot_all, place_all, mlp_blocks = start(tokens, cotangent, places, mlp_send, 2)
    w_mlp = lax.all_gather(mlp_blocks, "shard", axis=1).reshape(D, 3 * ff_width)
    w_gu = w_mlp[:, : 2 * ff_width]
    w_down = w_mlp[:, 2 * ff_width :]

    seg_all, pos_all = place_all[:, 0], place_all[:, 1]
    spots = jnp.arange(seq)
    allowed = (seg_all[:, :, None] == seg_all[:, None, :]) & (
        spots[:, None] >= spots[None, :]
    )[None]
    mask = jnp.where(allowed, 0.0, NEG_FILL).astype(FULL)
    half = ROT // 2
    lane = np.arange(128) % HEAD
    angle_rate = (ROPE_BASE ** (-((lane % half) * 2.0 / ROT))).astype(np.float32)
    angles = pos_all.reshape(-1).astype(FULL)[:, None] * angle_rate[None, :]
    sines = jnp.sin(angles)
    tables = (
        jnp.where(lane < ROT, jnp.cos(angles), 1.0),
        jnp.where(lane < half, -sines, 0.0),
        jnp.where((lane >= half) & (lane < ROT), sines, 0.0),
    )
    bias = lax.dynamic_slice(norm_vals[2:5], (0, my_dp * width), (3, width)).reshape(1, 3 * width)

    normed1, queries, keys, values, mixture = attn_forward(
        tok_all, norm_vals, w_qkv, bias, mask, tables
    )
    group = N_DP * seq
    normed1 = normed1.reshape(group, D)
    mixture = mixture.reshape(group, width)
    attn_part = jnp.dot(mixture, w_out, preferred_element_type=FULL).astype(LOW)
    resid, normed2 = mid_forward(attn_part.reshape(N_DP, seq, D), tokens, norm_vals, 3)
    normed2 = normed2.reshape(group, D)
    cot_flat = cot_all.reshape(group, D)

    gate_up = jnp.dot(normed2, w_gu, preferred_element_type=FULL)
    hidden_f, act_pull = jax.vjp(activate, gate_up[:, :ff_width], gate_up[:, ff_width:])
    hidden = hidden_f.astype(LOW)
    grad_hidden = jnp.dot(cot_flat, w_down, preferred_element_type=FULL)
    grad_gate, grad_up = act_pull(grad_hidden)
    grad_gu = jnp.concatenate([grad_gate, grad_up], 1).astype(LOW)
    norm2_part = lax.dot_general(grad_gu, w_gu, LAST_DIMS, preferred_element_type=FULL)
    grad_resid, grad_attn_out, sums2 = mid_backward(
        norm2_part.astype(LOW).reshape(N_DP, seq, D), resid, cotangent, norm_vals, 4
    )
    part_gu = lax.dot_general(normed2, grad_gu, LEAD_DIMS, preferred_element_type=FULL)
    part_down = lax.dot_general(cot_flat, hidden, LEAD_DIMS, preferred_element_type=FULL)
    part_mlp = jnp.concatenate([part_gu.astype(LOW), part_down.astype(LOW)], 1)
    mlp_sum = lax.psum_scatter(
        part_mlp.reshape(N_DP, N_SH, rows, 3 * ff_width), "shard", scatter_dimension=1
    )
    out_part = lax.dot_general(hidden, w_down, LAST_DIMS, preferred_element_type=FULL)

    grad_qkv, bias_sums = attn_backward(
        grad_attn_out, w_out, queries, keys, values, mask, tables
    )
    grad_qkv = grad_qkv.reshape(group, 3 * width)
    grad_attn_out = grad_attn_out.reshape(group, D)
    part_qkv = lax.dot_general(normed1, grad_qkv, LEAD_DIMS, preferred_element_type=FULL)
    part_out = lax.dot_general(mixture, grad_attn_out, LEAD_DIMS, preferred_element_type=FULL)
    qkv_sum = lax.psum_scatter(
        part_qkv.astype(LOW).reshape(N_DP, N_SH, rows, 3 * width), "shard", scatter_dimension=1
    )
    out_sum = lax.psum_scatter(
        part_out.astype(LOW), "shard", scatter_dimension=0, tiled=True
    )
    norm1_part = lax.dot_general(grad_qkv, w_qkv, LAST_DIMS, preferred_element_type=FULL)
    input_grad, block_out, sums1 = last_rows(
        norm1_part.astype(LOW).reshape(N_DP, seq, D),
        out_part.astype(LOW).reshape(N_DP, seq, D),
        tokens,
        resid,
        grad_resid,
        norm_vals,
        5,
    )
    bias_term = lax.dynamic_update_slice(
        jnp.zeros((3, D), FULL), bias_sums[0].reshape(3, width), (0, my_dp * width)
    )
    norm_term = jnp.concatenate([sums1[:2], bias_term, sums2[:2], jnp.zeros((1, D), FULL)], 0)
    norm_grad = lax.dynamic_slice(sum_small(norm_term, 6), (0, my_cols), (7, rows))

    def square_sum(array):
        array = array.astype(FULL)
        return jnp.sum(array * array)

    squares = (
        square_sum(qkv_sum) + square_sum(out_sum) + square_sum(mlp_sum) + square_sum(norm_grad)
    )
    overall = sum_small(jnp.broadcast_to(squares, (8, 128)), 7)[0, 0]
    qkv_grad, mlp_grad = exchange([qkv_sum, mlp_sum], 8)
    grad_size = jnp.sqrt(overall)
    factor = CLIP_NORM / jnp.maximum(grad_size, CLIP_NORM)
    factor_box = factor.reshape(1, 1)
    attn_new, attn_first_new, attn_second_new = adam_apply(
        factor_box, qkv_grad, out_sum, attn_master, attn_first, attn_second, 3
    )
    mlp_new, mlp_first_new, mlp_second_new = adam_apply(
        factor_box, mlp_grad, None, mlp_master, mlp_first, mlp_second, 3
    )
    norm_new, norm_first_new, norm_second_new = adam_update(
        norm_master, norm_first, norm_second, norm_grad, factor, RATE_VECTOR, 0.0
    )
    return (
        block_out,
        input_grad,
        grad_size,
        attn_new,
        mlp_new,
        norm_new,
        attn_first_new,
        mlp_first_new,
        norm_first_new,
        attn_second_new,
        mlp_second_new,
        norm_second_new,
    )


def solution(mesh):
    in_specs = (
        P(("dp", "shard"), None),
        P(("dp", "shard"), None),
        P(("dp", "shard")),
        P(("dp", "shard")),
        P(("dp", "shard"), None),
        P(("dp", "shard"), None),
        P(None, ("dp", "shard")),
        P(("dp", "shard"), None),
        P(("dp", "shard"), None),
        P(None, ("dp", "shard")),
        P(("dp", "shard"), None),
        P(("dp", "shard"), None),
        P(None, ("dp", "shard")),
    )
    out_specs = (
        P(("dp", "shard"), None),
        P(("dp", "shard"), None),
        P(),
        P(("dp", "shard"), None),
        P(("dp", "shard"), None),
        P(None, ("dp", "shard")),
        P(("dp", "shard"), None),
        P(("dp", "shard"), None),
        P(None, ("dp", "shard")),
        P(("dp", "shard"), None),
        P(("dp", "shard"), None),
        P(None, ("dp", "shard")),
    )
    fast = dict(mesh.shape) == dict(dp=4, shard=8)
    body = per_device_fast if fast else per_device_any
    return jax.shard_map(
        body, mesh=mesh, in_specs=in_specs, out_specs=out_specs, check_vma=False
    )
```

```python
import functools

import numpy as np
import jax
import jax.numpy as jnp
from jax import lax
from jax.experimental import pallas as pl
from jax.experimental.pallas import tpu as pltpu
from jax.sharding import PartitionSpec as P

D = 2048
HEADS = 32
HEAD = 64
FF = 5632
ROT = 16
STEP = 10


NORM_EPS = 1e-05
NEG_FILL = -1e30
ROPE_BASE = 10000.0
CLIP_NORM = 1.0
BETA_ONE = 0.9
BETA_TWO = 0.95
ADAM_EPS = 1e-08
RATE_MATRIX = 0.02
RATE_VECTOR = 0.2
DECAY_MATRIX = 0.1
LEAD_DIMS = (((0,), (0,)), ((), ()))
LAST_DIMS = (((1,), (1,)), ((), ()))


def layer_norm(values_in, gain_vec, shift_vec):
    average = jnp.mean(values_in, axis=-1, keepdims=True)
    centered = values_in - average
    variance = jnp.mean(centered * centered, axis=-1, keepdims=True)
    return centered * lax.rsqrt(variance + NORM_EPS) * gain_vec + shift_vec


def rotary_tables(position_ids):
    half_rot = ROT // 2
    inverse_freq = ROPE_BASE ** (-(jnp.arange(half_rot, dtype=jnp.float32) * 2.0 / ROT))
    angles = position_ids.astype(jnp.float32)[:, None] * inverse_freq[None, :]
    return (jnp.cos(angles)[:, None, :], jnp.sin(angles)[:, None, :])


def rotate(heads_in, cos_table, sin_table):
    half_rot = ROT // 2
    first_half = heads_in[..., :half_rot]
    second_half = heads_in[..., half_rot:ROT]
    rest_part = heads_in[..., ROT:]
    turned_one = first_half * cos_table - second_half * sin_table
    turned_two = second_half * cos_table + first_half * sin_table
    return jnp.concatenate([turned_one, turned_two, rest_part], -1)


def pad_last(array, size):
    missing = size - array.shape[-1]
    if missing == 0:
        return array
    return jnp.pad(array, [(0, 0)] * (array.ndim - 1) + [(0, missing)])


def activate(gate_part, up_part):
    return jax.nn.silu(gate_part) * up_part


def adam_update(master, first, second, grads, factor, rate, decay):
    clipped = grads * factor
    first_new = BETA_ONE * first + (1.0 - BETA_ONE) * clipped
    second_new = BETA_TWO * second + (1.0 - BETA_TWO) * clipped * clipped
    first_hat = first_new / (1.0 - BETA_ONE**STEP)
    second_hat = second_new / (1.0 - BETA_TWO**STEP)
    master_new = master - rate * (first_hat / (jnp.sqrt(second_hat) + ADAM_EPS) + decay * master)
    return (master_new, first_new, second_new)


def exchange_dp(blocks):
    return lax.all_to_all(blocks, "dp", 0, 0, tiled=True)


def gather_dp(rows):
    return lax.all_gather(rows, "dp", axis=0, tiled=True)


def scatter_sum_dp(parts):
    return lax.psum_scatter(parts, "dp", scatter_dimension=0, tiled=True)


def gather_shard(block):
    return lax.all_gather(block, "shard", axis=1)


def scatter_sum_shard(parts):
    return lax.psum_scatter(parts, "shard", scatter_dimension=1)


def layer_stats(values_in):
    average = jnp.mean(values_in, axis=-1, keepdims=True)
    centered = values_in - average
    variance = jnp.mean(centered * centered, axis=-1, keepdims=True)
    inverse = lax.rsqrt(variance + NORM_EPS)
    return centered * inverse, inverse


def layer_back(grads, gain_vec, unit, inverse):
    scaled = grads * gain_vec
    mean_one = jnp.mean(scaled, axis=-1, keepdims=True)
    mean_two = jnp.mean(scaled * unit, axis=-1, keepdims=True)
    return inverse * (scaled - mean_one - unit * mean_two)


def per_device_any(
    tokens,
    cotangent,
    segments,
    positions,
    attn_master,
    mlp_master,
    norm_master,
    attn_first,
    mlp_first,
    norm_first,
    attn_second,
    mlp_second,
    norm_second,
):
    low = jnp.bfloat16
    full = jnp.float32
    n_dp = lax.axis_size("dp")
    n_sh = lax.axis_size("shard")
    seq = tokens.shape[0]
    rows = attn_master.shape[0]
    heads = HEADS // n_dp
    width = D // n_dp
    ff_width = -(-FF // (128 * n_dp)) * 128
    ff_pad = ff_width * n_dp
    scale = HEAD ** (-0.5)

    qkv_send = attn_master[:, : 3 * D].astype(low).reshape(rows, 3, n_dp, width)
    qkv_send = qkv_send.transpose(2, 0, 1, 3).reshape(n_dp, rows, 3 * width)
    mlp_send = pad_last(mlp_master.astype(low).reshape(rows, 3, FF), ff_pad)
    mlp_send = mlp_send.reshape(rows, 3, n_dp, ff_width)
    mlp_send = mlp_send.transpose(2, 0, 1, 3).reshape(n_dp, rows, 3 * ff_width)
    norm_full = lax.all_gather(norm_master.astype(low), ("dp", "shard"), axis=1, tiled=True)
    norm_vals = norm_full.astype(full)
    w_qkv = gather_shard(exchange_dp(qkv_send)).reshape(D, 3 * width)
    w_out = gather_shard(attn_master[None, :, 3 * D :].astype(low)).reshape(width, D)
    tokens_all = gather_dp(tokens)
    places_all = gather_dp(jnp.stack([segments, positions], 0)[None])
    cot_all = gather_dp(cotangent)
    w_mlp = gather_shard(exchange_dp(mlp_send)).reshape(D, 3 * ff_width)
    w_gu = w_mlp[:, : 2 * ff_width]
    w_down = w_mlp[:, 2 * ff_width :]
    seg_all, pos_all = places_all[:, 0], places_all[:, 1]

    inputs_all = tokens_all.astype(full)
    unit1, _ = layer_stats(inputs_all)
    normed1 = (unit1 * norm_vals[0] + norm_vals[1]).astype(low)
    my_dp = lax.axis_index("dp")
    bias = lax.dynamic_slice(norm_vals[2:5], (0, my_dp * width), (3, width)).reshape(3 * width)
    qkv = jnp.dot(normed1, w_qkv, preferred_element_type=full) + bias
    qkv = qkv.reshape(n_dp * seq, 3 * heads, HEAD)
    cos_table, sin_table = rotary_tables(pos_all.reshape(-1))

    def split(array):
        return array.reshape(n_dp, seq, heads, HEAD)

    queries = split(rotate(qkv[:, :heads], cos_table, sin_table).astype(low))
    key_rows = split(rotate(qkv[:, heads : 2 * heads], cos_table, sin_table).astype(low))
    values = split(qkv[:, 2 * heads :].astype(low))
    places = jnp.arange(seq)
    allowed = (seg_all[:, :, None] == seg_all[:, None, :]) & (
        places[:, None] >= places[None, :]
    )[None]
    scores = (
        jnp.einsum("gshd,gthd->ghst", queries, key_rows, preferred_element_type=full) * scale
    )
    scores = jnp.where(allowed[:, None], scores, NEG_FILL)
    attend = jax.nn.softmax(scores, axis=-1)
    attend_low = attend.astype(low)
    mixture = (
        jnp.einsum("ghst,gthd->gshd", attend_low, values, preferred_element_type=full)
        .reshape(n_dp * seq, width)
        .astype(low)
    )
    attn_part = jnp.dot(mixture, w_out, preferred_element_type=full).astype(low)
    resid = tokens.astype(full) + scatter_sum_dp(attn_part).astype(full)
    unit2, inverse2 = layer_stats(resid)
    normed2 = gather_dp((unit2 * norm_vals[5] + norm_vals[6]).astype(low))
    gate_up = jnp.dot(normed2, w_gu, preferred_element_type=full)
    hidden_f, act_pull = jax.vjp(activate, gate_up[:, :ff_width], gate_up[:, ff_width:])
    hidden = hidden_f.astype(low)
    grad_hidden = jnp.dot(cot_all, w_down, preferred_element_type=full)
    grad_gate, grad_up = act_pull(grad_hidden)
    grad_gu = jnp.concatenate([grad_gate, grad_up], 1).astype(low)
    norm2_part = lax.dot_general(grad_gu, w_gu, LAST_DIMS, preferred_element_type=full)
    grad_norm2 = scatter_sum_dp(norm2_part.astype(low)).astype(full)
    out_part = lax.dot_general(hidden, w_down, LAST_DIMS, preferred_element_type=full)
    block_out = (resid + scatter_sum_dp(out_part.astype(low)).astype(full)).astype(low)
    part_gu = lax.dot_general(normed2, grad_gu, LEAD_DIMS, preferred_element_type=full)
    part_down = lax.dot_general(cot_all, hidden, LEAD_DIMS, preferred_element_type=full)
    part_mlp = jnp.concatenate([part_gu.astype(low), part_down.astype(low)], 1)
    mlp_sum = scatter_sum_shard(part_mlp.reshape(n_dp, n_sh, rows, 3 * ff_width))

    grad_gain2 = jnp.sum(grad_norm2 * unit2, axis=0)
    grad_shift2 = jnp.sum(grad_norm2, axis=0)
    grad_resid = cotangent.astype(full) + layer_back(grad_norm2, norm_vals[5], unit2, inverse2)
    grad_attn_out = gather_dp(grad_resid.astype(low))
    grad_mixture = lax.dot_general(grad_attn_out, w_out, LAST_DIMS, preferred_element_type=full)
    grad_mixture = split(grad_mixture.astype(low))
    grad_attend = jnp.einsum("gshd,gthd->ghst", grad_mixture, values, preferred_element_type=full)
    grad_values = jnp.einsum(
        "ghst,gshd->gthd", attend_low, grad_mixture, preferred_element_type=full
    )
    grad_scores = (
        attend * (grad_attend - jnp.sum(attend * grad_attend, axis=-1, keepdims=True))
    ).astype(low)
    grad_queries = (
        jnp.einsum("ghst,gthd->gshd", grad_scores, key_rows, preferred_element_type=full) * scale
    )
    grad_keys = (
        jnp.einsum("ghst,gshd->gthd", grad_scores, queries, preferred_element_type=full) * scale
    )

    def turn_back(grads):
        grads = grads.reshape(n_dp * seq, heads, HEAD)
        return rotate(grads, cos_table, -sin_table).reshape(n_dp * seq, width)

    grad_qkv = jnp.concatenate(
        [
            turn_back(grad_queries),
            turn_back(grad_keys),
            grad_values.reshape(n_dp * seq, width),
        ],
        1,
    ).astype(low)
    part_qkv = lax.dot_general(normed1, grad_qkv, LEAD_DIMS, preferred_element_type=full)
    part_out = lax.dot_general(mixture, grad_attn_out, LEAD_DIMS, preferred_element_type=full)
    qkv_sum = scatter_sum_shard(part_qkv.astype(low).reshape(n_dp, n_sh, rows, 3 * width))
    out_sum = scatter_sum_shard(part_out.astype(low).reshape(1, n_sh, rows, D))[0].astype(full)

    norm1_part = lax.dot_general(grad_qkv, w_qkv, LAST_DIMS, preferred_element_type=full)
    grad_gain1 = jnp.sum(norm1_part * unit1, axis=0)
    grad_shift1 = jnp.sum(norm1_part, axis=0)
    grad_bias = jnp.sum(grad_qkv, axis=0, dtype=full).reshape(3, width)
    grad_norm1 = scatter_sum_dp(norm1_part.astype(low)).astype(full)
    own_unit1, own_inverse1 = layer_stats(tokens.astype(full))
    input_grad = grad_resid + layer_back(grad_norm1, norm_vals[0], own_unit1, own_inverse1)
    norm_term = lax.dynamic_update_slice(
        jnp.zeros((3, D), full), grad_bias, (0, my_dp * width)
    )
    norm_term = jnp.concatenate(
        [grad_gain1[None], grad_shift1[None], norm_term, grad_gain2[None], grad_shift2[None]], 0
    )
    norm_grad = lax.psum_scatter(norm_term, ("dp", "shard"), scatter_dimension=1, tiled=True)

    def columns_back(summed, parts, part_width, keep):
        back = exchange_dp(summed).reshape(n_dp, rows, parts, part_width)
        back = back.transpose(1, 2, 0, 3).reshape(rows, parts, n_dp * part_width)
        return back[:, :, :keep].reshape(rows, parts * keep).astype(full)

    mlp_grad = columns_back(mlp_sum, 3, ff_width, FF)
    attn_grad = jnp.concatenate([columns_back(qkv_sum, 3, width, D), out_sum], 1)
    squares = (
        jnp.sum(attn_grad * attn_grad)
        + jnp.sum(mlp_grad * mlp_grad)
        + jnp.sum(norm_grad * norm_grad)
    )
    overall = lax.psum(squares, ("dp", "shard"))
    grad_size = jnp.sqrt(overall)
    factor = CLIP_NORM / jnp.maximum(grad_size, CLIP_NORM)
    attn_new, attn_first_new, attn_second_new = adam_update(
        attn_master, attn_first, attn_second, attn_grad, factor, RATE_MATRIX, DECAY_MATRIX
    )
    mlp_new, mlp_first_new, mlp_second_new = adam_update(
        mlp_master, mlp_first, mlp_second, mlp_grad, factor, RATE_MATRIX, DECAY_MATRIX
    )
    norm_new, norm_first_new, norm_second_new = adam_update(
        norm_master, norm_first, norm_second, norm_grad, factor, RATE_VECTOR, 0.0
    )
    return (
        block_out,
        input_grad,
        grad_size,
        attn_new,
        mlp_new,
        norm_new,
        attn_first_new,
        mlp_first_new,
        norm_first_new,
        attn_second_new,
        mlp_second_new,
        norm_second_new,
    )


MESH = pl.DeviceIdType.MESH
ANY = pl.BlockSpec(memory_space=pl.ANY)
VMEM = pl.BlockSpec(memory_space=pltpu.VMEM)
LOW = jnp.bfloat16
FULL = jnp.float32
N_DP = 4
N_SH = 8
BIG_VMEM = 56 * 1024 * 1024


def dp_peer(step):
    mine = lax.axis_index("dp")
    if step == 1:
        return mine + 1 - 2 * (mine % 2)
    if step == 2:
        return (mine + 2) % 4
    return 3 - mine


def to_dp(step):
    return (dp_peer(step), lax.axis_index("shard"))


def to_shard(step):
    return (lax.axis_index("dp"), (lax.axis_index("shard") + step) % N_SH)


def cost(micros):
    return pl.CostEstimate(flops=0, bytes_accessed=int(micros * 3.0e6), transcendentals=0)


def greet(peers):
    barrier = pltpu.get_barrier_semaphore()
    for peer in peers:
        pl.semaphore_signal(barrier, inc=1, device_id=peer, device_id_type=MESH)
    pl.semaphore_wait(barrier, len(peers))


def remote(source, target, sems, index, peer):
    return pltpu.make_async_remote_copy(
        src_ref=source,
        dst_ref=target,
        send_sem=sems[0].at[index],
        recv_sem=sems[1].at[index],
        device_id=peer,
        device_id_type=MESH,
    )


def sems(count):
    return [pltpu.SemaphoreType.DMA((count,)), pltpu.SemaphoreType.DMA((count,))]


def comm_params(number):
    return pltpu.CompilerParams(
        collective_id=number, has_side_effects=True, vmem_limit_bytes=BIG_VMEM
    )


def first_kernel(
    qkv_ref, norm_ref, qkv_out, norm_out, near, send, recv, send_a, recv_a, send_b, recv_b, local
):
    mine = lax.axis_index("dp")
    place = lax.axis_index("shard")
    greet([to_dp(k) for k in (1, 2, 3)] + [to_shard(j) for j in range(1, N_SH)])
    small = [
        remote(norm_ref, near.at[mine], (send_a, recv_a), k - 1, to_dp(k)) for k in (1, 2, 3)
    ]
    for copy in small:
        copy.start()
    large = [
        remote(qkv_ref.at[dp_peer(k)], qkv_out.at[mine], (send, recv), k - 1, to_dp(k))
        for k in (3, 1, 2)
    ]
    keep = pltpu.make_async_copy(qkv_ref.at[mine], qkv_out.at[mine], local.at[0])
    for copy in large:
        copy.start()
    keep.start()
    near[mine] = norm_ref[...]
    for copy in small:
        copy.wait()
    norm_out[place] = near[...]
    far = [
        remote(near, norm_out.at[place], (send_b, recv_b), j - 1, to_shard(j))
        for j in range(1, N_SH)
    ]
    for copy in far:
        copy.start()
    for copy in far + large:
        copy.wait()
    keep.wait()


def first_exchange(qkv_send, norm_own, number):
    shape = (N_DP,) + norm_own.shape
    return pl.pallas_call(
        first_kernel,
        out_shape=[
            jax.ShapeDtypeStruct(qkv_send.shape, qkv_send.dtype),
            jax.ShapeDtypeStruct((N_SH,) + shape, FULL),
        ],
        in_specs=[ANY, VMEM],
        out_specs=[ANY, VMEM],
        scratch_shapes=[pltpu.VMEM(shape, FULL)]
        + sems(3)
        + sems(3)
        + sems(N_SH - 1)
        + [pltpu.SemaphoreType.DMA((1,))],
        compiler_params=comm_params(number),
        cost_estimate=cost(18),
        name="first_exchange",
    )(qkv_send, norm_own)


def spread_plan(own, result, sem_pair, base):
    half = own.shape[0] // 2
    top, bottom = pl.ds(0, half), pl.ds(half, half)
    sent = [
        remote(own.at[top], result.at[1, top], sem_pair, base + 0, to_dp(1)),
        remote(own.at[bottom], result.at[2, bottom], sem_pair, base + 1, to_dp(2)),
        remote(own.at[bottom], result.at[1, bottom], sem_pair, base + 2, to_dp(1)),
        remote(own.at[top], result.at[2, top], sem_pair, base + 3, to_dp(2)),
    ]
    passed = [
        remote(result.at[1, top], result.at[3, top], sem_pair, base + 4, to_dp(2)),
        remote(result.at[2, bottom], result.at[3, bottom], sem_pair, base + 5, to_dp(1)),
    ]
    return sent, passed


def spread(own, result, sem_pair, base):
    sent, passed = spread_plan(own, result, sem_pair, base)
    for copy in sent:
        copy.start()
    return sent, passed


def pass_on(sent, passed):
    sent[0].wait_recv()
    passed[0].start()
    sent[1].wait_recv()
    passed[1].start()


def spread_end(sent, passed):
    sent[2].wait_recv()
    sent[3].wait_recv()
    passed[0].wait_recv()
    passed[1].wait_recv()
    for copy in sent + passed:
        copy.wait_send()


def start_kernel(tok_ref, place_ref, mlp_ref, tok_all, place_all, mlp_out, send, recv, local):
    mine = lax.axis_index("dp")
    greet([to_dp(k) for k in (1, 2, 3)])
    pair = (send, recv)
    copies = [
        remote(place_ref, place_all.at[k], pair, 6 + k - 1, to_dp(k)) for k in (1, 2, 3)
    ]
    copies += [
        remote(mlp_ref.at[dp_peer(k)], mlp_out.at[mine], pair, 9 + k - 1, to_dp(k))
        for k in (3, 1, 2)
    ]
    own = [
        pltpu.make_async_copy(tok_ref, tok_all.at[0], local.at[0]),
        pltpu.make_async_copy(place_ref, place_all.at[0], local.at[1]),
        pltpu.make_async_copy(mlp_ref.at[mine], mlp_out.at[mine], local.at[2]),
    ]
    for copy in copies:
        copy.start()
    tok = spread(tok_ref, tok_all, pair, 0)
    for copy in own:
        copy.start()
    pass_on(*tok)
    spread_end(*tok)
    for copy in copies + own:
        copy.wait()


def start(tokens, places, mlp_send, number):
    return pl.pallas_call(
        start_kernel,
        out_shape=[
            jax.ShapeDtypeStruct((N_DP,) + tokens.shape, tokens.dtype),
            jax.ShapeDtypeStruct((N_DP,) + places.shape, places.dtype),
            jax.ShapeDtypeStruct(mlp_send.shape, mlp_send.dtype),
        ],
        in_specs=[ANY] * 3,
        out_specs=[ANY] * 3,
        scratch_shapes=sems(12) + [pltpu.SemaphoreType.DMA((3,))],
        compiler_params=comm_params(number),
        cost_estimate=cost(70),
        name="start",
    )(tokens, places, mlp_send)


def unit_rows(values):
    average = jnp.mean(values, axis=-1, keepdims=True)
    centered = values - average
    variance = jnp.mean(centered * centered, axis=-1, keepdims=True)
    inverse = lax.rsqrt(variance + NORM_EPS)
    return centered * inverse, inverse


def turn(value, cos_ref, up_ref, down_ref, sign):
    left = pltpu.roll(value, 128 - ROT // 2, 1)
    right = pltpu.roll(value, ROT // 2, 1)
    return value * cos_ref[...] + sign * (left * up_ref[...] + right * down_ref[...])


def head_masks():
    lane = lax.broadcasted_iota(jnp.int32, (1, 128), 1)
    return [lane < HEAD, lane >= HEAD]


def softmax_rows(queries, keys, bias):
    scores = lax.dot_general(queries, keys, LAST_DIMS, preferred_element_type=FULL)
    scores = scores * (HEAD ** (-0.5)) + bias
    top = jnp.max(scores, axis=-1, keepdims=True)
    weights = jnp.exp(scores - top)
    return weights / jnp.sum(weights, axis=-1, keepdims=True)


def attn_forward_kernel(
    cot_ref, tok_ref, norm_ref, w_ref, b_ref, mask_ref, cos_ref, up_ref, down_ref,
    cot_all, normed_ref, q_ref, k_ref, v_ref, mix_ref, qkv_ref, send, recv, local,
):
    width = q_ref.shape[-1]
    step, last = pl.program_id(0), pl.num_programs(0) - 1
    sent, passed = spread_plan(cot_ref, cot_all, (send, recv), 0)
    keep = pltpu.make_async_copy(cot_ref, cot_all.at[0], local.at[0])

    @pl.when(step == 0)
    def _():
        greet([to_dp(1), to_dp(2)])
        for copy in sent:
            copy.start()
        keep.start()

    @pl.when(step == last)
    def _():
        pass_on(sent, passed)

    unit, _ = unit_rows(tok_ref[0].astype(FULL))
    normed_ref[0] = (unit * norm_ref[0:1, :] + norm_ref[1:2, :]).astype(LOW)
    qkv_ref[...] = jnp.dot(normed_ref[0], w_ref[...], preferred_element_type=FULL) + b_ref[...]
    masks = head_masks()
    for pair in range(width // 128):
        here = slice(pair * 128, pair * 128 + 128)
        queries = turn(qkv_ref[:, here], cos_ref, up_ref, down_ref, 1.0).astype(LOW)
        there = slice(width + pair * 128, width + pair * 128 + 128)
        keys = turn(qkv_ref[:, there], cos_ref, up_ref, down_ref, 1.0).astype(LOW)
        there = slice(2 * width + pair * 128, 2 * width + pair * 128 + 128)
        values = qkv_ref[:, there].astype(LOW)
        q_ref[0, :, here] = queries
        k_ref[0, :, here] = keys
        v_ref[0, :, here] = values
        total = None
        for mask in masks:
            attend = softmax_rows(queries, jnp.where(mask, keys, 0), mask_ref[0])
            part = jnp.dot(
                attend.astype(LOW), jnp.where(mask, values, 0), preferred_element_type=FULL
            )
            total = part if total is None else total + part
        mix_ref[0, :, here] = total.astype(LOW)

    @pl.when(step == last)
    def _():
        spread_end(sent, passed)
        keep.wait()


def group_spec(array):
    return pl.BlockSpec((1,) + array.shape[1:], lambda g: (g, 0, 0))


def whole_spec(array):
    return pl.BlockSpec(array.shape, lambda g: (0,) * len(array.shape))


def attn_forward(cotangent, tokens, norm_vals, w_qkv, bias, mask, tables, number):
    groups, seq, _ = tokens.shape
    width = w_qkv.shape[1] // 3
    row_spec = pl.BlockSpec((seq, 128), lambda g: (g, 0))
    part = jax.ShapeDtypeStruct((groups, seq, width), LOW)
    normed = jax.ShapeDtypeStruct(tokens.shape, LOW)
    return pl.pallas_call(
        attn_forward_kernel,
        grid=(groups,),
        out_shape=[normed, normed, part, part, part, part],
        in_specs=[
            ANY,
            group_spec(tokens),
            whole_spec(norm_vals),
            whole_spec(w_qkv),
            whole_spec(bias),
            group_spec(mask),
            row_spec,
            row_spec,
            row_spec,
        ],
        out_specs=[ANY, group_spec(normed)] + [group_spec(part)] * 4,
        scratch_shapes=[pltpu.VMEM((seq, 3 * width), FULL)]
        + sems(6)
        + [pltpu.SemaphoreType.DMA((1,))],
        compiler_params=comm_params(number),
        cost_estimate=pl.CostEstimate(
            flops=2 * groups * seq * (D * 3 * width + 2 * seq * width * 2),
            bytes_accessed=2 * (w_qkv.size + 3 * tokens.size),
            transcendentals=groups * seq * seq * (width // HEAD),
        ),
        name="attn_forward",
    )(cotangent, tokens, norm_vals, w_qkv, bias, mask, *tables)


def attn_backward_kernel(
    part_hbm, normed_hbm, mix_hbm, gao_hbm, resid_ref, gao_ref, w_ref, q_ref, k_ref, v_ref,
    mask_ref, cos_ref, up_ref, down_ref,
    block_ref, grad_ref, sum_ref, attn_ref,
    gm_ref, parts, normed, mix, gao, grads_all, out, diag, full, send, recv, local,
):
    width = q_ref.shape[-1]
    rows = q_ref.shape[1]
    step, last = pl.program_id(0), pl.num_programs(0) - 1
    total = RowSum(parts, (out, diag, full), (send, recv), 0)
    loads = [
        pltpu.make_async_copy(part_hbm, parts, local.at[0]),
        pltpu.make_async_copy(mix_hbm, mix, local.at[1]),
        pltpu.make_async_copy(gao_hbm, gao, local.at[2]),
        pltpu.make_async_copy(normed_hbm, normed, local.at[3]),
    ]

    @pl.when(step == 0)
    def _():
        for copy in loads:
            copy.start()
        greet([to_dp(1), to_dp(2)])
        loads[0].wait()
        for k in (3, 1, 2):
            total.send(k)
        sum_ref[...] = jnp.zeros_like(sum_ref)

    @pl.when(step == 2)
    def _():
        total.relay()

    scale = HEAD ** (-0.5)
    gm_ref[...] = lax.dot_general(
        gao_ref[0], w_ref[...], LAST_DIMS, preferred_element_type=FULL
    ).astype(LOW)
    masks = head_masks()
    for pair in range(width // 128):
        here = slice(pair * 128, pair * 128 + 128)
        queries, keys, values = q_ref[0, :, here], k_ref[0, :, here], v_ref[0, :, here]
        grads = gm_ref[:, here]
        grad_q = grad_k = grad_v = 0.0
        for mask in masks:
            keys_one = jnp.where(mask, keys, 0)
            attend = softmax_rows(queries, keys_one, mask_ref[0])
            grad_attend = lax.dot_general(
                grads, jnp.where(mask, values, 0), LAST_DIMS, preferred_element_type=FULL
            )
            grad_v += lax.dot_general(
                attend.astype(LOW),
                jnp.where(mask, grads, 0),
                LEAD_DIMS,
                preferred_element_type=FULL,
            )
            mean = jnp.sum(attend * grad_attend, axis=-1, keepdims=True)
            grad_scores = (attend * (grad_attend - mean)).astype(LOW)
            grad_q += jnp.dot(grad_scores, keys_one, preferred_element_type=FULL)
            grad_k += lax.dot_general(
                grad_scores, jnp.where(mask, queries, 0), LEAD_DIMS, preferred_element_type=FULL
            )
        grad_q = turn(grad_q * scale, cos_ref, up_ref, down_ref, -1.0)
        grad_k = turn(grad_k * scale, cos_ref, up_ref, down_ref, -1.0)
        for n, grad in enumerate((grad_q, grad_k, grad_v)):
            start = n * width + pair * 128
            grad_ref[0, :, start : start + 128] = grad.astype(LOW)
    grads_all[pl.ds(pl.multiple_of(step * rows, rows), rows)] = grad_ref[0]
    sum_ref[0:1, :] += jnp.sum(grad_ref[0].astype(FULL), axis=0, keepdims=True)

    @pl.when(step == last)
    def _():
        for copy in loads[1:]:
            copy.wait()

        def one_shard(index, carry):
            here = pl.ds(pl.multiple_of(index * 256, 256), 256)
            attn_ref[index, :, : 3 * width] = lax.dot_general(
                normed[:, here], grads_all[...], LEAD_DIMS, preferred_element_type=FULL
            ).astype(LOW)
            return carry

        lax.fori_loop(0, N_SH, one_shard, 0)
        for pair in range(width // 128):
            value = lax.dot_general(
                mix[:, pair * 128 : pair * 128 + 128],
                gao[...],
                LEAD_DIMS,
                preferred_element_type=FULL,
            ).astype(LOW)
            for side in range(2):
                for part in range(N_DP):
                    attn_ref[2 * pair + side, part * 64 : part * 64 + 64, 3 * width :] = value[
                        side * 64 : side * 64 + 64, part * width : part * width + width
                    ]
        total.finish()

        def body(here):
            block_ref[here] = (resid_ref[here] + total.rows(here)).astype(LOW)

        in_chunks(rows, body)


def attn_backward(
    out_part, normed1, mixture, resid, gao, w_out, queries, keys, values, mask, tables, number
):
    groups, seq, cols = gao.shape
    width = queries.shape[-1]
    row_spec = pl.BlockSpec((seq, 128), lambda g: (g, 0))
    grad = jax.ShapeDtypeStruct((groups, seq, 3 * width), LOW)
    sums = jax.ShapeDtypeStruct((8, 3 * width), FULL)
    flat = groups * seq
    return pl.pallas_call(
        attn_backward_kernel,
        grid=(groups,),
        out_shape=[
            jax.ShapeDtypeStruct(resid.shape, LOW),
            grad,
            sums,
            jax.ShapeDtypeStruct((N_SH, D // N_SH, 4 * width), LOW),
        ],
        in_specs=[
            ANY,
            ANY,
            ANY,
            ANY,
            VMEM,
            group_spec(gao),
            VMEM,
            group_spec(queries),
            group_spec(keys),
            group_spec(values),
            group_spec(mask),
            row_spec,
            row_spec,
            row_spec,
        ],
        out_specs=[VMEM, group_spec(grad), whole_spec(sums), VMEM],
        scratch_shapes=[
            pltpu.VMEM((seq, width), LOW),
            pltpu.VMEM(gao.shape, LOW),
            pltpu.VMEM((flat, cols), LOW),
            pltpu.VMEM((flat, width), LOW),
            pltpu.VMEM((flat, cols), LOW),
            pltpu.VMEM((flat, 3 * width), LOW),
        ]
        + row_sum_scratch(seq, cols)
        + sems(6)
        + [pltpu.SemaphoreType.DMA((4,))],
        compiler_params=comm_params(number),
        cost_estimate=cost(55),
        name="attn_backward",
    )(
        out_part,
        normed1.reshape(flat, cols),
        mixture.reshape(flat, width),
        gao.reshape(flat, cols),
        resid,
        gao,
        w_out,
        queries,
        keys,
        values,
        mask,
        *tables,
    )


class RowSum:
    scratch = 3

    def __init__(self, parts, scratch, pair, base):
        self.parts = parts
        self.out, self.diag, self.full = scratch
        self.half = parts.shape[1] // 2
        self.top, self.bottom = pl.ds(0, self.half), pl.ds(self.half, self.half)
        top, bottom = self.top, self.bottom
        self.first = [
            remote(parts.at[3, top], self.diag.at[0], pair, base + 0, to_dp(1)),
            remote(parts.at[3, bottom], self.diag.at[1], pair, base + 1, to_dp(2)),
            remote(parts.at[1, top], self.full.at[0, top], pair, base + 2, to_dp(1)),
            remote(parts.at[2, bottom], self.full.at[1, bottom], pair, base + 3, to_dp(2)),
        ]
        self.second = [
            remote(self.out.at[0], self.full.at[0, bottom], pair, base + 4, to_dp(1)),
            remote(self.out.at[1], self.full.at[1, top], pair, base + 5, to_dp(2)),
        ]

    def send(self, k):
        for copy in {3: self.first[:2], 1: self.first[2:3], 2: self.first[3:]}[k]:
            copy.start()

    def relay(self):
        self.first[1].wait_recv()
        self.out[0] = (
            self.parts[1, self.bottom].astype(FULL) + self.diag[1].astype(FULL)
        ).astype(LOW)
        self.second[0].start()
        self.first[0].wait_recv()
        self.out[1] = (self.parts[2, self.top].astype(FULL) + self.diag[0].astype(FULL)).astype(
            LOW
        )
        self.second[1].start()

    def finish(self):
        self.first[2].wait_recv()
        self.first[3].wait_recv()
        self.second[0].wait_recv()
        self.second[1].wait_recv()
        for copy in self.first + self.second:
            copy.wait_send()

    def rows(self, part):
        return (
            self.parts[0, part].astype(FULL)
            + self.full[0, part].astype(FULL)
            + self.full[1, part].astype(FULL)
        )


def row_sum_scratch(rows, cols):
    return [
        pltpu.VMEM((2, rows // 2, cols), LOW),
        pltpu.VMEM((2, rows // 2, cols), LOW),
        pltpu.VMEM((2, rows, cols), LOW),
    ]


CHUNK = 32


def in_chunks(rows, body):
    def step(index, carry):
        body(pl.ds(pl.multiple_of(index * CHUNK, CHUNK), CHUNK))
        return carry

    lax.fori_loop(0, rows // CHUNK, step, 0)


def mid_forward_kernel(
    mix_ref, w_ref, tok_ref, norm_ref, resid_ref, normed_all,
    parts, out, diag, full, own, send, recv, local,
):
    rows = tok_ref.shape[0]
    greet([to_dp(1), to_dp(2)])
    total = RowSum(parts, (out, diag, full), (send, recv), 0)
    for k in (3, 1, 2, 0):
        parts[k] = jnp.dot(mix_ref[k], w_ref[...], preferred_element_type=FULL).astype(LOW)
        if k:
            total.send(k)
    total.relay()
    total.finish()

    def body(here):
        resid = tok_ref[here].astype(FULL) + total.rows(here)
        resid_ref[here] = resid
        unit, _ = unit_rows(resid)
        own[here] = (unit * norm_ref[5:6, :] + norm_ref[6:7, :]).astype(LOW)

    in_chunks(rows, body)
    keep = pltpu.make_async_copy(own, normed_all.at[0], local.at[0])
    sent = spread(own, normed_all, (send, recv), 6)
    keep.start()
    pass_on(*sent)
    spread_end(*sent)
    keep.wait()


def mid_forward(mixture, w_out, tokens, norm_vals, number):
    rows, cols = tokens.shape
    group = (N_DP, rows, cols)
    return pl.pallas_call(
        mid_forward_kernel,
        out_shape=[
            jax.ShapeDtypeStruct(tokens.shape, FULL),
            jax.ShapeDtypeStruct(group, LOW),
        ],
        in_specs=[VMEM] * 4,
        out_specs=[VMEM, ANY],
        scratch_shapes=[pltpu.VMEM(group, LOW)]
        + row_sum_scratch(rows, cols)
        + [pltpu.VMEM((rows, cols), LOW)]
        + sems(12)
        + [pltpu.SemaphoreType.DMA((1,))],
        compiler_params=comm_params(number),
        cost_estimate=cost(92),
        name="mid_forward",
    )(mixture, w_out, tokens, norm_vals)


def mid_backward_kernel(
    ggu_hbm, w_hbm, hid_hbm, resid_ref, cot_ref, norm_ref,
    grad_ref, gao_all, sum_ref, part_ref,
    ggu, w_gu, w_down, hid, parts, out, diag, full, own, send, recv, local,
):
    rows = resid_ref.shape[0]
    two = w_gu.shape[1]
    loads = [pltpu.make_async_copy(w_hbm.at[:, pl.ds(0, two)], w_gu, local.at[0])]
    loads += [pltpu.make_async_copy(ggu_hbm.at[k], ggu.at[k], local.at[1 + k]) for k in range(4)]
    loads += [
        pltpu.make_async_copy(w_hbm.at[:, pl.ds(two, two // 2)], w_down, local.at[5]),
        pltpu.make_async_copy(hid_hbm, hid, local.at[6]),
    ]
    for n in (0, 4, 2, 3, 1, 5, 6):
        loads[n].start()
    greet([to_dp(1), to_dp(2)])
    total = RowSum(parts, (out, diag, full), (send, recv), 0)
    loads[0].wait()
    for k in (3, 1, 2, 0):
        loads[1 + k].wait()
        parts[k] = lax.dot_general(
            ggu[k], w_gu[...], LAST_DIMS, preferred_element_type=FULL
        ).astype(LOW)
        if k:
            total.send(k)
    sum_ref[...] = jnp.zeros_like(sum_ref)

    def out_part(k):
        part_ref[k] = lax.dot_general(
            hid[k], w_down[...], LAST_DIMS, preferred_element_type=FULL
        ).astype(LOW)

    total.relay()
    loads[5].wait()
    loads[6].wait()
    out_part(0)
    out_part(1)
    total.finish()

    def body(here):
        grads = total.rows(here)
        unit, inverse = unit_rows(resid_ref[here])
        sum_ref[0:1, :] += jnp.sum(grads * unit, axis=0, keepdims=True)
        sum_ref[1:2, :] += jnp.sum(grads, axis=0, keepdims=True)
        grad = cot_ref[here].astype(FULL) + layer_back(grads, norm_ref[5:6, :], unit, inverse)
        grad_ref[here] = grad
        own[here] = grad.astype(LOW)

    in_chunks(rows, body)
    keep = pltpu.make_async_copy(own, gao_all.at[0], local.at[7])
    sent = spread(own, gao_all, (send, recv), 6)
    keep.start()
    out_part(2)
    pass_on(*sent)
    out_part(3)
    spread_end(*sent)
    keep.wait()


def mid_backward(grad_gu, w_mlp, hidden, resid, cotangent, norm_vals, number):
    rows, cols = resid.shape
    group = (N_DP, rows, cols)
    two, one = grad_gu.shape[-1], hidden.shape[-1]
    return pl.pallas_call(
        mid_backward_kernel,
        out_shape=[
            jax.ShapeDtypeStruct(resid.shape, FULL),
            jax.ShapeDtypeStruct(group, LOW),
            jax.ShapeDtypeStruct((8, cols), FULL),
            jax.ShapeDtypeStruct(group, LOW),
        ],
        in_specs=[ANY] * 3 + [VMEM] * 3,
        out_specs=[VMEM, ANY, VMEM, VMEM],
        scratch_shapes=[
            pltpu.VMEM((N_DP, rows, two), LOW),
            pltpu.VMEM((cols, two), LOW),
            pltpu.VMEM((cols, one), LOW),
            pltpu.VMEM((N_DP, rows, one), LOW),
            pltpu.VMEM(group, LOW),
        ]
        + row_sum_scratch(rows, cols)
        + [pltpu.VMEM((rows, cols), LOW)]
        + sems(12)
        + [pltpu.SemaphoreType.DMA((8,))],
        compiler_params=comm_params(number),
        cost_estimate=cost(105),
        name="mid_backward",
    )(grad_gu, w_mlp, hidden, resid, cotangent, norm_vals)


def last_rows_kernel(
    grad_qkv_ref, w_ref, gu_hbm, down_hbm, tok_ref, grad_ref, norm_ref, rest_ref,
    input_ref, total_ref, gu_out, down_out,
    parts, out, diag, full, sum_ref, near, far, send, recv, send_a, recv_a, send_b, recv_b,
    send_c, recv_c, local,
):
    rows = tok_ref.shape[0]
    mine = lax.axis_index("dp")
    greet([to_dp(k) for k in (1, 2, 3)] + [to_shard(j) for j in range(1, N_SH)])
    total = RowSum(parts, (out, diag, full), (send, recv), 0)
    for k in (3, 1, 2, 0):
        parts[k] = lax.dot_general(
            grad_qkv_ref[k], w_ref[...], LAST_DIMS, preferred_element_type=FULL
        ).astype(LOW)
        if k:
            total.send(k)
    sum_ref[...] = rest_ref[...]
    total.relay()
    blocks = []
    for n, (source, target) in enumerate(((gu_hbm, gu_out), (down_hbm, down_out))):
        for k in (3, 1, 2):
            blocks.append(
                remote(
                    source.at[dp_peer(k)],
                    target.at[mine],
                    (send_c, recv_c),
                    3 * n + k - 1,
                    to_dp(k),
                )
            )
        blocks.append(pltpu.make_async_copy(source.at[mine], target.at[mine], local.at[n]))
    total.finish()
    for copy in blocks:
        copy.start()

    def body(here):
        grads = total.rows(here)
        unit, inverse = unit_rows(tok_ref[here].astype(FULL))
        sum_ref[0:1, :] += jnp.sum(grads * unit, axis=0, keepdims=True)
        sum_ref[1:2, :] += jnp.sum(grads, axis=0, keepdims=True)
        input_ref[here] = grad_ref[here] + layer_back(grads, norm_ref[0:1, :], unit, inverse)

    in_chunks(rows, body)
    small = [
        remote(sum_ref, near.at[k - 1], (send_a, recv_a), k - 1, to_dp(k)) for k in (1, 2, 3)
    ]
    for copy in small:
        copy.start()
    for copy in small:
        copy.wait()
    sum_ref[...] = sum_ref[...] + near[0] + near[1] + near[2]
    small = [
        remote(sum_ref, far.at[j - 1], (send_b, recv_b), j - 1, to_shard(j))
        for j in range(1, N_SH)
    ]
    for copy in small:
        copy.start()
    for copy in small:
        copy.wait()
    result = sum_ref[...]
    for j in range(N_SH - 1):
        result = result + far[j]
    total_ref[...] = result
    for copy in blocks:
        copy.wait()


def last_rows(grad_qkv, w_qkv, gu_sum, down_sum, tokens, grad_resid, norm_vals, rest, number):
    rows, cols = tokens.shape
    return pl.pallas_call(
        last_rows_kernel,
        out_shape=[
            jax.ShapeDtypeStruct(tokens.shape, FULL),
            jax.ShapeDtypeStruct(rest.shape, FULL),
            jax.ShapeDtypeStruct(gu_sum.shape, gu_sum.dtype),
            jax.ShapeDtypeStruct(down_sum.shape, down_sum.dtype),
        ],
        in_specs=[VMEM, VMEM, ANY, ANY] + [VMEM] * 4,
        out_specs=[VMEM, VMEM, ANY, ANY],
        scratch_shapes=[pltpu.VMEM((N_DP, rows, cols), LOW)]
        + row_sum_scratch(rows, cols)
        + [
            pltpu.VMEM(rest.shape, FULL),
            pltpu.VMEM((N_DP - 1,) + rest.shape, FULL),
            pltpu.VMEM((N_SH - 1,) + rest.shape, FULL),
        ]
        + sems(6)
        + sems(N_DP - 1)
        + sems(N_SH - 1)
        + sems(6)
        + [pltpu.SemaphoreType.DMA((2,))],
        compiler_params=comm_params(number),
        cost_estimate=cost(80),
        name="last_rows",
    )(grad_qkv, w_qkv, gu_sum, down_sum, tokens, grad_resid, norm_vals, rest)


def tail_kernel(
    attn_ref, rest_ref, qkv_out, total_ref, near, far, part,
    send, recv, send_a, recv_a, send_b, recv_b, local,
):
    mine = lax.axis_index("dp")
    greet([to_dp(k) for k in (1, 2, 3)] + [to_shard(j) for j in range(1, N_SH)])
    cols = pl.ds(0, qkv_out.shape[-1])
    blocks = [
        remote(
            attn_ref.at[dp_peer(k), :, cols], qkv_out.at[mine], (send, recv), k - 1, to_dp(k)
        )
        for k in (3, 1, 2)
    ]
    blocks.append(pltpu.make_async_copy(attn_ref.at[mine, :, cols], qkv_out.at[mine], local.at[0]))
    for copy in blocks:
        copy.start()

    def body(index, total):
        here = pl.ds(pl.multiple_of(index * 16, 16), 16)
        for k in range(N_DP):
            values = attn_ref[k, here].astype(FULL)
            values = values * values
            for start in range(0, values.shape[1], 128):
                piece = values[:, start : start + 128]
                total = total + piece[:8] + piece[8:]
        return total

    squares = lax.fori_loop(0, attn_ref.shape[1] // 16, body, rest_ref[...])
    part[...] = squares
    small = [remote(part, near.at[k - 1], (send_a, recv_a), k - 1, to_dp(k)) for k in (1, 2, 3)]
    for copy in small:
        copy.start()
    for copy in small:
        copy.wait()
    part[...] = part[...] + near[0] + near[1] + near[2]
    small = [
        remote(part, far.at[j - 1], (send_b, recv_b), j - 1, to_shard(j)) for j in range(1, N_SH)
    ]
    for copy in small:
        copy.start()
    for copy in small:
        copy.wait()
    total = part[...]
    for j in range(N_SH - 1):
        total = total + far[j]
    total_ref[...] = total
    for copy in blocks:
        copy.wait()


def tail(attn_sum, rest, number):
    width = attn_sum.shape[-1] // 4
    return pl.pallas_call(
        tail_kernel,
        out_shape=[
            jax.ShapeDtypeStruct(attn_sum.shape[:2] + (3 * width,), LOW),
            jax.ShapeDtypeStruct(rest.shape, FULL),
        ],
        in_specs=[VMEM, VMEM],
        out_specs=[ANY, VMEM],
        scratch_shapes=[
            pltpu.VMEM((N_DP - 1,) + rest.shape, FULL),
            pltpu.VMEM((N_SH - 1,) + rest.shape, FULL),
            pltpu.VMEM(rest.shape, FULL),
        ]
        + sems(3)
        + sems(N_DP - 1)
        + sems(N_SH - 1)
        + [pltpu.SemaphoreType.DMA((1,))],
        compiler_params=comm_params(number),
        cost_estimate=cost(15),
        name="tail",
    )(attn_sum, rest)


FIRST_HAT = 1.0 / (1.0 - BETA_ONE**STEP)
SECOND_HAT = 1.0 / (1.0 - BETA_TWO**STEP)


def adam_step(grads, factor, master, first, second):
    clipped = grads.astype(FULL) * factor
    first_new = BETA_ONE * first + (1.0 - BETA_ONE) * clipped
    second_new = BETA_TWO * second + (1.0 - BETA_TWO) * clipped * clipped
    ratio = first_new * (RATE_MATRIX * FIRST_HAT) / (jnp.sqrt(second_new * SECOND_HAT) + ADAM_EPS)
    return (master * (1.0 - RATE_MATRIX * DECAY_MATRIX) - ratio, first_new, second_new)


def adam_mlp_kernel(factor_ref, gu_ref, down_ref, *refs):
    ins, outs = refs[:3], refs[3:]

    def update(grads):
        values = adam_step(grads, factor_ref[0, 0], *[ref[...] for ref in ins])
        for ref, value in zip(outs, values):
            ref[...] = value

    step = pl.program_id(0)

    @pl.when(step < 2 * N_DP)
    def _():
        update(gu_ref[0])

    @pl.when(step >= 2 * N_DP)
    def _():
        update(down_ref[0])


def adam_attn_kernel(factor_ref, qkv_ref, out_ref, *refs):
    ins, outs = refs[:3], refs[3:]
    step = pl.program_id(0)
    width = qkv_ref.shape[-1]

    def update(grads, here):
        values = adam_step(grads, factor_ref[0, 0], *[ref[:, here] for ref in ins])
        for ref, value in zip(outs, values):
            ref[:, here] = value

    for side in range(2):
        here = slice(side * width, side * width + width)

        @pl.when(step < 6)
        def _():
            update(qkv_ref[side], here)

        @pl.when(step >= 6)
        def _():
            update(out_ref[:, here], here)


def adam_call(kernel, factor, grads, grad_specs, states, width, name):
    rows, cols = states[0].shape
    column = pl.BlockSpec((rows, width), lambda j: (0, j))
    size = states[0].size
    return pl.pallas_call(
        kernel,
        grid=(cols // width,),
        out_shape=[jax.ShapeDtypeStruct((rows, cols), FULL)] * 3,
        in_specs=[pl.BlockSpec(memory_space=pltpu.SMEM)] + grad_specs + [column] * 3,
        out_specs=[column] * 3,
        compiler_params=pltpu.CompilerParams(vmem_limit_bytes=BIG_VMEM),
        cost_estimate=pl.CostEstimate(
            flops=20 * size, bytes_accessed=26 * size, transcendentals=size
        ),
        name=name,
    )(factor, *grads, *states)


def adam_mlp(factor, gu_blocks, down_blocks, states):
    rows = states[0].shape[0]
    width = down_blocks.shape[-1]
    last = 2 * N_DP - 1
    specs = [
        pl.BlockSpec(
            (1, rows, width),
            lambda j: (jnp.minimum(j, last) % N_DP, 0, jnp.minimum(j, last) // N_DP),
        ),
        pl.BlockSpec((1, rows, width), lambda j: (jnp.maximum(j - last - 1, 0), 0, 0)),
    ]
    grads = [gu_blocks, down_blocks]
    return adam_call(adam_mlp_kernel, factor, grads, specs, states, width, "adam_mlp")


def adam_attn(factor, qkv_blocks, out_grad, states):
    rows = states[0].shape[0]
    width = qkv_blocks.shape[-1] // 3
    specs = [
        pl.BlockSpec(
            (2, rows, width), lambda j: (jnp.minimum(j, 5) % 2, 0, jnp.minimum(j, 5) // 2)
        ),
        pl.BlockSpec((rows, 2 * width), lambda j: (0, jnp.maximum(j - 6, 0))),
    ]
    grads = [qkv_blocks, out_grad]
    return adam_call(adam_attn_kernel, factor, grads, specs, states, 2 * width, "adam_attn")


def per_device_fast(
    tokens,
    cotangent,
    segments,
    positions,
    attn_master,
    mlp_master,
    norm_master,
    attn_first,
    mlp_first,
    norm_first,
    attn_second,
    mlp_second,
    norm_second,
):
    seq = tokens.shape[0]
    rows = attn_master.shape[0]
    width = D // N_DP
    ff_width = FF // N_DP
    group = N_DP * seq
    my_dp = lax.axis_index("dp")
    my_shard = lax.axis_index("shard")

    def by_shard(array):
        parts = array.reshape(array.shape[0], N_DP, N_SH, rows)
        return parts.transpose(0, 2, 1, 3).reshape(array.shape)

    def by_place(array):
        parts = array.reshape(array.shape[0], N_SH, N_DP, rows)
        return parts.transpose(0, 2, 1, 3).reshape(array.shape)

    qkv_send = attn_master[:, : 3 * D].astype(LOW).reshape(rows, 3, N_DP, width)
    qkv_send = qkv_send.transpose(2, 0, 1, 3).reshape(N_DP, rows, 3 * width)
    norm_low = lax.optimization_barrier(norm_master.astype(LOW)).astype(FULL)
    norm_own = jnp.pad(norm_low, ((0, 1), (0, 128 - rows)))
    qkv_blocks, norm_all = first_exchange(qkv_send, norm_own, 0)

    def gather_rows(blocks):
        return lax.all_gather(blocks.reshape(-1, blocks.shape[-1]), "shard", axis=0, tiled=True)

    w_qkv = gather_rows(qkv_blocks)
    w_out = gather_rows(by_shard(attn_master[:, 3 * D :].astype(LOW)))
    norm_all = norm_all[:, :, :7, :rows]
    norm_vals = norm_all.transpose(2, 0, 1, 3).reshape(7, D)
    norm_vals = jnp.concatenate([norm_vals, jnp.zeros((1, D), FULL)], 0)
    bias_all = norm_all.transpose(2, 1, 0, 3)[2:5].reshape(3, N_DP, width)
    bias = lax.dynamic_index_in_dim(bias_all, my_dp, 1).reshape(1, 3 * width)
    mlp_send = mlp_master.astype(LOW).reshape(rows, 3, N_DP, ff_width)
    mlp_send = mlp_send.transpose(2, 0, 1, 3).reshape(N_DP, rows, 3 * ff_width)
    places = jnp.stack([segments, positions], 0)
    tokens = by_shard(tokens)
    cotangent = by_shard(cotangent)
    tok_all, place_all, mlp_blocks = start(tokens, places, mlp_send, 1)
    w_mlp = gather_rows(mlp_blocks)
    w_gu, w_down = w_mlp[:, : 2 * ff_width], w_mlp[:, 2 * ff_width :]

    seg_all, pos_all = place_all[:, 0], place_all[:, 1]
    spots = jnp.arange(seq)
    allowed = (seg_all[:, :, None] == seg_all[:, None, :]) & (
        spots[:, None] >= spots[None, :]
    )[None]
    mask = jnp.where(allowed, 0.0, NEG_FILL).astype(FULL)
    half = ROT // 2
    lane = np.arange(128) % HEAD
    angle_rate = (ROPE_BASE ** (-((lane % half) * 2.0 / ROT))).astype(np.float32)
    angles = pos_all.reshape(-1).astype(FULL)[:, None] * angle_rate[None, :]
    sines = jnp.sin(angles)
    tables = (
        jnp.where(lane < ROT, jnp.cos(angles), 1.0),
        jnp.where(lane < half, -sines, 0.0),
        jnp.where((lane >= half) & (lane < ROT), sines, 0.0),
    )

    cot_all, normed1, queries, keys, values, mixture = attn_forward(
        cotangent, tok_all, norm_vals, w_qkv, bias, mask, tables, 2
    )
    resid, normed2 = mid_forward(mixture, w_out, tokens, norm_vals, 3)
    normed2 = normed2.reshape(group, D)
    cot_flat = cot_all.reshape(group, D)

    gate_up = jnp.dot(normed2, w_gu, preferred_element_type=FULL)
    hidden_f, act_pull = jax.vjp(activate, gate_up[:, :ff_width], gate_up[:, ff_width:])
    hidden = hidden_f.astype(LOW)
    part_down = lax.dot_general(cot_flat, hidden, LEAD_DIMS, preferred_element_type=FULL)
    down_sum = lax.psum_scatter(
        part_down.astype(LOW), "shard", scatter_dimension=0, tiled=True
    )
    grad_hidden = jnp.dot(cot_flat, w_down, preferred_element_type=FULL)
    grad_gate, grad_up = act_pull(grad_hidden)
    grad_gu = jnp.concatenate([grad_gate, grad_up], 1).astype(LOW)
    part_gu = lax.dot_general(normed2, grad_gu, LEAD_DIMS, preferred_element_type=FULL)
    part_gu = part_gu.astype(LOW)
    grad_gu, part_gu = lax.optimization_barrier((grad_gu, part_gu))
    gu_sum = lax.psum_scatter(part_gu, "shard", scatter_dimension=0, tiled=True)
    grad_resid, grad_attn_out, sums2, out_part = mid_backward(
        grad_gu.reshape(N_DP, seq, 2 * ff_width),
        w_mlp,
        hidden.reshape(N_DP, seq, ff_width),
        resid,
        cotangent,
        norm_vals,
        4,
    )
    grad_attn_out, down_sum = lax.optimization_barrier((grad_attn_out, down_sum))
    block_out, grad_qkv, bias_sums, part_attn = attn_backward(
        out_part,
        normed1,
        mixture,
        resid,
        grad_attn_out,
        w_out,
        queries,
        keys,
        values,
        mask,
        tables,
        9,
    )
    grad_qkv, part_attn, gu_sum = lax.optimization_barrier((grad_qkv, part_attn, gu_sum))
    attn_sum = lax.psum_scatter(
        part_attn.reshape(D, 4 * width), "shard", scatter_dimension=0, tiled=True
    )
    bias_term = lax.dynamic_update_slice(
        jnp.zeros((3, D), FULL), bias_sums[0].reshape(3, width), (0, my_dp * width)
    )
    rest = jnp.concatenate(
        [jnp.zeros((2, D), FULL), bias_term, sums2[:2], jnp.zeros((1, D), FULL)], 0
    )
    gu_blocks = gu_sum.reshape(N_DP, rows, 2 * ff_width)
    down_blocks = down_sum.reshape(N_DP, rows, ff_width)
    input_grad, norm_sums, gu_grad, down_grad = last_rows(
        grad_qkv, w_qkv, gu_blocks, down_blocks, tokens, grad_resid, norm_vals, rest, 5
    )
    input_grad, block_out = by_place(input_grad), by_place(block_out)
    own_features = lax.dynamic_slice(norm_sums, (0, (my_shard * N_DP + my_dp) * rows), (8, rows))
    own_biases = lax.dynamic_slice(norm_sums, (0, (my_dp * N_SH + my_shard) * rows), (8, rows))
    norm_grad = jnp.concatenate([own_features[:2], own_biases[2:5], own_features[5:7]], 0)

    def square_sum(array):
        array = array.astype(FULL)
        return jnp.sum(array * array)

    squares = square_sum(norm_grad) + square_sum(gu_sum) + square_sum(down_sum)
    squares = jnp.pad(squares.reshape(1, 1), ((0, 7), (0, 127)))
    attn_sum = attn_sum.reshape(N_DP, rows, 4 * width)
    qkv_grad, total = tail(attn_sum, squares, 6)
    overall = jnp.sum(total)
    out_grad = by_place(attn_sum[:, :, 3 * width :].transpose(1, 0, 2).reshape(rows, D))
    grad_size = jnp.sqrt(overall)
    factor = CLIP_NORM / jnp.maximum(grad_size, CLIP_NORM)
    box = factor.reshape(1, 1)
    attn_new, attn_first_new, attn_second_new = adam_attn(
        box, qkv_grad, out_grad, [attn_master, attn_first, attn_second]
    )
    mlp_new, mlp_first_new, mlp_second_new = adam_mlp(
        box, gu_grad, down_grad, [mlp_master, mlp_first, mlp_second]
    )
    norm_new, norm_first_new, norm_second_new = adam_update(
        norm_master, norm_first, norm_second, norm_grad, factor, RATE_VECTOR, 0.0
    )
    return (
        block_out,
        input_grad,
        grad_size,
        attn_new,
        mlp_new,
        norm_new,
        attn_first_new,
        mlp_first_new,
        norm_first_new,
        attn_second_new,
        mlp_second_new,
        norm_second_new,
    )


def solution(mesh):
    in_specs = (
        P(("dp", "shard"), None),
        P(("dp", "shard"), None),
        P(("dp", "shard")),
        P(("dp", "shard")),
        P(("dp", "shard"), None),
        P(("dp", "shard"), None),
        P(None, ("dp", "shard")),
        P(("dp", "shard"), None),
        P(("dp", "shard"), None),
        P(None, ("dp", "shard")),
        P(("dp", "shard"), None),
        P(("dp", "shard"), None),
        P(None, ("dp", "shard")),
    )
    out_specs = (
        P(("dp", "shard"), None),
        P(("dp", "shard"), None),
        P(),
        P(("dp", "shard"), None),
        P(("dp", "shard"), None),
        P(None, ("dp", "shard")),
        P(("dp", "shard"), None),
        P(("dp", "shard"), None),
        P(None, ("dp", "shard")),
        P(("dp", "shard"), None),
        P(("dp", "shard"), None),
        P(None, ("dp", "shard")),
    )
    fast = dict(mesh.shape) == dict(dp=4, shard=8)
    body = per_device_fast if fast else per_device_any
    return jax.shard_map(
        body, mesh=mesh, in_specs=in_specs, out_specs=out_specs, check_vma=False
    )
```

```python
import functools

import numpy as np
import jax
import jax.numpy as jnp
from jax import lax
from jax.experimental import pallas as pl
from jax.experimental.pallas import tpu as pltpu
from jax.sharding import PartitionSpec as P

D = 2048
HEADS = 32
HEAD = 64
FF = 5632
ROT = 16
STEP = 10


NORM_EPS = 1e-05
NEG_FILL = -1e30
ROPE_BASE = 10000.0
CLIP_NORM = 1.0
BETA_ONE = 0.9
BETA_TWO = 0.95
ADAM_EPS = 1e-08
RATE_MATRIX = 0.02
RATE_VECTOR = 0.2
DECAY_MATRIX = 0.1
LEAD_DIMS = (((0,), (0,)), ((), ()))
LAST_DIMS = (((1,), (1,)), ((), ()))


def layer_norm(values_in, gain_vec, shift_vec):
    average = jnp.mean(values_in, axis=-1, keepdims=True)
    centered = values_in - average
    variance = jnp.mean(centered * centered, axis=-1, keepdims=True)
    return centered * lax.rsqrt(variance + NORM_EPS) * gain_vec + shift_vec


def rotary_tables(position_ids):
    half_rot = ROT // 2
    inverse_freq = ROPE_BASE ** (-(jnp.arange(half_rot, dtype=jnp.float32) * 2.0 / ROT))
    angles = position_ids.astype(jnp.float32)[:, None] * inverse_freq[None, :]
    return (jnp.cos(angles)[:, None, :], jnp.sin(angles)[:, None, :])


def rotate(heads_in, cos_table, sin_table):
    half_rot = ROT // 2
    first_half = heads_in[..., :half_rot]
    second_half = heads_in[..., half_rot:ROT]
    rest_part = heads_in[..., ROT:]
    turned_one = first_half * cos_table - second_half * sin_table
    turned_two = second_half * cos_table + first_half * sin_table
    return jnp.concatenate([turned_one, turned_two, rest_part], -1)


def pad_last(array, size):
    missing = size - array.shape[-1]
    if missing == 0:
        return array
    return jnp.pad(array, [(0, 0)] * (array.ndim - 1) + [(0, missing)])


def activate(gate_part, up_part):
    return jax.nn.silu(gate_part) * up_part


def adam_update(master, first, second, grads, factor, rate, decay):
    clipped = grads * factor
    first_new = BETA_ONE * first + (1.0 - BETA_ONE) * clipped
    second_new = BETA_TWO * second + (1.0 - BETA_TWO) * clipped * clipped
    first_hat = first_new / (1.0 - BETA_ONE**STEP)
    second_hat = second_new / (1.0 - BETA_TWO**STEP)
    master_new = master - rate * (first_hat / (jnp.sqrt(second_hat) + ADAM_EPS) + decay * master)
    return (master_new, first_new, second_new)


def exchange_dp(blocks):
    return lax.all_to_all(blocks, "dp", 0, 0, tiled=True)


def gather_dp(rows):
    return lax.all_gather(rows, "dp", axis=0, tiled=True)


def scatter_sum_dp(parts):
    return lax.psum_scatter(parts, "dp", scatter_dimension=0, tiled=True)


def gather_shard(block):
    return lax.all_gather(block, "shard", axis=1)


def scatter_sum_shard(parts):
    return lax.psum_scatter(parts, "shard", scatter_dimension=1)


def layer_stats(values_in):
    average = jnp.mean(values_in, axis=-1, keepdims=True)
    centered = values_in - average
    variance = jnp.mean(centered * centered, axis=-1, keepdims=True)
    inverse = lax.rsqrt(variance + NORM_EPS)
    return centered * inverse, inverse


def layer_back(grads, gain_vec, unit, inverse):
    scaled = grads * gain_vec
    mean_one = jnp.mean(scaled, axis=-1, keepdims=True)
    mean_two = jnp.mean(scaled * unit, axis=-1, keepdims=True)
    return inverse * (scaled - mean_one - unit * mean_two)


def per_device_any(
    tokens,
    cotangent,
    segments,
    positions,
    attn_master,
    mlp_master,
    norm_master,
    attn_first,
    mlp_first,
    norm_first,
    attn_second,
    mlp_second,
    norm_second,
):
    low = jnp.bfloat16
    full = jnp.float32
    n_dp = lax.axis_size("dp")
    n_sh = lax.axis_size("shard")
    seq = tokens.shape[0]
    rows = attn_master.shape[0]
    heads = HEADS // n_dp
    width = D // n_dp
    ff_width = -(-FF // (128 * n_dp)) * 128
    ff_pad = ff_width * n_dp
    scale = HEAD ** (-0.5)

    qkv_send = attn_master[:, : 3 * D].astype(low).reshape(rows, 3, n_dp, width)
    qkv_send = qkv_send.transpose(2, 0, 1, 3).reshape(n_dp, rows, 3 * width)
    mlp_send = pad_last(mlp_master.astype(low).reshape(rows, 3, FF), ff_pad)
    mlp_send = mlp_send.reshape(rows, 3, n_dp, ff_width)
    mlp_send = mlp_send.transpose(2, 0, 1, 3).reshape(n_dp, rows, 3 * ff_width)
    norm_full = lax.all_gather(norm_master.astype(low), ("dp", "shard"), axis=1, tiled=True)
    norm_vals = norm_full.astype(full)
    w_qkv = gather_shard(exchange_dp(qkv_send)).reshape(D, 3 * width)
    w_out = gather_shard(attn_master[None, :, 3 * D :].astype(low)).reshape(width, D)
    tokens_all = gather_dp(tokens)
    places_all = gather_dp(jnp.stack([segments, positions], 0)[None])
    cot_all = gather_dp(cotangent)
    w_mlp = gather_shard(exchange_dp(mlp_send)).reshape(D, 3 * ff_width)
    w_gu = w_mlp[:, : 2 * ff_width]
    w_down = w_mlp[:, 2 * ff_width :]
    seg_all, pos_all = places_all[:, 0], places_all[:, 1]

    inputs_all = tokens_all.astype(full)
    unit1, _ = layer_stats(inputs_all)
    normed1 = (unit1 * norm_vals[0] + norm_vals[1]).astype(low)
    my_dp = lax.axis_index("dp")
    bias = lax.dynamic_slice(norm_vals[2:5], (0, my_dp * width), (3, width)).reshape(3 * width)
    qkv = jnp.dot(normed1, w_qkv, preferred_element_type=full) + bias
    qkv = qkv.reshape(n_dp * seq, 3 * heads, HEAD)
    cos_table, sin_table = rotary_tables(pos_all.reshape(-1))

    def split(array):
        return array.reshape(n_dp, seq, heads, HEAD)

    queries = split(rotate(qkv[:, :heads], cos_table, sin_table).astype(low))
    key_rows = split(rotate(qkv[:, heads : 2 * heads], cos_table, sin_table).astype(low))
    values = split(qkv[:, 2 * heads :].astype(low))
    places = jnp.arange(seq)
    allowed = (seg_all[:, :, None] == seg_all[:, None, :]) & (
        places[:, None] >= places[None, :]
    )[None]
    scores = (
        jnp.einsum("gshd,gthd->ghst", queries, key_rows, preferred_element_type=full) * scale
    )
    scores = jnp.where(allowed[:, None], scores, NEG_FILL)
    attend = jax.nn.softmax(scores, axis=-1)
    attend_low = attend.astype(low)
    mixture = (
        jnp.einsum("ghst,gthd->gshd", attend_low, values, preferred_element_type=full)
        .reshape(n_dp * seq, width)
        .astype(low)
    )
    attn_part = jnp.dot(mixture, w_out, preferred_element_type=full).astype(low)
    resid = tokens.astype(full) + scatter_sum_dp(attn_part).astype(full)
    unit2, inverse2 = layer_stats(resid)
    normed2 = gather_dp((unit2 * norm_vals[5] + norm_vals[6]).astype(low))
    gate_up = jnp.dot(normed2, w_gu, preferred_element_type=full)
    hidden_f, act_pull = jax.vjp(activate, gate_up[:, :ff_width], gate_up[:, ff_width:])
    hidden = hidden_f.astype(low)
    grad_hidden = jnp.dot(cot_all, w_down, preferred_element_type=full)
    grad_gate, grad_up = act_pull(grad_hidden)
    grad_gu = jnp.concatenate([grad_gate, grad_up], 1).astype(low)
    norm2_part = lax.dot_general(grad_gu, w_gu, LAST_DIMS, preferred_element_type=full)
    grad_norm2 = scatter_sum_dp(norm2_part.astype(low)).astype(full)
    out_part = lax.dot_general(hidden, w_down, LAST_DIMS, preferred_element_type=full)
    block_out = (resid + scatter_sum_dp(out_part.astype(low)).astype(full)).astype(low)
    part_gu = lax.dot_general(normed2, grad_gu, LEAD_DIMS, preferred_element_type=full)
    part_down = lax.dot_general(cot_all, hidden, LEAD_DIMS, preferred_element_type=full)
    part_mlp = jnp.concatenate([part_gu.astype(low), part_down.astype(low)], 1)
    mlp_sum = scatter_sum_shard(part_mlp.reshape(n_dp, n_sh, rows, 3 * ff_width))

    grad_gain2 = jnp.sum(grad_norm2 * unit2, axis=0)
    grad_shift2 = jnp.sum(grad_norm2, axis=0)
    grad_resid = cotangent.astype(full) + layer_back(grad_norm2, norm_vals[5], unit2, inverse2)
    grad_attn_out = gather_dp(grad_resid.astype(low))
    grad_mixture = lax.dot_general(grad_attn_out, w_out, LAST_DIMS, preferred_element_type=full)
    grad_mixture = split(grad_mixture.astype(low))
    grad_attend = jnp.einsum("gshd,gthd->ghst", grad_mixture, values, preferred_element_type=full)
    grad_values = jnp.einsum(
        "ghst,gshd->gthd", attend_low, grad_mixture, preferred_element_type=full
    )
    grad_scores = (
        attend * (grad_attend - jnp.sum(attend * grad_attend, axis=-1, keepdims=True))
    ).astype(low)
    grad_queries = (
        jnp.einsum("ghst,gthd->gshd", grad_scores, key_rows, preferred_element_type=full) * scale
    )
    grad_keys = (
        jnp.einsum("ghst,gshd->gthd", grad_scores, queries, preferred_element_type=full) * scale
    )

    def turn_back(grads):
        grads = grads.reshape(n_dp * seq, heads, HEAD)
        return rotate(grads, cos_table, -sin_table).reshape(n_dp * seq, width)

    grad_qkv = jnp.concatenate(
        [
            turn_back(grad_queries),
            turn_back(grad_keys),
            grad_values.reshape(n_dp * seq, width),
        ],
        1,
    ).astype(low)
    part_qkv = lax.dot_general(normed1, grad_qkv, LEAD_DIMS, preferred_element_type=full)
    part_out = lax.dot_general(mixture, grad_attn_out, LEAD_DIMS, preferred_element_type=full)
    qkv_sum = scatter_sum_shard(part_qkv.astype(low).reshape(n_dp, n_sh, rows, 3 * width))
    out_sum = scatter_sum_shard(part_out.astype(low).reshape(1, n_sh, rows, D))[0].astype(full)

    norm1_part = lax.dot_general(grad_qkv, w_qkv, LAST_DIMS, preferred_element_type=full)
    grad_gain1 = jnp.sum(norm1_part * unit1, axis=0)
    grad_shift1 = jnp.sum(norm1_part, axis=0)
    grad_bias = jnp.sum(grad_qkv, axis=0, dtype=full).reshape(3, width)
    grad_norm1 = scatter_sum_dp(norm1_part.astype(low)).astype(full)
    own_unit1, own_inverse1 = layer_stats(tokens.astype(full))
    input_grad = grad_resid + layer_back(grad_norm1, norm_vals[0], own_unit1, own_inverse1)
    norm_term = lax.dynamic_update_slice(
        jnp.zeros((3, D), full), grad_bias, (0, my_dp * width)
    )
    norm_term = jnp.concatenate(
        [grad_gain1[None], grad_shift1[None], norm_term, grad_gain2[None], grad_shift2[None]], 0
    )
    norm_grad = lax.psum_scatter(norm_term, ("dp", "shard"), scatter_dimension=1, tiled=True)

    def columns_back(summed, parts, part_width, keep):
        back = exchange_dp(summed).reshape(n_dp, rows, parts, part_width)
        back = back.transpose(1, 2, 0, 3).reshape(rows, parts, n_dp * part_width)
        return back[:, :, :keep].reshape(rows, parts * keep).astype(full)

    mlp_grad = columns_back(mlp_sum, 3, ff_width, FF)
    attn_grad = jnp.concatenate([columns_back(qkv_sum, 3, width, D), out_sum], 1)
    squares = (
        jnp.sum(attn_grad * attn_grad)
        + jnp.sum(mlp_grad * mlp_grad)
        + jnp.sum(norm_grad * norm_grad)
    )
    overall = lax.psum(squares, ("dp", "shard"))
    grad_size = jnp.sqrt(overall)
    factor = CLIP_NORM / jnp.maximum(grad_size, CLIP_NORM)
    attn_new, attn_first_new, attn_second_new = adam_update(
        attn_master, attn_first, attn_second, attn_grad, factor, RATE_MATRIX, DECAY_MATRIX
    )
    mlp_new, mlp_first_new, mlp_second_new = adam_update(
        mlp_master, mlp_first, mlp_second, mlp_grad, factor, RATE_MATRIX, DECAY_MATRIX
    )
    norm_new, norm_first_new, norm_second_new = adam_update(
        norm_master, norm_first, norm_second, norm_grad, factor, RATE_VECTOR, 0.0
    )
    return (
        block_out,
        input_grad,
        grad_size,
        attn_new,
        mlp_new,
        norm_new,
        attn_first_new,
        mlp_first_new,
        norm_first_new,
        attn_second_new,
        mlp_second_new,
        norm_second_new,
    )


MESH = pl.DeviceIdType.MESH
ANY = pl.BlockSpec(memory_space=pl.ANY)
VMEM = pl.BlockSpec(memory_space=pltpu.VMEM)
LOW = jnp.bfloat16
FULL = jnp.float32
N_DP = 4
N_SH = 8
BIG_VMEM = 56 * 1024 * 1024


def dp_peer(step):
    mine = lax.axis_index("dp")
    if step == 1:
        return mine + 1 - 2 * (mine % 2)
    if step == 2:
        return (mine + 2) % 4
    return 3 - mine


def to_dp(step):
    return (dp_peer(step), lax.axis_index("shard"))


def to_shard(step):
    return (lax.axis_index("dp"), (lax.axis_index("shard") + step) % N_SH)


def cost(micros):
    return pl.CostEstimate(flops=0, bytes_accessed=int(micros * 3.0e6), transcendentals=0)


def greet(peers):
    barrier = pltpu.get_barrier_semaphore()
    for peer in peers:
        pl.semaphore_signal(barrier, inc=1, device_id=peer, device_id_type=MESH)
    pl.semaphore_wait(barrier, len(peers))


def remote(source, target, sems, index, peer):
    return pltpu.make_async_remote_copy(
        src_ref=source,
        dst_ref=target,
        send_sem=sems[0].at[index],
        recv_sem=sems[1].at[index],
        device_id=peer,
        device_id_type=MESH,
    )


def sems(count):
    return [pltpu.SemaphoreType.DMA((count,)), pltpu.SemaphoreType.DMA((count,))]


def comm_params(number):
    return pltpu.CompilerParams(
        collective_id=number, has_side_effects=True, vmem_limit_bytes=BIG_VMEM
    )


def to_places(value):
    size = value.shape[1] // (N_DP * N_SH)
    starts = [(n * N_DP + d) * size for d in range(N_DP) for n in range(N_SH)]
    return jnp.concatenate([value[:, start : start + size] for start in starts], axis=1)


def to_shards(value):
    size = value.shape[1] // (N_DP * N_SH)
    starts = [(d * N_SH + n) * size for n in range(N_SH) for d in range(N_DP)]
    return jnp.concatenate([value[:, start : start + size] for start in starts], axis=1)


CHUNK = 32


def in_chunks(rows, body):
    def step(index, carry):
        body(pl.ds(pl.multiple_of(index * CHUNK, CHUNK), CHUNK))
        return carry

    lax.fori_loop(0, rows // CHUNK, step, 0)


def spread_plan(own, result, sem_pair, base):
    half = own.shape[0] // 2
    top, bottom = pl.ds(0, half), pl.ds(half, half)
    sent = [
        remote(own.at[top], result.at[1, top], sem_pair, base + 0, to_dp(1)),
        remote(own.at[bottom], result.at[2, bottom], sem_pair, base + 1, to_dp(2)),
        remote(own.at[bottom], result.at[1, bottom], sem_pair, base + 2, to_dp(1)),
        remote(own.at[top], result.at[2, top], sem_pair, base + 3, to_dp(2)),
    ]
    passed = [
        remote(result.at[1, top], result.at[3, top], sem_pair, base + 4, to_dp(2)),
        remote(result.at[2, bottom], result.at[3, bottom], sem_pair, base + 5, to_dp(1)),
    ]
    return sent, passed


def spread(own, result, sem_pair, base):
    sent, passed = spread_plan(own, result, sem_pair, base)
    for copy in sent:
        copy.start()
    return sent, passed


def pass_on(sent, passed):
    sent[0].wait_recv()
    passed[0].start()
    sent[1].wait_recv()
    passed[1].start()


def spread_end(sent, passed):
    sent[2].wait_recv()
    sent[3].wait_recv()
    passed[0].wait_recv()
    passed[1].wait_recv()
    for copy in sent + passed:
        copy.wait_send()


SLABS = 6


def start_kernel(
    attn_hbm, mlp_hbm, norm_ref, tok_hbm, cot_hbm, place_ref,
    w_qkv, w_out, norm_all, tok_all, place_all, gu_out, down_out, tok_own, cot_own,
    attn_in, mlp_in, tok_in, cot_in, qkv_send, out_send, norm_send, gu_send, down_send,
    tok_low, cot_low,
    up_send, up_recv, down_s, down_recv, core_send, core_recv, send, recv, local,
):
    mine, place = lax.axis_index("dp"), lax.axis_index("shard")
    line, core = place // 2, place % 2
    width, ff_width = qkv_send.shape[-1] // 3, down_send.shape[-1]
    above, below = (mine, place + 2), (mine, place - 2)
    partner = (mine, place + 1 - 2 * core)
    has_above, has_below = line < N_SH // 2 - 1, line > 0
    pair = (send, recv)
    loads = [
        pltpu.make_async_copy(attn_hbm, attn_in, local.at[0]),
        pltpu.make_async_copy(tok_hbm, tok_in, local.at[1]),
        pltpu.make_async_copy(mlp_hbm, mlp_in, local.at[2]),
        pltpu.make_async_copy(cot_hbm, cot_in, local.at[3]),
    ]
    for copy in loads:
        copy.start()

    barrier = pltpu.get_barrier_semaphore()
    for peer in [to_dp(k) for k in (1, 2, 3)] + [partner]:
        pl.semaphore_signal(barrier, inc=1, device_id=peer, device_id_type=MESH)

    @pl.when(has_above)
    def _():
        pl.semaphore_signal(barrier, inc=1, device_id=above, device_id_type=MESH)

    @pl.when(has_below)
    def _():
        pl.semaphore_signal(barrier, inc=1, device_id=below, device_id_type=MESH)

    norm_send[...] = jnp.zeros_like(norm_send)
    norm_send[0:7, 0 : norm_ref.shape[1]] = norm_ref[...].astype(LOW).astype(FULL)
    loads[0].wait()
    for part in range(3):
        for d in range(N_DP):
            begin = part * D + d * width
            qkv_send[d, :, part * width : part * width + width] = attn_in[
                :, begin : begin + width
            ].astype(LOW)
    out_send[...] = to_shards(attn_in[:, 3 * D :]).astype(LOW)

    @pl.when(has_above & has_below)
    def _():
        pl.semaphore_wait(barrier, 6)

    @pl.when(jnp.logical_not(has_above & has_below))
    def _():
        pl.semaphore_wait(barrier, 5)

    def slab(n, shard):
        if n == 0:
            return w_qkv.at[shard, mine]
        if n == 1:
            return w_out.at[shard]
        if n == 2:
            return norm_all.at[shard]
        return w_qkv.at[shard, dp_peer(n - 2)]

    def source(n):
        return {0: qkv_send.at[mine], 1: out_send}.get(n, slab(n, place))

    def along(n, shard, hop, sem_pair, peer, held=None):
        start = slab(n, shard) if held is None else held
        return remote(start, slab(n, shard), sem_pair, hop * SLABS + n, peer)

    ups, downs, cores = (up_send, up_recv), (down_s, down_recv), (core_send, core_recv)

    def pass_block(n, origin, hop, held, upward, downward):
        shard = 2 * origin + core
        if upward:

            @pl.when(has_above)
            def _():
                along(n, shard, hop, ups, above, held).start()

        if downward:

            @pl.when(has_below)
            def _():
                along(n, shard, hop, downs, below, held).start()

        along(n, shard, origin, cores, partner, held).start()

    norms = [
        remote(norm_send, norm_all.at[place, mine], pair, 21 + k - 1, to_dp(k)) for k in (1, 2, 3)
    ]
    trade = [
        remote(qkv_send.at[dp_peer(k)], w_qkv.at[place, mine], pair, k - 1, to_dp(k))
        for k in (1, 2, 3)
    ]
    own = [
        pltpu.make_async_copy(qkv_send.at[mine], w_qkv.at[place, mine], local.at[4]),
        pltpu.make_async_copy(out_send, w_out.at[place], local.at[5]),
        pltpu.make_async_copy(norm_send, norm_all.at[place, mine], local.at[6]),
        pltpu.make_async_copy(place_ref, place_all.at[0], local.at[7]),
    ]
    for copy in norms + trade:
        copy.start()
    pass_block(0, line, 0, source(0), True, True)
    pass_block(1, line, 0, source(1), True, True)
    for copy in own:
        copy.start()

    loads[1].wait()

    def permute_tokens(here):
        tok_low[here] = to_shards(tok_in[here].astype(FULL)).astype(LOW)

    in_chunks(tok_in.shape[0], permute_tokens)
    places = [
        remote(place_ref, place_all.at[k], pair, 9 + k - 1, to_dp(k)) for k in (1, 2, 3)
    ]
    for copy in places:
        copy.start()
    tok = spread(tok_low, tok_all, pair, 3)
    keep = [
        pltpu.make_async_copy(tok_low, tok_all.at[0], local.at[8]),
        pltpu.make_async_copy(tok_low, tok_own, local.at[9]),
    ]
    for copy in keep:
        copy.start()

    own[2].wait()
    for copy in norms:
        copy.wait_recv()
    pass_block(2, line, 0, None, True, True)
    for k in (1, 2, 3):
        trade[k - 1].wait_recv()
        pass_block(2 + k, line, 0, None, True, True)

    loads[2].wait()
    for d in range(N_DP):
        for part in range(2):
            begin = part * FF + d * ff_width
            gu_send[d, :, part * ff_width : part * ff_width + ff_width] = mlp_in[
                :, begin : begin + ff_width
            ].astype(LOW)
        begin = 2 * FF + d * ff_width
        down_send[d] = mlp_in[:, begin : begin + ff_width].astype(LOW)
    blocks = []
    for n, (held, target) in enumerate(((gu_send, gu_out), (down_send, down_out))):
        for k in (3, 1, 2):
            blocks.append(
                remote(held.at[dp_peer(k)], target.at[mine], pair, 12 + 3 * n + k - 1, to_dp(k))
            )
        blocks.append(pltpu.make_async_copy(held.at[mine], target.at[mine], local.at[10 + n]))

    loads[3].wait()

    def permute_cotangent(here):
        cot_low[here] = to_shards(cot_in[here].astype(FULL)).astype(LOW)

    in_chunks(cot_in.shape[0], permute_cotangent)
    keep.append(pltpu.make_async_copy(cot_low, cot_own, local.at[12]))
    keep[2].start()

    def hop_step(hop):
        for n in range(SLABS):

            @pl.when(line >= hop)
            def _():
                shard = place - 2 * hop
                along(n, shard, hop - 1, ups, above).wait_recv()
                pass_block(n, line - hop, hop, None, True, False)

            @pl.when(line + hop < N_SH // 2)
            def _():
                shard = place + 2 * hop
                along(n, shard, hop - 1, downs, below).wait_recv()
                pass_block(n, line + hop, hop, None, False, True)

    hop_step(1)
    pass_on(*tok)
    for copy in blocks:
        copy.start()
    hop_step(2)
    hop_step(3)

    spread_end(*tok)
    for copy in blocks + own[:2] + own[3:] + keep + places:
        copy.wait()
    for copy in norms + trade:
        copy.wait_send()
    for hop in range(N_SH // 2 - 1):
        for n in range(SLABS):

            @pl.when(has_above & (line >= hop))
            def _():
                along(n, place - 2 * hop, hop, ups, above).wait_send()

            @pl.when(has_below & (line + hop < N_SH // 2))
            def _():
                along(n, place + 2 * hop, hop, downs, below).wait_send()

    for origin in range(N_SH // 2):
        for n in range(SLABS):
            along(n, 2 * origin + core, origin, cores, partner).wait_send()
            along(n, 2 * origin + 1 - core, origin, cores, partner).wait_recv()


def start(attn_master, mlp_master, norm_master, tokens, cotangent, places, number):
    rows = attn_master.shape[0]
    width, ff_width = D // N_DP, FF // N_DP
    seq = tokens.shape[0]
    norm_shape = (8, 128)
    hops = (N_SH // 2 - 1) * SLABS
    return pl.pallas_call(
        start_kernel,
        out_shape=[
            jax.ShapeDtypeStruct((N_SH, N_DP, rows, 3 * width), LOW),
            jax.ShapeDtypeStruct((N_SH, rows, D), LOW),
            jax.ShapeDtypeStruct((N_SH, N_DP) + norm_shape, FULL),
            jax.ShapeDtypeStruct((N_DP, seq, D), LOW),
            jax.ShapeDtypeStruct((N_DP,) + places.shape, places.dtype),
            jax.ShapeDtypeStruct((N_DP, rows, 2 * ff_width), LOW),
            jax.ShapeDtypeStruct((N_DP, rows, ff_width), LOW),
            jax.ShapeDtypeStruct((seq, D), LOW),
            jax.ShapeDtypeStruct((seq, D), LOW),
        ],
        in_specs=[ANY, ANY, VMEM, ANY, ANY, ANY],
        out_specs=[ANY] * 9,
        scratch_shapes=[
            pltpu.VMEM(attn_master.shape, FULL),
            pltpu.VMEM(mlp_master.shape, FULL),
            pltpu.VMEM(tokens.shape, LOW),
            pltpu.VMEM(tokens.shape, LOW),
            pltpu.VMEM((N_DP, rows, 3 * width), LOW),
            pltpu.VMEM((rows, D), LOW),
            pltpu.VMEM(norm_shape, FULL),
            pltpu.VMEM((N_DP, rows, 2 * ff_width), LOW),
            pltpu.VMEM((N_DP, rows, ff_width), LOW),
            pltpu.VMEM(tokens.shape, LOW),
            pltpu.VMEM(tokens.shape, LOW),
        ]
        + sems(hops)
        + sems(hops)
        + sems((N_SH // 2) * SLABS)
        + sems(24)
        + [pltpu.SemaphoreType.DMA((13,))],
        compiler_params=comm_params(number),
        cost_estimate=cost(90),
        name="start",
    )(attn_master, mlp_master, norm_master, tokens, cotangent, places)


def unit_rows(values):
    average = jnp.mean(values, axis=-1, keepdims=True)
    centered = values - average
    variance = jnp.mean(centered * centered, axis=-1, keepdims=True)
    inverse = lax.rsqrt(variance + NORM_EPS)
    return centered * inverse, inverse


def turn(value, cos_ref, up_ref, down_ref, sign):
    left = pltpu.roll(value, 128 - ROT // 2, 1)
    right = pltpu.roll(value, ROT // 2, 1)
    return value * cos_ref[...] + sign * (left * up_ref[...] + right * down_ref[...])


def head_masks():
    lane = lax.broadcasted_iota(jnp.int32, (1, 128), 1)
    return [lane < HEAD, lane >= HEAD]


def softmax_rows(queries, keys, bias):
    scores = lax.dot_general(queries, keys, LAST_DIMS, preferred_element_type=FULL)
    scores = scores * (HEAD ** (-0.5)) + bias
    top = jnp.max(scores, axis=-1, keepdims=True)
    weights = jnp.exp(scores - top)
    return weights / jnp.sum(weights, axis=-1, keepdims=True)


def fill_tables(place_ref, rate_ref, cos_ref, up_ref, down_ref, mask_ref):
    seq = place_ref.shape[-1]
    half = ROT // 2
    row = place_ref[0].astype(FULL)
    columns = jnp.transpose(jnp.broadcast_to(row[0:1], (8, seq)))[:, 0:1]
    spots = jnp.transpose(jnp.broadcast_to(row[1:2], (8, seq)))[:, 0:1]
    angles = spots * rate_ref[0:1, :]
    lane = lax.broadcasted_iota(jnp.int32, (1, 128), 1) % HEAD
    sines = jnp.sin(angles)
    cos_ref[...] = jnp.where(lane < ROT, jnp.cos(angles), 1.0)
    up_ref[...] = jnp.where(lane < half, -sines, 0.0)
    down_ref[...] = jnp.where((lane >= half) & (lane < ROT), sines, 0.0)
    later = lax.broadcasted_iota(jnp.int32, (seq, seq), 0) >= lax.broadcasted_iota(
        jnp.int32, (seq, seq), 1
    )
    mask_ref[0] = jnp.where((columns == row[0:1]) & later, 0.0, NEG_FILL)


def attn_forward_kernel(
    cot_ref, tok_ref, place_ref, rate_ref, norm_ref, w_ref, b_ref,
    cot_all, normed_ref, q_ref, k_ref, v_ref, mix_ref, cos_ref, up_ref, down_ref, mask_ref,
    qkv_ref, send, recv, local,
):
    width = q_ref.shape[-1]
    step, last = pl.program_id(0), pl.num_programs(0) - 1
    sent, passed = spread_plan(cot_ref, cot_all, (send, recv), 0)
    keep = pltpu.make_async_copy(cot_ref, cot_all.at[0], local.at[0])

    @pl.when(step == 0)
    def _():
        greet([to_dp(1), to_dp(2)])
        for copy in sent:
            copy.start()
        keep.start()

    @pl.when(step == last)
    def _():
        pass_on(sent, passed)

    fill_tables(place_ref, rate_ref, cos_ref, up_ref, down_ref, mask_ref)
    unit, _ = unit_rows(tok_ref[0].astype(FULL))
    normed_ref[0] = (unit * norm_ref[0:1, :] + norm_ref[1:2, :]).astype(LOW)
    qkv_ref[...] = jnp.dot(normed_ref[0], w_ref[...], preferred_element_type=FULL) + b_ref[...]
    masks = head_masks()
    for pair in range(width // 128):
        here = slice(pair * 128, pair * 128 + 128)
        queries = turn(qkv_ref[:, here], cos_ref, up_ref, down_ref, 1.0).astype(LOW)
        there = slice(width + pair * 128, width + pair * 128 + 128)
        keys = turn(qkv_ref[:, there], cos_ref, up_ref, down_ref, 1.0).astype(LOW)
        there = slice(2 * width + pair * 128, 2 * width + pair * 128 + 128)
        values = qkv_ref[:, there].astype(LOW)
        q_ref[0, :, here] = queries
        k_ref[0, :, here] = keys
        v_ref[0, :, here] = values
        total = None
        for mask in masks:
            attend = softmax_rows(queries, jnp.where(mask, keys, 0), mask_ref[0])
            part = jnp.dot(
                attend.astype(LOW), jnp.where(mask, values, 0), preferred_element_type=FULL
            )
            total = part if total is None else total + part
        mix_ref[0, :, here] = total.astype(LOW)

    @pl.when(step == last)
    def _():
        spread_end(sent, passed)
        keep.wait()


def group_spec(array):
    return pl.BlockSpec((1,) + array.shape[1:], lambda g: (g, 0, 0))


def whole_spec(array):
    return pl.BlockSpec(array.shape, lambda g: (0,) * len(array.shape))


def attn_forward(cotangent, tokens, places, rates, norm_vals, w_qkv, bias, number):
    groups, seq, _ = tokens.shape
    width = w_qkv.shape[1] // 3
    row_spec = pl.BlockSpec((seq, 128), lambda g: (g, 0))
    part = jax.ShapeDtypeStruct((groups, seq, width), LOW)
    normed = jax.ShapeDtypeStruct(tokens.shape, LOW)
    table = jax.ShapeDtypeStruct((groups * seq, 128), FULL)
    mask = jax.ShapeDtypeStruct((groups, seq, seq), FULL)
    return pl.pallas_call(
        attn_forward_kernel,
        grid=(groups,),
        out_shape=[normed, normed, part, part, part, part, table, table, table, mask],
        in_specs=[
            ANY,
            group_spec(tokens),
            group_spec(places),
            whole_spec(rates),
            whole_spec(norm_vals),
            whole_spec(w_qkv),
            whole_spec(bias),
        ],
        out_specs=[ANY, group_spec(normed)]
        + [group_spec(part)] * 4
        + [row_spec] * 3
        + [group_spec(mask)],
        scratch_shapes=[pltpu.VMEM((seq, 3 * width), FULL)]
        + sems(6)
        + [pltpu.SemaphoreType.DMA((1,))],
        compiler_params=comm_params(number),
        cost_estimate=pl.CostEstimate(
            flops=2 * groups * seq * (D * 3 * width + 2 * seq * width * 2),
            bytes_accessed=2 * (w_qkv.size + 3 * tokens.size),
            transcendentals=groups * seq * seq * (width // HEAD),
        ),
        name="attn_forward",
    )(cotangent, tokens, places, rates, norm_vals, w_qkv, bias)


def attn_backward_kernel(
    part_hbm, normed_hbm, mix_hbm, gao_hbm, resid_ref, gao_ref, w_ref, q_ref, k_ref, v_ref,
    mask_ref, cos_ref, up_ref, down_ref,
    block_ref, grad_ref, sum_ref, attn_ref,
    gm_ref, parts, normed, mix, gao, grads_all, out, diag, full, send, recv, local,
):
    width = q_ref.shape[-1]
    rows = q_ref.shape[1]
    step, last = pl.program_id(0), pl.num_programs(0) - 1
    total = RowSum(parts, (out, diag, full), (send, recv), 0)
    loads = [
        pltpu.make_async_copy(part_hbm, parts, local.at[0]),
        pltpu.make_async_copy(mix_hbm, mix, local.at[1]),
        pltpu.make_async_copy(gao_hbm, gao, local.at[2]),
        pltpu.make_async_copy(normed_hbm, normed, local.at[3]),
    ]

    @pl.when(step == 0)
    def _():
        for copy in loads:
            copy.start()
        greet([to_dp(1), to_dp(2)])
        loads[0].wait()
        for k in (3, 1, 2):
            total.send(k)
        sum_ref[...] = jnp.zeros_like(sum_ref)

    @pl.when(step == 2)
    def _():
        total.relay()

    scale = HEAD ** (-0.5)
    gm_ref[...] = lax.dot_general(
        gao_ref[0], w_ref[...], LAST_DIMS, preferred_element_type=FULL
    ).astype(LOW)
    masks = head_masks()
    for pair in range(width // 128):
        here = slice(pair * 128, pair * 128 + 128)
        queries, keys, values = q_ref[0, :, here], k_ref[0, :, here], v_ref[0, :, here]
        grads = gm_ref[:, here]
        grad_q = grad_k = grad_v = 0.0
        for mask in masks:
            keys_one = jnp.where(mask, keys, 0)
            attend = softmax_rows(queries, keys_one, mask_ref[0])
            grad_attend = lax.dot_general(
                grads, jnp.where(mask, values, 0), LAST_DIMS, preferred_element_type=FULL
            )
            grad_v += lax.dot_general(
                attend.astype(LOW),
                jnp.where(mask, grads, 0),
                LEAD_DIMS,
                preferred_element_type=FULL,
            )
            mean = jnp.sum(attend * grad_attend, axis=-1, keepdims=True)
            grad_scores = (attend * (grad_attend - mean)).astype(LOW)
            grad_q += jnp.dot(grad_scores, keys_one, preferred_element_type=FULL)
            grad_k += lax.dot_general(
                grad_scores, jnp.where(mask, queries, 0), LEAD_DIMS, preferred_element_type=FULL
            )
        grad_q = turn(grad_q * scale, cos_ref, up_ref, down_ref, -1.0)
        grad_k = turn(grad_k * scale, cos_ref, up_ref, down_ref, -1.0)
        for n, grad in enumerate((grad_q, grad_k, grad_v)):
            start = n * width + pair * 128
            grad_ref[0, :, start : start + 128] = grad.astype(LOW)
    grads_all[pl.ds(pl.multiple_of(step * rows, rows), rows)] = grad_ref[0]
    sum_ref[0:1, :] += jnp.sum(grad_ref[0].astype(FULL), axis=0, keepdims=True)

    @pl.when(step == last)
    def _():
        for copy in loads[1:]:
            copy.wait()

        def one_shard(index, carry):
            here = pl.ds(pl.multiple_of(index * 256, 256), 256)
            attn_ref[index, :, : 3 * width] = lax.dot_general(
                normed[:, here], grads_all[...], LEAD_DIMS, preferred_element_type=FULL
            ).astype(LOW)
            return carry

        lax.fori_loop(0, N_SH, one_shard, 0)
        for pair in range(width // 128):
            value = lax.dot_general(
                mix[:, pair * 128 : pair * 128 + 128],
                gao[...],
                LEAD_DIMS,
                preferred_element_type=FULL,
            ).astype(LOW)
            for side in range(2):
                for part in range(N_DP):
                    attn_ref[2 * pair + side, part * 64 : part * 64 + 64, 3 * width :] = value[
                        side * 64 : side * 64 + 64, part * width : part * width + width
                    ]
        total.finish()

        def body(here):
            block_ref[here] = to_places(resid_ref[here] + total.rows(here)).astype(LOW)

        in_chunks(rows, body)


def attn_backward(
    out_part, normed1, mixture, resid, gao, w_out, queries, keys, values, mask, tables, number
):
    groups, seq, cols = gao.shape
    width = queries.shape[-1]
    row_spec = pl.BlockSpec((seq, 128), lambda g: (g, 0))
    grad = jax.ShapeDtypeStruct((groups, seq, 3 * width), LOW)
    sums = jax.ShapeDtypeStruct((8, 3 * width), FULL)
    flat = groups * seq
    return pl.pallas_call(
        attn_backward_kernel,
        grid=(groups,),
        out_shape=[
            jax.ShapeDtypeStruct(resid.shape, LOW),
            grad,
            sums,
            jax.ShapeDtypeStruct((N_SH, D // N_SH, 4 * width), LOW),
        ],
        in_specs=[
            ANY,
            ANY,
            ANY,
            ANY,
            VMEM,
            group_spec(gao),
            VMEM,
            group_spec(queries),
            group_spec(keys),
            group_spec(values),
            group_spec(mask),
            row_spec,
            row_spec,
            row_spec,
        ],
        out_specs=[VMEM, group_spec(grad), whole_spec(sums), VMEM],
        scratch_shapes=[
            pltpu.VMEM((seq, width), LOW),
            pltpu.VMEM(gao.shape, LOW),
            pltpu.VMEM((flat, cols), LOW),
            pltpu.VMEM((flat, width), LOW),
            pltpu.VMEM((flat, cols), LOW),
            pltpu.VMEM((flat, 3 * width), LOW),
        ]
        + row_sum_scratch(seq, cols)
        + sems(6)
        + [pltpu.SemaphoreType.DMA((4,))],
        compiler_params=comm_params(number),
        cost_estimate=cost(55),
        name="attn_backward",
    )(
        out_part,
        normed1.reshape(flat, cols),
        mixture.reshape(flat, width),
        gao.reshape(flat, cols),
        resid,
        gao,
        w_out,
        queries,
        keys,
        values,
        mask,
        *tables,
    )


class RowSum:
    scratch = 3

    def __init__(self, parts, scratch, pair, base):
        self.parts = parts
        self.out, self.diag, self.full = scratch
        self.half = parts.shape[1] // 2
        self.top, self.bottom = pl.ds(0, self.half), pl.ds(self.half, self.half)
        top, bottom = self.top, self.bottom
        self.first = [
            remote(parts.at[3, top], self.diag.at[0], pair, base + 0, to_dp(1)),
            remote(parts.at[3, bottom], self.diag.at[1], pair, base + 1, to_dp(2)),
            remote(parts.at[1, top], self.full.at[0, top], pair, base + 2, to_dp(1)),
            remote(parts.at[2, bottom], self.full.at[1, bottom], pair, base + 3, to_dp(2)),
        ]
        self.second = [
            remote(self.out.at[0], self.full.at[0, bottom], pair, base + 4, to_dp(1)),
            remote(self.out.at[1], self.full.at[1, top], pair, base + 5, to_dp(2)),
        ]

    def send(self, k):
        for copy in {3: self.first[:2], 1: self.first[2:3], 2: self.first[3:]}[k]:
            copy.start()

    def relay(self):
        self.first[1].wait_recv()
        self.out[0] = (
            self.parts[1, self.bottom].astype(FULL) + self.diag[1].astype(FULL)
        ).astype(LOW)
        self.second[0].start()
        self.first[0].wait_recv()
        self.out[1] = (self.parts[2, self.top].astype(FULL) + self.diag[0].astype(FULL)).astype(
            LOW
        )
        self.second[1].start()

    def finish(self):
        self.first[2].wait_recv()
        self.first[3].wait_recv()
        self.second[0].wait_recv()
        self.second[1].wait_recv()
        for copy in self.first + self.second:
            copy.wait_send()

    def rows(self, part):
        return (
            self.parts[0, part].astype(FULL)
            + self.full[0, part].astype(FULL)
            + self.full[1, part].astype(FULL)
        )


def row_sum_scratch(rows, cols):
    return [
        pltpu.VMEM((2, rows // 2, cols), LOW),
        pltpu.VMEM((2, rows // 2, cols), LOW),
        pltpu.VMEM((2, rows, cols), LOW),
    ]


def mid_forward_kernel(
    mix_ref, w_ref, tok_ref, norm_ref, resid_ref, normed_all,
    parts, out, diag, full, own, send, recv, local,
):
    rows = tok_ref.shape[0]
    greet([to_dp(1), to_dp(2)])
    total = RowSum(parts, (out, diag, full), (send, recv), 0)
    for k in (3, 1, 2, 0):
        parts[k] = jnp.dot(mix_ref[k], w_ref[...], preferred_element_type=FULL).astype(LOW)
        if k:
            total.send(k)
    total.relay()
    total.finish()

    def body(here):
        resid = tok_ref[here].astype(FULL) + total.rows(here)
        resid_ref[here] = resid
        unit, _ = unit_rows(resid)
        own[here] = (unit * norm_ref[5:6, :] + norm_ref[6:7, :]).astype(LOW)

    in_chunks(rows, body)
    keep = pltpu.make_async_copy(own, normed_all.at[0], local.at[0])
    sent = spread(own, normed_all, (send, recv), 6)
    keep.start()
    pass_on(*sent)
    spread_end(*sent)
    keep.wait()


def mid_forward(mixture, w_out, tokens, norm_vals, number):
    rows, cols = tokens.shape
    group = (N_DP, rows, cols)
    return pl.pallas_call(
        mid_forward_kernel,
        out_shape=[
            jax.ShapeDtypeStruct(tokens.shape, FULL),
            jax.ShapeDtypeStruct(group, LOW),
        ],
        in_specs=[VMEM] * 4,
        out_specs=[VMEM, ANY],
        scratch_shapes=[pltpu.VMEM(group, LOW)]
        + row_sum_scratch(rows, cols)
        + [pltpu.VMEM((rows, cols), LOW)]
        + sems(12)
        + [pltpu.SemaphoreType.DMA((1,))],
        compiler_params=comm_params(number),
        cost_estimate=cost(92),
        name="mid_forward",
    )(mixture, w_out, tokens, norm_vals)


def mid_backward_kernel(
    ggu_hbm, wgu_hbm, wdown_hbm, hid_hbm, resid_ref, cot_ref, norm_ref,
    grad_ref, gao_all, sum_ref, part_ref,
    ggu, w_gu, w_down, hid, parts, out, diag, full, own, send, recv, local,
):
    rows = resid_ref.shape[0]
    loads = [pltpu.make_async_copy(wgu_hbm, w_gu, local.at[0])]
    loads += [pltpu.make_async_copy(ggu_hbm.at[k], ggu.at[k], local.at[1 + k]) for k in range(4)]
    loads += [
        pltpu.make_async_copy(wdown_hbm, w_down, local.at[5]),
        pltpu.make_async_copy(hid_hbm, hid, local.at[6]),
    ]
    for n in (0, 4, 2, 3, 1, 5, 6):
        loads[n].start()
    greet([to_dp(1), to_dp(2)])
    total = RowSum(parts, (out, diag, full), (send, recv), 0)
    loads[0].wait()
    for k in (3, 1, 2, 0):
        loads[1 + k].wait()
        parts[k] = lax.dot_general(
            ggu[k], w_gu[...], LAST_DIMS, preferred_element_type=FULL
        ).astype(LOW)
        if k:
            total.send(k)
    sum_ref[...] = jnp.zeros_like(sum_ref)

    def out_part(k):
        part_ref[k] = lax.dot_general(
            hid[k], w_down[...], LAST_DIMS, preferred_element_type=FULL
        ).astype(LOW)

    total.relay()
    loads[5].wait()
    loads[6].wait()
    out_part(0)
    out_part(1)
    total.finish()

    def body(here):
        grads = total.rows(here)
        unit, inverse = unit_rows(resid_ref[here])
        sum_ref[0:1, :] += jnp.sum(grads * unit, axis=0, keepdims=True)
        sum_ref[1:2, :] += jnp.sum(grads, axis=0, keepdims=True)
        grad = cot_ref[here].astype(FULL) + layer_back(grads, norm_ref[5:6, :], unit, inverse)
        grad_ref[here] = grad
        own[here] = grad.astype(LOW)

    in_chunks(rows, body)
    keep = pltpu.make_async_copy(own, gao_all.at[0], local.at[7])
    sent = spread(own, gao_all, (send, recv), 6)
    keep.start()
    out_part(2)
    pass_on(*sent)
    out_part(3)
    spread_end(*sent)
    keep.wait()


def mid_backward(grad_gu, w_gu, w_down, hidden, resid, cotangent, norm_vals, number):
    rows, cols = resid.shape
    group = (N_DP, rows, cols)
    two, one = grad_gu.shape[-1], hidden.shape[-1]
    return pl.pallas_call(
        mid_backward_kernel,
        out_shape=[
            jax.ShapeDtypeStruct(resid.shape, FULL),
            jax.ShapeDtypeStruct(group, LOW),
            jax.ShapeDtypeStruct((8, cols), FULL),
            jax.ShapeDtypeStruct(group, LOW),
        ],
        in_specs=[ANY] * 4 + [VMEM] * 3,
        out_specs=[VMEM, ANY, VMEM, VMEM],
        scratch_shapes=[
            pltpu.VMEM((N_DP, rows, two), LOW),
            pltpu.VMEM((cols, two), LOW),
            pltpu.VMEM((cols, one), LOW),
            pltpu.VMEM((N_DP, rows, one), LOW),
            pltpu.VMEM(group, LOW),
        ]
        + row_sum_scratch(rows, cols)
        + [pltpu.VMEM((rows, cols), LOW)]
        + sems(12)
        + [pltpu.SemaphoreType.DMA((8,))],
        compiler_params=comm_params(number),
        cost_estimate=cost(105),
        name="mid_backward",
    )(grad_gu, w_gu, w_down, hidden, resid, cotangent, norm_vals)


LINE = N_SH // 2
PIECES = 4


class LineSum:
    def __init__(self, terms_hbm, scratch, sem_refs):
        (self.terms, self.other, self.up_in, self.down_in, self.up_out, self.down_out) = scratch
        self.hbm = terms_hbm
        (core_s, core_r, up_s, up_r, down_s, down_r, self.local) = sem_refs
        self.core_sems, self.up_sems, self.down_sems = (core_s, core_r), (up_s, up_r), (down_s, down_r)
        mine, place = lax.axis_index("dp"), lax.axis_index("shard")
        self.line, self.core = place // 2, place % 2
        self.above, self.below = (mine, place + 2), (mine, place - 2)
        self.partner = (mine, place + 1 - 2 * self.core)
        self.size = self.terms.shape[1] // PIECES
        self.steps = (LINE - 1) * PIECES

    def at_end(self):
        return (self.line == 0) | (self.line == LINE - 1)

    def rows(self, piece):
        return pl.ds(pl.multiple_of(piece * self.size, self.size), self.size)

    def core_copy(self, target, piece):
        here = self.rows(piece)
        return remote(
            self.hbm.at[2 * target + 1 - self.core, here],
            self.other.at[target, here],
            self.core_sems,
            target * PIECES + piece,
            self.partner,
        )

    def load(self, target):
        return pltpu.make_async_copy(
            self.hbm.at[2 * target + self.core], self.terms.at[target], self.local.at[target]
        )

    def load_all(self):
        for target in range(LINE):
            self.load(target).start()

    def start(self):
        for targets in ((LINE - 1, 0), (LINE - 2, 1)):
            for piece in range(PIECES):
                for target in targets:
                    self.core_copy(target, piece).start()
        for target in range(LINE):
            self.load(target).wait()

    def own(self, target, piece):
        self.core_copy(target, piece).wait_recv()
        here = self.rows(piece)
        return self.terms[target, here].astype(FULL) + self.other[target, here].astype(FULL)

    def up_copy(self, index):
        return remote(
            self.up_out.at[index], self.up_in.at[index], self.up_sems, index, self.above
        )

    def down_copy(self, index):
        return remote(
            self.down_out.at[index], self.down_in.at[index], self.down_sems, index, self.below
        )

    def up(self, index):
        target, piece = LINE - 1 - index // PIECES, index % PIECES

        @pl.when(target > self.line)
        def _():
            self.up_out[index] = self.own(target, piece).astype(LOW)

            @pl.when(self.line > 0)
            def _():
                self.up_copy(index).wait_recv()
                self.up_out[index] = (
                    self.up_out[index].astype(FULL) + self.up_in[index].astype(FULL)
                ).astype(LOW)

            self.up_copy(index).start()

    def down(self, index):
        target, piece = index // PIECES, index % PIECES

        @pl.when(target < self.line)
        def _():
            self.down_out[index] = self.own(target, piece).astype(LOW)

            @pl.when(self.line < LINE - 1)
            def _():
                self.down_copy(index).wait_recv()
                self.down_out[index] = (
                    self.down_out[index].astype(FULL) + self.down_in[index].astype(FULL)
                ).astype(LOW)

            self.down_copy(index).start()

    def run(self, begin, end):
        def step(index, carry):
            @pl.when(self.line < LINE // 2)
            def _():
                @pl.when(index < self.steps)
                def _():
                    self.up(index)

                @pl.when(index > 0)
                def _():
                    self.down(index - 1)

            @pl.when(self.line >= LINE // 2)
            def _():
                @pl.when(index < self.steps)
                def _():
                    self.down(index)

                @pl.when(index > 0)
                def _():
                    self.up(index - 1)

            return carry

        lax.fori_loop(begin, end, step, 0)

    def finish(self, piece, result):
        here = self.rows(piece)
        result[here] = self.own(self.line, piece)

        @pl.when(self.line > 0)
        def _():
            index = (LINE - 1 - self.line) * PIECES + piece
            self.up_copy(index).wait_recv()
            result[here] = result[here] + self.up_in[index].astype(FULL)

        @pl.when(self.line < LINE - 1)
        def _():
            index = self.line * PIECES + piece
            self.down_copy(index).wait_recv()
            result[here] = result[here] + self.down_in[index].astype(FULL)

    def drain(self):
        def step(index, carry):
            @pl.when(LINE - 1 - index // PIECES > self.line)
            def _():
                self.up_copy(index).wait_send()

            @pl.when(index // PIECES < self.line)
            def _():
                self.down_copy(index).wait_send()

            return carry

        lax.fori_loop(0, self.steps, step, 0)

        def step_core(index, carry):
            self.core_copy(index // PIECES, index % PIECES).wait_send()
            return carry

        lax.fori_loop(0, LINE * PIECES, step_core, 0)


def line_sum_scratch(rows, cols):
    steps = (LINE - 1) * PIECES
    return (
        [pltpu.VMEM((LINE, rows, cols), LOW)] * 2
        + [pltpu.VMEM((steps, rows // PIECES, cols), LOW)] * 4
        + sems(LINE * PIECES)
        + sems(steps)
        + sems(steps)
        + [pltpu.SemaphoreType.DMA((LINE,))]
    )


def fold(values, total):
    values = values * values
    for start in range(0, values.shape[1], 128):
        total = total + values[:, start : start + 128]
    return total


def last_kernel(
    attn_hbm, grad_qkv_hbm, w_hbm, gu_hbm, down_hbm, tok_hbm, grad_hbm, norm_ref, rest_ref,
    input_ref, norm_total_ref, gu_out, down_out, qkv_out, out_ref, total_ref,
    grad_qkv_ref, w_ref, tok_ref, grad_ref, gu_in, down_in_low,
    parts, out, diag, full, sum_ref, near, far, part, near_part, far_part, attn_sum, attn_low,
    terms, other, up_in, down_in, up_out, down_out_pieces,
    core_s, core_r, up_s, up_r, down_s, down_r, term_local,
    send, recv, send_a, recv_a, send_b, recv_b, send_c, recv_c, send_d, recv_d, local,
):
    rows = tok_ref.shape[0]
    mine, place = lax.axis_index("dp"), lax.axis_index("shard")
    loads = [
        pltpu.make_async_copy(source, target, local.at[3 + n])
        for n, (source, target) in enumerate(
            (
                (w_hbm, w_ref),
                (grad_qkv_hbm, grad_qkv_ref),
                (tok_hbm, tok_ref),
                (grad_hbm, grad_ref),
                (gu_hbm, gu_in),
                (down_hbm, down_in_low),
            )
        )
    ]
    line = LineSum(
        attn_hbm,
        (terms, other, up_in, down_in, up_out, down_out_pieces),
        (core_s, core_r, up_s, up_r, down_s, down_r, term_local),
    )
    line.load_all()
    for copy in loads:
        copy.start()
    greet([to_dp(k) for k in (1, 2, 3)] + [to_shard(j) for j in range(1, N_SH)])
    line.start()
    total = RowSum(parts, (out, diag, full), (send, recv), 0)
    blocks = []
    for n, (held, target) in enumerate(((gu_hbm, gu_out), (down_hbm, down_out))):
        for k in (3, 1, 2):
            blocks.append(
                remote(
                    held.at[dp_peer(k)], target.at[mine], (send_c, recv_c), 3 * n + k - 1, to_dp(k)
                )
            )
        blocks.append(pltpu.make_async_copy(held.at[mine], target.at[mine], local.at[n]))
    for copy in blocks[4:]:
        copy.start()
    middle = jnp.logical_not(line.at_end())
    line.run(0, 1)

    def norm1_part(k):
        parts[k] = lax.dot_general(
            grad_qkv_ref[k], w_ref[...], LAST_DIMS, preferred_element_type=FULL
        ).astype(LOW)
        if k:
            total.send(k)

    def middle_run(begin, end):
        @pl.when(middle)
        def _():
            line.run(begin, end)

    loads[0].wait()
    loads[1].wait()
    norm1_part(3)

    @pl.when(line.at_end())
    def _():
        line.run(1, line.steps + 1)

    middle_run(1, 2)
    norm1_part(1)
    middle_run(2, 3)
    norm1_part(2)
    middle_run(3, 4)
    norm1_part(0)
    sum_ref[...] = rest_ref[...]
    middle_run(4, 6)
    total.relay()
    loads[4].wait()
    loads[5].wait()

    def square_low(array, value):
        def step(index, value):
            here = pl.ds(pl.multiple_of(index * 16, 16), 16)
            for k in range(N_DP):
                rows16 = array[k, here].astype(FULL)
                value = fold(rows16[8:], fold(rows16[:8], value))
            return value

        return lax.fori_loop(0, array.shape[1] // 16, step, value)

    part[...] = square_low(down_in_low, square_low(gu_in, jnp.zeros(part.shape, FULL)))
    middle_run(6, 9)
    total.finish()
    loads[2].wait()
    loads[3].wait()

    def body(here):
        grads = total.rows(here)
        unit, inverse = unit_rows(tok_ref[here].astype(FULL))
        sum_ref[0:1, :] += jnp.sum(grads * unit, axis=0, keepdims=True)
        sum_ref[1:2, :] += jnp.sum(grads, axis=0, keepdims=True)
        input_ref[here] = to_places(
            grad_ref[here] + layer_back(grads, norm_ref[0:1, :], unit, inverse)
        )

    in_chunks(rows, body)
    norm_near = [
        remote(sum_ref, near.at[k - 1], (send_a, recv_a), k - 1, to_dp(k)) for k in (1, 2, 3)
    ]
    for copy in norm_near + blocks[:4]:
        copy.start()
    for copy in norm_near:
        copy.wait()
    sum_ref[...] = sum_ref[...] + near[0] + near[1] + near[2]
    norm_far = [
        remote(sum_ref, far.at[j - 1], (send_b, recv_b), j - 1, to_shard(j))
        for j in range(1, N_SH)
    ]
    for copy in norm_far:
        copy.start()

    width = qkv_out.shape[-1]
    size = qkv_out.shape[1]

    def trade(sender, owner):
        return pltpu.make_async_remote_copy(
            src_ref=attn_low.at[owner],
            dst_ref=qkv_out.at[sender],
            send_sem=send_d.at[owner],
            recv_sem=recv_d.at[sender],
            device_id=(owner, place),
            device_id_type=MESH,
        )

    squares = part[...]
    for d in range(N_DP):
        line.finish(d, attn_sum)

        def square(index, value, d=d):
            here = pl.ds(pl.multiple_of(d * size + index * 8, 8), 8)
            return fold(attn_sum[here], value)

        squares = lax.fori_loop(0, size // 8, square, squares)
        attn_low[d] = attn_sum[d * size : d * size + size, :width].astype(LOW)

        @pl.when(mine != d)
        def _(d=d):
            trade(mine, d).start()

    part[...] = squares
    small = [
        remote(part, near_part.at[k - 1], (send_a, recv_a), 2 + k, to_dp(k)) for k in (1, 2, 3)
    ]
    for copy in small:
        copy.start()
    keep = pltpu.make_async_copy(attn_low.at[mine], qkv_out.at[mine], local.at[2])
    keep.start()
    for copy in small:
        copy.wait()
    part[...] = part[...] + near_part[0] + near_part[1] + near_part[2]
    small = [
        remote(part, far_part.at[j - 1], (send_b, recv_b), N_SH - 2 + j, to_shard(j))
        for j in range(1, N_SH)
    ]
    for copy in small:
        copy.start()
    out_ref[...] = to_places(
        jnp.concatenate(
            [attn_sum[d * size : d * size + size, width:] for d in range(N_DP)], axis=1
        )
    )
    for copy in norm_far:
        copy.wait()
    norm_total = sum_ref[...]
    for j in range(N_SH - 1):
        norm_total = norm_total + far[j]
    norm_total_ref[...] = norm_total
    squares = fold(norm_total, part[...])
    for copy in small:
        copy.wait()
    for j in range(N_SH - 1):
        squares = squares + far_part[j]
    total_ref[0, 0] = jnp.sum(squares)
    line.drain()
    for copy in blocks:
        copy.wait()
    keep.wait()
    for d in range(N_DP):

        @pl.when(mine != d)
        def _(d=d):
            trade(mine, d).wait_send()
            trade(d, mine).wait_recv()


def last(
    part_attn, grad_qkv, w_qkv, gu_sum, down_sum, tokens, grad_resid, norm_vals, rest, number
):
    rows, cols = tokens.shape
    square_shape = (8, 128)
    block = part_attn.shape[1:]
    width = grad_qkv.shape[-1]
    size = block[0] // N_DP
    return pl.pallas_call(
        last_kernel,
        out_shape=[
            jax.ShapeDtypeStruct(tokens.shape, FULL),
            jax.ShapeDtypeStruct(rest.shape, FULL),
            jax.ShapeDtypeStruct(gu_sum.shape, gu_sum.dtype),
            jax.ShapeDtypeStruct(down_sum.shape, down_sum.dtype),
            jax.ShapeDtypeStruct((N_DP, size, width), LOW),
            jax.ShapeDtypeStruct((size, D), FULL),
            jax.ShapeDtypeStruct((1, 1), FULL),
        ],
        in_specs=[ANY] * 7 + [VMEM] * 2,
        out_specs=[VMEM, VMEM, ANY, ANY, ANY, VMEM, pl.BlockSpec(memory_space=pltpu.SMEM)],
        scratch_shapes=[
            pltpu.VMEM(a.shape, a.dtype)
            for a in (grad_qkv, w_qkv, tokens, grad_resid, gu_sum, down_sum)
        ]
        + [pltpu.VMEM((N_DP, rows, cols), LOW)]
        + row_sum_scratch(rows, cols)
        + [
            pltpu.VMEM(rest.shape, FULL),
            pltpu.VMEM((N_DP - 1,) + rest.shape, FULL),
            pltpu.VMEM((N_SH - 1,) + rest.shape, FULL),
            pltpu.VMEM(square_shape, FULL),
            pltpu.VMEM((N_DP - 1,) + square_shape, FULL),
            pltpu.VMEM((N_SH - 1,) + square_shape, FULL),
            pltpu.VMEM(block, FULL),
            pltpu.VMEM((N_DP, size, width), LOW),
        ]
        + line_sum_scratch(*block)
        + sems(6)
        + sems(2 * (N_DP - 1))
        + sems(2 * (N_SH - 1))
        + sems(6)
        + sems(N_DP)
        + [pltpu.SemaphoreType.DMA((9,))],
        compiler_params=comm_params(number),
        cost_estimate=cost(90),
        name="last",
    )(
        part_attn, grad_qkv, w_qkv, gu_sum, down_sum, tokens, grad_resid, norm_vals, rest
    )


def column_cuts(cols):
    return [(c, min(c + 256, cols)) for c in range(0, cols, 256)]


def weight_grad(left, right, stage, target, sem, first_sem):
    size = stage.shape[1]
    count = target.shape[0] // size

    def store(index, slot):
        here = pl.ds(pl.multiple_of(index * size, size), size)
        return pltpu.make_async_copy(stage.at[slot], target.at[here], sem.at[first_sem + slot])

    def step(index, carry):
        slot = index % 2

        @pl.when(index >= 2)
        def _():
            store(index - 2, slot).wait()

        here = pl.ds(pl.multiple_of(index * size, size), size)
        stage[slot] = lax.dot_general(
            left[:, here], right[...], LEAD_DIMS, preferred_element_type=FULL
        ).astype(LOW)
        store(index, slot).start()
        return carry

    lax.fori_loop(0, count, step, 0)
    for index in (count - 2, count - 1):
        store(index, index % 2).wait()


def mlp_one_kernel(
    x_hbm, cot_hbm, wgu_hbm, hid_out, gate_out, up_out, part_out,
    x_ref, cot_ref, w_gu, hid, gate_stage, up_stage, grad_stage, local, loads, stores,
):
    total = x_ref.shape[0]
    cols = hid.shape[1]
    cuts = column_cuts(cols)
    block = total // 2

    def weight_loads(n):
        begin, end = cuts[n]
        return [
            pltpu.make_async_copy(
                wgu_hbm.at[:, pl.ds(at, end - begin)],
                w_gu.at[:, pl.ds(at, end - begin)],
                loads.at[2 * n + i],
            )
            for i, at in enumerate((begin, cols + begin))
        ]

    def stage_stores(n):
        begin, end = cuts[n]
        return [
            pltpu.make_async_copy(
                stage.at[n % 2, :, pl.ds(0, end - begin)],
                target.at[:, pl.ds(begin, end - begin)],
                stores.at[2 * i + n % 2],
            )
            for i, (stage, target) in enumerate(((gate_stage, gate_out), (up_stage, up_out)))
        ]

    data = [
        pltpu.make_async_copy(x_hbm, x_ref, local.at[0]),
        pltpu.make_async_copy(cot_hbm, cot_ref, local.at[1]),
    ]
    for copy in weight_loads(0) + data[:1]:
        copy.start()
    for n in range(1, len(cuts)):
        for copy in weight_loads(n):
            copy.start()
    data[1].start()
    data[0].wait()
    for n, (begin, end) in enumerate(cuts):
        for copy in weight_loads(n):
            copy.wait()
        if n >= 2:
            for copy in stage_stores(n - 2):
                copy.wait()

        def rows(index, carry, begin=begin, end=end, slot=n % 2):
            here = pl.ds(pl.multiple_of(index * block, block), block)
            gate = jnp.dot(x_ref[here], w_gu[:, begin:end], preferred_element_type=FULL)
            up = jnp.dot(
                x_ref[here], w_gu[:, cols + begin : cols + end], preferred_element_type=FULL
            )
            hid[here, begin:end] = (gate / (1.0 + jnp.exp(-gate)) * up).astype(LOW)
            gate_stage[slot, here, : end - begin] = gate
            up_stage[slot, here, : end - begin] = up
            return carry

        lax.fori_loop(0, total // block, rows, 0)
        for copy in stage_stores(n):
            copy.start()
    out = pltpu.make_async_copy(hid, hid_out, local.at[2])
    out.start()
    data[1].wait()
    weight_grad(cot_ref, hid, grad_stage, part_out, local, 3)
    for n in (len(cuts) - 2, len(cuts) - 1):
        for copy in stage_stores(n):
            copy.wait()
    out.wait()


def mlp_one(normed2, cotangent, w_gu):
    total, width = normed2.shape
    cols = w_gu.shape[1] // 2
    values = jax.ShapeDtypeStruct((total, cols), FULL)
    return pl.pallas_call(
        mlp_one_kernel,
        out_shape=[
            jax.ShapeDtypeStruct((total, cols), LOW),
            values,
            values,
            jax.ShapeDtypeStruct((width, cols), LOW),
        ],
        in_specs=[ANY] * 3,
        out_specs=[ANY] * 4,
        scratch_shapes=[
            pltpu.VMEM((total, width), LOW),
            pltpu.VMEM((total, width), LOW),
            pltpu.VMEM((width, 2 * cols), LOW),
            pltpu.VMEM((total, cols), LOW),
            pltpu.VMEM((2, total, 256), FULL),
            pltpu.VMEM((2, total, 256), FULL),
            pltpu.VMEM((2, 512, cols), LOW),
            pltpu.SemaphoreType.DMA((5,)),
            pltpu.SemaphoreType.DMA((2 * len(column_cuts(cols)),)),
            pltpu.SemaphoreType.DMA((4,)),
        ],
        compiler_params=pltpu.CompilerParams(vmem_limit_bytes=BIG_VMEM),
        cost_estimate=cost(30),
        name="mlp_one",
    )(normed2, cotangent, w_gu)


def mlp_two_kernel(
    x_hbm, cot_hbm, wdown_hbm, gate_hbm, up_hbm, ggu_out, part_out,
    x_ref, cot_ref, w_down, gate_stage, up_stage, ggu, grad_stage, local, loads,
):
    total = x_ref.shape[0]
    cols = w_down.shape[1]
    cuts = column_cuts(cols)
    block = total // 2

    def chunk_loads(n):
        begin, end = cuts[n]
        here = pl.ds(begin, end - begin)
        stage = pl.ds(0, end - begin)
        return [
            pltpu.make_async_copy(source, target, loads.at[3 * (n % 2) + i])
            for i, (source, target) in enumerate(
                (
                    (wdown_hbm.at[:, here], w_down.at[:, here]),
                    (gate_hbm.at[:, here], gate_stage.at[n % 2, :, stage]),
                    (up_hbm.at[:, here], up_stage.at[n % 2, :, stage]),
                )
            )
        ]

    data = [
        pltpu.make_async_copy(cot_hbm, cot_ref, local.at[0]),
        pltpu.make_async_copy(x_hbm, x_ref, local.at[1]),
    ]
    data[0].start()
    for copy in chunk_loads(0) + chunk_loads(1):
        copy.start()
    data[1].start()
    data[0].wait()
    for n, (begin, end) in enumerate(cuts):
        for copy in chunk_loads(n):
            copy.wait()

        def rows(index, carry, begin=begin, end=end, slot=n % 2):
            here = pl.ds(pl.multiple_of(index * block, block), block)
            grad = jnp.dot(cot_ref[here], w_down[:, begin:end], preferred_element_type=FULL)
            gate = gate_stage[slot, here, : end - begin]
            up = up_stage[slot, here, : end - begin]
            sig = 1.0 / (1.0 + jnp.exp(-gate))
            ggu[here, begin:end] = (grad * up * sig * (1.0 + gate * (1.0 - sig))).astype(LOW)
            ggu[here, cols + begin : cols + end] = (grad * gate * sig).astype(LOW)
            return carry

        lax.fori_loop(0, total // block, rows, 0)
        if n + 2 < len(cuts):
            for copy in chunk_loads(n + 2):
                copy.start()
    out = pltpu.make_async_copy(ggu, ggu_out, local.at[2])
    out.start()
    data[1].wait()
    weight_grad(x_ref, ggu, grad_stage, part_out, local, 3)
    out.wait()


def mlp_two(normed2, cotangent, w_down, gate, up):
    total, width = normed2.shape
    cols = w_down.shape[1]
    return pl.pallas_call(
        mlp_two_kernel,
        out_shape=[
            jax.ShapeDtypeStruct((total, 2 * cols), LOW),
            jax.ShapeDtypeStruct((width, 2 * cols), LOW),
        ],
        in_specs=[ANY] * 5,
        out_specs=[ANY] * 2,
        scratch_shapes=[
            pltpu.VMEM((total, width), LOW),
            pltpu.VMEM((total, width), LOW),
            pltpu.VMEM((width, cols), LOW),
            pltpu.VMEM((2, total, 256), FULL),
            pltpu.VMEM((2, total, 256), FULL),
            pltpu.VMEM((total, 2 * cols), LOW),
            pltpu.VMEM((2, 256, 2 * cols), LOW),
            pltpu.SemaphoreType.DMA((5,)),
            pltpu.SemaphoreType.DMA((6,)),
        ],
        compiler_params=pltpu.CompilerParams(vmem_limit_bytes=BIG_VMEM),
        cost_estimate=cost(30),
        name="mlp_two",
    )(normed2, cotangent, w_down, gate, up)


FIRST_HAT = 1.0 / (1.0 - BETA_ONE**STEP)
SECOND_HAT = 1.0 / (1.0 - BETA_TWO**STEP)


def clip_factor(total_ref, width):
    total = jnp.full((1, width), total_ref[0, 0], FULL)
    return CLIP_NORM / jnp.maximum(jnp.sqrt(total), CLIP_NORM)


def adam_step(grads, factor, master, first, second):
    clipped = grads.astype(FULL) * factor
    first_new = BETA_ONE * first + (1.0 - BETA_ONE) * clipped
    second_new = BETA_TWO * second + (1.0 - BETA_TWO) * clipped * clipped
    ratio = first_new * (RATE_MATRIX * FIRST_HAT) / (jnp.sqrt(second_new * SECOND_HAT) + ADAM_EPS)
    return (master * (1.0 - RATE_MATRIX * DECAY_MATRIX) - ratio, first_new, second_new)


def adam_mlp_kernel(total_ref, gu_ref, down_ref, *refs):
    ins, outs = refs[:3], refs[3:]
    factor = clip_factor(total_ref, gu_ref.shape[-1])

    def update(grads):
        values = adam_step(grads, factor, *[ref[...] for ref in ins])
        for ref, value in zip(outs, values):
            ref[...] = value

    step = pl.program_id(0)

    @pl.when(step < 2 * N_DP)
    def _():
        update(gu_ref[0])

    @pl.when(step >= 2 * N_DP)
    def _():
        update(down_ref[0])


def adam_attn_kernel(total_ref, qkv_ref, out_ref, *refs):
    ins, outs = refs[:3], refs[3:]
    step = pl.program_id(0)
    width = qkv_ref.shape[-1]
    factor = clip_factor(total_ref, width)

    def update(grads, here):
        values = adam_step(grads, factor, *[ref[:, here] for ref in ins])
        for ref, value in zip(outs, values):
            ref[:, here] = value

    for side in range(2):
        here = slice(side * width, side * width + width)

        @pl.when(step < 6)
        def _():
            update(qkv_ref[side], here)

        @pl.when(step >= 6)
        def _():
            update(out_ref[:, here], here)


def adam_call(kernel, factor, grads, grad_specs, states, width, name):
    rows, cols = states[0].shape
    column = pl.BlockSpec((rows, width), lambda j: (0, j))
    size = states[0].size
    return pl.pallas_call(
        kernel,
        grid=(cols // width,),
        out_shape=[jax.ShapeDtypeStruct((rows, cols), FULL)] * 3,
        in_specs=[pl.BlockSpec(memory_space=pltpu.SMEM)] + grad_specs + [column] * 3,
        out_specs=[column] * 3,
        compiler_params=pltpu.CompilerParams(vmem_limit_bytes=BIG_VMEM),
        cost_estimate=pl.CostEstimate(
            flops=20 * size, bytes_accessed=26 * size, transcendentals=size
        ),
        name=name,
    )(factor, *grads, *states)


def adam_mlp(factor, gu_blocks, down_blocks, states):
    rows = states[0].shape[0]
    width = down_blocks.shape[-1]
    last = 2 * N_DP - 1
    specs = [
        pl.BlockSpec(
            (1, rows, width),
            lambda j: (jnp.minimum(j, last) % N_DP, 0, jnp.minimum(j, last) // N_DP),
        ),
        pl.BlockSpec((1, rows, width), lambda j: (jnp.maximum(j - last - 1, 0), 0, 0)),
    ]
    grads = [gu_blocks, down_blocks]
    return adam_call(adam_mlp_kernel, factor, grads, specs, states, width, "adam_mlp")


def adam_attn(factor, qkv_blocks, out_grad, states):
    rows = states[0].shape[0]
    width = qkv_blocks.shape[-1] // 3
    specs = [
        pl.BlockSpec(
            (2, rows, width), lambda j: (jnp.minimum(j, 5) % 2, 0, jnp.minimum(j, 5) // 2)
        ),
        pl.BlockSpec((rows, 2 * width), lambda j: (0, jnp.maximum(j - 6, 0))),
    ]
    grads = [qkv_blocks, out_grad]
    return adam_call(adam_attn_kernel, factor, grads, specs, states, 2 * width, "adam_attn")


def per_device_fast(
    tokens,
    cotangent,
    segments,
    positions,
    attn_master,
    mlp_master,
    norm_master,
    attn_first,
    mlp_first,
    norm_first,
    attn_second,
    mlp_second,
    norm_second,
):
    seq = tokens.shape[0]
    rows = attn_master.shape[0]
    width = D // N_DP
    ff_width = FF // N_DP
    group = N_DP * seq
    my_dp = lax.axis_index("dp")
    my_shard = lax.axis_index("shard")

    places = jnp.stack([segments, positions], 0)
    w_qkv, w_out, norm_all, tok_all, place_all, gu_blocks, down_blocks, tokens, cotangent = start(
        attn_master, mlp_master, norm_master, tokens, cotangent, places, 0
    )
    w_qkv = w_qkv.reshape(D, 3 * width)
    w_out = w_out.reshape(width, D)

    def gather_rows(blocks):
        return lax.all_gather(blocks.reshape(-1, blocks.shape[-1]), "shard", axis=0, tiled=True)

    norm_all = norm_all[:, :, :7, :rows]
    norm_vals = norm_all.transpose(2, 0, 1, 3).reshape(7, D)
    norm_vals = jnp.concatenate([norm_vals, jnp.zeros((1, D), FULL)], 0)
    bias_all = norm_all.transpose(2, 1, 0, 3)[2:5].reshape(3, N_DP, width)
    bias = lax.dynamic_index_in_dim(bias_all, my_dp, 1).reshape(1, 3 * width)
    w_gu = gather_rows(gu_blocks)
    w_down = gather_rows(down_blocks)

    rates = ROPE_BASE ** (-((np.arange(128) % (ROT // 2)) * 2.0 / ROT))
    rates = np.broadcast_to(rates.astype(np.float32), (8, 128))
    cot_all, normed1, queries, keys, values, mixture, *tables, mask = attn_forward(
        cotangent, tok_all, place_all, rates, norm_vals, w_qkv, bias, 2
    )
    resid, normed2 = mid_forward(mixture, w_out, tokens, norm_vals, 3)
    normed2 = normed2.reshape(group, D)
    cot_flat = cot_all.reshape(group, D)

    hidden, gate, up, part_down = mlp_one(normed2, cot_flat, w_gu)
    down_sum = lax.psum_scatter(part_down, "shard", scatter_dimension=0, tiled=True)
    grad_gu, part_gu = mlp_two(normed2, cot_flat, w_down, gate, up)
    gu_sum = lax.psum_scatter(part_gu, "shard", scatter_dimension=0, tiled=True)
    grad_resid, grad_attn_out, sums2, out_part = mid_backward(
        grad_gu.reshape(N_DP, seq, 2 * ff_width),
        w_gu,
        w_down,
        hidden.reshape(N_DP, seq, ff_width),
        resid,
        cotangent,
        norm_vals,
        4,
    )
    grad_attn_out, down_sum = lax.optimization_barrier((grad_attn_out, down_sum))
    block_out, grad_qkv, bias_sums, part_attn = attn_backward(
        out_part,
        normed1,
        mixture,
        resid,
        grad_attn_out,
        w_out,
        queries,
        keys,
        values,
        mask,
        tables,
        9,
    )
    bias_term = lax.dynamic_update_slice(
        jnp.zeros((3, D), FULL), bias_sums[0].reshape(3, width), (0, my_dp * width)
    )
    rest = jnp.concatenate(
        [jnp.zeros((2, D), FULL), bias_term, sums2[:2], jnp.zeros((1, D), FULL)], 0
    )
    gu_blocks = gu_sum.reshape(N_DP, rows, 2 * ff_width)
    down_blocks = down_sum.reshape(N_DP, rows, ff_width)
    input_grad, norm_sums, gu_grad, down_grad, qkv_grad, out_grad, box = last(
        part_attn,
        grad_qkv,
        w_qkv,
        gu_blocks,
        down_blocks,
        tokens,
        grad_resid,
        norm_vals,
        rest,
        5,
    )
    own_features = lax.dynamic_slice(norm_sums, (0, (my_shard * N_DP + my_dp) * rows), (8, rows))
    own_biases = lax.dynamic_slice(norm_sums, (0, (my_dp * N_SH + my_shard) * rows), (8, rows))
    norm_grad = jnp.concatenate([own_features[:2], own_biases[2:5], own_features[5:7]], 0)
    grad_size = jnp.sqrt(box[0, 0])
    factor = CLIP_NORM / jnp.maximum(grad_size, CLIP_NORM)
    attn_new, attn_first_new, attn_second_new = adam_attn(
        box, qkv_grad, out_grad, [attn_master, attn_first, attn_second]
    )
    mlp_new, mlp_first_new, mlp_second_new = adam_mlp(
        box, gu_grad, down_grad, [mlp_master, mlp_first, mlp_second]
    )
    norm_new, norm_first_new, norm_second_new = adam_update(
        norm_master, norm_first, norm_second, norm_grad, factor, RATE_VECTOR, 0.0
    )
    return (
        block_out,
        input_grad,
        grad_size,
        attn_new,
        mlp_new,
        norm_new,
        attn_first_new,
        mlp_first_new,
        norm_first_new,
        attn_second_new,
        mlp_second_new,
        norm_second_new,
    )


def solution(mesh):
    in_specs = (
        P(("dp", "shard"), None),
        P(("dp", "shard"), None),
        P(("dp", "shard")),
        P(("dp", "shard")),
        P(("dp", "shard"), None),
        P(("dp", "shard"), None),
        P(None, ("dp", "shard")),
        P(("dp", "shard"), None),
        P(("dp", "shard"), None),
        P(None, ("dp", "shard")),
        P(("dp", "shard"), None),
        P(("dp", "shard"), None),
        P(None, ("dp", "shard")),
    )
    out_specs = (
        P(("dp", "shard"), None),
        P(("dp", "shard"), None),
        P(),
        P(("dp", "shard"), None),
        P(("dp", "shard"), None),
        P(None, ("dp", "shard")),
        P(("dp", "shard"), None),
        P(("dp", "shard"), None),
        P(None, ("dp", "shard")),
        P(("dp", "shard"), None),
        P(("dp", "shard"), None),
        P(None, ("dp", "shard")),
    )
    fast = dict(mesh.shape) == dict(dp=4, shard=8)
    body = per_device_fast if fast else per_device_any
    return jax.shard_map(
        body, mesh=mesh, in_specs=in_specs, out_specs=out_specs, check_vma=False
    )
```

```python
import functools

import numpy as np
import jax
import jax.numpy as jnp
from jax import lax
from jax.experimental import pallas as pl
from jax.experimental.pallas import tpu as pltpu
from jax.sharding import PartitionSpec as P

D = 2048
HEADS = 32
HEAD = 64
FF = 5632
ROT = 16
STEP = 10


NORM_EPS = 1e-05
NEG_FILL = -1e30
ROPE_BASE = 10000.0
CLIP_NORM = 1.0
BETA_ONE = 0.9
BETA_TWO = 0.95
ADAM_EPS = 1e-08
RATE_MATRIX = 0.02
RATE_VECTOR = 0.2
DECAY_MATRIX = 0.1
LEAD_DIMS = (((0,), (0,)), ((), ()))
LAST_DIMS = (((1,), (1,)), ((), ()))


def layer_norm(values_in, gain_vec, shift_vec):
    average = jnp.mean(values_in, axis=-1, keepdims=True)
    centered = values_in - average
    variance = jnp.mean(centered * centered, axis=-1, keepdims=True)
    return centered * lax.rsqrt(variance + NORM_EPS) * gain_vec + shift_vec


def rotary_tables(position_ids):
    half_rot = ROT // 2
    inverse_freq = ROPE_BASE ** (-(jnp.arange(half_rot, dtype=jnp.float32) * 2.0 / ROT))
    angles = position_ids.astype(jnp.float32)[:, None] * inverse_freq[None, :]
    return (jnp.cos(angles)[:, None, :], jnp.sin(angles)[:, None, :])


def rotate(heads_in, cos_table, sin_table):
    half_rot = ROT // 2
    first_half = heads_in[..., :half_rot]
    second_half = heads_in[..., half_rot:ROT]
    rest_part = heads_in[..., ROT:]
    turned_one = first_half * cos_table - second_half * sin_table
    turned_two = second_half * cos_table + first_half * sin_table
    return jnp.concatenate([turned_one, turned_two, rest_part], -1)


def pad_last(array, size):
    missing = size - array.shape[-1]
    if missing == 0:
        return array
    return jnp.pad(array, [(0, 0)] * (array.ndim - 1) + [(0, missing)])


def activate(gate_part, up_part):
    return jax.nn.silu(gate_part) * up_part


def adam_update(master, first, second, grads, factor, rate, decay):
    clipped = grads * factor
    first_new = BETA_ONE * first + (1.0 - BETA_ONE) * clipped
    second_new = BETA_TWO * second + (1.0 - BETA_TWO) * clipped * clipped
    first_hat = first_new / (1.0 - BETA_ONE**STEP)
    second_hat = second_new / (1.0 - BETA_TWO**STEP)
    master_new = master - rate * (first_hat / (jnp.sqrt(second_hat) + ADAM_EPS) + decay * master)
    return (master_new, first_new, second_new)


def exchange_dp(blocks):
    return lax.all_to_all(blocks, "dp", 0, 0, tiled=True)


def gather_dp(rows):
    return lax.all_gather(rows, "dp", axis=0, tiled=True)


def scatter_sum_dp(parts):
    return lax.psum_scatter(parts, "dp", scatter_dimension=0, tiled=True)


def gather_shard(block):
    return lax.all_gather(block, "shard", axis=1)


def scatter_sum_shard(parts):
    return lax.psum_scatter(parts, "shard", scatter_dimension=1)


def layer_stats(values_in):
    average = jnp.mean(values_in, axis=-1, keepdims=True)
    centered = values_in - average
    variance = jnp.mean(centered * centered, axis=-1, keepdims=True)
    inverse = lax.rsqrt(variance + NORM_EPS)
    return centered * inverse, inverse


def layer_back(grads, gain_vec, unit, inverse):
    scaled = grads * gain_vec
    mean_one = jnp.mean(scaled, axis=-1, keepdims=True)
    mean_two = jnp.mean(scaled * unit, axis=-1, keepdims=True)
    return inverse * (scaled - mean_one - unit * mean_two)


def per_device_any(
    tokens,
    cotangent,
    segments,
    positions,
    attn_master,
    mlp_master,
    norm_master,
    attn_first,
    mlp_first,
    norm_first,
    attn_second,
    mlp_second,
    norm_second,
):
    low = jnp.bfloat16
    full = jnp.float32
    n_dp = lax.axis_size("dp")
    n_sh = lax.axis_size("shard")
    seq = tokens.shape[0]
    rows = attn_master.shape[0]
    heads = HEADS // n_dp
    width = D // n_dp
    ff_width = -(-FF // (128 * n_dp)) * 128
    ff_pad = ff_width * n_dp
    scale = HEAD ** (-0.5)

    qkv_send = attn_master[:, : 3 * D].astype(low).reshape(rows, 3, n_dp, width)
    qkv_send = qkv_send.transpose(2, 0, 1, 3).reshape(n_dp, rows, 3 * width)
    mlp_send = pad_last(mlp_master.astype(low).reshape(rows, 3, FF), ff_pad)
    mlp_send = mlp_send.reshape(rows, 3, n_dp, ff_width)
    mlp_send = mlp_send.transpose(2, 0, 1, 3).reshape(n_dp, rows, 3 * ff_width)
    norm_full = lax.all_gather(norm_master.astype(low), ("dp", "shard"), axis=1, tiled=True)
    norm_vals = norm_full.astype(full)
    w_qkv = gather_shard(exchange_dp(qkv_send)).reshape(D, 3 * width)
    w_out = gather_shard(attn_master[None, :, 3 * D :].astype(low)).reshape(width, D)
    tokens_all = gather_dp(tokens)
    places_all = gather_dp(jnp.stack([segments, positions], 0)[None])
    cot_all = gather_dp(cotangent)
    w_mlp = gather_shard(exchange_dp(mlp_send)).reshape(D, 3 * ff_width)
    w_gu = w_mlp[:, : 2 * ff_width]
    w_down = w_mlp[:, 2 * ff_width :]
    seg_all, pos_all = places_all[:, 0], places_all[:, 1]

    inputs_all = tokens_all.astype(full)
    unit1, _ = layer_stats(inputs_all)
    normed1 = (unit1 * norm_vals[0] + norm_vals[1]).astype(low)
    my_dp = lax.axis_index("dp")
    bias = lax.dynamic_slice(norm_vals[2:5], (0, my_dp * width), (3, width)).reshape(3 * width)
    qkv = jnp.dot(normed1, w_qkv, preferred_element_type=full) + bias
    qkv = qkv.reshape(n_dp * seq, 3 * heads, HEAD)
    cos_table, sin_table = rotary_tables(pos_all.reshape(-1))

    def split(array):
        return array.reshape(n_dp, seq, heads, HEAD)

    queries = split(rotate(qkv[:, :heads], cos_table, sin_table).astype(low))
    key_rows = split(rotate(qkv[:, heads : 2 * heads], cos_table, sin_table).astype(low))
    values = split(qkv[:, 2 * heads :].astype(low))
    places = jnp.arange(seq)
    allowed = (seg_all[:, :, None] == seg_all[:, None, :]) & (
        places[:, None] >= places[None, :]
    )[None]
    scores = (
        jnp.einsum("gshd,gthd->ghst", queries, key_rows, preferred_element_type=full) * scale
    )
    scores = jnp.where(allowed[:, None], scores, NEG_FILL)
    attend = jax.nn.softmax(scores, axis=-1)
    attend_low = attend.astype(low)
    mixture = (
        jnp.einsum("ghst,gthd->gshd", attend_low, values, preferred_element_type=full)
        .reshape(n_dp * seq, width)
        .astype(low)
    )
    attn_part = jnp.dot(mixture, w_out, preferred_element_type=full).astype(low)
    resid = tokens.astype(full) + scatter_sum_dp(attn_part).astype(full)
    unit2, inverse2 = layer_stats(resid)
    normed2 = gather_dp((unit2 * norm_vals[5] + norm_vals[6]).astype(low))
    gate_up = jnp.dot(normed2, w_gu, preferred_element_type=full)
    hidden_f, act_pull = jax.vjp(activate, gate_up[:, :ff_width], gate_up[:, ff_width:])
    hidden = hidden_f.astype(low)
    grad_hidden = jnp.dot(cot_all, w_down, preferred_element_type=full)
    grad_gate, grad_up = act_pull(grad_hidden)
    grad_gu = jnp.concatenate([grad_gate, grad_up], 1).astype(low)
    norm2_part = lax.dot_general(grad_gu, w_gu, LAST_DIMS, preferred_element_type=full)
    grad_norm2 = scatter_sum_dp(norm2_part.astype(low)).astype(full)
    out_part = lax.dot_general(hidden, w_down, LAST_DIMS, preferred_element_type=full)
    block_out = (resid + scatter_sum_dp(out_part.astype(low)).astype(full)).astype(low)
    part_gu = lax.dot_general(normed2, grad_gu, LEAD_DIMS, preferred_element_type=full)
    part_down = lax.dot_general(cot_all, hidden, LEAD_DIMS, preferred_element_type=full)
    part_mlp = jnp.concatenate([part_gu.astype(low), part_down.astype(low)], 1)
    mlp_sum = scatter_sum_shard(part_mlp.reshape(n_dp, n_sh, rows, 3 * ff_width))

    grad_gain2 = jnp.sum(grad_norm2 * unit2, axis=0)
    grad_shift2 = jnp.sum(grad_norm2, axis=0)
    grad_resid = cotangent.astype(full) + layer_back(grad_norm2, norm_vals[5], unit2, inverse2)
    grad_attn_out = gather_dp(grad_resid.astype(low))
    grad_mixture = lax.dot_general(grad_attn_out, w_out, LAST_DIMS, preferred_element_type=full)
    grad_mixture = split(grad_mixture.astype(low))
    grad_attend = jnp.einsum("gshd,gthd->ghst", grad_mixture, values, preferred_element_type=full)
    grad_values = jnp.einsum(
        "ghst,gshd->gthd", attend_low, grad_mixture, preferred_element_type=full
    )
    grad_scores = (
        attend * (grad_attend - jnp.sum(attend * grad_attend, axis=-1, keepdims=True))
    ).astype(low)
    grad_queries = (
        jnp.einsum("ghst,gthd->gshd", grad_scores, key_rows, preferred_element_type=full) * scale
    )
    grad_keys = (
        jnp.einsum("ghst,gshd->gthd", grad_scores, queries, preferred_element_type=full) * scale
    )

    def turn_back(grads):
        grads = grads.reshape(n_dp * seq, heads, HEAD)
        return rotate(grads, cos_table, -sin_table).reshape(n_dp * seq, width)

    grad_qkv = jnp.concatenate(
        [
            turn_back(grad_queries),
            turn_back(grad_keys),
            grad_values.reshape(n_dp * seq, width),
        ],
        1,
    ).astype(low)
    part_qkv = lax.dot_general(normed1, grad_qkv, LEAD_DIMS, preferred_element_type=full)
    part_out = lax.dot_general(mixture, grad_attn_out, LEAD_DIMS, preferred_element_type=full)
    qkv_sum = scatter_sum_shard(part_qkv.astype(low).reshape(n_dp, n_sh, rows, 3 * width))
    out_sum = scatter_sum_shard(part_out.astype(low).reshape(1, n_sh, rows, D))[0].astype(full)

    norm1_part = lax.dot_general(grad_qkv, w_qkv, LAST_DIMS, preferred_element_type=full)
    grad_gain1 = jnp.sum(norm1_part * unit1, axis=0)
    grad_shift1 = jnp.sum(norm1_part, axis=0)
    grad_bias = jnp.sum(grad_qkv, axis=0, dtype=full).reshape(3, width)
    grad_norm1 = scatter_sum_dp(norm1_part.astype(low)).astype(full)
    own_unit1, own_inverse1 = layer_stats(tokens.astype(full))
    input_grad = grad_resid + layer_back(grad_norm1, norm_vals[0], own_unit1, own_inverse1)
    norm_term = lax.dynamic_update_slice(
        jnp.zeros((3, D), full), grad_bias, (0, my_dp * width)
    )
    norm_term = jnp.concatenate(
        [grad_gain1[None], grad_shift1[None], norm_term, grad_gain2[None], grad_shift2[None]], 0
    )
    norm_grad = lax.psum_scatter(norm_term, ("dp", "shard"), scatter_dimension=1, tiled=True)

    def columns_back(summed, parts, part_width, keep):
        back = exchange_dp(summed).reshape(n_dp, rows, parts, part_width)
        back = back.transpose(1, 2, 0, 3).reshape(rows, parts, n_dp * part_width)
        return back[:, :, :keep].reshape(rows, parts * keep).astype(full)

    mlp_grad = columns_back(mlp_sum, 3, ff_width, FF)
    attn_grad = jnp.concatenate([columns_back(qkv_sum, 3, width, D), out_sum], 1)
    squares = (
        jnp.sum(attn_grad * attn_grad)
        + jnp.sum(mlp_grad * mlp_grad)
        + jnp.sum(norm_grad * norm_grad)
    )
    overall = lax.psum(squares, ("dp", "shard"))
    grad_size = jnp.sqrt(overall)
    factor = CLIP_NORM / jnp.maximum(grad_size, CLIP_NORM)
    attn_new, attn_first_new, attn_second_new = adam_update(
        attn_master, attn_first, attn_second, attn_grad, factor, RATE_MATRIX, DECAY_MATRIX
    )
    mlp_new, mlp_first_new, mlp_second_new = adam_update(
        mlp_master, mlp_first, mlp_second, mlp_grad, factor, RATE_MATRIX, DECAY_MATRIX
    )
    norm_new, norm_first_new, norm_second_new = adam_update(
        norm_master, norm_first, norm_second, norm_grad, factor, RATE_VECTOR, 0.0
    )
    return (
        block_out,
        input_grad,
        grad_size,
        attn_new,
        mlp_new,
        norm_new,
        attn_first_new,
        mlp_first_new,
        norm_first_new,
        attn_second_new,
        mlp_second_new,
        norm_second_new,
    )


MESH = pl.DeviceIdType.MESH
ANY = pl.BlockSpec(memory_space=pl.ANY)
VMEM = pl.BlockSpec(memory_space=pltpu.VMEM)
LOW = jnp.bfloat16
FULL = jnp.float32
N_DP = 4
N_SH = 8
BIG_VMEM = 56 * 1024 * 1024


def dp_peer(step):
    mine = lax.axis_index("dp")
    if step == 1:
        return mine + 1 - 2 * (mine % 2)
    if step == 2:
        return (mine + 2) % 4
    return 3 - mine


def to_dp(step):
    return (dp_peer(step), lax.axis_index("shard"))


def to_shard(step):
    return (lax.axis_index("dp"), (lax.axis_index("shard") + step) % N_SH)


def cost(micros):
    return pl.CostEstimate(flops=0, bytes_accessed=int(micros * 3.0e6), transcendentals=0)


def greet(peers):
    barrier = pltpu.get_barrier_semaphore()
    for peer in peers:
        pl.semaphore_signal(barrier, inc=1, device_id=peer, device_id_type=MESH)
    pl.semaphore_wait(barrier, len(peers))


def remote(source, target, sems, index, peer):
    return pltpu.make_async_remote_copy(
        src_ref=source,
        dst_ref=target,
        send_sem=sems[0].at[index],
        recv_sem=sems[1].at[index],
        device_id=peer,
        device_id_type=MESH,
    )


def sems(count):
    return [pltpu.SemaphoreType.DMA((count,)), pltpu.SemaphoreType.DMA((count,))]


def comm_params(number):
    return pltpu.CompilerParams(
        collective_id=number, has_side_effects=True, vmem_limit_bytes=BIG_VMEM
    )


def to_places(value):
    size = value.shape[1] // (N_DP * N_SH)
    starts = [(n * N_DP + d) * size for d in range(N_DP) for n in range(N_SH)]
    return jnp.concatenate([value[:, start : start + size] for start in starts], axis=1)


def to_shards(value):
    size = value.shape[1] // (N_DP * N_SH)
    starts = [(d * N_SH + n) * size for n in range(N_SH) for d in range(N_DP)]
    return jnp.concatenate([value[:, start : start + size] for start in starts], axis=1)


CHUNK = 32


def in_chunks(rows, body):
    def step(index, carry):
        body(pl.ds(pl.multiple_of(index * CHUNK, CHUNK), CHUNK))
        return carry

    lax.fori_loop(0, rows // CHUNK, step, 0)


def spread_plan(own, result, sem_pair, base):
    half = own.shape[0] // 2
    top, bottom = pl.ds(0, half), pl.ds(half, half)
    sent = [
        remote(own.at[top], result.at[1, top], sem_pair, base + 0, to_dp(1)),
        remote(own.at[bottom], result.at[2, bottom], sem_pair, base + 1, to_dp(2)),
        remote(own.at[bottom], result.at[1, bottom], sem_pair, base + 2, to_dp(1)),
        remote(own.at[top], result.at[2, top], sem_pair, base + 3, to_dp(2)),
    ]
    passed = [
        remote(result.at[1, top], result.at[3, top], sem_pair, base + 4, to_dp(2)),
        remote(result.at[2, bottom], result.at[3, bottom], sem_pair, base + 5, to_dp(1)),
    ]
    return sent, passed


def spread(own, result, sem_pair, base):
    sent, passed = spread_plan(own, result, sem_pair, base)
    for copy in sent:
        copy.start()
    return sent, passed


def pass_on(sent, passed):
    sent[0].wait_recv()
    passed[0].start()
    sent[1].wait_recv()
    passed[1].start()


def spread_end(sent, passed):
    sent[2].wait_recv()
    sent[3].wait_recv()
    passed[0].wait_recv()
    passed[1].wait_recv()
    for copy in sent + passed:
        copy.wait_send()


SLABS = 6


def start_kernel(
    attn_hbm, mlp_hbm, norm_ref, tok_hbm, cot_hbm, place_ref,
    w_qkv, w_out, norm_all, tok_all, place_all, gu_out, down_out, tok_own, cot_own,
    attn_in, mlp_in, tok_in, cot_in, qkv_send, out_send, norm_send, gu_send, down_send,
    tok_low, cot_low,
    up_send, up_recv, down_s, down_recv, core_send, core_recv, send, recv, local,
):
    mine, place = lax.axis_index("dp"), lax.axis_index("shard")
    line, core = place // 2, place % 2
    width, ff_width = qkv_send.shape[-1] // 3, down_send.shape[-1]
    above, below = (mine, place + 2), (mine, place - 2)
    partner = (mine, place + 1 - 2 * core)
    has_above, has_below = line < N_SH // 2 - 1, line > 0
    pair = (send, recv)
    loads = [
        pltpu.make_async_copy(attn_hbm, attn_in, local.at[0]),
        pltpu.make_async_copy(tok_hbm, tok_in, local.at[1]),
        pltpu.make_async_copy(mlp_hbm, mlp_in, local.at[2]),
        pltpu.make_async_copy(cot_hbm, cot_in, local.at[3]),
    ]
    for copy in loads:
        copy.start()

    barrier = pltpu.get_barrier_semaphore()
    for peer in [to_dp(k) for k in (1, 2, 3)] + [partner]:
        pl.semaphore_signal(barrier, inc=1, device_id=peer, device_id_type=MESH)

    @pl.when(has_above)
    def _():
        pl.semaphore_signal(barrier, inc=1, device_id=above, device_id_type=MESH)

    @pl.when(has_below)
    def _():
        pl.semaphore_signal(barrier, inc=1, device_id=below, device_id_type=MESH)

    norm_send[...] = jnp.zeros_like(norm_send)
    norm_send[0:7, 0 : norm_ref.shape[1]] = norm_ref[...].astype(LOW).astype(FULL)
    loads[0].wait()
    for part in range(3):
        for d in range(N_DP):
            begin = part * D + d * width
            qkv_send[d, :, part * width : part * width + width] = attn_in[
                :, begin : begin + width
            ].astype(LOW)
    out_send[...] = to_shards(attn_in[:, 3 * D :]).astype(LOW)

    @pl.when(has_above & has_below)
    def _():
        pl.semaphore_wait(barrier, 6)

    @pl.when(jnp.logical_not(has_above & has_below))
    def _():
        pl.semaphore_wait(barrier, 5)

    def slab(n, shard):
        if n == 0:
            return w_qkv.at[shard, mine]
        if n == 1:
            return w_out.at[shard]
        if n == 2:
            return norm_all.at[shard]
        return w_qkv.at[shard, dp_peer(n - 2)]

    def source(n):
        return {0: qkv_send.at[mine], 1: out_send}.get(n, slab(n, place))

    def along(n, shard, hop, sem_pair, peer, held=None):
        start = slab(n, shard) if held is None else held
        return remote(start, slab(n, shard), sem_pair, hop * SLABS + n, peer)

    ups, downs, cores = (up_send, up_recv), (down_s, down_recv), (core_send, core_recv)

    def pass_block(n, origin, hop, held, upward, downward):
        shard = 2 * origin + core
        if upward:

            @pl.when(has_above)
            def _():
                along(n, shard, hop, ups, above, held).start()

        if downward:

            @pl.when(has_below)
            def _():
                along(n, shard, hop, downs, below, held).start()

        along(n, shard, origin, cores, partner, held).start()

    norms = [
        remote(norm_send, norm_all.at[place, mine], pair, 21 + k - 1, to_dp(k)) for k in (1, 2, 3)
    ]
    trade = [
        remote(qkv_send.at[dp_peer(k)], w_qkv.at[place, mine], pair, k - 1, to_dp(k))
        for k in (1, 2, 3)
    ]
    own = [
        pltpu.make_async_copy(qkv_send.at[mine], w_qkv.at[place, mine], local.at[4]),
        pltpu.make_async_copy(out_send, w_out.at[place], local.at[5]),
        pltpu.make_async_copy(norm_send, norm_all.at[place, mine], local.at[6]),
        pltpu.make_async_copy(place_ref, place_all.at[0], local.at[7]),
    ]
    for copy in norms + trade:
        copy.start()
    pass_block(0, line, 0, source(0), True, True)
    pass_block(1, line, 0, source(1), True, True)
    for copy in own:
        copy.start()

    loads[1].wait()

    def permute_tokens(here):
        tok_low[here] = to_shards(tok_in[here].astype(FULL)).astype(LOW)

    in_chunks(tok_in.shape[0], permute_tokens)
    places = [
        remote(place_ref, place_all.at[k], pair, 9 + k - 1, to_dp(k)) for k in (1, 2, 3)
    ]
    for copy in places:
        copy.start()
    tok = spread(tok_low, tok_all, pair, 3)
    keep = [
        pltpu.make_async_copy(tok_low, tok_all.at[0], local.at[8]),
        pltpu.make_async_copy(tok_low, tok_own, local.at[9]),
    ]
    for copy in keep:
        copy.start()

    own[2].wait()
    for copy in norms:
        copy.wait_recv()
    pass_block(2, line, 0, None, True, True)
    for k in (1, 2, 3):
        trade[k - 1].wait_recv()
        pass_block(2 + k, line, 0, None, True, True)

    loads[2].wait()
    for d in range(N_DP):
        for part in range(2):
            begin = part * FF + d * ff_width
            gu_send[d, :, part * ff_width : part * ff_width + ff_width] = mlp_in[
                :, begin : begin + ff_width
            ].astype(LOW)
        begin = 2 * FF + d * ff_width
        down_send[d] = mlp_in[:, begin : begin + ff_width].astype(LOW)
    blocks = []
    for n, (held, target) in enumerate(((gu_send, gu_out), (down_send, down_out))):
        for k in (3, 1, 2):
            blocks.append(
                remote(held.at[dp_peer(k)], target.at[mine], pair, 12 + 3 * n + k - 1, to_dp(k))
            )
        blocks.append(pltpu.make_async_copy(held.at[mine], target.at[mine], local.at[10 + n]))

    loads[3].wait()

    def permute_cotangent(here):
        cot_low[here] = to_shards(cot_in[here].astype(FULL)).astype(LOW)

    in_chunks(cot_in.shape[0], permute_cotangent)
    keep.append(pltpu.make_async_copy(cot_low, cot_own, local.at[12]))
    keep[2].start()

    def hop_step(hop):
        for n in range(SLABS):

            @pl.when(line >= hop)
            def _():
                shard = place - 2 * hop
                along(n, shard, hop - 1, ups, above).wait_recv()
                pass_block(n, line - hop, hop, None, True, False)

            @pl.when(line + hop < N_SH // 2)
            def _():
                shard = place + 2 * hop
                along(n, shard, hop - 1, downs, below).wait_recv()
                pass_block(n, line + hop, hop, None, False, True)

    hop_step(1)
    pass_on(*tok)
    for copy in blocks:
        copy.start()
    hop_step(2)
    hop_step(3)

    spread_end(*tok)
    for copy in blocks + own[:2] + own[3:] + keep + places:
        copy.wait()
    for copy in norms + trade:
        copy.wait_send()
    for hop in range(N_SH // 2 - 1):
        for n in range(SLABS):

            @pl.when(has_above & (line >= hop))
            def _():
                along(n, place - 2 * hop, hop, ups, above).wait_send()

            @pl.when(has_below & (line + hop < N_SH // 2))
            def _():
                along(n, place + 2 * hop, hop, downs, below).wait_send()

    for origin in range(N_SH // 2):
        for n in range(SLABS):
            along(n, 2 * origin + core, origin, cores, partner).wait_send()
            along(n, 2 * origin + 1 - core, origin, cores, partner).wait_recv()


def start(attn_master, mlp_master, norm_master, tokens, cotangent, places, number):
    rows = attn_master.shape[0]
    width, ff_width = D // N_DP, FF // N_DP
    seq = tokens.shape[0]
    norm_shape = (8, 128)
    hops = (N_SH // 2 - 1) * SLABS
    return pl.pallas_call(
        start_kernel,
        out_shape=[
            jax.ShapeDtypeStruct((N_SH, N_DP, rows, 3 * width), LOW),
            jax.ShapeDtypeStruct((N_SH, rows, D), LOW),
            jax.ShapeDtypeStruct((N_SH, N_DP) + norm_shape, FULL),
            jax.ShapeDtypeStruct((N_DP, seq, D), LOW),
            jax.ShapeDtypeStruct((N_DP,) + places.shape, places.dtype),
            jax.ShapeDtypeStruct((N_DP, rows, 2 * ff_width), LOW),
            jax.ShapeDtypeStruct((N_DP, rows, ff_width), LOW),
            jax.ShapeDtypeStruct((seq, D), LOW),
            jax.ShapeDtypeStruct((seq, D), LOW),
        ],
        in_specs=[ANY, ANY, VMEM, ANY, ANY, ANY],
        out_specs=[ANY] * 9,
        scratch_shapes=[
            pltpu.VMEM(attn_master.shape, FULL),
            pltpu.VMEM(mlp_master.shape, FULL),
            pltpu.VMEM(tokens.shape, LOW),
            pltpu.VMEM(tokens.shape, LOW),
            pltpu.VMEM((N_DP, rows, 3 * width), LOW),
            pltpu.VMEM((rows, D), LOW),
            pltpu.VMEM(norm_shape, FULL),
            pltpu.VMEM((N_DP, rows, 2 * ff_width), LOW),
            pltpu.VMEM((N_DP, rows, ff_width), LOW),
            pltpu.VMEM(tokens.shape, LOW),
            pltpu.VMEM(tokens.shape, LOW),
        ]
        + sems(hops)
        + sems(hops)
        + sems((N_SH // 2) * SLABS)
        + sems(24)
        + [pltpu.SemaphoreType.DMA((13,))],
        compiler_params=comm_params(number),
        cost_estimate=cost(90),
        name="start",
    )(attn_master, mlp_master, norm_master, tokens, cotangent, places)


def unit_rows(values):
    average = jnp.mean(values, axis=-1, keepdims=True)
    centered = values - average
    variance = jnp.mean(centered * centered, axis=-1, keepdims=True)
    inverse = lax.rsqrt(variance + NORM_EPS)
    return centered * inverse, inverse


def turn(value, cos_ref, up_ref, down_ref, sign):
    left = pltpu.roll(value, 128 - ROT // 2, 1)
    right = pltpu.roll(value, ROT // 2, 1)
    return value * cos_ref[...] + sign * (left * up_ref[...] + right * down_ref[...])


def head_masks():
    lane = lax.broadcasted_iota(jnp.int32, (1, 128), 1)
    return [lane < HEAD, lane >= HEAD]


def softmax_rows(queries, keys, bias):
    scores = lax.dot_general(queries, keys, LAST_DIMS, preferred_element_type=FULL)
    scores = scores * (HEAD ** (-0.5)) + bias
    top = jnp.max(scores, axis=-1, keepdims=True)
    weights = jnp.exp(scores - top)
    return weights / jnp.sum(weights, axis=-1, keepdims=True)


def fill_tables(place_ref, rate_ref, cos_ref, up_ref, down_ref, mask_ref):
    seq = place_ref.shape[-1]
    half = ROT // 2
    row = place_ref[0].astype(FULL)
    columns = jnp.transpose(jnp.broadcast_to(row[0:1], (8, seq)))[:, 0:1]
    spots = jnp.transpose(jnp.broadcast_to(row[1:2], (8, seq)))[:, 0:1]
    angles = spots * rate_ref[0:1, :]
    lane = lax.broadcasted_iota(jnp.int32, (1, 128), 1) % HEAD
    sines = jnp.sin(angles)
    cos_ref[...] = jnp.where(lane < ROT, jnp.cos(angles), 1.0)
    up_ref[...] = jnp.where(lane < half, -sines, 0.0)
    down_ref[...] = jnp.where((lane >= half) & (lane < ROT), sines, 0.0)
    later = lax.broadcasted_iota(jnp.int32, (seq, seq), 0) >= lax.broadcasted_iota(
        jnp.int32, (seq, seq), 1
    )
    mask_ref[0] = jnp.where((columns == row[0:1]) & later, 0.0, NEG_FILL)


def attn_forward_kernel(
    cot_ref, tok_ref, place_ref, rate_ref, norm_ref, w_ref, b_ref,
    cot_all, normed_ref, q_ref, k_ref, v_ref, mix_ref, cos_ref, up_ref, down_ref, mask_ref,
    qkv_ref, send, recv,
):
    width = q_ref.shape[-1]
    step, last = pl.program_id(0), pl.num_programs(0) - 1
    sent = [
        remote(cot_ref, cot_all.at[k - 1], (send, recv), k - 1, to_dp(k)) for k in (1, 2)
    ]

    @pl.when(step == 0)
    def _():
        greet([to_dp(1), to_dp(2)])
        for copy in sent:
            copy.start()

    fill_tables(place_ref, rate_ref, cos_ref, up_ref, down_ref, mask_ref)
    unit, _ = unit_rows(tok_ref[0].astype(FULL))
    normed_ref[0] = (unit * norm_ref[0:1, :] + norm_ref[1:2, :]).astype(LOW)
    qkv_ref[...] = jnp.dot(normed_ref[0], w_ref[...], preferred_element_type=FULL) + b_ref[...]
    masks = head_masks()
    for pair in range(width // 128):
        here = slice(pair * 128, pair * 128 + 128)
        queries = turn(qkv_ref[:, here], cos_ref, up_ref, down_ref, 1.0).astype(LOW)
        there = slice(width + pair * 128, width + pair * 128 + 128)
        keys = turn(qkv_ref[:, there], cos_ref, up_ref, down_ref, 1.0).astype(LOW)
        there = slice(2 * width + pair * 128, 2 * width + pair * 128 + 128)
        values = qkv_ref[:, there].astype(LOW)
        q_ref[0, :, here] = queries
        k_ref[0, :, here] = keys
        v_ref[0, :, here] = values
        total = None
        for mask in masks:
            attend = softmax_rows(queries, jnp.where(mask, keys, 0), mask_ref[0])
            part = jnp.dot(
                attend.astype(LOW), jnp.where(mask, values, 0), preferred_element_type=FULL
            )
            total = part if total is None else total + part
        mix_ref[0, :, here] = total.astype(LOW)

    @pl.when(step == last)
    def _():
        for copy in sent:
            copy.wait()


def group_spec(array):
    return pl.BlockSpec((1,) + array.shape[1:], lambda g: (g, 0, 0))


def whole_spec(array):
    return pl.BlockSpec(array.shape, lambda g: (0,) * len(array.shape))


def attn_forward(cotangent, tokens, places, rates, norm_vals, w_qkv, bias, number):
    groups, seq, _ = tokens.shape
    width = w_qkv.shape[1] // 3
    row_spec = pl.BlockSpec((seq, 128), lambda g: (g, 0))
    part = jax.ShapeDtypeStruct((groups, seq, width), LOW)
    normed = jax.ShapeDtypeStruct(tokens.shape, LOW)
    near = jax.ShapeDtypeStruct((2,) + tokens.shape[1:], LOW)
    table = jax.ShapeDtypeStruct((groups * seq, 128), FULL)
    mask = jax.ShapeDtypeStruct((groups, seq, seq), FULL)
    return pl.pallas_call(
        attn_forward_kernel,
        grid=(groups,),
        out_shape=[near, normed, part, part, part, part, table, table, table, mask],
        in_specs=[
            ANY,
            group_spec(tokens),
            group_spec(places),
            whole_spec(rates),
            whole_spec(norm_vals),
            whole_spec(w_qkv),
            whole_spec(bias),
        ],
        out_specs=[ANY, group_spec(normed)]
        + [group_spec(part)] * 4
        + [row_spec] * 3
        + [group_spec(mask)],
        scratch_shapes=[pltpu.VMEM((seq, 3 * width), FULL)]
        + sems(2),
        compiler_params=comm_params(number),
        cost_estimate=pl.CostEstimate(
            flops=2 * groups * seq * (D * 3 * width + 2 * seq * width * 2),
            bytes_accessed=2 * (w_qkv.size + 3 * tokens.size),
            transcendentals=groups * seq * seq * (width // HEAD),
        ),
        name="attn_forward",
    )(cotangent, tokens, places, rates, norm_vals, w_qkv, bias)


def attn_backward_kernel(
    part_hbm, normed_hbm, mix_hbm, gao_hbm, resid_hbm, gao_ref, w_ref, q_ref, k_ref, v_ref,
    mask_ref, cos_ref, up_ref, down_ref,
    block_ref, grad_ref, sum_ref, attn_hbm,
    gm_ref, parts, normed, mix, gao, resid_ref, wo_grad, stage, grads_all, out, diag, full,
    send, recv, local,
):
    width = q_ref.shape[-1]
    rows = q_ref.shape[1]
    step, last = pl.program_id(0), pl.num_programs(0) - 1
    total = RowSum(parts, (out, diag, full), (send, recv), 0, source=part_hbm)
    loads = [
        pltpu.make_async_copy(part_hbm, parts, local.at[0]),
        pltpu.make_async_copy(mix_hbm, mix, local.at[1]),
        pltpu.make_async_copy(gao_hbm, gao, local.at[2]),
        pltpu.make_async_copy(normed_hbm, normed, local.at[3]),
        pltpu.make_async_copy(resid_hbm, resid_ref, local.at[4]),
    ]

    @pl.when(step == 0)
    def _():
        loads[0].start()
        greet([to_dp(1), to_dp(2)])
        for k in (3, 1, 2):
            total.send(k)
        for copy in loads[1:]:
            copy.start()
        sum_ref[...] = jnp.zeros_like(sum_ref)

    @pl.when(step == 2)
    def _():
        loads[0].wait()
        total.relay()

    scale = HEAD ** (-0.5)
    gm_ref[...] = lax.dot_general(
        gao_ref[0], w_ref[...], LAST_DIMS, preferred_element_type=FULL
    ).astype(LOW)
    masks = head_masks()
    for pair in range(width // 128):
        here = slice(pair * 128, pair * 128 + 128)
        queries, keys, values = q_ref[0, :, here], k_ref[0, :, here], v_ref[0, :, here]
        grads = gm_ref[:, here]
        grad_q = grad_k = grad_v = 0.0
        for mask in masks:
            keys_one = jnp.where(mask, keys, 0)
            attend = softmax_rows(queries, keys_one, mask_ref[0])
            grad_attend = lax.dot_general(
                grads, jnp.where(mask, values, 0), LAST_DIMS, preferred_element_type=FULL
            )
            grad_v += lax.dot_general(
                attend.astype(LOW),
                jnp.where(mask, grads, 0),
                LEAD_DIMS,
                preferred_element_type=FULL,
            )
            mean = jnp.sum(attend * grad_attend, axis=-1, keepdims=True)
            grad_scores = (attend * (grad_attend - mean)).astype(LOW)
            grad_q += jnp.dot(grad_scores, keys_one, preferred_element_type=FULL)
            grad_k += lax.dot_general(
                grad_scores, jnp.where(mask, queries, 0), LEAD_DIMS, preferred_element_type=FULL
            )
        grad_q = turn(grad_q * scale, cos_ref, up_ref, down_ref, -1.0)
        grad_k = turn(grad_k * scale, cos_ref, up_ref, down_ref, -1.0)
        for n, grad in enumerate((grad_q, grad_k, grad_v)):
            start = n * width + pair * 128
            grad_ref[0, :, start : start + 128] = grad.astype(LOW)
    grads_all[pl.ds(pl.multiple_of(step * rows, rows), rows)] = grad_ref[0]
    sum_ref[0:1, :] += jnp.sum(grad_ref[0].astype(FULL), axis=0, keepdims=True)

    @pl.when(step == last)
    def _():
        for copy in loads[1:]:
            copy.wait()

        for pair in range(width // 128):
            wo_grad[pair * 128 : pair * 128 + 128, :] = lax.dot_general(
                mix[:, pair * 128 : pair * 128 + 128],
                gao[...],
                LEAD_DIMS,
                preferred_element_type=FULL,
            ).astype(LOW)

        def store(index, slot):
            return pltpu.make_async_copy(stage.at[slot], attn_hbm.at[index], local.at[5 + slot])

        def one_shard(index, carry):
            slot = index % 2

            @pl.when(index >= 2)
            def _():
                store(index - 2, slot).wait()

            here = pl.ds(pl.multiple_of(index * 256, 256), 256)
            stage[slot, :, : 3 * width] = lax.dot_general(
                normed[:, here], grads_all[...], LEAD_DIMS, preferred_element_type=FULL
            ).astype(LOW)
            side = pl.ds(pl.multiple_of(index * 64, 64), 64)
            for part in range(N_DP):
                stage[slot, part * 64 : part * 64 + 64, 3 * width :] = wo_grad[
                    side, part * width : part * width + width
                ]
            store(index, slot).start()
            return carry

        lax.fori_loop(0, N_SH, one_shard, 0)
        for index in (N_SH - 2, N_SH - 1):
            store(index, index % 2).wait()
        total.finish()

        def body(here):
            block_ref[here] = to_places(resid_ref[here] + total.rows(here)).astype(LOW)

        in_chunks(rows, body)


def attn_backward(
    out_part, normed1, mixture, resid, gao, w_out, queries, keys, values, mask, tables, number
):
    groups, seq, cols = gao.shape
    width = queries.shape[-1]
    row_spec = pl.BlockSpec((seq, 128), lambda g: (g, 0))
    grad = jax.ShapeDtypeStruct((groups, seq, 3 * width), LOW)
    sums = jax.ShapeDtypeStruct((8, 3 * width), FULL)
    flat = groups * seq
    return pl.pallas_call(
        attn_backward_kernel,
        grid=(groups,),
        out_shape=[
            jax.ShapeDtypeStruct(resid.shape, LOW),
            grad,
            sums,
            jax.ShapeDtypeStruct((N_SH, D // N_SH, 4 * width), LOW),
        ],
        in_specs=[
            ANY,
            ANY,
            ANY,
            ANY,
            ANY,
            group_spec(gao),
            VMEM,
            group_spec(queries),
            group_spec(keys),
            group_spec(values),
            group_spec(mask),
            row_spec,
            row_spec,
            row_spec,
        ],
        out_specs=[VMEM, group_spec(grad), whole_spec(sums), ANY],
        scratch_shapes=[
            pltpu.VMEM((seq, width), LOW),
            pltpu.VMEM(gao.shape, LOW),
            pltpu.VMEM((flat, cols), LOW),
            pltpu.VMEM((flat, width), LOW),
            pltpu.VMEM((flat, cols), LOW),
            pltpu.VMEM(resid.shape, FULL),
            pltpu.VMEM((width, cols), LOW),
            pltpu.VMEM((2, D // N_SH, 4 * width), LOW),
            pltpu.VMEM((flat, 3 * width), LOW),
        ]
        + row_sum_scratch(seq, cols)
        + sems(6)
        + [pltpu.SemaphoreType.DMA((7,))],
        compiler_params=comm_params(number),
        cost_estimate=cost(55),
        name="attn_backward",
    )(
        out_part,
        normed1.reshape(flat, cols),
        mixture.reshape(flat, width),
        gao.reshape(flat, cols),
        resid,
        gao,
        w_out,
        queries,
        keys,
        values,
        mask,
        *tables,
    )


class RowSum:
    scratch = 3

    def __init__(self, parts, scratch, pair, base, pieces=1, column_base=0, source=None):
        self.parts, self.pair = parts, pair
        self.pieces, self.column_base = pieces, column_base
        self.out, self.diag, self.full = scratch
        self.half = parts.shape[1] // 2
        self.top, self.bottom = pl.ds(0, self.half), pl.ds(self.half, self.half)
        top, bottom = self.top, self.bottom
        parts = parts if source is None else source
        whole = [
            lambda: remote(parts.at[3, top], self.diag.at[0], pair, base + 0, to_dp(1)),
            lambda: remote(parts.at[3, bottom], self.diag.at[1], pair, base + 1, to_dp(2)),
        ]
        self.first = [make() if pieces == 1 else None for make in whole] + [
            remote(parts.at[1, top], self.full.at[0, top], pair, base + 2, to_dp(1)),
            remote(parts.at[2, bottom], self.full.at[1, bottom], pair, base + 3, to_dp(2)),
        ]
        self.second = [
            remote(self.out.at[0], self.full.at[0, bottom], pair, base + 4, to_dp(1)),
            remote(self.out.at[1], self.full.at[1, top], pair, base + 5, to_dp(2)),
        ]

    def send_columns(self, cols, index):
        for copy in self.column_copies(cols, index):
            copy.start()

    def column_copies(self, cols, index):
        here = pl.ds(cols.start, cols.stop - cols.start)
        return [
            remote(
                self.parts.at[3, rows, here],
                self.diag.at[side, rows_in, here],
                self.pair,
                self.column_base + 2 * index + side,
                to_dp(1 + side),
            )
            for side, rows, rows_in in (
                (0, self.top, pl.ds(0, self.half)),
                (1, self.bottom, pl.ds(0, self.half)),
            )
        ]

    def send(self, k):
        for copy in {3: self.first[:2], 1: self.first[2:3], 2: self.first[3:]}[k]:
            copy.start()

    def diag_wait(self, side):
        if self.pieces == 1:
            self.first[side].wait_recv()
            return
        size = self.parts.shape[2] // self.pieces
        for n in range(self.pieces):
            self.column_copies(slice(n * size, n * size + size), n)[side].wait_recv()

    def relay(self):
        self.diag_wait(1)
        self.out[0] = (
            self.parts[1, self.bottom].astype(FULL) + self.diag[1].astype(FULL)
        ).astype(LOW)
        self.second[0].start()
        self.diag_wait(0)
        self.out[1] = (self.parts[2, self.top].astype(FULL) + self.diag[0].astype(FULL)).astype(
            LOW
        )
        self.second[1].start()

    def finish(self):
        self.first[2].wait_recv()
        self.first[3].wait_recv()
        self.second[0].wait_recv()
        self.second[1].wait_recv()
        for copy in self.first[2:] + self.second:
            copy.wait_send()
        size = self.parts.shape[2] // self.pieces
        for n in range(self.pieces):
            if self.pieces > 1:
                for copy in self.column_copies(slice(n * size, n * size + size), n):
                    copy.wait_send()
        if self.pieces == 1:
            for copy in self.first[:2]:
                copy.wait_send()

    def rows(self, part):
        return (
            self.parts[0, part].astype(FULL)
            + self.full[0, part].astype(FULL)
            + self.full[1, part].astype(FULL)
        )


def row_sum_scratch(rows, cols):
    return [
        pltpu.VMEM((2, rows // 2, cols), LOW),
        pltpu.VMEM((2, rows // 2, cols), LOW),
        pltpu.VMEM((2, rows, cols), LOW),
    ]


def mid_forward_kernel(
    mix_ref, w_ref, tok_ref, norm_ref, resid_hbm, normed_all,
    resid_ref, parts, out, diag, full, own, send, recv, local,
):
    rows = tok_ref.shape[0]
    greet([to_dp(1), to_dp(2)])
    total = RowSum(parts, (out, diag, full), (send, recv), 0)
    for k in (3, 1, 2, 0):
        parts[k] = jnp.dot(mix_ref[k], w_ref[...], preferred_element_type=FULL).astype(LOW)
        if k:
            total.send(k)
    total.relay()
    total.finish()

    def body(here):
        resid = tok_ref[here].astype(FULL) + total.rows(here)
        resid_ref[here] = resid
        unit, _ = unit_rows(resid)
        own[here] = (unit * norm_ref[5:6, :] + norm_ref[6:7, :]).astype(LOW)

    in_chunks(rows, body)
    sent = spread(own, normed_all, (send, recv), 6)
    stores = [
        pltpu.make_async_copy(own, normed_all.at[0], local.at[0]),
        pltpu.make_async_copy(resid_ref, resid_hbm, local.at[1]),
    ]
    for copy in stores:
        copy.start()
    pass_on(*sent)
    spread_end(*sent)
    for copy in stores:
        copy.wait()


def mid_forward(mixture, w_out, tokens, norm_vals, number):
    rows, cols = tokens.shape
    group = (N_DP, rows, cols)
    return pl.pallas_call(
        mid_forward_kernel,
        out_shape=[
            jax.ShapeDtypeStruct(tokens.shape, FULL),
            jax.ShapeDtypeStruct(group, LOW),
        ],
        in_specs=[VMEM] * 4,
        out_specs=[ANY, ANY],
        scratch_shapes=[pltpu.VMEM((rows, cols), FULL), pltpu.VMEM(group, LOW)]
        + row_sum_scratch(rows, cols)
        + [pltpu.VMEM((rows, cols), LOW)]
        + sems(12)
        + [pltpu.SemaphoreType.DMA((2,))],
        compiler_params=comm_params(number),
        cost_estimate=cost(92),
        name="mid_forward",
    )(mixture, w_out, tokens, norm_vals)


def mid_backward_kernel(
    ggu_hbm, wgu_hbm, wdown_hbm, hid_hbm, resid_hbm, cot_hbm, norm_ref,
    grad_hbm, gao_all, sum_ref, part_hbm,
    ggu, w_gu, w_down, hid, resid_ref, cot_ref, grad_ref, part_ref, parts, out, diag, full, own,
    send, recv, local,
):
    rows, cols = resid_ref.shape
    pieces = 4
    size = cols // pieces
    weights = [
        pltpu.make_async_copy(
            wgu_hbm.at[pl.ds(n * size, size)], w_gu.at[pl.ds(n * size, size)], local.at[8 + n]
        )
        for n in range(pieces)
    ]
    grads_in = [pltpu.make_async_copy(ggu_hbm.at[k], ggu.at[k], local.at[k]) for k in range(4)]
    later = [
        pltpu.make_async_copy(resid_hbm, resid_ref, local.at[4]),
        pltpu.make_async_copy(cot_hbm, cot_ref, local.at[5]),
        pltpu.make_async_copy(wdown_hbm, w_down, local.at[6]),
        pltpu.make_async_copy(hid_hbm, hid, local.at[7]),
    ]
    for copy in [grads_in[3]] + weights + [grads_in[k] for k in (1, 2, 0)] + later:
        copy.start()
    greet([to_dp(1), to_dp(2)])
    total = RowSum(parts, (out, diag, full), (send, recv), 0, pieces, 12)
    grads_in[3].wait()
    for n in range(pieces):
        weights[n].wait()
        here = slice(n * size, n * size + size)
        parts[3, :, here] = lax.dot_general(
            ggu[3], w_gu[here, :], LAST_DIMS, preferred_element_type=FULL
        ).astype(LOW)
        total.send_columns(here, n)
    for k in (1, 2, 0):
        grads_in[k].wait()
        parts[k] = lax.dot_general(
            ggu[k], w_gu[...], LAST_DIMS, preferred_element_type=FULL
        ).astype(LOW)
        if k:
            total.send(k)
    sum_ref[...] = jnp.zeros_like(sum_ref)

    def out_part(k):
        part_ref[k] = lax.dot_general(
            hid[k], w_down[...], LAST_DIMS, preferred_element_type=FULL
        ).astype(LOW)

    total.relay()
    for copy in later:
        copy.wait()
    out_part(0)
    out_part(1)
    out_part(2)
    total.finish()

    def body(here):
        grads = total.rows(here)
        unit, inverse = unit_rows(resid_ref[here])
        sum_ref[0:1, :] += jnp.sum(grads * unit, axis=0, keepdims=True)
        sum_ref[1:2, :] += jnp.sum(grads, axis=0, keepdims=True)
        grad = cot_ref[here].astype(FULL) + layer_back(grads, norm_ref[5:6, :], unit, inverse)
        grad_ref[here] = grad
        own[here] = grad.astype(LOW)

    in_chunks(rows, body)
    sent = spread(own, gao_all, (send, recv), 6)
    stores = [
        pltpu.make_async_copy(own, gao_all.at[0], local.at[0]),
        pltpu.make_async_copy(grad_ref, grad_hbm, local.at[1]),
    ]
    for copy in stores:
        copy.start()
    out_part(3)
    stores.append(pltpu.make_async_copy(part_ref, part_hbm, local.at[2]))
    stores[2].start()
    pass_on(*sent)
    spread_end(*sent)
    for copy in stores:
        copy.wait()


def mid_backward(grad_gu, w_gu, w_down, hidden, resid, cotangent, norm_vals, number):
    rows, cols = resid.shape
    group = (N_DP, rows, cols)
    return pl.pallas_call(
        mid_backward_kernel,
        out_shape=[
            jax.ShapeDtypeStruct(resid.shape, FULL),
            jax.ShapeDtypeStruct(group, LOW),
            jax.ShapeDtypeStruct((8, cols), FULL),
            jax.ShapeDtypeStruct(group, LOW),
        ],
        in_specs=[ANY] * 6 + [VMEM],
        out_specs=[ANY, ANY, VMEM, ANY],
        scratch_shapes=[
            pltpu.VMEM(array.shape, array.dtype)
            for array in (grad_gu, w_gu, w_down, hidden, resid, cotangent, resid)
        ]
        + [pltpu.VMEM(group, LOW)] * 2
        + row_sum_scratch(rows, cols)
        + [pltpu.VMEM((rows, cols), LOW)]
        + sems(20)
        + [pltpu.SemaphoreType.DMA((12,))],
        compiler_params=comm_params(number),
        cost_estimate=cost(100),
        name="mid_backward",
    )(grad_gu, w_gu, w_down, hidden, resid, cotangent, norm_vals)


LINE = N_SH // 2
PIECES = 4


class LineSum:
    def __init__(self, terms_hbm, scratch, sem_refs):
        (self.terms, self.other, self.up_in, self.down_in, self.up_out, self.down_out) = scratch
        self.hbm = terms_hbm
        (core_s, core_r, up_s, up_r, down_s, down_r, self.local) = sem_refs
        self.core_sems, self.up_sems, self.down_sems = (core_s, core_r), (up_s, up_r), (down_s, down_r)
        mine, place = lax.axis_index("dp"), lax.axis_index("shard")
        self.line, self.core = place // 2, place % 2
        self.above, self.below = (mine, place + 2), (mine, place - 2)
        self.partner = (mine, place + 1 - 2 * self.core)
        self.size = self.terms.shape[1] // PIECES
        self.steps = (LINE - 1) * PIECES

    def at_end(self):
        return (self.line == 0) | (self.line == LINE - 1)

    def rows(self, piece):
        return pl.ds(pl.multiple_of(piece * self.size, self.size), self.size)

    def core_copy(self, target, piece):
        here = self.rows(piece)
        return remote(
            self.hbm.at[2 * target + 1 - self.core, here],
            self.other.at[target, here],
            self.core_sems,
            target * PIECES + piece,
            self.partner,
        )

    def load(self, target):
        return pltpu.make_async_copy(
            self.hbm.at[2 * target + self.core], self.terms.at[target], self.local.at[target]
        )

    def load_all(self):
        for target in range(LINE):
            self.load(target).start()

    def start(self):
        for targets in ((LINE - 1, 0), (LINE - 2, 1)):
            for piece in range(PIECES):
                for target in targets:
                    self.core_copy(target, piece).start()
        for target in range(LINE):
            self.load(target).wait()

    def own(self, target, piece):
        self.core_copy(target, piece).wait_recv()
        here = self.rows(piece)
        return self.terms[target, here].astype(FULL) + self.other[target, here].astype(FULL)

    def up_copy(self, index):
        return remote(
            self.up_out.at[index], self.up_in.at[index], self.up_sems, index, self.above
        )

    def down_copy(self, index):
        return remote(
            self.down_out.at[index], self.down_in.at[index], self.down_sems, index, self.below
        )

    def up(self, index):
        target, piece = LINE - 1 - index // PIECES, index % PIECES

        @pl.when(target > self.line)
        def _():
            self.up_out[index] = self.own(target, piece).astype(LOW)

            @pl.when(self.line > 0)
            def _():
                self.up_copy(index).wait_recv()
                self.up_out[index] = (
                    self.up_out[index].astype(FULL) + self.up_in[index].astype(FULL)
                ).astype(LOW)

            self.up_copy(index).start()

    def down(self, index):
        target, piece = index // PIECES, index % PIECES

        @pl.when(target < self.line)
        def _():
            self.down_out[index] = self.own(target, piece).astype(LOW)

            @pl.when(self.line < LINE - 1)
            def _():
                self.down_copy(index).wait_recv()
                self.down_out[index] = (
                    self.down_out[index].astype(FULL) + self.down_in[index].astype(FULL)
                ).astype(LOW)

            self.down_copy(index).start()

    def run(self, begin, end):
        def step(index, carry):
            @pl.when(self.line < LINE // 2)
            def _():
                @pl.when(index < self.steps)
                def _():
                    self.up(index)

                @pl.when(index > 0)
                def _():
                    self.down(index - 1)

            @pl.when(self.line >= LINE // 2)
            def _():
                @pl.when(index < self.steps)
                def _():
                    self.down(index)

                @pl.when(index > 0)
                def _():
                    self.up(index - 1)

            return carry

        lax.fori_loop(begin, end, step, 0)

    def finish(self, piece, result):
        here = self.rows(piece)
        result[here] = self.own(self.line, piece)

        @pl.when(self.line > 0)
        def _():
            index = (LINE - 1 - self.line) * PIECES + piece
            self.up_copy(index).wait_recv()
            result[here] = result[here] + self.up_in[index].astype(FULL)

        @pl.when(self.line < LINE - 1)
        def _():
            index = self.line * PIECES + piece
            self.down_copy(index).wait_recv()
            result[here] = result[here] + self.down_in[index].astype(FULL)

    def drain(self):
        def step(index, carry):
            @pl.when(LINE - 1 - index // PIECES > self.line)
            def _():
                self.up_copy(index).wait_send()

            @pl.when(index // PIECES < self.line)
            def _():
                self.down_copy(index).wait_send()

            return carry

        lax.fori_loop(0, self.steps, step, 0)

        def step_core(index, carry):
            self.core_copy(index // PIECES, index % PIECES).wait_send()
            return carry

        lax.fori_loop(0, LINE * PIECES, step_core, 0)


def line_sum_scratch(rows, cols):
    steps = (LINE - 1) * PIECES
    return (
        [pltpu.VMEM((LINE, rows, cols), LOW)] * 2
        + [pltpu.VMEM((steps, rows // PIECES, cols), LOW)] * 4
        + sems(LINE * PIECES)
        + sems(steps)
        + sems(steps)
        + [pltpu.SemaphoreType.DMA((LINE,))]
    )


def fold(values, total):
    values = values * values
    for start in range(0, values.shape[1], 128):
        total = total + values[:, start : start + 128]
    return total


def last_kernel(
    attn_hbm, grad_qkv_hbm, w_hbm, gu_hbm, down_hbm, tok_hbm, grad_hbm, norm_ref, rest_ref,
    input_ref, norm_total_ref, gu_out, down_out, qkv_out, out_ref, total_ref,
    grad_qkv_ref, w_ref, tok_ref, grad_ref, gu_in, down_in_low,
    parts, out, diag, full, sum_ref, near, far, part, near_part, far_part, attn_sum, attn_low,
    terms, other, up_in, down_in, up_out, down_out_pieces,
    core_s, core_r, up_s, up_r, down_s, down_r, term_local,
    send, recv, send_a, recv_a, send_b, recv_b, send_c, recv_c, send_d, recv_d, local,
):
    rows = tok_ref.shape[0]
    mine, place = lax.axis_index("dp"), lax.axis_index("shard")
    loads = [
        pltpu.make_async_copy(source, target, local.at[3 + n])
        for n, (source, target) in enumerate(
            (
                (w_hbm, w_ref),
                (grad_qkv_hbm, grad_qkv_ref),
                (tok_hbm, tok_ref),
                (grad_hbm, grad_ref),
                (gu_hbm, gu_in),
                (down_hbm, down_in_low),
            )
        )
    ]
    line = LineSum(
        attn_hbm,
        (terms, other, up_in, down_in, up_out, down_out_pieces),
        (core_s, core_r, up_s, up_r, down_s, down_r, term_local),
    )
    line.load_all()
    for copy in loads:
        copy.start()
    greet([to_dp(k) for k in (1, 2, 3)] + [to_shard(j) for j in range(1, N_SH)])
    line.start()
    total = RowSum(parts, (out, diag, full), (send, recv), 0)
    blocks = []
    for n, (held, target) in enumerate(((gu_hbm, gu_out), (down_hbm, down_out))):
        for k in (3, 1, 2):
            blocks.append(
                remote(
                    held.at[dp_peer(k)], target.at[mine], (send_c, recv_c), 3 * n + k - 1, to_dp(k)
                )
            )
    keeps = [
        pltpu.make_async_copy(gu_in.at[mine], gu_out.at[mine], local.at[0]),
        pltpu.make_async_copy(down_in_low.at[mine], down_out.at[mine], local.at[1]),
    ]
    for copy in blocks[3:]:
        copy.start()
    middle = jnp.logical_not(line.at_end())
    line.run(0, 1)

    def norm1_part(k):
        parts[k] = lax.dot_general(
            grad_qkv_ref[k], w_ref[...], LAST_DIMS, preferred_element_type=FULL
        ).astype(LOW)
        if k:
            total.send(k)

    def middle_run(begin, end):
        @pl.when(middle)
        def _():
            line.run(begin, end)

    loads[0].wait()
    loads[1].wait()
    norm1_part(3)

    @pl.when(line.at_end())
    def _():
        line.run(1, line.steps + 1)

    middle_run(1, 2)
    norm1_part(1)
    middle_run(2, 3)
    norm1_part(2)
    middle_run(3, 4)
    norm1_part(0)
    sum_ref[...] = rest_ref[...]
    middle_run(4, 6)
    total.relay()
    for copy in blocks[:3]:
        copy.start()
    loads[4].wait()
    loads[5].wait()
    for copy in keeps:
        copy.start()

    def square_low(array, value):
        def step(index, value):
            here = pl.ds(pl.multiple_of(index * 16, 16), 16)
            for k in range(N_DP):
                rows16 = array[k, here].astype(FULL)
                value = fold(rows16[8:], fold(rows16[:8], value))
            return value

        return lax.fori_loop(0, array.shape[1] // 16, step, value)

    part[...] = square_low(down_in_low, square_low(gu_in, jnp.zeros(part.shape, FULL)))
    middle_run(6, 9)
    total.finish()
    loads[2].wait()
    loads[3].wait()

    def body(here):
        grads = total.rows(here)
        unit, inverse = unit_rows(tok_ref[here].astype(FULL))
        sum_ref[0:1, :] += jnp.sum(grads * unit, axis=0, keepdims=True)
        sum_ref[1:2, :] += jnp.sum(grads, axis=0, keepdims=True)
        input_ref[here] = to_places(
            grad_ref[here] + layer_back(grads, norm_ref[0:1, :], unit, inverse)
        )

    in_chunks(rows, body)
    norm_near = [
        remote(sum_ref, near.at[k - 1], (send_a, recv_a), k - 1, to_dp(k)) for k in (1, 2, 3)
    ]
    for copy in norm_near:
        copy.start()
    for copy in norm_near:
        copy.wait()
    sum_ref[...] = sum_ref[...] + near[0] + near[1] + near[2]
    norm_far = [
        remote(sum_ref, far.at[j - 1], (send_b, recv_b), j - 1, to_shard(j))
        for j in range(1, N_SH)
    ]
    for copy in norm_far:
        copy.start()

    width = qkv_out.shape[-1]
    size = qkv_out.shape[1]

    def trade(sender, owner):
        return pltpu.make_async_remote_copy(
            src_ref=attn_low.at[owner],
            dst_ref=qkv_out.at[sender],
            send_sem=send_d.at[owner],
            recv_sem=recv_d.at[sender],
            device_id=(owner, place),
            device_id_type=MESH,
        )

    squares = part[...]
    for d in range(N_DP):
        line.finish(d, attn_sum)

        def square(index, value, d=d):
            here = pl.ds(pl.multiple_of(d * size + index * 8, 8), 8)
            return fold(attn_sum[here], value)

        squares = lax.fori_loop(0, size // 8, square, squares)
        attn_low[d] = attn_sum[d * size : d * size + size, :width].astype(LOW)

        @pl.when(mine != d)
        def _(d=d):
            trade(mine, d).start()

    part[...] = squares
    small = [
        remote(part, near_part.at[k - 1], (send_a, recv_a), 2 + k, to_dp(k)) for k in (1, 2, 3)
    ]
    for copy in small:
        copy.start()
    keep = pltpu.make_async_copy(attn_low.at[mine], qkv_out.at[mine], local.at[2])
    keep.start()
    for copy in small:
        copy.wait()
    part[...] = part[...] + near_part[0] + near_part[1] + near_part[2]
    small = [
        remote(part, far_part.at[j - 1], (send_b, recv_b), N_SH - 2 + j, to_shard(j))
        for j in range(1, N_SH)
    ]
    for copy in small:
        copy.start()
    out_ref[...] = to_places(
        jnp.concatenate(
            [attn_sum[d * size : d * size + size, width:] for d in range(N_DP)], axis=1
        )
    )
    for copy in norm_far:
        copy.wait()
    norm_total = sum_ref[...]
    for j in range(N_SH - 1):
        norm_total = norm_total + far[j]
    norm_total_ref[...] = norm_total
    squares = fold(norm_total, part[...])
    for copy in small:
        copy.wait()
    for j in range(N_SH - 1):
        squares = squares + far_part[j]
    total_ref[0, 0] = jnp.sum(squares)
    line.drain()
    for copy in blocks + keeps + [keep]:
        copy.wait()
    for d in range(N_DP):

        @pl.when(mine != d)
        def _(d=d):
            trade(mine, d).wait_send()
            trade(d, mine).wait_recv()


def last(
    part_attn, grad_qkv, w_qkv, gu_sum, down_sum, tokens, grad_resid, norm_vals, rest, number
):
    rows, cols = tokens.shape
    square_shape = (8, 128)
    block = part_attn.shape[1:]
    width = grad_qkv.shape[-1]
    size = block[0] // N_DP
    return pl.pallas_call(
        last_kernel,
        out_shape=[
            jax.ShapeDtypeStruct(tokens.shape, FULL),
            jax.ShapeDtypeStruct(rest.shape, FULL),
            jax.ShapeDtypeStruct(gu_sum.shape, gu_sum.dtype),
            jax.ShapeDtypeStruct(down_sum.shape, down_sum.dtype),
            jax.ShapeDtypeStruct((N_DP, size, width), LOW),
            jax.ShapeDtypeStruct((size, D), FULL),
            jax.ShapeDtypeStruct((1, 1), FULL),
        ],
        in_specs=[ANY] * 7 + [VMEM] * 2,
        out_specs=[VMEM, VMEM, ANY, ANY, ANY, VMEM, pl.BlockSpec(memory_space=pltpu.SMEM)],
        scratch_shapes=[
            pltpu.VMEM(a.shape, a.dtype)
            for a in (grad_qkv, w_qkv, tokens, grad_resid, gu_sum, down_sum)
        ]
        + [pltpu.VMEM((N_DP, rows, cols), LOW)]
        + row_sum_scratch(rows, cols)
        + [
            pltpu.VMEM(rest.shape, FULL),
            pltpu.VMEM((N_DP - 1,) + rest.shape, FULL),
            pltpu.VMEM((N_SH - 1,) + rest.shape, FULL),
            pltpu.VMEM(square_shape, FULL),
            pltpu.VMEM((N_DP - 1,) + square_shape, FULL),
            pltpu.VMEM((N_SH - 1,) + square_shape, FULL),
            pltpu.VMEM(block, FULL),
            pltpu.VMEM((N_DP, size, width), LOW),
        ]
        + line_sum_scratch(*block)
        + sems(6)
        + sems(2 * (N_DP - 1))
        + sems(2 * (N_SH - 1))
        + sems(6)
        + sems(N_DP)
        + [pltpu.SemaphoreType.DMA((9,))],
        compiler_params=comm_params(number),
        cost_estimate=cost(90),
        name="last",
    )(
        part_attn, grad_qkv, w_qkv, gu_sum, down_sum, tokens, grad_resid, norm_vals, rest
    )


def column_cuts(cols):
    return [(c, min(c + 256, cols)) for c in range(0, cols, 256)]


def weight_grad(left, right, stage, target, sem, first_sem):
    size = stage.shape[1]
    count = target.shape[0] // size

    def store(index, slot):
        here = pl.ds(pl.multiple_of(index * size, size), size)
        return pltpu.make_async_copy(stage.at[slot], target.at[here], sem.at[first_sem + slot])

    def step(index, carry):
        slot = index % 2

        @pl.when(index >= 2)
        def _():
            store(index - 2, slot).wait()

        here = pl.ds(pl.multiple_of(index * size, size), size)
        stage[slot] = lax.dot_general(
            left[:, here], right[...], LEAD_DIMS, preferred_element_type=FULL
        ).astype(LOW)
        store(index, slot).start()
        return carry

    lax.fori_loop(0, count, step, 0)
    for index in (count - 2, count - 1):
        store(index, index % 2).wait()


def mlp_one_kernel(
    x_hbm, own_hbm, near_hbm, wgu_hbm, hid_out, gate_out, up_out, part_out, far_out,
    x_ref, cot_ref, w_gu, hid, gate_stage, up_stage, grad_stage, local, loads, stores, send, recv,
):
    total = x_ref.shape[0]
    known = N_DP - 1
    seq = total // N_DP
    half = seq // 2
    greet([to_dp(1), to_dp(2)])
    passed = [
        remote(
            near_hbm.at[0, pl.ds(0, half)],
            cot_ref.at[pl.ds(known * seq, half)],
            (send, recv),
            0,
            to_dp(2),
        ),
        remote(
            near_hbm.at[1, pl.ds(half, half)],
            cot_ref.at[pl.ds(known * seq + half, half)],
            (send, recv),
            1,
            to_dp(1),
        ),
    ]
    for copy in passed:
        copy.start()
    cols = hid.shape[1]
    cuts = column_cuts(cols)
    block = total // 2

    def weight_loads(n):
        begin, end = cuts[n]
        return [
            pltpu.make_async_copy(
                wgu_hbm.at[:, pl.ds(at, end - begin)],
                w_gu.at[:, pl.ds(at, end - begin)],
                loads.at[2 * n + i],
            )
            for i, at in enumerate((begin, cols + begin))
        ]

    def stage_stores(n):
        begin, end = cuts[n]
        return [
            pltpu.make_async_copy(
                stage.at[n % 2, :, pl.ds(0, end - begin)],
                target.at[:, pl.ds(begin, end - begin)],
                stores.at[2 * i + n % 2],
            )
            for i, (stage, target) in enumerate(((gate_stage, gate_out), (up_stage, up_out)))
        ]

    data = [pltpu.make_async_copy(x_hbm, x_ref, local.at[0])]
    for copy in weight_loads(0) + data:
        copy.start()
    for n in range(1, len(cuts)):
        for copy in weight_loads(n):
            copy.start()
    data += [
        pltpu.make_async_copy(source, cot_ref.at[pl.ds(k * seq, seq)], local.at[5 + k])
        for k, source in enumerate((own_hbm, near_hbm.at[0], near_hbm.at[1]))
    ]
    for copy in data[1:]:
        copy.start()
    data[0].wait()
    for n, (begin, end) in enumerate(cuts):
        for copy in weight_loads(n):
            copy.wait()
        if n >= 2:
            for copy in stage_stores(n - 2):
                copy.wait()

        def rows(index, carry, begin=begin, end=end, slot=n % 2):
            here = pl.ds(pl.multiple_of(index * block, block), block)
            gate = jnp.dot(x_ref[here], w_gu[:, begin:end], preferred_element_type=FULL)
            up = jnp.dot(
                x_ref[here], w_gu[:, cols + begin : cols + end], preferred_element_type=FULL
            )
            hid[here, begin:end] = (gate / (1.0 + jnp.exp(-gate)) * up).astype(LOW)
            gate_stage[slot, here, : end - begin] = gate
            up_stage[slot, here, : end - begin] = up
            return carry

        lax.fori_loop(0, total // block, rows, 0)
        for copy in stage_stores(n):
            copy.start()
    outs = [
        pltpu.make_async_copy(hid, hid_out, local.at[2]),
        pltpu.make_async_copy(cot_ref.at[pl.ds(known * seq, seq)], far_out, local.at[1]),
    ]
    outs[0].start()
    for copy in data[1:]:
        copy.wait()
    for copy in passed:
        copy.wait()
    outs[1].start()
    weight_grad(cot_ref, hid, grad_stage, part_out, local, 3)
    for n in (len(cuts) - 2, len(cuts) - 1):
        for copy in stage_stores(n):
            copy.wait()
    for copy in outs:
        copy.wait()


def mlp_one(normed2, cotangent, near, w_gu, number):
    total, width = normed2.shape
    cols = w_gu.shape[1] // 2
    values = jax.ShapeDtypeStruct((total, cols), FULL)
    return pl.pallas_call(
        mlp_one_kernel,
        out_shape=[
            jax.ShapeDtypeStruct((total, cols), LOW),
            values,
            values,
            jax.ShapeDtypeStruct((width, cols), LOW),
            jax.ShapeDtypeStruct(cotangent.shape, LOW),
        ],
        in_specs=[ANY] * 4,
        out_specs=[ANY] * 5,
        scratch_shapes=[
            pltpu.VMEM((total, width), LOW),
            pltpu.VMEM((total, width), LOW),
            pltpu.VMEM((width, 2 * cols), LOW),
            pltpu.VMEM((total, cols), LOW),
            pltpu.VMEM((2, total, 256), FULL),
            pltpu.VMEM((2, total, 256), FULL),
            pltpu.VMEM((2, 512, cols), LOW),
            pltpu.SemaphoreType.DMA((8,)),
            pltpu.SemaphoreType.DMA((2 * len(column_cuts(cols)),)),
            pltpu.SemaphoreType.DMA((4,)),
        ]
        + sems(2),
        compiler_params=comm_params(number),
        cost_estimate=cost(30),
        name="mlp_one",
    )(normed2, cotangent, near, w_gu)


def mlp_two_kernel(
    x_hbm, own_hbm, near_hbm, far_hbm, wdown_hbm, gate_hbm, up_hbm, ggu_out, part_out,
    x_ref, cot_ref, w_down, gate_stage, up_stage, ggu, grad_stage, local, loads,
):
    total = x_ref.shape[0]
    cols = w_down.shape[1]
    cuts = column_cuts(cols)
    block = total // 2

    def chunk_loads(n):
        begin, end = cuts[n]
        here = pl.ds(begin, end - begin)
        stage = pl.ds(0, end - begin)
        return [
            pltpu.make_async_copy(source, target, loads.at[3 * (n % 2) + i])
            for i, (source, target) in enumerate(
                (
                    (wdown_hbm.at[:, here], w_down.at[:, here]),
                    (gate_hbm.at[:, here], gate_stage.at[n % 2, :, stage]),
                    (up_hbm.at[:, here], up_stage.at[n % 2, :, stage]),
                )
            )
        ]

    seq = total // N_DP
    data = [pltpu.make_async_copy(x_hbm, x_ref, local.at[1])]
    data += [
        pltpu.make_async_copy(source, cot_ref.at[pl.ds(k * seq, seq)], local.at[5 + k])
        for k, source in enumerate((own_hbm, near_hbm.at[0], near_hbm.at[1], far_hbm))
    ]
    for copy in data[1:] + chunk_loads(0) + chunk_loads(1) + data[:1]:
        copy.start()
    for copy in data[1:]:
        copy.wait()
    for n, (begin, end) in enumerate(cuts):
        for copy in chunk_loads(n):
            copy.wait()

        def rows(index, carry, begin=begin, end=end, slot=n % 2):
            here = pl.ds(pl.multiple_of(index * block, block), block)
            grad = jnp.dot(cot_ref[here], w_down[:, begin:end], preferred_element_type=FULL)
            gate = gate_stage[slot, here, : end - begin]
            up = up_stage[slot, here, : end - begin]
            sig = 1.0 / (1.0 + jnp.exp(-gate))
            ggu[here, begin:end] = (grad * up * sig * (1.0 + gate * (1.0 - sig))).astype(LOW)
            ggu[here, cols + begin : cols + end] = (grad * gate * sig).astype(LOW)
            return carry

        lax.fori_loop(0, total // block, rows, 0)
        if n + 2 < len(cuts):
            for copy in chunk_loads(n + 2):
                copy.start()
    out = pltpu.make_async_copy(ggu, ggu_out, local.at[2])
    out.start()
    data[0].wait()
    weight_grad(x_ref, ggu, grad_stage, part_out, local, 3)
    out.wait()


def mlp_two(normed2, cotangent, near, far, w_down, gate, up):
    total, width = normed2.shape
    cols = w_down.shape[1]
    return pl.pallas_call(
        mlp_two_kernel,
        out_shape=[
            jax.ShapeDtypeStruct((total, 2 * cols), LOW),
            jax.ShapeDtypeStruct((width, 2 * cols), LOW),
        ],
        in_specs=[ANY] * 7,
        out_specs=[ANY] * 2,
        scratch_shapes=[
            pltpu.VMEM((total, width), LOW),
            pltpu.VMEM((total, width), LOW),
            pltpu.VMEM((width, cols), LOW),
            pltpu.VMEM((2, total, 256), FULL),
            pltpu.VMEM((2, total, 256), FULL),
            pltpu.VMEM((total, 2 * cols), LOW),
            pltpu.VMEM((2, 256, 2 * cols), LOW),
            pltpu.SemaphoreType.DMA((9,)),
            pltpu.SemaphoreType.DMA((6,)),
        ],
        compiler_params=pltpu.CompilerParams(vmem_limit_bytes=BIG_VMEM),
        cost_estimate=cost(30),
        name="mlp_two",
    )(normed2, cotangent, near, far, w_down, gate, up)


FIRST_HAT = 1.0 / (1.0 - BETA_ONE**STEP)
SECOND_HAT = 1.0 / (1.0 - BETA_TWO**STEP)


def clip_factor(total_ref, width):
    total = jnp.full((1, width), total_ref[0, 0], FULL)
    return CLIP_NORM / jnp.maximum(jnp.sqrt(total), CLIP_NORM)


def adam_step(grads, factor, master, first, second):
    clipped = grads.astype(FULL) * factor
    first_new = BETA_ONE * first + (1.0 - BETA_ONE) * clipped
    second_new = BETA_TWO * second + (1.0 - BETA_TWO) * clipped * clipped
    ratio = first_new * (RATE_MATRIX * FIRST_HAT) / (jnp.sqrt(second_new * SECOND_HAT) + ADAM_EPS)
    return (master * (1.0 - RATE_MATRIX * DECAY_MATRIX) - ratio, first_new, second_new)


def adam_kernel(total_ref, qkv_ref, out_ref, gu_ref, down_ref, *refs):
    factor = clip_factor(total_ref, 128)[:, 0:1]

    def update(begin, grads, states, results):
        here = slice(begin, begin + grads.shape[1])
        values = adam_step(grads, factor, *[ref[:, here] for ref in states])
        for ref, value in zip(results, values):
            ref[:, here] = value

    attn, mlp = (refs[0:3], refs[6:9]), (refs[3:6], refs[9:12])
    width, ff_width = qkv_ref.shape[-1] // 3, down_ref.shape[-1]
    for d in range(N_DP):
        for part in range(3):
            here = slice(part * width, part * width + width)
            update(part * D + d * width, qkv_ref[d, :, here], *attn)
        for part in range(2):
            here = slice(part * ff_width, part * ff_width + ff_width)
            update(part * FF + d * ff_width, gu_ref[d, :, here], *mlp)
        update(2 * FF + d * ff_width, down_ref[d], *mlp)
    update(3 * D, out_ref[...], *attn)


def adam(total, qkv_grad, out_grad, gu_grad, down_grad, states):
    rows = out_grad.shape[0]
    size = 16

    def block(array):
        if array.ndim == 3:
            return pl.BlockSpec((N_DP, size, array.shape[-1]), lambda j: (0, j, 0))
        return pl.BlockSpec((size, array.shape[-1]), lambda j: (j, 0))

    grads = [qkv_grad, out_grad, gu_grad, down_grad]
    count = sum(array.size for array in states)
    return pl.pallas_call(
        adam_kernel,
        grid=(rows // size,),
        out_shape=[jax.ShapeDtypeStruct(array.shape, FULL) for array in states],
        in_specs=[pl.BlockSpec(memory_space=pltpu.SMEM)]
        + [block(array) for array in grads + states],
        out_specs=[block(array) for array in states],
        compiler_params=pltpu.CompilerParams(vmem_limit_bytes=BIG_VMEM),
        cost_estimate=pl.CostEstimate(
            flops=6 * count, bytes_accessed=9 * count, transcendentals=count // 3
        ),
        name="adam",
    )(total, *grads, *states)


def per_device_fast(
    tokens,
    cotangent,
    segments,
    positions,
    attn_master,
    mlp_master,
    norm_master,
    attn_first,
    mlp_first,
    norm_first,
    attn_second,
    mlp_second,
    norm_second,
):
    seq = tokens.shape[0]
    rows = attn_master.shape[0]
    width = D // N_DP
    ff_width = FF // N_DP
    group = N_DP * seq
    my_dp = lax.axis_index("dp")
    my_shard = lax.axis_index("shard")

    places = jnp.stack([segments, positions], 0)
    w_qkv, w_out, norm_all, tok_all, place_all, gu_blocks, down_blocks, tokens, cotangent = start(
        attn_master, mlp_master, norm_master, tokens, cotangent, places, 0
    )
    w_qkv = w_qkv.reshape(D, 3 * width)
    w_out = w_out.reshape(width, D)

    def gather_rows(blocks):
        return lax.all_gather(blocks.reshape(-1, blocks.shape[-1]), "shard", axis=0, tiled=True)

    norm_all = norm_all[:, :, :7, :rows]
    norm_vals = norm_all.transpose(2, 0, 1, 3).reshape(7, D)
    norm_vals = jnp.concatenate([norm_vals, jnp.zeros((1, D), FULL)], 0)
    bias_all = norm_all.transpose(2, 1, 0, 3)[2:5].reshape(3, N_DP, width)
    bias = lax.dynamic_index_in_dim(bias_all, my_dp, 1).reshape(1, 3 * width)
    w_gu = gather_rows(gu_blocks)
    w_down = gather_rows(down_blocks)

    rates = ROPE_BASE ** (-((np.arange(128) % (ROT // 2)) * 2.0 / ROT))
    rates = np.broadcast_to(rates.astype(np.float32), (8, 128))
    cot_near, normed1, queries, keys, values, mixture, *tables, mask = attn_forward(
        cotangent, tok_all, place_all, rates, norm_vals, w_qkv, bias, 2
    )
    resid, normed2 = mid_forward(mixture, w_out, tokens, norm_vals, 3)
    normed2 = normed2.reshape(group, D)

    hidden, gate, up, part_down, cot_far = mlp_one(normed2, cotangent, cot_near, w_gu, 1)
    down_sum = lax.psum_scatter(part_down, "shard", scatter_dimension=0, tiled=True)
    grad_gu, part_gu = mlp_two(normed2, cotangent, cot_near, cot_far, w_down, gate, up)
    gu_sum = lax.psum_scatter(part_gu, "shard", scatter_dimension=0, tiled=True)
    grad_resid, grad_attn_out, sums2, out_part = mid_backward(
        grad_gu.reshape(N_DP, seq, 2 * ff_width),
        w_gu,
        w_down,
        hidden.reshape(N_DP, seq, ff_width),
        resid,
        cotangent,
        norm_vals,
        4,
    )
    grad_attn_out, down_sum = lax.optimization_barrier((grad_attn_out, down_sum))
    block_out, grad_qkv, bias_sums, part_attn = attn_backward(
        out_part,
        normed1,
        mixture,
        resid,
        grad_attn_out,
        w_out,
        queries,
        keys,
        values,
        mask,
        tables,
        9,
    )
    bias_term = lax.dynamic_update_slice(
        jnp.zeros((3, D), FULL), bias_sums[0].reshape(3, width), (0, my_dp * width)
    )
    rest = jnp.concatenate(
        [jnp.zeros((2, D), FULL), bias_term, sums2[:2], jnp.zeros((1, D), FULL)], 0
    )
    gu_blocks = gu_sum.reshape(N_DP, rows, 2 * ff_width)
    down_blocks = down_sum.reshape(N_DP, rows, ff_width)
    input_grad, norm_sums, gu_grad, down_grad, qkv_grad, out_grad, box = last(
        part_attn,
        grad_qkv,
        w_qkv,
        gu_blocks,
        down_blocks,
        tokens,
        grad_resid,
        norm_vals,
        rest,
        5,
    )
    own_features = lax.dynamic_slice(norm_sums, (0, (my_shard * N_DP + my_dp) * rows), (8, rows))
    own_biases = lax.dynamic_slice(norm_sums, (0, (my_dp * N_SH + my_shard) * rows), (8, rows))
    norm_grad = jnp.concatenate([own_features[:2], own_biases[2:5], own_features[5:7]], 0)
    grad_size = jnp.sqrt(box[0, 0])
    factor = CLIP_NORM / jnp.maximum(grad_size, CLIP_NORM)
    states = [attn_master, attn_first, attn_second, mlp_master, mlp_first, mlp_second]
    results = adam(box, qkv_grad, out_grad, gu_grad, down_grad, states)
    attn_new, attn_first_new, attn_second_new, mlp_new, mlp_first_new, mlp_second_new = results
    norm_new, norm_first_new, norm_second_new = adam_update(
        norm_master, norm_first, norm_second, norm_grad, factor, RATE_VECTOR, 0.0
    )
    return (
        block_out,
        input_grad,
        grad_size,
        attn_new,
        mlp_new,
        norm_new,
        attn_first_new,
        mlp_first_new,
        norm_first_new,
        attn_second_new,
        mlp_second_new,
        norm_second_new,
    )


def solution(mesh):
    in_specs = (
        P(("dp", "shard"), None),
        P(("dp", "shard"), None),
        P(("dp", "shard")),
        P(("dp", "shard")),
        P(("dp", "shard"), None),
        P(("dp", "shard"), None),
        P(None, ("dp", "shard")),
        P(("dp", "shard"), None),
        P(("dp", "shard"), None),
        P(None, ("dp", "shard")),
        P(("dp", "shard"), None),
        P(("dp", "shard"), None),
        P(None, ("dp", "shard")),
    )
    out_specs = (
        P(("dp", "shard"), None),
        P(("dp", "shard"), None),
        P(),
        P(("dp", "shard"), None),
        P(("dp", "shard"), None),
        P(None, ("dp", "shard")),
        P(("dp", "shard"), None),
        P(("dp", "shard"), None),
        P(None, ("dp", "shard")),
        P(("dp", "shard"), None),
        P(("dp", "shard"), None),
        P(None, ("dp", "shard")),
    )
    fast = dict(mesh.shape) == dict(dp=4, shard=8)
    body = per_device_fast if fast else per_device_any
    return jax.shard_map(
        body, mesh=mesh, in_specs=in_specs, out_specs=out_specs, check_vma=False
    )
```

```python
import functools

import numpy as np
import jax
import jax.numpy as jnp
from jax import lax
from jax.experimental import pallas as pl
from jax.experimental.pallas import tpu as pltpu
from jax.sharding import PartitionSpec as P

D = 2048
HEADS = 32
HEAD = 64
FF = 5632
ROT = 16
STEP = 10


NORM_EPS = 1e-05
NEG_FILL = -1e30
ROPE_BASE = 10000.0
CLIP_NORM = 1.0
BETA_ONE = 0.9
BETA_TWO = 0.95
ADAM_EPS = 1e-08
RATE_MATRIX = 0.02
RATE_VECTOR = 0.2
DECAY_MATRIX = 0.1
LEAD_DIMS = (((0,), (0,)), ((), ()))
LAST_DIMS = (((1,), (1,)), ((), ()))


def layer_norm(values_in, gain_vec, shift_vec):
    average = jnp.mean(values_in, axis=-1, keepdims=True)
    centered = values_in - average
    variance = jnp.mean(centered * centered, axis=-1, keepdims=True)
    return centered * lax.rsqrt(variance + NORM_EPS) * gain_vec + shift_vec


def rotary_tables(position_ids):
    half_rot = ROT // 2
    inverse_freq = ROPE_BASE ** (-(jnp.arange(half_rot, dtype=jnp.float32) * 2.0 / ROT))
    angles = position_ids.astype(jnp.float32)[:, None] * inverse_freq[None, :]
    return (jnp.cos(angles)[:, None, :], jnp.sin(angles)[:, None, :])


def rotate(heads_in, cos_table, sin_table):
    half_rot = ROT // 2
    first_half = heads_in[..., :half_rot]
    second_half = heads_in[..., half_rot:ROT]
    rest_part = heads_in[..., ROT:]
    turned_one = first_half * cos_table - second_half * sin_table
    turned_two = second_half * cos_table + first_half * sin_table
    return jnp.concatenate([turned_one, turned_two, rest_part], -1)


def pad_last(array, size):
    missing = size - array.shape[-1]
    if missing == 0:
        return array
    return jnp.pad(array, [(0, 0)] * (array.ndim - 1) + [(0, missing)])


def activate(gate_part, up_part):
    return jax.nn.silu(gate_part) * up_part


def adam_update(master, first, second, grads, factor, rate, decay):
    clipped = grads * factor
    first_new = BETA_ONE * first + (1.0 - BETA_ONE) * clipped
    second_new = BETA_TWO * second + (1.0 - BETA_TWO) * clipped * clipped
    first_hat = first_new / (1.0 - BETA_ONE**STEP)
    second_hat = second_new / (1.0 - BETA_TWO**STEP)
    master_new = master - rate * (first_hat / (jnp.sqrt(second_hat) + ADAM_EPS) + decay * master)
    return (master_new, first_new, second_new)


def exchange_dp(blocks):
    return lax.all_to_all(blocks, "dp", 0, 0, tiled=True)


def gather_dp(rows):
    return lax.all_gather(rows, "dp", axis=0, tiled=True)


def scatter_sum_dp(parts):
    return lax.psum_scatter(parts, "dp", scatter_dimension=0, tiled=True)


def gather_shard(block):
    return lax.all_gather(block, "shard", axis=1)


def scatter_sum_shard(parts):
    return lax.psum_scatter(parts, "shard", scatter_dimension=1)


def layer_stats(values_in):
    average = jnp.mean(values_in, axis=-1, keepdims=True)
    centered = values_in - average
    variance = jnp.mean(centered * centered, axis=-1, keepdims=True)
    inverse = lax.rsqrt(variance + NORM_EPS)
    return centered * inverse, inverse


def layer_back(grads, gain_vec, unit, inverse):
    scaled = grads * gain_vec
    mean_one = jnp.mean(scaled, axis=-1, keepdims=True)
    mean_two = jnp.mean(scaled * unit, axis=-1, keepdims=True)
    return inverse * (scaled - mean_one - unit * mean_two)


def per_device_any(
    tokens,
    cotangent,
    segments,
    positions,
    attn_master,
    mlp_master,
    norm_master,
    attn_first,
    mlp_first,
    norm_first,
    attn_second,
    mlp_second,
    norm_second,
):
    low = jnp.bfloat16
    full = jnp.float32
    n_dp = lax.axis_size("dp")
    n_sh = lax.axis_size("shard")
    seq = tokens.shape[0]
    rows = attn_master.shape[0]
    heads = HEADS // n_dp
    width = D // n_dp
    ff_width = -(-FF // (128 * n_dp)) * 128
    ff_pad = ff_width * n_dp
    scale = HEAD ** (-0.5)

    qkv_send = attn_master[:, : 3 * D].astype(low).reshape(rows, 3, n_dp, width)
    qkv_send = qkv_send.transpose(2, 0, 1, 3).reshape(n_dp, rows, 3 * width)
    mlp_send = pad_last(mlp_master.astype(low).reshape(rows, 3, FF), ff_pad)
    mlp_send = mlp_send.reshape(rows, 3, n_dp, ff_width)
    mlp_send = mlp_send.transpose(2, 0, 1, 3).reshape(n_dp, rows, 3 * ff_width)
    norm_full = lax.all_gather(norm_master.astype(low), ("dp", "shard"), axis=1, tiled=True)
    norm_vals = norm_full.astype(full)
    w_qkv = gather_shard(exchange_dp(qkv_send)).reshape(D, 3 * width)
    w_out = gather_shard(attn_master[None, :, 3 * D :].astype(low)).reshape(width, D)
    tokens_all = gather_dp(tokens)
    places_all = gather_dp(jnp.stack([segments, positions], 0)[None])
    cot_all = gather_dp(cotangent)
    w_mlp = gather_shard(exchange_dp(mlp_send)).reshape(D, 3 * ff_width)
    w_gu = w_mlp[:, : 2 * ff_width]
    w_down = w_mlp[:, 2 * ff_width :]
    seg_all, pos_all = places_all[:, 0], places_all[:, 1]

    inputs_all = tokens_all.astype(full)
    unit1, _ = layer_stats(inputs_all)
    normed1 = (unit1 * norm_vals[0] + norm_vals[1]).astype(low)
    my_dp = lax.axis_index("dp")
    bias = lax.dynamic_slice(norm_vals[2:5], (0, my_dp * width), (3, width)).reshape(3 * width)
    qkv = jnp.dot(normed1, w_qkv, preferred_element_type=full) + bias
    qkv = qkv.reshape(n_dp * seq, 3 * heads, HEAD)
    cos_table, sin_table = rotary_tables(pos_all.reshape(-1))

    def split(array):
        return array.reshape(n_dp, seq, heads, HEAD)

    queries = split(rotate(qkv[:, :heads], cos_table, sin_table).astype(low))
    key_rows = split(rotate(qkv[:, heads : 2 * heads], cos_table, sin_table).astype(low))
    values = split(qkv[:, 2 * heads :].astype(low))
    places = jnp.arange(seq)
    allowed = (seg_all[:, :, None] == seg_all[:, None, :]) & (
        places[:, None] >= places[None, :]
    )[None]
    scores = (
        jnp.einsum("gshd,gthd->ghst", queries, key_rows, preferred_element_type=full) * scale
    )
    scores = jnp.where(allowed[:, None], scores, NEG_FILL)
    attend = jax.nn.softmax(scores, axis=-1)
    attend_low = attend.astype(low)
    mixture = (
        jnp.einsum("ghst,gthd->gshd", attend_low, values, preferred_element_type=full)
        .reshape(n_dp * seq, width)
        .astype(low)
    )
    attn_part = jnp.dot(mixture, w_out, preferred_element_type=full).astype(low)
    resid = tokens.astype(full) + scatter_sum_dp(attn_part).astype(full)
    unit2, inverse2 = layer_stats(resid)
    normed2 = gather_dp((unit2 * norm_vals[5] + norm_vals[6]).astype(low))
    gate_up = jnp.dot(normed2, w_gu, preferred_element_type=full)
    hidden_f, act_pull = jax.vjp(activate, gate_up[:, :ff_width], gate_up[:, ff_width:])
    hidden = hidden_f.astype(low)
    grad_hidden = jnp.dot(cot_all, w_down, preferred_element_type=full)
    grad_gate, grad_up = act_pull(grad_hidden)
    grad_gu = jnp.concatenate([grad_gate, grad_up], 1).astype(low)
    norm2_part = lax.dot_general(grad_gu, w_gu, LAST_DIMS, preferred_element_type=full)
    grad_norm2 = scatter_sum_dp(norm2_part.astype(low)).astype(full)
    out_part = lax.dot_general(hidden, w_down, LAST_DIMS, preferred_element_type=full)
    block_out = (resid + scatter_sum_dp(out_part.astype(low)).astype(full)).astype(low)
    part_gu = lax.dot_general(normed2, grad_gu, LEAD_DIMS, preferred_element_type=full)
    part_down = lax.dot_general(cot_all, hidden, LEAD_DIMS, preferred_element_type=full)
    part_mlp = jnp.concatenate([part_gu.astype(low), part_down.astype(low)], 1)
    mlp_sum = scatter_sum_shard(part_mlp.reshape(n_dp, n_sh, rows, 3 * ff_width))

    grad_gain2 = jnp.sum(grad_norm2 * unit2, axis=0)
    grad_shift2 = jnp.sum(grad_norm2, axis=0)
    grad_resid = cotangent.astype(full) + layer_back(grad_norm2, norm_vals[5], unit2, inverse2)
    grad_attn_out = gather_dp(grad_resid.astype(low))
    grad_mixture = lax.dot_general(grad_attn_out, w_out, LAST_DIMS, preferred_element_type=full)
    grad_mixture = split(grad_mixture.astype(low))
    grad_attend = jnp.einsum("gshd,gthd->ghst", grad_mixture, values, preferred_element_type=full)
    grad_values = jnp.einsum(
        "ghst,gshd->gthd", attend_low, grad_mixture, preferred_element_type=full
    )
    grad_scores = (
        attend * (grad_attend - jnp.sum(attend * grad_attend, axis=-1, keepdims=True))
    ).astype(low)
    grad_queries = (
        jnp.einsum("ghst,gthd->gshd", grad_scores, key_rows, preferred_element_type=full) * scale
    )
    grad_keys = (
        jnp.einsum("ghst,gshd->gthd", grad_scores, queries, preferred_element_type=full) * scale
    )

    def turn_back(grads):
        grads = grads.reshape(n_dp * seq, heads, HEAD)
        return rotate(grads, cos_table, -sin_table).reshape(n_dp * seq, width)

    grad_qkv = jnp.concatenate(
        [
            turn_back(grad_queries),
            turn_back(grad_keys),
            grad_values.reshape(n_dp * seq, width),
        ],
        1,
    ).astype(low)
    part_qkv = lax.dot_general(normed1, grad_qkv, LEAD_DIMS, preferred_element_type=full)
    part_out = lax.dot_general(mixture, grad_attn_out, LEAD_DIMS, preferred_element_type=full)
    qkv_sum = scatter_sum_shard(part_qkv.astype(low).reshape(n_dp, n_sh, rows, 3 * width))
    out_sum = scatter_sum_shard(part_out.astype(low).reshape(1, n_sh, rows, D))[0].astype(full)

    norm1_part = lax.dot_general(grad_qkv, w_qkv, LAST_DIMS, preferred_element_type=full)
    grad_gain1 = jnp.sum(norm1_part * unit1, axis=0)
    grad_shift1 = jnp.sum(norm1_part, axis=0)
    grad_bias = jnp.sum(grad_qkv, axis=0, dtype=full).reshape(3, width)
    grad_norm1 = scatter_sum_dp(norm1_part.astype(low)).astype(full)
    own_unit1, own_inverse1 = layer_stats(tokens.astype(full))
    input_grad = grad_resid + layer_back(grad_norm1, norm_vals[0], own_unit1, own_inverse1)
    norm_term = lax.dynamic_update_slice(
        jnp.zeros((3, D), full), grad_bias, (0, my_dp * width)
    )
    norm_term = jnp.concatenate(
        [grad_gain1[None], grad_shift1[None], norm_term, grad_gain2[None], grad_shift2[None]], 0
    )
    norm_grad = lax.psum_scatter(norm_term, ("dp", "shard"), scatter_dimension=1, tiled=True)

    def columns_back(summed, parts, part_width, keep):
        back = exchange_dp(summed).reshape(n_dp, rows, parts, part_width)
        back = back.transpose(1, 2, 0, 3).reshape(rows, parts, n_dp * part_width)
        return back[:, :, :keep].reshape(rows, parts * keep).astype(full)

    mlp_grad = columns_back(mlp_sum, 3, ff_width, FF)
    attn_grad = jnp.concatenate([columns_back(qkv_sum, 3, width, D), out_sum], 1)
    squares = (
        jnp.sum(attn_grad * attn_grad)
        + jnp.sum(mlp_grad * mlp_grad)
        + jnp.sum(norm_grad * norm_grad)
    )
    overall = lax.psum(squares, ("dp", "shard"))
    grad_size = jnp.sqrt(overall)
    factor = CLIP_NORM / jnp.maximum(grad_size, CLIP_NORM)
    attn_new, attn_first_new, attn_second_new = adam_update(
        attn_master, attn_first, attn_second, attn_grad, factor, RATE_MATRIX, DECAY_MATRIX
    )
    mlp_new, mlp_first_new, mlp_second_new = adam_update(
        mlp_master, mlp_first, mlp_second, mlp_grad, factor, RATE_MATRIX, DECAY_MATRIX
    )
    norm_new, norm_first_new, norm_second_new = adam_update(
        norm_master, norm_first, norm_second, norm_grad, factor, RATE_VECTOR, 0.0
    )
    return (
        block_out,
        input_grad,
        grad_size,
        attn_new,
        mlp_new,
        norm_new,
        attn_first_new,
        mlp_first_new,
        norm_first_new,
        attn_second_new,
        mlp_second_new,
        norm_second_new,
    )


MESH = pl.DeviceIdType.MESH
ANY = pl.BlockSpec(memory_space=pl.ANY)
VMEM = pl.BlockSpec(memory_space=pltpu.VMEM)
LOW = jnp.bfloat16
FULL = jnp.float32
N_DP = 4
N_SH = 8
BIG_VMEM = 60 * 1024 * 1024


def dp_peer(step):
    mine = lax.axis_index("dp")
    if step == 1:
        return mine + 1 - 2 * (mine % 2)
    if step == 2:
        return (mine + 2) % 4
    return 3 - mine


def to_dp(step):
    return (dp_peer(step), lax.axis_index("shard"))


def to_shard(step):
    return (lax.axis_index("dp"), (lax.axis_index("shard") + step) % N_SH)


def cost(micros):
    return pl.CostEstimate(flops=0, bytes_accessed=int(micros * 3.0e6), transcendentals=0)


def greet(peers):
    barrier = pltpu.get_barrier_semaphore()
    for peer in peers:
        pl.semaphore_signal(barrier, inc=1, device_id=peer, device_id_type=MESH)
    pl.semaphore_wait(barrier, len(peers))


def remote(source, target, sems, index, peer):
    return pltpu.make_async_remote_copy(
        src_ref=source,
        dst_ref=target,
        send_sem=sems[0].at[index],
        recv_sem=sems[1].at[index],
        device_id=peer,
        device_id_type=MESH,
    )


def sems(count):
    return [pltpu.SemaphoreType.DMA((count,)), pltpu.SemaphoreType.DMA((count,))]


def comm_params(number):
    return pltpu.CompilerParams(
        collective_id=number, has_side_effects=True, vmem_limit_bytes=BIG_VMEM
    )


def to_places(value):
    size = value.shape[1] // (N_DP * N_SH)
    starts = [(n * N_DP + d) * size for d in range(N_DP) for n in range(N_SH)]
    return jnp.concatenate([value[:, start : start + size] for start in starts], axis=1)


def to_shards(value):
    size = value.shape[1] // (N_DP * N_SH)
    starts = [(d * N_SH + n) * size for n in range(N_SH) for d in range(N_DP)]
    return jnp.concatenate([value[:, start : start + size] for start in starts], axis=1)


CHUNK = 32


def in_chunks(rows, body):
    def step(index, carry):
        body(pl.ds(pl.multiple_of(index * CHUNK, CHUNK), CHUNK))
        return carry

    lax.fori_loop(0, rows // CHUNK, step, 0)


def spread_plan(own, result, sem_pair, base):
    half = own.shape[0] // 2
    top, bottom = pl.ds(0, half), pl.ds(half, half)
    sent = [
        remote(own.at[top], result.at[1, top], sem_pair, base + 0, to_dp(1)),
        remote(own.at[bottom], result.at[2, bottom], sem_pair, base + 1, to_dp(2)),
        remote(own.at[bottom], result.at[1, bottom], sem_pair, base + 2, to_dp(1)),
        remote(own.at[top], result.at[2, top], sem_pair, base + 3, to_dp(2)),
    ]
    passed = [
        remote(result.at[1, top], result.at[3, top], sem_pair, base + 4, to_dp(2)),
        remote(result.at[2, bottom], result.at[3, bottom], sem_pair, base + 5, to_dp(1)),
    ]
    return sent, passed


def spread(own, result, sem_pair, base):
    sent, passed = spread_plan(own, result, sem_pair, base)
    for copy in sent:
        copy.start()
    return sent, passed


def pass_on(sent, passed):
    sent[0].wait_recv()
    passed[0].start()
    sent[1].wait_recv()
    passed[1].start()


def spread_end(sent, passed):
    sent[2].wait_recv()
    sent[3].wait_recv()
    passed[0].wait_recv()
    passed[1].wait_recv()
    for copy in sent + passed:
        copy.wait_send()


SLABS = 6


def start_kernel(
    attn_hbm, mlp_hbm, norm_ref, tok_hbm, cot_hbm, place_ref,
    w_qkv, w_out, norm_all, tok_all, place_all, gu_out, down_out, tok_own, cot_own,
    attn_in, mlp_in, tok_in, cot_in, qkv_send, out_send, norm_send, gu_send, down_send,
    tok_low, cot_low,
    up_send, up_recv, down_s, down_recv, core_send, core_recv, send, recv, local,
):
    mine, place = lax.axis_index("dp"), lax.axis_index("shard")
    line, core = place // 2, place % 2
    width, ff_width = qkv_send.shape[-1] // 3, down_send.shape[-1]
    above, below = (mine, place + 2), (mine, place - 2)
    partner = (mine, place + 1 - 2 * core)
    has_above, has_below = line < N_SH // 2 - 1, line > 0
    pair = (send, recv)
    loads = [
        pltpu.make_async_copy(attn_hbm, attn_in, local.at[0]),
        pltpu.make_async_copy(tok_hbm, tok_in, local.at[1]),
        pltpu.make_async_copy(mlp_hbm, mlp_in, local.at[2]),
        pltpu.make_async_copy(cot_hbm, cot_in, local.at[3]),
    ]
    for copy in loads:
        copy.start()

    barrier = pltpu.get_barrier_semaphore()
    for peer in [to_dp(k) for k in (1, 2, 3)] + [partner]:
        pl.semaphore_signal(barrier, inc=1, device_id=peer, device_id_type=MESH)

    @pl.when(has_above)
    def _():
        pl.semaphore_signal(barrier, inc=1, device_id=above, device_id_type=MESH)

    @pl.when(has_below)
    def _():
        pl.semaphore_signal(barrier, inc=1, device_id=below, device_id_type=MESH)

    norm_send[...] = jnp.zeros_like(norm_send)
    norm_send[0:7, 0 : norm_ref.shape[1]] = norm_ref[...].astype(LOW).astype(FULL)
    loads[0].wait()
    for part in range(3):
        for d in range(N_DP):
            begin = part * D + d * width
            qkv_send[d, :, part * width : part * width + width] = attn_in[
                :, begin : begin + width
            ].astype(LOW)
    out_send[...] = to_shards(attn_in[:, 3 * D :]).astype(LOW)

    @pl.when(has_above & has_below)
    def _():
        pl.semaphore_wait(barrier, 6)

    @pl.when(jnp.logical_not(has_above & has_below))
    def _():
        pl.semaphore_wait(barrier, 5)

    def slab(n, shard):
        if n == 0:
            return w_qkv.at[shard, mine]
        if n == 1:
            return w_out.at[shard]
        if n == 2:
            return norm_all.at[shard]
        return w_qkv.at[shard, dp_peer(n - 2)]

    def source(n):
        return {0: qkv_send.at[mine], 1: out_send}.get(n, slab(n, place))

    def along(n, shard, hop, sem_pair, peer, held=None):
        start = slab(n, shard) if held is None else held
        return remote(start, slab(n, shard), sem_pair, hop * SLABS + n, peer)

    ups, downs, cores = (up_send, up_recv), (down_s, down_recv), (core_send, core_recv)

    def pass_block(n, origin, hop, held, upward, downward):
        shard = 2 * origin + core
        if upward:

            @pl.when(has_above)
            def _():
                along(n, shard, hop, ups, above, held).start()

        if downward:

            @pl.when(has_below)
            def _():
                along(n, shard, hop, downs, below, held).start()

        along(n, shard, origin, cores, partner, held).start()

    norms = [
        remote(norm_send, norm_all.at[place, mine], pair, 21 + k - 1, to_dp(k)) for k in (1, 2, 3)
    ]
    trade = [
        remote(qkv_send.at[dp_peer(k)], w_qkv.at[place, mine], pair, k - 1, to_dp(k))
        for k in (1, 2, 3)
    ]
    own = [
        pltpu.make_async_copy(qkv_send.at[mine], w_qkv.at[place, mine], local.at[4]),
        pltpu.make_async_copy(out_send, w_out.at[place], local.at[5]),
        pltpu.make_async_copy(norm_send, norm_all.at[place, mine], local.at[6]),
        pltpu.make_async_copy(place_ref, place_all.at[0], local.at[7]),
    ]
    for copy in norms + trade:
        copy.start()
    pass_block(0, line, 0, source(0), True, True)
    pass_block(1, line, 0, source(1), True, True)
    for copy in own:
        copy.start()

    loads[1].wait()

    def permute_tokens(here):
        tok_low[here] = to_shards(tok_in[here].astype(FULL)).astype(LOW)

    in_chunks(tok_in.shape[0], permute_tokens)
    places = [
        remote(place_ref, place_all.at[k], pair, 9 + k - 1, to_dp(k)) for k in (1, 2, 3)
    ]
    for copy in places:
        copy.start()
    tok = spread(tok_low, tok_all, pair, 3)
    keep = [
        pltpu.make_async_copy(tok_low, tok_all.at[0], local.at[8]),
        pltpu.make_async_copy(tok_low, tok_own, local.at[9]),
    ]
    for copy in keep:
        copy.start()

    own[2].wait()
    for copy in norms:
        copy.wait_recv()
    pass_block(2, line, 0, None, True, True)
    for k in (1, 2, 3):
        trade[k - 1].wait_recv()
        pass_block(2 + k, line, 0, None, True, True)

    loads[2].wait()
    for d in range(N_DP):
        for part in range(2):
            begin = part * FF + d * ff_width
            gu_send[d, :, part * ff_width : part * ff_width + ff_width] = mlp_in[
                :, begin : begin + ff_width
            ].astype(LOW)
        begin = 2 * FF + d * ff_width
        down_send[d] = mlp_in[:, begin : begin + ff_width].astype(LOW)
    blocks = []
    for n, (held, target) in enumerate(((gu_send, gu_out), (down_send, down_out))):
        for k in (3, 1, 2):
            blocks.append(
                remote(held.at[dp_peer(k)], target.at[mine], pair, 12 + 3 * n + k - 1, to_dp(k))
            )
        blocks.append(pltpu.make_async_copy(held.at[mine], target.at[mine], local.at[10 + n]))

    loads[3].wait()

    def permute_cotangent(here):
        cot_low[here] = to_shards(cot_in[here].astype(FULL)).astype(LOW)

    in_chunks(cot_in.shape[0], permute_cotangent)
    keep.append(pltpu.make_async_copy(cot_low, cot_own, local.at[12]))
    keep[2].start()

    def hop_step(hop):
        for n in range(SLABS):

            @pl.when(line >= hop)
            def _():
                shard = place - 2 * hop
                along(n, shard, hop - 1, ups, above).wait_recv()
                pass_block(n, line - hop, hop, None, True, False)

            @pl.when(line + hop < N_SH // 2)
            def _():
                shard = place + 2 * hop
                along(n, shard, hop - 1, downs, below).wait_recv()
                pass_block(n, line + hop, hop, None, False, True)

    hop_step(1)
    pass_on(*tok)
    for copy in blocks:
        copy.start()
    hop_step(2)
    hop_step(3)

    spread_end(*tok)
    for copy in blocks + own[:2] + own[3:] + keep + places:
        copy.wait()
    for copy in norms + trade:
        copy.wait_send()
    for hop in range(N_SH // 2 - 1):
        for n in range(SLABS):

            @pl.when(has_above & (line >= hop))
            def _():
                along(n, place - 2 * hop, hop, ups, above).wait_send()

            @pl.when(has_below & (line + hop < N_SH // 2))
            def _():
                along(n, place + 2 * hop, hop, downs, below).wait_send()

    for origin in range(N_SH // 2):
        for n in range(SLABS):
            along(n, 2 * origin + core, origin, cores, partner).wait_send()
            along(n, 2 * origin + 1 - core, origin, cores, partner).wait_recv()


def start(attn_master, mlp_master, norm_master, tokens, cotangent, places, number):
    rows = attn_master.shape[0]
    width, ff_width = D // N_DP, FF // N_DP
    seq = tokens.shape[0]
    norm_shape = (8, 128)
    hops = (N_SH // 2 - 1) * SLABS
    return pl.pallas_call(
        start_kernel,
        out_shape=[
            jax.ShapeDtypeStruct((N_SH, N_DP, rows, 3 * width), LOW),
            jax.ShapeDtypeStruct((N_SH, rows, D), LOW),
            jax.ShapeDtypeStruct((N_SH, N_DP) + norm_shape, FULL),
            jax.ShapeDtypeStruct((N_DP, seq, D), LOW),
            jax.ShapeDtypeStruct((N_DP,) + places.shape, places.dtype),
            jax.ShapeDtypeStruct((N_DP, rows, 2 * ff_width), LOW),
            jax.ShapeDtypeStruct((N_DP, rows, ff_width), LOW),
            jax.ShapeDtypeStruct((seq, D), LOW),
            jax.ShapeDtypeStruct((seq, D), LOW),
        ],
        in_specs=[ANY, ANY, VMEM, ANY, ANY, ANY],
        out_specs=[ANY] * 9,
        scratch_shapes=[
            pltpu.VMEM(attn_master.shape, FULL),
            pltpu.VMEM(mlp_master.shape, FULL),
            pltpu.VMEM(tokens.shape, LOW),
            pltpu.VMEM(tokens.shape, LOW),
            pltpu.VMEM((N_DP, rows, 3 * width), LOW),
            pltpu.VMEM((rows, D), LOW),
            pltpu.VMEM(norm_shape, FULL),
            pltpu.VMEM((N_DP, rows, 2 * ff_width), LOW),
            pltpu.VMEM((N_DP, rows, ff_width), LOW),
            pltpu.VMEM(tokens.shape, LOW),
            pltpu.VMEM(tokens.shape, LOW),
        ]
        + sems(hops)
        + sems(hops)
        + sems((N_SH // 2) * SLABS)
        + sems(24)
        + [pltpu.SemaphoreType.DMA((13,))],
        compiler_params=comm_params(number),
        cost_estimate=cost(90),
        name="start",
    )(attn_master, mlp_master, norm_master, tokens, cotangent, places)


def unit_rows(values):
    average = jnp.mean(values, axis=-1, keepdims=True)
    centered = values - average
    variance = jnp.mean(centered * centered, axis=-1, keepdims=True)
    inverse = lax.rsqrt(variance + NORM_EPS)
    return centered * inverse, inverse


def turn(value, cos_ref, up_ref, down_ref, sign):
    left = pltpu.roll(value, 128 - ROT // 2, 1)
    right = pltpu.roll(value, ROT // 2, 1)
    return value * cos_ref[...] + sign * (left * up_ref[...] + right * down_ref[...])


def head_masks():
    lane = lax.broadcasted_iota(jnp.int32, (1, 128), 1)
    return [lane < HEAD, lane >= HEAD]


def softmax_rows(queries, keys, bias):
    scores = lax.dot_general(queries, keys, LAST_DIMS, preferred_element_type=FULL)
    scores = scores * (HEAD ** (-0.5)) + bias
    top = jnp.max(scores, axis=-1, keepdims=True)
    weights = jnp.exp(scores - top)
    return weights / jnp.sum(weights, axis=-1, keepdims=True)


def fill_tables(place_ref, rate_ref, cos_ref, up_ref, down_ref, mask_ref):
    seq = place_ref.shape[-1]
    half = ROT // 2
    row = place_ref[0].astype(FULL)
    columns = jnp.transpose(jnp.broadcast_to(row[0:1], (8, seq)))[:, 0:1]
    spots = jnp.transpose(jnp.broadcast_to(row[1:2], (8, seq)))[:, 0:1]
    angles = spots * rate_ref[0:1, :]
    lane = lax.broadcasted_iota(jnp.int32, (1, 128), 1) % HEAD
    sines = jnp.sin(angles)
    cos_ref[...] = jnp.where(lane < ROT, jnp.cos(angles), 1.0)
    up_ref[...] = jnp.where(lane < half, -sines, 0.0)
    down_ref[...] = jnp.where((lane >= half) & (lane < ROT), sines, 0.0)
    later = lax.broadcasted_iota(jnp.int32, (seq, seq), 0) >= lax.broadcasted_iota(
        jnp.int32, (seq, seq), 1
    )
    mask_ref[0] = jnp.where((columns == row[0:1]) & later, 0.0, NEG_FILL)


def attn_forward_kernel(
    cot_ref, tok_ref, place_ref, rate_ref, norm_all, w_ref,
    cot_all, norm_ref, normed_ref, q_ref, k_ref, v_ref, mix_ref, cos_ref, up_ref, down_ref, mask_ref,
    qkv_ref, b_ref, send, recv,
):
    width = q_ref.shape[-1]
    step, last = pl.program_id(0), pl.num_programs(0) - 1
    mine = lax.axis_index("dp")
    sent = [
        remote(cot_ref, cot_all.at[k - 1], (send, recv), k - 1, to_dp(k)) for k in (1, 2)
    ]

    @pl.when(step == 0)
    def _():
        greet([to_dp(1), to_dp(2)])
        for copy in sent:
            copy.start()
        size = w_ref.shape[0] // (N_DP * N_SH)
        norm_ref[...] = jnp.concatenate(
            [norm_all[n, d, :, :size] for n in range(N_SH) for d in range(N_DP)], axis=1
        )
        for part in range(3):
            b_ref[0:1, part * width : part * width + width] = jnp.concatenate(
                [norm_all[n, mine, 2 + part : 3 + part, :size] for n in range(N_SH)], axis=1
            )

    fill_tables(place_ref, rate_ref, cos_ref, up_ref, down_ref, mask_ref)
    unit, _ = unit_rows(tok_ref[0].astype(FULL))
    normed_ref[0] = (unit * norm_ref[0:1, :] + norm_ref[1:2, :]).astype(LOW)
    qkv_ref[...] = jnp.dot(normed_ref[0], w_ref[...], preferred_element_type=FULL) + b_ref[0:1, :]
    masks = head_masks()
    for pair in range(width // 128):
        here = slice(pair * 128, pair * 128 + 128)
        queries = turn(qkv_ref[:, here], cos_ref, up_ref, down_ref, 1.0).astype(LOW)
        there = slice(width + pair * 128, width + pair * 128 + 128)
        keys = turn(qkv_ref[:, there], cos_ref, up_ref, down_ref, 1.0).astype(LOW)
        there = slice(2 * width + pair * 128, 2 * width + pair * 128 + 128)
        values = qkv_ref[:, there].astype(LOW)
        q_ref[0, :, here] = queries
        k_ref[0, :, here] = keys
        v_ref[0, :, here] = values
        total = None
        for mask in masks:
            attend = softmax_rows(queries, jnp.where(mask, keys, 0), mask_ref[0])
            part = jnp.dot(
                attend.astype(LOW), jnp.where(mask, values, 0), preferred_element_type=FULL
            )
            total = part if total is None else total + part
        mix_ref[0, :, here] = total.astype(LOW)

    @pl.when(step == last)
    def _():
        for copy in sent:
            copy.wait()


def group_spec(array):
    return pl.BlockSpec((1,) + array.shape[1:], lambda g: (g, 0, 0))


def whole_spec(array):
    return pl.BlockSpec(array.shape, lambda g: (0,) * len(array.shape))


def attn_forward(cotangent, tokens, places, rates, norm_all, w_qkv, number):
    groups, seq, _ = tokens.shape
    width = w_qkv.shape[1] // 3
    row_spec = pl.BlockSpec((seq, 128), lambda g: (g, 0))
    part = jax.ShapeDtypeStruct((groups, seq, width), LOW)
    normed = jax.ShapeDtypeStruct(tokens.shape, LOW)
    norms = jax.ShapeDtypeStruct((8, D), FULL)
    near = jax.ShapeDtypeStruct((2,) + tokens.shape[1:], LOW)
    table = jax.ShapeDtypeStruct((groups * seq, 128), FULL)
    mask = jax.ShapeDtypeStruct((groups, seq, seq), FULL)
    return pl.pallas_call(
        attn_forward_kernel,
        grid=(groups,),
        out_shape=[near, norms, normed, part, part, part, part, table, table, table, mask],
        in_specs=[
            ANY,
            group_spec(tokens),
            group_spec(places),
            whole_spec(rates),
            whole_spec(norm_all),
            whole_spec(w_qkv),
        ],
        out_specs=[ANY, whole_spec(norms), group_spec(normed)]
        + [group_spec(part)] * 4
        + [row_spec] * 3
        + [group_spec(mask)],
        scratch_shapes=[pltpu.VMEM((seq, 3 * width), FULL), pltpu.VMEM((8, 3 * width), FULL)]
        + sems(2),
        compiler_params=comm_params(number),
        cost_estimate=pl.CostEstimate(
            flops=2 * groups * seq * (D * 3 * width + 2 * seq * width * 2),
            bytes_accessed=2 * (w_qkv.size + 3 * tokens.size),
            transcendentals=groups * seq * seq * (width // HEAD),
        ),
        name="attn_forward",
    )(cotangent, tokens, places, rates, norm_all, w_qkv)


def attn_backward_kernel(
    part_hbm, normed_hbm, mix_hbm, gao_hbm, resid_hbm, gao_ref, w_ref, q_ref, k_ref, v_ref,
    mask_ref, cos_ref, up_ref, down_ref,
    block_ref, grad_ref, sum_ref, attn_hbm,
    gm_ref, parts, normed, mix, gao, resid_ref, wo_grad, stage, grads_all, out, diag, full,
    send, recv, local,
):
    width = q_ref.shape[-1]
    rows = q_ref.shape[1]
    step, last = pl.program_id(0), pl.num_programs(0) - 1
    total = RowSum(parts, (out, diag, full), (send, recv), 0, source=part_hbm)
    loads = [
        pltpu.make_async_copy(part_hbm, parts, local.at[0]),
        pltpu.make_async_copy(mix_hbm, mix, local.at[1]),
        pltpu.make_async_copy(gao_hbm, gao, local.at[2]),
        pltpu.make_async_copy(normed_hbm, normed, local.at[3]),
        pltpu.make_async_copy(resid_hbm, resid_ref, local.at[4]),
    ]

    @pl.when(step == 0)
    def _():
        loads[0].start()
        greet([to_dp(1), to_dp(2)])
        for k in (3, 1, 2):
            total.send(k)
        for copy in loads[1:]:
            copy.start()
        sum_ref[...] = jnp.zeros_like(sum_ref)

    @pl.when(step == 2)
    def _():
        loads[0].wait()
        total.relay()

    scale = HEAD ** (-0.5)
    gm_ref[...] = lax.dot_general(
        gao_ref[0], w_ref[...], LAST_DIMS, preferred_element_type=FULL
    ).astype(LOW)
    masks = head_masks()
    for pair in range(width // 128):
        here = slice(pair * 128, pair * 128 + 128)
        queries, keys, values = q_ref[0, :, here], k_ref[0, :, here], v_ref[0, :, here]
        grads = gm_ref[:, here]
        grad_q = grad_k = grad_v = 0.0
        for mask in masks:
            keys_one = jnp.where(mask, keys, 0)
            attend = softmax_rows(queries, keys_one, mask_ref[0])
            grad_attend = lax.dot_general(
                grads, jnp.where(mask, values, 0), LAST_DIMS, preferred_element_type=FULL
            )
            grad_v += lax.dot_general(
                attend.astype(LOW),
                jnp.where(mask, grads, 0),
                LEAD_DIMS,
                preferred_element_type=FULL,
            )
            mean = jnp.sum(attend * grad_attend, axis=-1, keepdims=True)
            grad_scores = (attend * (grad_attend - mean)).astype(LOW)
            grad_q += jnp.dot(grad_scores, keys_one, preferred_element_type=FULL)
            grad_k += lax.dot_general(
                grad_scores, jnp.where(mask, queries, 0), LEAD_DIMS, preferred_element_type=FULL
            )
        grad_q = turn(grad_q * scale, cos_ref, up_ref, down_ref, -1.0)
        grad_k = turn(grad_k * scale, cos_ref, up_ref, down_ref, -1.0)
        for n, grad in enumerate((grad_q, grad_k, grad_v)):
            start = n * width + pair * 128
            grad_ref[0, :, start : start + 128] = grad.astype(LOW)
    grads_all[pl.ds(pl.multiple_of(step * rows, rows), rows)] = grad_ref[0]
    sum_ref[0:1, :] += jnp.sum(grad_ref[0].astype(FULL), axis=0, keepdims=True)

    @pl.when(step == last)
    def _():
        for copy in loads[1:]:
            copy.wait()

        for pair in range(width // 128):
            wo_grad[pair * 128 : pair * 128 + 128, :] = lax.dot_general(
                mix[:, pair * 128 : pair * 128 + 128],
                gao[...],
                LEAD_DIMS,
                preferred_element_type=FULL,
            ).astype(LOW)

        def store(index, slot):
            return pltpu.make_async_copy(stage.at[slot], attn_hbm.at[index], local.at[5 + slot])

        def one_shard(index, carry):
            slot = index % 2

            @pl.when(index >= 2)
            def _():
                store(index - 2, slot).wait()

            here = pl.ds(pl.multiple_of(index * 256, 256), 256)
            stage[slot, :, : 3 * width] = lax.dot_general(
                normed[:, here], grads_all[...], LEAD_DIMS, preferred_element_type=FULL
            ).astype(LOW)
            side = pl.ds(pl.multiple_of(index * 64, 64), 64)
            for part in range(N_DP):
                stage[slot, part * 64 : part * 64 + 64, 3 * width :] = wo_grad[
                    side, part * width : part * width + width
                ]
            store(index, slot).start()
            return carry

        lax.fori_loop(0, N_SH, one_shard, 0)
        for index in (N_SH - 2, N_SH - 1):
            store(index, index % 2).wait()
        total.finish()

        def body(here):
            block_ref[here] = to_places(resid_ref[here] + total.rows(here)).astype(LOW)

        in_chunks(rows, body)


def attn_backward(
    out_part, normed1, mixture, resid, gao, w_out, queries, keys, values, mask, tables, number
):
    groups, seq, cols = gao.shape
    width = queries.shape[-1]
    row_spec = pl.BlockSpec((seq, 128), lambda g: (g, 0))
    grad = jax.ShapeDtypeStruct((groups, seq, 3 * width), LOW)
    sums = jax.ShapeDtypeStruct((8, 3 * width), FULL)
    flat = groups * seq
    return pl.pallas_call(
        attn_backward_kernel,
        grid=(groups,),
        out_shape=[
            jax.ShapeDtypeStruct(resid.shape, LOW),
            grad,
            sums,
            jax.ShapeDtypeStruct((N_SH, D // N_SH, 4 * width), LOW),
        ],
        in_specs=[
            ANY,
            ANY,
            ANY,
            ANY,
            ANY,
            group_spec(gao),
            VMEM,
            group_spec(queries),
            group_spec(keys),
            group_spec(values),
            group_spec(mask),
            row_spec,
            row_spec,
            row_spec,
        ],
        out_specs=[VMEM, group_spec(grad), whole_spec(sums), ANY],
        scratch_shapes=[
            pltpu.VMEM((seq, width), LOW),
            pltpu.VMEM(gao.shape, LOW),
            pltpu.VMEM((flat, cols), LOW),
            pltpu.VMEM((flat, width), LOW),
            pltpu.VMEM((flat, cols), LOW),
            pltpu.VMEM(resid.shape, FULL),
            pltpu.VMEM((width, cols), LOW),
            pltpu.VMEM((2, D // N_SH, 4 * width), LOW),
            pltpu.VMEM((flat, 3 * width), LOW),
        ]
        + row_sum_scratch(seq, cols)
        + sems(6)
        + [pltpu.SemaphoreType.DMA((7,))],
        compiler_params=comm_params(number),
        cost_estimate=cost(55),
        name="attn_backward",
    )(
        out_part,
        normed1.reshape(flat, cols),
        mixture.reshape(flat, width),
        gao.reshape(flat, cols),
        resid,
        gao,
        w_out,
        queries,
        keys,
        values,
        mask,
        *tables,
    )


class RowSum:
    scratch = 3

    def __init__(self, parts, scratch, pair, base, pieces=1, column_base=0, source=None):
        self.parts, self.pair = parts, pair
        self.pieces, self.column_base = pieces, column_base
        self.out, self.diag, self.full = scratch
        self.half = parts.shape[1] // 2
        self.top, self.bottom = pl.ds(0, self.half), pl.ds(self.half, self.half)
        top, bottom = self.top, self.bottom
        parts = parts if source is None else source
        whole = [
            lambda: remote(parts.at[3, top], self.diag.at[0], pair, base + 0, to_dp(1)),
            lambda: remote(parts.at[3, bottom], self.diag.at[1], pair, base + 1, to_dp(2)),
        ]
        self.first = [make() if pieces == 1 else None for make in whole] + [
            remote(parts.at[1, top], self.full.at[0, top], pair, base + 2, to_dp(1)),
            remote(parts.at[2, bottom], self.full.at[1, bottom], pair, base + 3, to_dp(2)),
        ]
        self.second = [
            remote(self.out.at[0], self.full.at[0, bottom], pair, base + 4, to_dp(1)),
            remote(self.out.at[1], self.full.at[1, top], pair, base + 5, to_dp(2)),
        ]

    def send_columns(self, cols, index):
        for copy in self.column_copies(cols, index):
            copy.start()

    def column_copies(self, cols, index):
        here = pl.ds(cols.start, cols.stop - cols.start)
        return [
            remote(
                self.parts.at[3, rows, here],
                self.diag.at[side, rows_in, here],
                self.pair,
                self.column_base + 2 * index + side,
                to_dp(1 + side),
            )
            for side, rows, rows_in in (
                (0, self.top, pl.ds(0, self.half)),
                (1, self.bottom, pl.ds(0, self.half)),
            )
        ]

    def send(self, k):
        for copy in {3: self.first[:2], 1: self.first[2:3], 2: self.first[3:]}[k]:
            copy.start()

    def diag_wait(self, side):
        if self.pieces == 1:
            self.first[side].wait_recv()
            return
        size = self.parts.shape[2] // self.pieces
        for n in range(self.pieces):
            self.column_copies(slice(n * size, n * size + size), n)[side].wait_recv()

    def relay(self):
        self.diag_wait(1)
        self.out[0] = (
            self.parts[1, self.bottom].astype(FULL) + self.diag[1].astype(FULL)
        ).astype(LOW)
        self.second[0].start()
        self.diag_wait(0)
        self.out[1] = (self.parts[2, self.top].astype(FULL) + self.diag[0].astype(FULL)).astype(
            LOW
        )
        self.second[1].start()

    def finish(self):
        self.first[2].wait_recv()
        self.first[3].wait_recv()
        self.second[0].wait_recv()
        self.second[1].wait_recv()
        for copy in self.first[2:] + self.second:
            copy.wait_send()
        size = self.parts.shape[2] // self.pieces
        for n in range(self.pieces):
            if self.pieces > 1:
                for copy in self.column_copies(slice(n * size, n * size + size), n):
                    copy.wait_send()
        if self.pieces == 1:
            for copy in self.first[:2]:
                copy.wait_send()

    def rows(self, part):
        return (
            self.parts[0, part].astype(FULL)
            + self.full[0, part].astype(FULL)
            + self.full[1, part].astype(FULL)
        )


def row_sum_scratch(rows, cols):
    return [
        pltpu.VMEM((2, rows // 2, cols), LOW),
        pltpu.VMEM((2, rows // 2, cols), LOW),
        pltpu.VMEM((2, rows, cols), LOW),
    ]


def mid_forward_kernel(
    mix_ref, w_ref, tok_ref, norm_ref, resid_hbm, normed_all,
    resid_ref, parts, out, diag, full, own, send, recv, local,
):
    rows = tok_ref.shape[0]
    greet([to_dp(1), to_dp(2)])
    total = RowSum(parts, (out, diag, full), (send, recv), 0)
    for k in (3, 1, 2, 0):
        parts[k] = jnp.dot(mix_ref[k], w_ref[...], preferred_element_type=FULL).astype(LOW)
        if k:
            total.send(k)
    total.relay()
    total.finish()

    def body(here):
        resid = tok_ref[here].astype(FULL) + total.rows(here)
        resid_ref[here] = resid
        unit, _ = unit_rows(resid)
        own[here] = (unit * norm_ref[5:6, :] + norm_ref[6:7, :]).astype(LOW)

    in_chunks(rows, body)
    sent = spread(own, normed_all, (send, recv), 6)
    stores = [
        pltpu.make_async_copy(own, normed_all.at[0], local.at[0]),
        pltpu.make_async_copy(resid_ref, resid_hbm, local.at[1]),
    ]
    for copy in stores:
        copy.start()
    pass_on(*sent)
    spread_end(*sent)
    for copy in stores:
        copy.wait()


def mid_forward(mixture, w_out, tokens, norm_vals, number):
    rows, cols = tokens.shape
    group = (N_DP, rows, cols)
    return pl.pallas_call(
        mid_forward_kernel,
        out_shape=[
            jax.ShapeDtypeStruct(tokens.shape, FULL),
            jax.ShapeDtypeStruct(group, LOW),
        ],
        in_specs=[VMEM] * 4,
        out_specs=[ANY, ANY],
        scratch_shapes=[pltpu.VMEM((rows, cols), FULL), pltpu.VMEM(group, LOW)]
        + row_sum_scratch(rows, cols)
        + [pltpu.VMEM((rows, cols), LOW)]
        + sems(12)
        + [pltpu.SemaphoreType.DMA((2,))],
        compiler_params=comm_params(number),
        cost_estimate=cost(92),
        name="mid_forward",
    )(mixture, w_out, tokens, norm_vals)


def mid_backward_kernel(
    x_hbm, own_cot, near_hbm, far_hbm, wgu_hbm, wdown_hbm, gate_hbm, up_hbm, resid_hbm, norm_ref,
    grad_hbm, own_hbm, sum_ref, part_hbm,
    left, w_gu, w_down, gate_stage, up_stage, ggu, resid_ref, grad_ref, parts,
    out, diag, full, own, send, recv, local, loads, pair_send, pair_recv, pair_local, ready,
):
    rows, cols = resid_ref.shape
    width = w_down.shape[1]
    pieces = 4
    size = cols // pieces
    order = (3, 1, 2, 0)
    seqs = [pl.ds(k * rows, rows) for k in range(N_DP)]
    sources = (own_cot, near_hbm.at[0], near_hbm.at[1], far_hbm)

    def data(k):
        return pltpu.make_async_copy(sources[k], left.at[seqs[k]], local.at[k])

    def stage_loads(n):
        k = order[n]
        return [
            pltpu.make_async_copy(source.at[seqs[k]], stage.at[n % 2], loads.at[2 * (n % 2) + i])
            for i, (source, stage) in enumerate(((gate_hbm, gate_stage), (up_hbm, up_stage)))
        ]

    weights = [
        pltpu.make_async_copy(
            wgu_hbm.at[pl.ds(2 * n, 2)], w_gu.at[pl.ds(2 * n, 2)], local.at[4 + n]
        )
        for n in range(pieces)
    ]
    down_load = pltpu.make_async_copy(wdown_hbm, w_down, loads.at[4])
    later = [
        pltpu.make_async_copy(resid_hbm, resid_ref, local.at[8]),
        pltpu.make_async_copy(own_cot, own, local.at[9]),
    ]
    for copy in [data(3), down_load] + stage_loads(0) + weights[:2] + [data(1)] + stage_loads(1):
        copy.start()
    for copy in weights[2:] + [data(2), data(0)] + later:
        copy.start()
    greet([to_dp(1), to_dp(2), partner()])

    total = RowSum(parts, (out, diag, full), (send, recv), 0, pieces, 6)
    down_load.wait()
    for n, k in enumerate(order):
        data(k).wait()
        for copy in stage_loads(n):
            copy.wait()
        here = slice(k * rows, k * rows + rows)
        for begin, end in column_cuts(width):
            grad = jnp.dot(left[here], w_down[:, begin:end], preferred_element_type=FULL)
            gate, up = gate_stage[n % 2, :, begin:end], up_stage[n % 2, :, begin:end]
            sig = 1.0 / (1.0 + jnp.exp(-gate))
            ggu[here, begin:end] = (grad * up * sig * (1.0 + gate * (1.0 - sig))).astype(LOW)
            ggu[here, width + begin : width + end] = (grad * gate * sig).astype(LOW)
        if n + 2 < N_DP:
            for copy in stage_loads(n + 2):
                copy.start()
        for piece in range(pieces):
            if n == 0:
                weights[piece].wait()
            columns = slice(piece * size, piece * size + size)
            parts[k, :, columns] = lax.dot_general(
                ggu[here],
                w_gu[2 * piece : 2 * piece + 2].reshape(size, 2 * width),
                LAST_DIMS,
                preferred_element_type=FULL,
            ).astype(LOW)
            if n == 0:
                total.send_columns(columns, piece)
        if k and n:
            total.send(k)
    reload = pltpu.make_async_copy(x_hbm, left, local.at[10])
    reload.start()
    pl.semaphore_signal(ready, inc=1, device_id=partner(), device_id_type=MESH)
    sum_ref[...] = jnp.zeros_like(sum_ref)
    total.relay()
    reload.wait()
    pl.semaphore_wait(ready, 1)
    buffers = (w_gu.at[pl.ds(4, 2)], w_gu.at[pl.ds(0, 4)], w_gu.at[pl.ds(6, 2)])
    grad = PairGrad(left, ggu, part_hbm, buffers + (pair_send, pair_recv, pair_local))
    grad.run()
    for copy in later:
        copy.wait()
    total.finish()

    def body(here):
        grads = total.rows(here)
        unit, inverse = unit_rows(resid_ref[here])
        sum_ref[0:1, :] += jnp.sum(grads * unit, axis=0, keepdims=True)
        sum_ref[1:2, :] += jnp.sum(grads, axis=0, keepdims=True)
        grad = own[here].astype(FULL) + layer_back(grads, norm_ref[5:6, :], unit, inverse)
        grad_ref[here] = grad
        own[here] = grad.astype(LOW)

    in_chunks(rows, body)
    stores = [
        pltpu.make_async_copy(own, own_hbm, local.at[0]),
        pltpu.make_async_copy(grad_ref, grad_hbm, local.at[1]),
    ]
    for copy in stores:
        copy.start()
    grad.end()
    for copy in stores:
        copy.wait()


def mid_backward(
    normed2, cotangent, near, far, w_gu, w_down, gate, up, resid, norm_vals, number
):
    rows, cols = resid.shape
    total, width = gate.shape
    blocks = (N_SH, cols // N_SH, 2 * width)
    return pl.pallas_call(
        mid_backward_kernel,
        out_shape=[
            jax.ShapeDtypeStruct(resid.shape, FULL),
            jax.ShapeDtypeStruct(resid.shape, LOW),
            jax.ShapeDtypeStruct((8, cols), FULL),
            jax.ShapeDtypeStruct((N_SH // 2,) + blocks[1:], LOW),
        ],
        in_specs=[ANY] * 9 + [VMEM],
        out_specs=[ANY, ANY, VMEM, ANY],
        scratch_shapes=[
            pltpu.VMEM(normed2.shape, LOW),
            pltpu.VMEM(blocks, LOW),
            pltpu.VMEM(w_down.shape, LOW),
            pltpu.VMEM((2, rows, width), FULL),
            pltpu.VMEM((2, rows, width), FULL),
            pltpu.VMEM((total, 2 * width), LOW),
            pltpu.VMEM(resid.shape, FULL),
            pltpu.VMEM(resid.shape, FULL),
            pltpu.VMEM((N_DP, rows, cols), LOW),
        ]
        + row_sum_scratch(rows, cols)
        + [pltpu.VMEM((rows, cols), LOW)]
        + sems(14)
        + [pltpu.SemaphoreType.DMA((11,)), pltpu.SemaphoreType.DMA((6,))]
        + sems(N_SH // 2)
        + [pltpu.SemaphoreType.DMA((2,)), pltpu.SemaphoreType.REGULAR],
        compiler_params=comm_params(number),
        cost_estimate=cost(70),
        name="mid_backward",
    )(normed2, cotangent, near, far, w_gu.reshape(blocks), w_down, gate, up, resid, norm_vals)


def share_kernel(own_ref, hid_hbm, wdown_hbm, gao_all, part_hbm, hid, w_down, part_ref, send, recv, local):
    loads = [
        pltpu.make_async_copy(wdown_hbm, w_down, local.at[0]),
        pltpu.make_async_copy(hid_hbm, hid, local.at[1]),
    ]
    for copy in loads:
        copy.start()
    greet([to_dp(1), to_dp(2)])
    sent = spread(own_ref, gao_all, (send, recv), 0)
    stores = [pltpu.make_async_copy(own_ref, gao_all.at[0], local.at[2])]
    stores[0].start()
    for copy in loads:
        copy.wait()
    for k in range(N_DP):
        part_ref[k] = lax.dot_general(
            hid[k], w_down[...], LAST_DIMS, preferred_element_type=FULL
        ).astype(LOW)
        stores.append(pltpu.make_async_copy(part_ref.at[k], part_hbm.at[k], local.at[3 + k]))
        stores[-1].start()
    pass_on(*sent)
    spread_end(*sent)
    for copy in stores:
        copy.wait()


def share(own, hidden, w_down, number):
    group = jax.ShapeDtypeStruct((N_DP,) + own.shape, LOW)
    return pl.pallas_call(
        share_kernel,
        out_shape=[group, group],
        in_specs=[VMEM, ANY, ANY],
        out_specs=[ANY, ANY],
        scratch_shapes=[
            pltpu.VMEM(hidden.shape, LOW),
            pltpu.VMEM(w_down.shape, LOW),
            pltpu.VMEM(group.shape, LOW),
        ]
        + sems(6)
        + [pltpu.SemaphoreType.DMA((3 + N_DP,))],
        compiler_params=comm_params(number),
        cost_estimate=cost(48),
        name="share",
    )(own, hidden, w_down)


LINE = N_SH // 2
PIECES = 4


class LineSum:
    def __init__(self, terms_hbm, scratch, sem_refs):
        (self.terms, self.other, self.up_in, self.down_in, self.up_out, self.down_out) = scratch
        self.hbm = terms_hbm
        (core_s, core_r, up_s, up_r, down_s, down_r, self.local) = sem_refs
        self.core_sems, self.up_sems, self.down_sems = (core_s, core_r), (up_s, up_r), (down_s, down_r)
        mine, place = lax.axis_index("dp"), lax.axis_index("shard")
        self.line, self.core = place // 2, place % 2
        self.above, self.below = (mine, place + 2), (mine, place - 2)
        self.partner = (mine, place + 1 - 2 * self.core)
        self.size = self.terms.shape[1] // PIECES
        self.steps = (LINE - 1) * PIECES

    def at_end(self):
        return (self.line == 0) | (self.line == LINE - 1)

    def rows(self, piece):
        return pl.ds(pl.multiple_of(piece * self.size, self.size), self.size)

    def core_copy(self, target, piece):
        here = self.rows(piece)
        return remote(
            self.hbm.at[2 * target + 1 - self.core, here],
            self.other.at[target, here],
            self.core_sems,
            target * PIECES + piece,
            self.partner,
        )

    def load(self, target):
        return pltpu.make_async_copy(
            self.hbm.at[2 * target + self.core], self.terms.at[target], self.local.at[target]
        )

    def load_all(self):
        for target in (LINE - 1, 0, LINE - 2, 1):
            self.load(target).start()

    def start(self):
        for targets in ((LINE - 1, 0), (LINE - 2, 1)):
            for piece in range(PIECES):
                for target in targets:
                    self.core_copy(target, piece).start()

    def own(self, target, piece):
        @pl.when(piece == 0)
        def _():
            self.load(target).wait()

        self.core_copy(target, piece).wait_recv()
        here = self.rows(piece)
        return self.terms[target, here].astype(FULL) + self.other[target, here].astype(FULL)

    def up_copy(self, index):
        return remote(
            self.up_out.at[index], self.up_in.at[index], self.up_sems, index, self.above
        )

    def down_copy(self, index):
        return remote(
            self.down_out.at[index], self.down_in.at[index], self.down_sems, index, self.below
        )

    def up(self, index):
        target, piece = LINE - 1 - index // PIECES, index % PIECES

        @pl.when(target > self.line)
        def _():
            self.up_out[index] = self.own(target, piece).astype(LOW)

            @pl.when(self.line > 0)
            def _():
                self.up_copy(index).wait_recv()
                self.up_out[index] = (
                    self.up_out[index].astype(FULL) + self.up_in[index].astype(FULL)
                ).astype(LOW)

            self.up_copy(index).start()

    def down(self, index):
        target, piece = index // PIECES, index % PIECES

        @pl.when(target < self.line)
        def _():
            self.down_out[index] = self.own(target, piece).astype(LOW)

            @pl.when(self.line < LINE - 1)
            def _():
                self.down_copy(index).wait_recv()
                self.down_out[index] = (
                    self.down_out[index].astype(FULL) + self.down_in[index].astype(FULL)
                ).astype(LOW)

            self.down_copy(index).start()

    def run(self, begin, end):
        def step(index, carry):
            @pl.when(self.line < LINE // 2)
            def _():
                @pl.when(index < self.steps)
                def _():
                    self.up(index)

                @pl.when(index > 0)
                def _():
                    self.down(index - 1)

            @pl.when(self.line >= LINE // 2)
            def _():
                @pl.when(index < self.steps)
                def _():
                    self.down(index)

                @pl.when(index > 0)
                def _():
                    self.up(index - 1)

            return carry

        lax.fori_loop(begin, end, step, 0)

    def finish(self, piece, result):
        here = self.rows(piece)
        result[here] = self.own(self.line, piece)

        @pl.when(self.line > 0)
        def _():
            index = (LINE - 1 - self.line) * PIECES + piece
            self.up_copy(index).wait_recv()
            result[here] = result[here] + self.up_in[index].astype(FULL)

        @pl.when(self.line < LINE - 1)
        def _():
            index = self.line * PIECES + piece
            self.down_copy(index).wait_recv()
            result[here] = result[here] + self.down_in[index].astype(FULL)

    def drain(self):
        def step(index, carry):
            @pl.when(LINE - 1 - index // PIECES > self.line)
            def _():
                self.up_copy(index).wait_send()

            @pl.when(index // PIECES < self.line)
            def _():
                self.down_copy(index).wait_send()

            return carry

        lax.fori_loop(0, self.steps, step, 0)

        def step_core(index, carry):
            self.core_copy(index // PIECES, index % PIECES).wait_send()
            return carry

        lax.fori_loop(0, LINE * PIECES, step_core, 0)


def line_sum_scratch(rows, cols):
    steps = (LINE - 1) * PIECES
    return (
        [pltpu.VMEM((LINE, rows, cols), LOW)] * 2
        + [pltpu.VMEM((steps, rows // PIECES, cols), LOW)] * 4
        + sems(LINE * PIECES)
        + sems(steps)
        + sems(steps)
        + [pltpu.SemaphoreType.DMA((LINE,))]
    )


def fold(values, total):
    values = values * values
    for start in range(0, values.shape[1], 128):
        total = total + values[:, start : start + 128]
    return total


def last_kernel(
    attn_hbm, grad_qkv_hbm, w_hbm, gu_hbm, down_hbm, tok_hbm, grad_hbm, norm_ref, bias_ref, two_ref,
    input_ref, norm_total_ref, gu_out, down_out, qkv_out, out_ref, total_ref,
    grad_qkv_ref, w_ref, tok_ref, grad_ref, gu_in, down_in_low,
    parts, out, diag, full, sum_ref, near, far, part, near_part, far_part, attn_sum, attn_low,
    terms, other, up_in, down_in, up_out, down_out_pieces,
    core_s, core_r, up_s, up_r, down_s, down_r, term_local,
    send, recv, send_a, recv_a, send_b, recv_b, send_c, recv_c, send_d, recv_d, local,
):
    rows = tok_ref.shape[0]
    mine, place = lax.axis_index("dp"), lax.axis_index("shard")
    loads = [
        pltpu.make_async_copy(source, target, local.at[3 + n])
        for n, (source, target) in enumerate(
            (
                (w_hbm, w_ref),
                (grad_qkv_hbm, grad_qkv_ref),
                (tok_hbm, tok_ref),
                (grad_hbm, grad_ref),
                (gu_hbm, gu_in),
                (down_hbm, down_in_low),
            )
        )
    ]
    line = LineSum(
        attn_hbm,
        (terms, other, up_in, down_in, up_out, down_out_pieces),
        (core_s, core_r, up_s, up_r, down_s, down_r, term_local),
    )
    line.load_all()
    for copy in loads:
        copy.start()
    greet([to_dp(k) for k in (1, 2, 3)] + [to_shard(j) for j in range(1, N_SH)])
    line.start()
    total = RowSum(parts, (out, diag, full), (send, recv), 0)
    blocks = []
    for n, (held, target) in enumerate(((gu_hbm, gu_out), (down_hbm, down_out))):
        for k in (3, 1, 2):
            blocks.append(
                remote(
                    held.at[dp_peer(k)], target.at[mine], (send_c, recv_c), 3 * n + k - 1, to_dp(k)
                )
            )
    keeps = [
        pltpu.make_async_copy(gu_in.at[mine], gu_out.at[mine], local.at[0]),
        pltpu.make_async_copy(down_in_low.at[mine], down_out.at[mine], local.at[1]),
    ]
    for copy in blocks[3:]:
        copy.start()
    middle = jnp.logical_not(line.at_end())
    line.run(0, 1)

    def norm1_part(k):
        parts[k] = lax.dot_general(
            grad_qkv_ref[k], w_ref[...], LAST_DIMS, preferred_element_type=FULL
        ).astype(LOW)
        if k:
            total.send(k)

    def middle_run(begin, end):
        @pl.when(middle)
        def _():
            line.run(begin, end)

    loads[0].wait()
    loads[1].wait()
    norm1_part(3)

    @pl.when(line.at_end())
    def _():
        line.run(1, line.steps + 1)

    middle_run(1, 2)
    norm1_part(1)
    middle_run(2, 3)
    norm1_part(2)
    middle_run(3, 4)
    norm1_part(0)
    sum_ref[...] = jnp.zeros_like(sum_ref)
    sum_ref[5:7, :] = two_ref[0:2, :]
    bias_width = bias_ref.shape[1] // 3
    for d in range(N_DP):

        @pl.when(mine == d)
        def _(d=d):
            for n in range(3):
                sum_ref[2 + n : 3 + n, d * bias_width : (d + 1) * bias_width] = bias_ref[
                    0:1, n * bias_width : (n + 1) * bias_width
                ]

    middle_run(4, 6)
    total.relay()
    for copy in blocks[:3]:
        copy.start()
    loads[4].wait()
    loads[5].wait()
    for copy in keeps:
        copy.start()

    def square_low(array, value):
        def step(index, value):
            here = pl.ds(pl.multiple_of(index * 16, 16), 16)
            for k in range(N_DP):
                rows16 = array[k, here].astype(FULL)
                value = fold(rows16[8:], fold(rows16[:8], value))
            return value

        return lax.fori_loop(0, array.shape[1] // 16, step, value)

    part[...] = square_low(down_in_low, square_low(gu_in, jnp.zeros(part.shape, FULL)))
    middle_run(6, 9)
    total.finish()
    loads[2].wait()
    loads[3].wait()

    def body(here):
        grads = total.rows(here)
        unit, inverse = unit_rows(tok_ref[here].astype(FULL))
        sum_ref[0:1, :] += jnp.sum(grads * unit, axis=0, keepdims=True)
        sum_ref[1:2, :] += jnp.sum(grads, axis=0, keepdims=True)
        input_ref[here] = to_places(
            grad_ref[here] + layer_back(grads, norm_ref[0:1, :], unit, inverse)
        )

    in_chunks(rows, body)
    norm_near = [
        remote(sum_ref, near.at[k - 1], (send_a, recv_a), k - 1, to_dp(k)) for k in (1, 2, 3)
    ]
    for copy in norm_near:
        copy.start()
    for copy in norm_near:
        copy.wait()
    sum_ref[...] = sum_ref[...] + near[0] + near[1] + near[2]
    norm_far = [
        remote(sum_ref, far.at[j - 1], (send_b, recv_b), j - 1, to_shard(j))
        for j in range(1, N_SH)
    ]
    for copy in norm_far:
        copy.start()

    width = qkv_out.shape[-1]
    size = qkv_out.shape[1]

    def trade(sender, owner):
        return pltpu.make_async_remote_copy(
            src_ref=attn_low.at[owner],
            dst_ref=qkv_out.at[sender],
            send_sem=send_d.at[owner],
            recv_sem=recv_d.at[sender],
            device_id=(owner, place),
            device_id_type=MESH,
        )

    squares = part[...]
    for d in range(N_DP):
        line.finish(d, attn_sum)

        def square(index, value, d=d):
            here = pl.ds(pl.multiple_of(d * size + index * 8, 8), 8)
            return fold(attn_sum[here], value)

        squares = lax.fori_loop(0, size // 8, square, squares)
        if d == N_DP - 1:
            part[...] = squares
            small = [
                remote(part, near_part.at[k - 1], (send_a, recv_a), 2 + k, to_dp(k))
                for k in (1, 2, 3)
            ]
            for copy in small:
                copy.start()
        attn_low[d] = attn_sum[d * size : d * size + size, :width].astype(LOW)

        @pl.when(mine != d)
        def _(d=d):
            trade(mine, d).start()

    keep = pltpu.make_async_copy(attn_low.at[mine], qkv_out.at[mine], local.at[2])
    keep.start()
    for copy in small:
        copy.wait()
    part[...] = part[...] + near_part[0] + near_part[1] + near_part[2]
    small = [
        remote(part, far_part.at[j - 1], (send_b, recv_b), N_SH - 2 + j, to_shard(j))
        for j in range(1, N_SH)
    ]
    for copy in small:
        copy.start()
    out_ref[...] = to_places(
        jnp.concatenate(
            [attn_sum[d * size : d * size + size, width:] for d in range(N_DP)], axis=1
        )
    )
    for copy in norm_far:
        copy.wait()
    norm_total = sum_ref[...]
    for j in range(N_SH - 1):
        norm_total = norm_total + far[j]
    norm_total_ref[...] = norm_total
    squares = fold(norm_total, part[...])
    for copy in small:
        copy.wait()
    for j in range(N_SH - 1):
        squares = squares + far_part[j]
    total_ref[0, 0] = jnp.sum(squares)
    line.drain()
    for copy in blocks + keeps + [keep]:
        copy.wait()
    for d in range(N_DP):

        @pl.when(mine != d)
        def _(d=d):
            trade(mine, d).wait_send()
            trade(d, mine).wait_recv()


def last(
    part_attn, grad_qkv, w_qkv, gu_sum, down_sum, tokens, grad_resid, norm_vals, biases, sums, number
):
    rows, cols = tokens.shape
    rest = sums
    square_shape = (8, 128)
    block = part_attn.shape[1:]
    width = grad_qkv.shape[-1]
    size = block[0] // N_DP
    return pl.pallas_call(
        last_kernel,
        out_shape=[
            jax.ShapeDtypeStruct(tokens.shape, FULL),
            jax.ShapeDtypeStruct(rest.shape, FULL),
            jax.ShapeDtypeStruct(gu_sum.shape, gu_sum.dtype),
            jax.ShapeDtypeStruct(down_sum.shape, down_sum.dtype),
            jax.ShapeDtypeStruct((N_DP, size, width), LOW),
            jax.ShapeDtypeStruct((size, D), FULL),
            jax.ShapeDtypeStruct((1, 1), FULL),
        ],
        in_specs=[ANY] * 7 + [VMEM] * 3,
        out_specs=[VMEM, VMEM, ANY, ANY, ANY, VMEM, pl.BlockSpec(memory_space=pltpu.SMEM)],
        scratch_shapes=[
            pltpu.VMEM(a.shape, a.dtype)
            for a in (grad_qkv, w_qkv, tokens, grad_resid, gu_sum, down_sum)
        ]
        + [pltpu.VMEM((N_DP, rows, cols), LOW)]
        + row_sum_scratch(rows, cols)
        + [
            pltpu.VMEM(rest.shape, FULL),
            pltpu.VMEM((N_DP - 1,) + rest.shape, FULL),
            pltpu.VMEM((N_SH - 1,) + rest.shape, FULL),
            pltpu.VMEM(square_shape, FULL),
            pltpu.VMEM((N_DP - 1,) + square_shape, FULL),
            pltpu.VMEM((N_SH - 1,) + square_shape, FULL),
            pltpu.VMEM(block, FULL),
            pltpu.VMEM((N_DP, size, width), LOW),
        ]
        + line_sum_scratch(*block)
        + sems(6)
        + sems(2 * (N_DP - 1))
        + sems(2 * (N_SH - 1))
        + sems(6)
        + sems(N_DP)
        + [pltpu.SemaphoreType.DMA((9,))],
        compiler_params=comm_params(number),
        cost_estimate=cost(90),
        name="last",
    )(
        part_attn,
        grad_qkv,
        w_qkv,
        gu_sum,
        down_sum,
        tokens,
        grad_resid,
        norm_vals,
        biases,
        sums,
    )


def column_cuts(cols):
    return [(c, min(c + 256, cols)) for c in range(0, cols, 256)]


class PairGrad:
    def __init__(self, left, right, target, scratch):
        self.left, self.right, self.target = left, right, target
        self.give, self.take, self.keep, send, recv, self.local = scratch
        self.pair = (send, recv)
        place = lax.axis_index("shard")
        self.core = place % 2
        self.partner = (lax.axis_index("dp"), place + 1 - 2 * self.core)
        self.size, self.count = self.give.shape[1], self.take.shape[0]

    def move(self, index):
        return remote(
            self.give.at[index % 2], self.take.at[index], self.pair, index, self.partner
        )

    def store(self, index):
        return pltpu.make_async_copy(
            self.keep.at[index % 2], self.target.at[index], self.local.at[index % 2]
        )

    def fill(self, target, index):
        here = pl.ds(pl.multiple_of(index * self.size, self.size), self.size)
        cols = self.right.shape[1]
        half = cols // 2 if cols > 2048 else cols
        for begin in range(0, cols, half):
            target[:, begin : begin + half] = lax.dot_general(
                self.left[:, here],
                self.right[:, begin : begin + half],
                LEAD_DIMS,
                preferred_element_type=FULL,
            ).astype(LOW)

    def add(self, index):
        self.move(index).wait_recv()
        slot = index % 2
        self.keep[slot] = (self.keep[slot].astype(FULL) + self.take[index].astype(FULL)).astype(LOW)
        self.store(index).start()

    def run(self):
        def step(index, carry):
            @pl.when(index >= 2)
            def _():
                self.move(index - 2).wait_send()
                self.store(index - 2).wait()

            self.fill(self.give.at[index % 2], 2 * index + 1 - self.core)
            self.move(index).start()
            self.fill(self.keep.at[index % 2], 2 * index + self.core)

            @pl.when(index >= 1)
            def _():
                self.add(index - 1)

            return carry

        lax.fori_loop(0, self.count, step, 0)
        self.add(self.count - 1)

    def end(self):
        for index in (self.count - 2, self.count - 1):
            self.move(index).wait_send()
            self.store(index).wait()


def pair_grad_scratch(rows, cols):
    size = rows // N_SH
    count = N_SH // 2
    return [
        pltpu.VMEM((2, size, cols), LOW),
        pltpu.VMEM((count, size, cols), LOW),
        pltpu.VMEM((2, size, cols), LOW),
        *sems(count),
        pltpu.SemaphoreType.DMA((2,)),
    ]


def partner():
    place = lax.axis_index("shard")
    return (lax.axis_index("dp"), place + 1 - 2 * (place % 2))


def mlp_one_kernel(
    x_hbm, own_hbm, near_hbm, wgu_hbm, hid_out, gate_out, up_out, part_out, far_out,
    x_ref, cot_ref, w_gu, hid, gate_stage, up_stage, local, loads, stores, send, recv,
    *grad_scratch,
):
    total = x_ref.shape[0]
    known = N_DP - 1
    seq = total // N_DP
    half = seq // 2
    greet([to_dp(1), to_dp(2), partner()])
    passed = [
        remote(
            near_hbm.at[0, pl.ds(0, half)],
            cot_ref.at[pl.ds(known * seq, half)],
            (send, recv),
            0,
            to_dp(2),
        ),
        remote(
            near_hbm.at[1, pl.ds(half, half)],
            cot_ref.at[pl.ds(known * seq + half, half)],
            (send, recv),
            1,
            to_dp(1),
        ),
    ]
    for copy in passed:
        copy.start()
    cols = hid.shape[1]
    cuts = column_cuts(cols)
    block = total // 2

    def weight_loads(n):
        begin, end = cuts[n]
        return [
            pltpu.make_async_copy(
                wgu_hbm.at[:, pl.ds(at, end - begin)],
                w_gu.at[:, pl.ds(at, end - begin)],
                loads.at[2 * n + i],
            )
            for i, at in enumerate((begin, cols + begin))
        ]

    def stage_stores(n):
        begin, end = cuts[n]
        return [
            pltpu.make_async_copy(
                stage.at[n % 2, :, pl.ds(0, end - begin)],
                target.at[:, pl.ds(begin, end - begin)],
                stores.at[2 * i + n % 2],
            )
            for i, (stage, target) in enumerate(((gate_stage, gate_out), (up_stage, up_out)))
        ]

    data = [pltpu.make_async_copy(x_hbm, x_ref, local.at[0])]
    for copy in weight_loads(0) + data:
        copy.start()
    for n in range(1, len(cuts)):
        for copy in weight_loads(n):
            copy.start()
    data += [
        pltpu.make_async_copy(source, cot_ref.at[pl.ds(k * seq, seq)], local.at[5 + k])
        for k, source in enumerate((own_hbm, near_hbm.at[0], near_hbm.at[1]))
    ]
    for copy in data[1:]:
        copy.start()
    data[0].wait()
    for n, (begin, end) in enumerate(cuts):
        for copy in weight_loads(n):
            copy.wait()
        if n >= 2:
            for copy in stage_stores(n - 2):
                copy.wait()

        def rows(index, carry, begin=begin, end=end, slot=n % 2):
            here = pl.ds(pl.multiple_of(index * block, block), block)
            gate = jnp.dot(x_ref[here], w_gu[:, begin:end], preferred_element_type=FULL)
            up = jnp.dot(
                x_ref[here], w_gu[:, cols + begin : cols + end], preferred_element_type=FULL
            )
            hid[here, begin:end] = (gate / (1.0 + jnp.exp(-gate)) * up).astype(LOW)
            gate_stage[slot, here, : end - begin] = gate
            up_stage[slot, here, : end - begin] = up
            return carry

        lax.fori_loop(0, total // block, rows, 0)
        for copy in stage_stores(n):
            copy.start()
    outs = [
        pltpu.make_async_copy(hid, hid_out, local.at[2]),
        pltpu.make_async_copy(cot_ref.at[pl.ds(known * seq, seq)], far_out, local.at[1]),
    ]
    outs[0].start()
    for copy in data[1:]:
        copy.wait()
    for copy in passed:
        copy.wait()
    outs[1].start()
    grad = PairGrad(cot_ref, hid, part_out, grad_scratch)
    grad.run()
    for n in (len(cuts) - 2, len(cuts) - 1):
        for copy in stage_stores(n):
            copy.wait()
    grad.end()
    for copy in outs:
        copy.wait()


def mlp_one(normed2, cotangent, near, w_gu, number):
    total, width = normed2.shape
    cols = w_gu.shape[1] // 2
    values = jax.ShapeDtypeStruct((total, cols), FULL)
    return pl.pallas_call(
        mlp_one_kernel,
        out_shape=[
            jax.ShapeDtypeStruct((total, cols), LOW),
            values,
            values,
            jax.ShapeDtypeStruct((N_SH // 2, width // N_SH, cols), LOW),
            jax.ShapeDtypeStruct(cotangent.shape, LOW),
        ],
        in_specs=[ANY] * 4,
        out_specs=[ANY] * 5,
        scratch_shapes=[
            pltpu.VMEM((total, width), LOW),
            pltpu.VMEM((total, width), LOW),
            pltpu.VMEM((width, 2 * cols), LOW),
            pltpu.VMEM((total, cols), LOW),
            pltpu.VMEM((2, total, 256), FULL),
            pltpu.VMEM((2, total, 256), FULL),
            pltpu.SemaphoreType.DMA((8,)),
            pltpu.SemaphoreType.DMA((2 * len(column_cuts(cols)),)),
            pltpu.SemaphoreType.DMA((4,)),
        ]
        + sems(2)
        + pair_grad_scratch(width, cols),
        compiler_params=comm_params(number),
        cost_estimate=cost(30),
        name="mlp_one",
    )(normed2, cotangent, near, w_gu)


FIRST_HAT = 1.0 / (1.0 - BETA_ONE**STEP)
SECOND_HAT = 1.0 / (1.0 - BETA_TWO**STEP)


def clip_factor(total_ref, width):
    total = jnp.full((1, width), total_ref[0, 0], FULL)
    return CLIP_NORM / jnp.maximum(jnp.sqrt(total), CLIP_NORM)


def adam_step(grads, factor, master, first, second):
    clipped = grads.astype(FULL) * factor
    first_new = BETA_ONE * first + (1.0 - BETA_ONE) * clipped
    second_new = BETA_TWO * second + (1.0 - BETA_TWO) * clipped * clipped
    ratio = first_new * (RATE_MATRIX * FIRST_HAT) / (jnp.sqrt(second_new * SECOND_HAT) + ADAM_EPS)
    return (master * (1.0 - RATE_MATRIX * DECAY_MATRIX) - ratio, first_new, second_new)


def adam_kernel(
    total_ref, norm_ref, master_ref, first_ref, second_ref, rows_ref, low_ref,
    qkv_ref, out_ref, gu_ref, down_ref, *refs,
):
    norm_outs, (rows_out, low_out), refs = refs[6:9], refs[9:11], refs[:6] + refs[11:]
    factor = clip_factor(total_ref, 128)[:, 0:1]
    rows_out[...] = rows_ref[...]
    low_out[...] = low_ref[...]

    @pl.when(pl.program_id(0) == 0)
    def _():
        size = master_ref.shape[1]
        mine, place = lax.axis_index("dp"), lax.axis_index("shard")
        grads = jnp.zeros((8, size), FULL)
        row = lax.broadcasted_iota(jnp.int32, (8, size), 0)
        bias = (row >= 2) & (row < 5)
        spot = jnp.where(bias, mine * N_SH + place, place * N_DP + mine)
        for n in range(N_DP * N_SH):
            grads = jnp.where(spot == n, norm_ref[:, n * size : n * size + size], grads)
        values = adam_update(
            master_ref[...], first_ref[...], second_ref[...], grads[:7], factor, RATE_VECTOR, 0.0
        )
        for ref, value in zip(norm_outs, values):
            ref[...] = value

    def update(begin, grads, states, results):
        here = slice(begin, begin + grads.shape[1])
        values = adam_step(grads, factor, *[ref[:, here] for ref in states])
        for ref, value in zip(results, values):
            ref[:, here] = value

    attn, mlp = (refs[0:3], refs[6:9]), (refs[3:6], refs[9:12])
    width, ff_width = qkv_ref.shape[-1] // 3, down_ref.shape[-1]
    for d in range(N_DP):
        for part in range(3):
            here = slice(part * width, part * width + width)
            update(part * D + d * width, qkv_ref[d, :, here], *attn)
        for part in range(2):
            here = slice(part * ff_width, part * ff_width + ff_width)
            update(part * FF + d * ff_width, gu_ref[d, :, here], *mlp)
        update(2 * FF + d * ff_width, down_ref[d], *mlp)
    update(3 * D, out_ref[...], *attn)


def adam(total, norm_sums, norm_states, row_outputs, grads, states):
    size = 16
    steps = states[0].shape[0] // size

    def block(array):
        if array.ndim == 3:
            return pl.BlockSpec((N_DP, size, array.shape[-1]), lambda j: (0, j, 0))
        return pl.BlockSpec((array.shape[0] // steps, array.shape[-1]), lambda j: (j, 0))

    def whole(array):
        return pl.BlockSpec(array.shape, lambda j: (0, 0))

    count = sum(array.size for array in states)
    outs = norm_states + row_outputs + states
    return pl.pallas_call(
        adam_kernel,
        grid=(steps,),
        out_shape=[jax.ShapeDtypeStruct(array.shape, array.dtype) for array in outs],
        in_specs=[pl.BlockSpec(memory_space=pltpu.SMEM)]
        + [whole(array) for array in [norm_sums] + norm_states]
        + [block(array) for array in row_outputs + grads + states],
        out_specs=[whole(array) for array in norm_states]
        + [block(array) for array in row_outputs + states],
        compiler_params=pltpu.CompilerParams(vmem_limit_bytes=BIG_VMEM),
        cost_estimate=pl.CostEstimate(
            flops=6 * count, bytes_accessed=9 * count, transcendentals=count // 3
        ),
        name="adam",
    )(total, norm_sums, *norm_states, *row_outputs, *grads, *states)


def per_device_fast(
    tokens,
    cotangent,
    segments,
    positions,
    attn_master,
    mlp_master,
    norm_master,
    attn_first,
    mlp_first,
    norm_first,
    attn_second,
    mlp_second,
    norm_second,
):
    seq = tokens.shape[0]
    rows = attn_master.shape[0]
    width = D // N_DP
    ff_width = FF // N_DP
    group = N_DP * seq
    my_dp = lax.axis_index("dp")
    my_shard = lax.axis_index("shard")

    places = jnp.stack([segments, positions], 0)
    w_qkv, w_out, norm_all, tok_all, place_all, gu_blocks, down_blocks, tokens, cotangent = start(
        attn_master, mlp_master, norm_master, tokens, cotangent, places, 0
    )
    w_qkv = w_qkv.reshape(D, 3 * width)
    w_out = w_out.reshape(width, D)

    def gather_rows(blocks):
        return lax.all_gather(blocks.reshape(-1, blocks.shape[-1]), "shard", axis=0, tiled=True)

    rates = ROPE_BASE ** (-((np.arange(128) % (ROT // 2)) * 2.0 / ROT))
    rates = np.broadcast_to(rates.astype(np.float32), (8, 128))
    w_gu = gather_rows(gu_blocks)
    w_down = gather_rows(down_blocks)
    results = attn_forward(cotangent, tok_all, place_all, rates, norm_all, w_qkv, 2)
    cot_near, norm_vals, normed1, queries, keys, values, mixture = results[:7]
    *tables, mask = results[7:]
    resid, normed2 = mid_forward(mixture, w_out, tokens, norm_vals, 3)
    normed2 = normed2.reshape(group, D)

    hidden, gate, up, part_down, cot_far = mlp_one(normed2, cotangent, cot_near, w_gu, 1)
    groups = [[place for place in range(N_SH) if place % 2 == core] for core in range(2)]

    def sum_line(blocks):
        blocks = blocks.reshape(-1, blocks.shape[-1])
        return lax.psum_scatter(
            blocks, "shard", scatter_dimension=0, axis_index_groups=groups, tiled=True
        )

    down_sum = sum_line(part_down)
    grad_resid, own_gao, sums2, part_gu = mid_backward(
        normed2, cotangent, cot_near, cot_far, w_gu, w_down, gate, up, resid, norm_vals, 4
    )
    gu_sum = sum_line(part_gu)
    grad_attn_out, out_part = share(own_gao, hidden.reshape(N_DP, seq, ff_width), w_down, 6)
    grad_attn_out, down_sum = lax.optimization_barrier((grad_attn_out, down_sum))
    block_out, grad_qkv, bias_sums, part_attn = attn_backward(
        out_part,
        normed1,
        mixture,
        resid,
        grad_attn_out,
        w_out,
        queries,
        keys,
        values,
        mask,
        tables,
        9,
    )
    gu_blocks = gu_sum.reshape(N_DP, rows, 2 * ff_width)
    down_blocks = down_sum.reshape(N_DP, rows, ff_width)
    input_grad, norm_sums, gu_grad, down_grad, qkv_grad, out_grad, box = last(
        part_attn,
        grad_qkv,
        w_qkv,
        gu_blocks,
        down_blocks,
        tokens,
        grad_resid,
        norm_vals,
        bias_sums,
        sums2,
        5,
    )
    results = adam(
        box,
        norm_sums,
        [norm_master, norm_first, norm_second],
        [input_grad, block_out],
        [qkv_grad, out_grad, gu_grad, down_grad],
        [attn_master, attn_first, attn_second, mlp_master, mlp_first, mlp_second],
    )
    norm_new, norm_first_new, norm_second_new, input_grad, block_out = results[:5]
    attn_new, attn_first_new, attn_second_new, mlp_new, mlp_first_new, mlp_second_new = results[5:]
    grad_size = jnp.sqrt(box[0, 0])
    return (
        block_out,
        input_grad,
        grad_size,
        attn_new,
        mlp_new,
        norm_new,
        attn_first_new,
        mlp_first_new,
        norm_first_new,
        attn_second_new,
        mlp_second_new,
        norm_second_new,
    )


def solution(mesh):
    in_specs = (
        P(("dp", "shard"), None),
        P(("dp", "shard"), None),
        P(("dp", "shard")),
        P(("dp", "shard")),
        P(("dp", "shard"), None),
        P(("dp", "shard"), None),
        P(None, ("dp", "shard")),
        P(("dp", "shard"), None),
        P(("dp", "shard"), None),
        P(None, ("dp", "shard")),
        P(("dp", "shard"), None),
        P(("dp", "shard"), None),
        P(None, ("dp", "shard")),
    )
    out_specs = (
        P(("dp", "shard"), None),
        P(("dp", "shard"), None),
        P(),
        P(("dp", "shard"), None),
        P(("dp", "shard"), None),
        P(None, ("dp", "shard")),
        P(("dp", "shard"), None),
        P(("dp", "shard"), None),
        P(None, ("dp", "shard")),
        P(("dp", "shard"), None),
        P(("dp", "shard"), None),
        P(None, ("dp", "shard")),
    )
    fast = dict(mesh.shape) == dict(dp=4, shard=8)
    body = per_device_fast if fast else per_device_any
    return jax.shard_map(
        body, mesh=mesh, in_specs=in_specs, out_specs=out_specs, check_vma=False
    )
```

```python
import functools

import numpy as np
import jax
import jax.numpy as jnp
from jax import lax
from jax.experimental import pallas as pl
from jax.experimental.pallas import tpu as pltpu
from jax.sharding import PartitionSpec as P

D = 2048
HEADS = 32
HEAD = 64
FF = 5632
ROT = 16
STEP = 10


NORM_EPS = 1e-05
NEG_FILL = -1e30
ROPE_BASE = 10000.0
CLIP_NORM = 1.0
BETA_ONE = 0.9
BETA_TWO = 0.95
ADAM_EPS = 1e-08
RATE_MATRIX = 0.02
RATE_VECTOR = 0.2
DECAY_MATRIX = 0.1
LEAD_DIMS = (((0,), (0,)), ((), ()))
LAST_DIMS = (((1,), (1,)), ((), ()))


def layer_norm(values_in, gain_vec, shift_vec):
    average = jnp.mean(values_in, axis=-1, keepdims=True)
    centered = values_in - average
    variance = jnp.mean(centered * centered, axis=-1, keepdims=True)
    return centered * lax.rsqrt(variance + NORM_EPS) * gain_vec + shift_vec


def rotary_tables(position_ids):
    half_rot = ROT // 2
    inverse_freq = ROPE_BASE ** (-(jnp.arange(half_rot, dtype=jnp.float32) * 2.0 / ROT))
    angles = position_ids.astype(jnp.float32)[:, None] * inverse_freq[None, :]
    return (jnp.cos(angles)[:, None, :], jnp.sin(angles)[:, None, :])


def rotate(heads_in, cos_table, sin_table):
    half_rot = ROT // 2
    first_half = heads_in[..., :half_rot]
    second_half = heads_in[..., half_rot:ROT]
    rest_part = heads_in[..., ROT:]
    turned_one = first_half * cos_table - second_half * sin_table
    turned_two = second_half * cos_table + first_half * sin_table
    return jnp.concatenate([turned_one, turned_two, rest_part], -1)


def pad_last(array, size):
    missing = size - array.shape[-1]
    if missing == 0:
        return array
    return jnp.pad(array, [(0, 0)] * (array.ndim - 1) + [(0, missing)])


def activate(gate_part, up_part):
    return jax.nn.silu(gate_part) * up_part


def adam_update(master, first, second, grads, factor, rate, decay):
    clipped = grads * factor
    first_new = BETA_ONE * first + (1.0 - BETA_ONE) * clipped
    second_new = BETA_TWO * second + (1.0 - BETA_TWO) * clipped * clipped
    first_hat = first_new / (1.0 - BETA_ONE**STEP)
    second_hat = second_new / (1.0 - BETA_TWO**STEP)
    master_new = master - rate * (first_hat / (jnp.sqrt(second_hat) + ADAM_EPS) + decay * master)
    return (master_new, first_new, second_new)


def exchange_dp(blocks):
    return lax.all_to_all(blocks, "dp", 0, 0, tiled=True)


def gather_dp(rows):
    return lax.all_gather(rows, "dp", axis=0, tiled=True)


def scatter_sum_dp(parts):
    return lax.psum_scatter(parts, "dp", scatter_dimension=0, tiled=True)


def gather_shard(block):
    return lax.all_gather(block, "shard", axis=1)


def scatter_sum_shard(parts):
    return lax.psum_scatter(parts, "shard", scatter_dimension=1)


def layer_stats(values_in):
    average = jnp.mean(values_in, axis=-1, keepdims=True)
    centered = values_in - average
    variance = jnp.mean(centered * centered, axis=-1, keepdims=True)
    inverse = lax.rsqrt(variance + NORM_EPS)
    return centered * inverse, inverse


def layer_back(grads, gain_vec, unit, inverse):
    scaled = grads * gain_vec
    mean_one = jnp.mean(scaled, axis=-1, keepdims=True)
    mean_two = jnp.mean(scaled * unit, axis=-1, keepdims=True)
    return inverse * (scaled - mean_one - unit * mean_two)


def per_device_any(
    tokens,
    cotangent,
    segments,
    positions,
    attn_master,
    mlp_master,
    norm_master,
    attn_first,
    mlp_first,
    norm_first,
    attn_second,
    mlp_second,
    norm_second,
):
    low = jnp.bfloat16
    full = jnp.float32
    n_dp = lax.axis_size("dp")
    n_sh = lax.axis_size("shard")
    seq = tokens.shape[0]
    rows = attn_master.shape[0]
    heads = HEADS // n_dp
    width = D // n_dp
    ff_width = -(-FF // (128 * n_dp)) * 128
    ff_pad = ff_width * n_dp
    scale = HEAD ** (-0.5)

    qkv_send = attn_master[:, : 3 * D].astype(low).reshape(rows, 3, n_dp, width)
    qkv_send = qkv_send.transpose(2, 0, 1, 3).reshape(n_dp, rows, 3 * width)
    mlp_send = pad_last(mlp_master.astype(low).reshape(rows, 3, FF), ff_pad)
    mlp_send = mlp_send.reshape(rows, 3, n_dp, ff_width)
    mlp_send = mlp_send.transpose(2, 0, 1, 3).reshape(n_dp, rows, 3 * ff_width)
    norm_full = lax.all_gather(norm_master.astype(low), ("dp", "shard"), axis=1, tiled=True)
    norm_vals = norm_full.astype(full)
    w_qkv = gather_shard(exchange_dp(qkv_send)).reshape(D, 3 * width)
    w_out = gather_shard(attn_master[None, :, 3 * D :].astype(low)).reshape(width, D)
    tokens_all = gather_dp(tokens)
    places_all = gather_dp(jnp.stack([segments, positions], 0)[None])
    cot_all = gather_dp(cotangent)
    w_mlp = gather_shard(exchange_dp(mlp_send)).reshape(D, 3 * ff_width)
    w_gu = w_mlp[:, : 2 * ff_width]
    w_down = w_mlp[:, 2 * ff_width :]
    seg_all, pos_all = places_all[:, 0], places_all[:, 1]

    inputs_all = tokens_all.astype(full)
    unit1, _ = layer_stats(inputs_all)
    normed1 = (unit1 * norm_vals[0] + norm_vals[1]).astype(low)
    my_dp = lax.axis_index("dp")
    bias = lax.dynamic_slice(norm_vals[2:5], (0, my_dp * width), (3, width)).reshape(3 * width)
    qkv = jnp.dot(normed1, w_qkv, preferred_element_type=full) + bias
    qkv = qkv.reshape(n_dp * seq, 3 * heads, HEAD)
    cos_table, sin_table = rotary_tables(pos_all.reshape(-1))

    def split(array):
        return array.reshape(n_dp, seq, heads, HEAD)

    queries = split(rotate(qkv[:, :heads], cos_table, sin_table).astype(low))
    key_rows = split(rotate(qkv[:, heads : 2 * heads], cos_table, sin_table).astype(low))
    values = split(qkv[:, 2 * heads :].astype(low))
    places = jnp.arange(seq)
    allowed = (seg_all[:, :, None] == seg_all[:, None, :]) & (
        places[:, None] >= places[None, :]
    )[None]
    scores = (
        jnp.einsum("gshd,gthd->ghst", queries, key_rows, preferred_element_type=full) * scale
    )
    scores = jnp.where(allowed[:, None], scores, NEG_FILL)
    attend = jax.nn.softmax(scores, axis=-1)
    attend_low = attend.astype(low)
    mixture = (
        jnp.einsum("ghst,gthd->gshd", attend_low, values, preferred_element_type=full)
        .reshape(n_dp * seq, width)
        .astype(low)
    )
    attn_part = jnp.dot(mixture, w_out, preferred_element_type=full).astype(low)
    resid = tokens.astype(full) + scatter_sum_dp(attn_part).astype(full)
    unit2, inverse2 = layer_stats(resid)
    normed2 = gather_dp((unit2 * norm_vals[5] + norm_vals[6]).astype(low))
    gate_up = jnp.dot(normed2, w_gu, preferred_element_type=full)
    hidden_f, act_pull = jax.vjp(activate, gate_up[:, :ff_width], gate_up[:, ff_width:])
    hidden = hidden_f.astype(low)
    grad_hidden = jnp.dot(cot_all, w_down, preferred_element_type=full)
    grad_gate, grad_up = act_pull(grad_hidden)
    grad_gu = jnp.concatenate([grad_gate, grad_up], 1).astype(low)
    norm2_part = lax.dot_general(grad_gu, w_gu, LAST_DIMS, preferred_element_type=full)
    grad_norm2 = scatter_sum_dp(norm2_part.astype(low)).astype(full)
    out_part = lax.dot_general(hidden, w_down, LAST_DIMS, preferred_element_type=full)
    block_out = (resid + scatter_sum_dp(out_part.astype(low)).astype(full)).astype(low)
    part_gu = lax.dot_general(normed2, grad_gu, LEAD_DIMS, preferred_element_type=full)
    part_down = lax.dot_general(cot_all, hidden, LEAD_DIMS, preferred_element_type=full)
    part_mlp = jnp.concatenate([part_gu.astype(low), part_down.astype(low)], 1)
    mlp_sum = scatter_sum_shard(part_mlp.reshape(n_dp, n_sh, rows, 3 * ff_width))

    grad_gain2 = jnp.sum(grad_norm2 * unit2, axis=0)
    grad_shift2 = jnp.sum(grad_norm2, axis=0)
    grad_resid = cotangent.astype(full) + layer_back(grad_norm2, norm_vals[5], unit2, inverse2)
    grad_attn_out = gather_dp(grad_resid.astype(low))
    grad_mixture = lax.dot_general(grad_attn_out, w_out, LAST_DIMS, preferred_element_type=full)
    grad_mixture = split(grad_mixture.astype(low))
    grad_attend = jnp.einsum("gshd,gthd->ghst", grad_mixture, values, preferred_element_type=full)
    grad_values = jnp.einsum(
        "ghst,gshd->gthd", attend_low, grad_mixture, preferred_element_type=full
    )
    grad_scores = (
        attend * (grad_attend - jnp.sum(attend * grad_attend, axis=-1, keepdims=True))
    ).astype(low)
    grad_queries = (
        jnp.einsum("ghst,gthd->gshd", grad_scores, key_rows, preferred_element_type=full) * scale
    )
    grad_keys = (
        jnp.einsum("ghst,gshd->gthd", grad_scores, queries, preferred_element_type=full) * scale
    )

    def turn_back(grads):
        grads = grads.reshape(n_dp * seq, heads, HEAD)
        return rotate(grads, cos_table, -sin_table).reshape(n_dp * seq, width)

    grad_qkv = jnp.concatenate(
        [
            turn_back(grad_queries),
            turn_back(grad_keys),
            grad_values.reshape(n_dp * seq, width),
        ],
        1,
    ).astype(low)
    part_qkv = lax.dot_general(normed1, grad_qkv, LEAD_DIMS, preferred_element_type=full)
    part_out = lax.dot_general(mixture, grad_attn_out, LEAD_DIMS, preferred_element_type=full)
    qkv_sum = scatter_sum_shard(part_qkv.astype(low).reshape(n_dp, n_sh, rows, 3 * width))
    out_sum = scatter_sum_shard(part_out.astype(low).reshape(1, n_sh, rows, D))[0].astype(full)

    norm1_part = lax.dot_general(grad_qkv, w_qkv, LAST_DIMS, preferred_element_type=full)
    grad_gain1 = jnp.sum(norm1_part * unit1, axis=0)
    grad_shift1 = jnp.sum(norm1_part, axis=0)
    grad_bias = jnp.sum(grad_qkv, axis=0, dtype=full).reshape(3, width)
    grad_norm1 = scatter_sum_dp(norm1_part.astype(low)).astype(full)
    own_unit1, own_inverse1 = layer_stats(tokens.astype(full))
    input_grad = grad_resid + layer_back(grad_norm1, norm_vals[0], own_unit1, own_inverse1)
    norm_term = lax.dynamic_update_slice(
        jnp.zeros((3, D), full), grad_bias, (0, my_dp * width)
    )
    norm_term = jnp.concatenate(
        [grad_gain1[None], grad_shift1[None], norm_term, grad_gain2[None], grad_shift2[None]], 0
    )
    norm_grad = lax.psum_scatter(norm_term, ("dp", "shard"), scatter_dimension=1, tiled=True)

    def columns_back(summed, parts, part_width, keep):
        back = exchange_dp(summed).reshape(n_dp, rows, parts, part_width)
        back = back.transpose(1, 2, 0, 3).reshape(rows, parts, n_dp * part_width)
        return back[:, :, :keep].reshape(rows, parts * keep).astype(full)

    mlp_grad = columns_back(mlp_sum, 3, ff_width, FF)
    attn_grad = jnp.concatenate([columns_back(qkv_sum, 3, width, D), out_sum], 1)
    squares = (
        jnp.sum(attn_grad * attn_grad)
        + jnp.sum(mlp_grad * mlp_grad)
        + jnp.sum(norm_grad * norm_grad)
    )
    overall = lax.psum(squares, ("dp", "shard"))
    grad_size = jnp.sqrt(overall)
    factor = CLIP_NORM / jnp.maximum(grad_size, CLIP_NORM)
    attn_new, attn_first_new, attn_second_new = adam_update(
        attn_master, attn_first, attn_second, attn_grad, factor, RATE_MATRIX, DECAY_MATRIX
    )
    mlp_new, mlp_first_new, mlp_second_new = adam_update(
        mlp_master, mlp_first, mlp_second, mlp_grad, factor, RATE_MATRIX, DECAY_MATRIX
    )
    norm_new, norm_first_new, norm_second_new = adam_update(
        norm_master, norm_first, norm_second, norm_grad, factor, RATE_VECTOR, 0.0
    )
    return (
        block_out,
        input_grad,
        grad_size,
        attn_new,
        mlp_new,
        norm_new,
        attn_first_new,
        mlp_first_new,
        norm_first_new,
        attn_second_new,
        mlp_second_new,
        norm_second_new,
    )


MESH = pl.DeviceIdType.MESH
ANY = pl.BlockSpec(memory_space=pl.ANY)
VMEM = pl.BlockSpec(memory_space=pltpu.VMEM)
LOW = jnp.bfloat16
FULL = jnp.float32
N_DP = 4
N_SH = 8
BIG_VMEM = 60 * 1024 * 1024


def dp_peer(step):
    mine = lax.axis_index("dp")
    if step == 1:
        return mine + 1 - 2 * (mine % 2)
    if step == 2:
        return (mine + 2) % 4
    return 3 - mine


def to_dp(step):
    return (dp_peer(step), lax.axis_index("shard"))


def to_shard(step):
    return (lax.axis_index("dp"), (lax.axis_index("shard") + step) % N_SH)


def cost(micros):
    return pl.CostEstimate(flops=0, bytes_accessed=int(micros * 3.0e6), transcendentals=0)


def greet(peers):
    barrier = pltpu.get_barrier_semaphore()
    for peer in peers:
        pl.semaphore_signal(barrier, inc=1, device_id=peer, device_id_type=MESH)
    pl.semaphore_wait(barrier, len(peers))


def remote(source, target, sems, index, peer):
    return pltpu.make_async_remote_copy(
        src_ref=source,
        dst_ref=target,
        send_sem=sems[0].at[index],
        recv_sem=sems[1].at[index],
        device_id=peer,
        device_id_type=MESH,
    )


def sems(count):
    return [pltpu.SemaphoreType.DMA((count,)), pltpu.SemaphoreType.DMA((count,))]


def comm_params(number):
    return pltpu.CompilerParams(
        collective_id=number, has_side_effects=True, vmem_limit_bytes=BIG_VMEM
    )


def to_places(value):
    size = value.shape[1] // (N_DP * N_SH)
    starts = [(n * N_DP + d) * size for d in range(N_DP) for n in range(N_SH)]
    return jnp.concatenate([value[:, start : start + size] for start in starts], axis=1)


def to_shards(value):
    size = value.shape[1] // (N_DP * N_SH)
    starts = [(d * N_SH + n) * size for n in range(N_SH) for d in range(N_DP)]
    return jnp.concatenate([value[:, start : start + size] for start in starts], axis=1)


CHUNK = 32


def in_chunks(rows, body):
    def step(index, carry):
        body(pl.ds(pl.multiple_of(index * CHUNK, CHUNK), CHUNK))
        return carry

    lax.fori_loop(0, rows // CHUNK, step, 0)


def spread_plan(own, result, sem_pair, base):
    half = own.shape[0] // 2
    top, bottom = pl.ds(0, half), pl.ds(half, half)
    sent = [
        remote(own.at[top], result.at[1, top], sem_pair, base + 0, to_dp(1)),
        remote(own.at[bottom], result.at[2, bottom], sem_pair, base + 1, to_dp(2)),
        remote(own.at[bottom], result.at[1, bottom], sem_pair, base + 2, to_dp(1)),
        remote(own.at[top], result.at[2, top], sem_pair, base + 3, to_dp(2)),
    ]
    passed = [
        remote(result.at[1, top], result.at[3, top], sem_pair, base + 4, to_dp(2)),
        remote(result.at[2, bottom], result.at[3, bottom], sem_pair, base + 5, to_dp(1)),
    ]
    return sent, passed


def spread(own, result, sem_pair, base):
    sent, passed = spread_plan(own, result, sem_pair, base)
    for copy in sent:
        copy.start()
    return sent, passed


def pass_on(sent, passed):
    sent[0].wait_recv()
    passed[0].start()
    sent[1].wait_recv()
    passed[1].start()


def spread_end(sent, passed):
    sent[2].wait_recv()
    sent[3].wait_recv()
    passed[0].wait_recv()
    passed[1].wait_recv()
    for copy in sent + passed:
        copy.wait_send()


SLABS = 6


def start_kernel(
    attn_hbm, mlp_hbm, norm_ref, tok_hbm, cot_hbm, seg_ref, pos_ref,
    seg_0, seg_1, seg_2, seg_3, pos_0, pos_1, pos_2, pos_3,
    w_qkv, w_out, norm_all, tok_all, gu_out, down_out, tok_own, cot_own,
    attn_in, mlp_in, tok_in, cot_in, qkv_send, out_send, norm_send, gu_send, down_send,
    tok_low, cot_low,
    up_send, up_recv, down_s, down_recv, core_send, core_recv, send, recv, local,
):
    mine, place = lax.axis_index("dp"), lax.axis_index("shard")
    line, core = place // 2, place % 2
    width, ff_width = qkv_send.shape[-1] // 3, down_send.shape[-1]
    above, below = (mine, place + 2), (mine, place - 2)
    partner = (mine, place + 1 - 2 * core)
    has_above, has_below = line < N_SH // 2 - 1, line > 0
    pair = (send, recv)
    loads = [
        pltpu.make_async_copy(attn_hbm, attn_in, local.at[0]),
        pltpu.make_async_copy(tok_hbm, tok_in, local.at[1]),
        pltpu.make_async_copy(mlp_hbm, mlp_in, local.at[2]),
        pltpu.make_async_copy(cot_hbm, cot_in, local.at[3]),
    ]
    for copy in loads:
        copy.start()

    barrier = pltpu.get_barrier_semaphore()
    for peer in [to_dp(k) for k in (1, 2, 3)] + [partner]:
        pl.semaphore_signal(barrier, inc=1, device_id=peer, device_id_type=MESH)

    @pl.when(has_above)
    def _():
        pl.semaphore_signal(barrier, inc=1, device_id=above, device_id_type=MESH)

    @pl.when(has_below)
    def _():
        pl.semaphore_signal(barrier, inc=1, device_id=below, device_id_type=MESH)

    norm_send[...] = jnp.zeros_like(norm_send)
    norm_send[0:7, 0 : norm_ref.shape[1]] = norm_ref[...].astype(LOW).astype(FULL)
    loads[0].wait()
    for part in range(3):
        for d in range(N_DP):
            begin = part * D + d * width
            qkv_send[d, :, part * width : part * width + width] = attn_in[
                :, begin : begin + width
            ].astype(LOW)
    out_send[...] = to_shards(attn_in[:, 3 * D :]).astype(LOW)

    @pl.when(has_above & has_below)
    def _():
        pl.semaphore_wait(barrier, 6)

    @pl.when(jnp.logical_not(has_above & has_below))
    def _():
        pl.semaphore_wait(barrier, 5)

    def slab(n, shard):
        if n == 0:
            return w_qkv.at[shard, mine]
        if n == 1:
            return w_out.at[shard]
        if n == 2:
            return norm_all.at[shard]
        return w_qkv.at[shard, dp_peer(n - 2)]

    def source(n):
        return {0: qkv_send.at[mine], 1: out_send}.get(n, slab(n, place))

    def along(n, shard, hop, sem_pair, peer, held=None):
        start = slab(n, shard) if held is None else held
        return remote(start, slab(n, shard), sem_pair, hop * SLABS + n, peer)

    ups, downs, cores = (up_send, up_recv), (down_s, down_recv), (core_send, core_recv)

    def pass_block(n, origin, hop, held, upward, downward):
        shard = 2 * origin + core
        if upward:

            @pl.when(has_above)
            def _():
                along(n, shard, hop, ups, above, held).start()

        if downward:

            @pl.when(has_below)
            def _():
                along(n, shard, hop, downs, below, held).start()

        along(n, shard, origin, cores, partner, held).start()

    norms = [
        remote(norm_send, norm_all.at[place, mine], pair, 21 + k - 1, to_dp(k)) for k in (1, 2, 3)
    ]
    trade = [
        remote(qkv_send.at[dp_peer(k)], w_qkv.at[place, mine], pair, k - 1, to_dp(k))
        for k in (1, 2, 3)
    ]
    own = [
        pltpu.make_async_copy(qkv_send.at[mine], w_qkv.at[place, mine], local.at[4]),
        pltpu.make_async_copy(out_send, w_out.at[place], local.at[5]),
        pltpu.make_async_copy(norm_send, norm_all.at[place, mine], local.at[6]),
        pltpu.make_async_copy(seg_ref, seg_0, local.at[7]),
        pltpu.make_async_copy(pos_ref, pos_0, local.at[13]),
    ]
    for copy in norms + trade:
        copy.start()
    pass_block(0, line, 0, source(0), True, True)
    pass_block(1, line, 0, source(1), True, True)
    for copy in own:
        copy.start()

    loads[1].wait()

    def permute_tokens(here):
        tok_low[here] = to_shards(tok_in[here].astype(FULL)).astype(LOW)

    in_chunks(tok_in.shape[0], permute_tokens)
    places = [
        remote(source, target, pair, base + k, to_dp(k + 1))
        for source, targets, base in (
            (seg_ref, (seg_1, seg_2, seg_3), 9),
            (pos_ref, (pos_1, pos_2, pos_3), 24),
        )
        for k, target in enumerate(targets)
    ]
    for copy in places:
        copy.start()
    tok = spread(tok_low, tok_all, pair, 3)
    keep = [
        pltpu.make_async_copy(tok_low, tok_all.at[0], local.at[8]),
        pltpu.make_async_copy(tok_low, tok_own, local.at[9]),
    ]
    for copy in keep:
        copy.start()

    own[2].wait()
    for copy in norms:
        copy.wait_recv()
    pass_block(2, line, 0, None, True, True)
    for k in (1, 2, 3):
        trade[k - 1].wait_recv()
        pass_block(2 + k, line, 0, None, True, True)

    loads[2].wait()
    for d in range(N_DP):
        for part in range(2):
            begin = part * FF + d * ff_width
            gu_send[d, :, part * ff_width : part * ff_width + ff_width] = mlp_in[
                :, begin : begin + ff_width
            ].astype(LOW)
        begin = 2 * FF + d * ff_width
        down_send[d] = mlp_in[:, begin : begin + ff_width].astype(LOW)
    blocks = []
    for n, (held, target) in enumerate(((gu_send, gu_out), (down_send, down_out))):
        for k in (3, 1, 2):
            blocks.append(
                remote(held.at[dp_peer(k)], target.at[mine], pair, 12 + 3 * n + k - 1, to_dp(k))
            )
        blocks.append(pltpu.make_async_copy(held.at[mine], target.at[mine], local.at[10 + n]))

    loads[3].wait()

    def permute_cotangent(here):
        cot_low[here] = to_shards(cot_in[here].astype(FULL)).astype(LOW)

    in_chunks(cot_in.shape[0], permute_cotangent)
    keep.append(pltpu.make_async_copy(cot_low, cot_own, local.at[12]))
    keep[2].start()

    def hop_step(hop):
        for n in range(SLABS):

            @pl.when(line >= hop)
            def _():
                shard = place - 2 * hop
                along(n, shard, hop - 1, ups, above).wait_recv()
                pass_block(n, line - hop, hop, None, True, False)

            @pl.when(line + hop < N_SH // 2)
            def _():
                shard = place + 2 * hop
                along(n, shard, hop - 1, downs, below).wait_recv()
                pass_block(n, line + hop, hop, None, False, True)

    hop_step(1)
    pass_on(*tok)
    for copy in blocks:
        copy.start()
    hop_step(2)
    hop_step(3)

    spread_end(*tok)
    for copy in blocks + own[:2] + own[3:] + keep + places:
        copy.wait()
    for copy in norms + trade:
        copy.wait_send()
    for hop in range(N_SH // 2 - 1):
        for n in range(SLABS):

            @pl.when(has_above & (line >= hop))
            def _():
                along(n, place - 2 * hop, hop, ups, above).wait_send()

            @pl.when(has_below & (line + hop < N_SH // 2))
            def _():
                along(n, place + 2 * hop, hop, downs, below).wait_send()

    for origin in range(N_SH // 2):
        for n in range(SLABS):
            along(n, 2 * origin + core, origin, cores, partner).wait_send()
            along(n, 2 * origin + 1 - core, origin, cores, partner).wait_recv()


def start(attn_master, mlp_master, norm_master, tokens, cotangent, segments, positions, number):
    rows = attn_master.shape[0]
    width, ff_width = D // N_DP, FF // N_DP
    seq = tokens.shape[0]
    norm_shape = (8, 128)
    hops = (N_SH // 2 - 1) * SLABS
    return pl.pallas_call(
        start_kernel,
        out_shape=[jax.ShapeDtypeStruct(segments.shape, segments.dtype)] * N_DP
        + [jax.ShapeDtypeStruct(positions.shape, positions.dtype)] * N_DP
        + [
            jax.ShapeDtypeStruct((N_SH, N_DP, rows, 3 * width), LOW),
            jax.ShapeDtypeStruct((N_SH, rows, D), LOW),
            jax.ShapeDtypeStruct((N_SH, N_DP) + norm_shape, FULL),
            jax.ShapeDtypeStruct((N_DP, seq, D), LOW),
            jax.ShapeDtypeStruct((N_DP, rows, 2 * ff_width), LOW),
            jax.ShapeDtypeStruct((N_DP, rows, ff_width), LOW),
            jax.ShapeDtypeStruct((seq, D), LOW),
            jax.ShapeDtypeStruct((seq, D), LOW),
        ],
        in_specs=[ANY, ANY, VMEM, ANY, ANY, ANY, ANY],
        out_specs=[ANY] * 16,
        scratch_shapes=[
            pltpu.VMEM(attn_master.shape, FULL),
            pltpu.VMEM(mlp_master.shape, FULL),
            pltpu.VMEM(tokens.shape, LOW),
            pltpu.VMEM(tokens.shape, LOW),
            pltpu.VMEM((N_DP, rows, 3 * width), LOW),
            pltpu.VMEM((rows, D), LOW),
            pltpu.VMEM(norm_shape, FULL),
            pltpu.VMEM((N_DP, rows, 2 * ff_width), LOW),
            pltpu.VMEM((N_DP, rows, ff_width), LOW),
            pltpu.VMEM(tokens.shape, LOW),
            pltpu.VMEM(tokens.shape, LOW),
        ]
        + sems(hops)
        + sems(hops)
        + sems((N_SH // 2) * SLABS)
        + sems(27)
        + [pltpu.SemaphoreType.DMA((14,))],
        compiler_params=comm_params(number),
        cost_estimate=cost(90),
        name="start",
    )(attn_master, mlp_master, norm_master, tokens, cotangent, segments, positions)


def unit_rows(values):
    average = jnp.mean(values, axis=-1, keepdims=True)
    centered = values - average
    variance = jnp.mean(centered * centered, axis=-1, keepdims=True)
    inverse = lax.rsqrt(variance + NORM_EPS)
    return centered * inverse, inverse


def turn(value, cos_ref, up_ref, down_ref, sign):
    left = pltpu.roll(value, 128 - ROT // 2, 1)
    right = pltpu.roll(value, ROT // 2, 1)
    return value * cos_ref[...] + sign * (left * up_ref[...] + right * down_ref[...])


def head_masks():
    lane = lax.broadcasted_iota(jnp.int32, (1, 128), 1)
    return [lane < HEAD, lane >= HEAD]


def softmax_rows(queries, keys, bias):
    scores = lax.dot_general(queries, keys, LAST_DIMS, preferred_element_type=FULL)
    scores = scores * (HEAD ** (-0.5)) + bias
    top = jnp.max(scores, axis=-1, keepdims=True)
    weights = jnp.exp(scores - top)
    return weights / jnp.sum(weights, axis=-1, keepdims=True)


def fill_tables(row, spot_row, rate_ref, cos_ref, up_ref, down_ref, mask_ref):
    seq = row.shape[-1]
    half = ROT // 2
    columns = jnp.transpose(jnp.broadcast_to(row, (8, seq)))[:, 0:1]
    spots = jnp.transpose(jnp.broadcast_to(spot_row, (8, seq)))[:, 0:1]
    angles = spots * rate_ref[0:1, :]
    lane = lax.broadcasted_iota(jnp.int32, (1, 128), 1) % HEAD
    sines = jnp.sin(angles)
    cos_ref[...] = jnp.where(lane < ROT, jnp.cos(angles), 1.0)
    up_ref[...] = jnp.where(lane < half, -sines, 0.0)
    down_ref[...] = jnp.where((lane >= half) & (lane < ROT), sines, 0.0)
    later = lax.broadcasted_iota(jnp.int32, (seq, seq), 0) >= lax.broadcasted_iota(
        jnp.int32, (seq, seq), 1
    )
    mask_ref[0] = jnp.where((columns == row) & later, 0.0, NEG_FILL)


def attn_forward_kernel(
    cot_ref, tok_ref, seg_0, seg_1, seg_2, seg_3, pos_0, pos_1, pos_2, pos_3, rate_ref, norm_all, w_ref,
    cot_all, norm_ref, normed_ref, q_ref, k_ref, v_ref, mix_ref, cos_ref, up_ref, down_ref, mask_ref,
    qkv_ref, b_ref, place_ref, send, recv,
):
    width = q_ref.shape[-1]
    step, last = pl.program_id(0), pl.num_programs(0) - 1
    mine = lax.axis_index("dp")
    sent = [
        remote(cot_ref, cot_all.at[k - 1], (send, recv), k - 1, to_dp(k)) for k in (1, 2)
    ]

    @pl.when(step == 0)
    def _():
        greet([to_dp(1), to_dp(2)])
        for copy in sent:
            copy.start()
        places = (seg_0, seg_1, seg_2, seg_3, pos_0, pos_1, pos_2, pos_3)
        for n, array in enumerate(places):
            place_ref[n : n + 1, :] = array[...].astype(FULL).reshape(1, array.shape[0])
        size = w_ref.shape[0] // (N_DP * N_SH)
        norm_ref[...] = jnp.concatenate(
            [norm_all[n, d, :, :size] for n in range(N_SH) for d in range(N_DP)], axis=1
        )
        for part in range(3):
            b_ref[0:1, part * width : part * width + width] = jnp.concatenate(
                [norm_all[n, mine, 2 + part : 3 + part, :size] for n in range(N_SH)], axis=1
            )

    fill_tables(
        place_ref[pl.ds(step, 1)],
        place_ref[pl.ds(N_DP + step, 1)],
        rate_ref,
        cos_ref,
        up_ref,
        down_ref,
        mask_ref,
    )
    unit, _ = unit_rows(tok_ref[0].astype(FULL))
    normed_ref[0] = (unit * norm_ref[0:1, :] + norm_ref[1:2, :]).astype(LOW)
    qkv_ref[...] = jnp.dot(normed_ref[0], w_ref[...], preferred_element_type=FULL) + b_ref[0:1, :]
    masks = head_masks()
    for pair in range(width // 128):
        here = slice(pair * 128, pair * 128 + 128)
        queries = turn(qkv_ref[:, here], cos_ref, up_ref, down_ref, 1.0).astype(LOW)
        there = slice(width + pair * 128, width + pair * 128 + 128)
        keys = turn(qkv_ref[:, there], cos_ref, up_ref, down_ref, 1.0).astype(LOW)
        there = slice(2 * width + pair * 128, 2 * width + pair * 128 + 128)
        values = qkv_ref[:, there].astype(LOW)
        q_ref[0, :, here] = queries
        k_ref[0, :, here] = keys
        v_ref[0, :, here] = values
        total = None
        for mask in masks:
            attend = softmax_rows(queries, jnp.where(mask, keys, 0), mask_ref[0])
            part = jnp.dot(
                attend.astype(LOW), jnp.where(mask, values, 0), preferred_element_type=FULL
            )
            total = part if total is None else total + part
        mix_ref[0, :, here] = total.astype(LOW)

    @pl.when(step == last)
    def _():
        for copy in sent:
            copy.wait()


def group_spec(array):
    return pl.BlockSpec((1,) + array.shape[1:], lambda g: (g, 0, 0))


def whole_spec(array):
    return pl.BlockSpec(array.shape, lambda g: (0,) * len(array.shape))


def attn_forward(cotangent, tokens, places, rates, norm_all, w_qkv, number):
    groups, seq, _ = tokens.shape
    width = w_qkv.shape[1] // 3
    row_spec = pl.BlockSpec((seq, 128), lambda g: (g, 0))
    part = jax.ShapeDtypeStruct((groups, seq, width), LOW)
    normed = jax.ShapeDtypeStruct(tokens.shape, LOW)
    norms = jax.ShapeDtypeStruct((8, D), FULL)
    near = jax.ShapeDtypeStruct((2,) + tokens.shape[1:], LOW)
    table = jax.ShapeDtypeStruct((groups * seq, 128), FULL)
    mask = jax.ShapeDtypeStruct((groups, seq, seq), FULL)
    return pl.pallas_call(
        attn_forward_kernel,
        grid=(groups,),
        out_shape=[near, norms, normed, part, part, part, part, table, table, table, mask],
        in_specs=[
            ANY,
            group_spec(tokens),
            *[VMEM] * len(places),
            whole_spec(rates),
            whole_spec(norm_all),
            whole_spec(w_qkv),
        ],
        out_specs=[ANY, whole_spec(norms), group_spec(normed)]
        + [group_spec(part)] * 4
        + [row_spec] * 3
        + [group_spec(mask)],
        scratch_shapes=[
            pltpu.VMEM((seq, 3 * width), FULL),
            pltpu.VMEM((8, 3 * width), FULL),
            pltpu.VMEM((2 * N_DP, seq), FULL),
        ]
        + sems(2),
        compiler_params=comm_params(number),
        cost_estimate=pl.CostEstimate(
            flops=2 * groups * seq * (D * 3 * width + 2 * seq * width * 2),
            bytes_accessed=2 * (w_qkv.size + 3 * tokens.size),
            transcendentals=groups * seq * seq * (width // HEAD),
        ),
        name="attn_forward",
    )(cotangent, tokens, *places, rates, norm_all, w_qkv)


def attn_backward_kernel(
    part_hbm, normed_hbm, mix_hbm, gao_hbm, resid_hbm, gao_ref, w_ref, q_ref, k_ref, v_ref,
    mask_ref, cos_ref, up_ref, down_ref,
    block_ref, grad_ref, sum_ref, attn_hbm,
    gm_ref, parts, normed, mix, gao, resid_ref, wo_grad, stage, grads_all, out, diag, full,
    send, recv, local,
):
    width = q_ref.shape[-1]
    rows = q_ref.shape[1]
    step, last = pl.program_id(0), pl.num_programs(0) - 1
    total = RowSum(parts, (out, diag, full), (send, recv), 0, source=part_hbm)
    loads = [
        pltpu.make_async_copy(part_hbm, parts, local.at[0]),
        pltpu.make_async_copy(mix_hbm, mix, local.at[1]),
        pltpu.make_async_copy(gao_hbm, gao, local.at[2]),
        pltpu.make_async_copy(normed_hbm, normed, local.at[3]),
        pltpu.make_async_copy(resid_hbm, resid_ref, local.at[4]),
    ]

    @pl.when(step == 0)
    def _():
        loads[0].start()
        greet([to_dp(1), to_dp(2)])
        for k in (3, 1, 2):
            total.send(k)
        for copy in loads[1:]:
            copy.start()
        sum_ref[...] = jnp.zeros_like(sum_ref)

    @pl.when(step == 2)
    def _():
        loads[0].wait()
        total.relay()

    scale = HEAD ** (-0.5)
    gm_ref[...] = lax.dot_general(
        gao_ref[0], w_ref[...], LAST_DIMS, preferred_element_type=FULL
    ).astype(LOW)
    masks = head_masks()
    for pair in range(width // 128):
        here = slice(pair * 128, pair * 128 + 128)
        queries, keys, values = q_ref[0, :, here], k_ref[0, :, here], v_ref[0, :, here]
        grads = gm_ref[:, here]
        grad_q = grad_k = grad_v = 0.0
        for mask in masks:
            keys_one = jnp.where(mask, keys, 0)
            attend = softmax_rows(queries, keys_one, mask_ref[0])
            grad_attend = lax.dot_general(
                grads, jnp.where(mask, values, 0), LAST_DIMS, preferred_element_type=FULL
            )
            grad_v += lax.dot_general(
                attend.astype(LOW),
                jnp.where(mask, grads, 0),
                LEAD_DIMS,
                preferred_element_type=FULL,
            )
            mean = jnp.sum(attend * grad_attend, axis=-1, keepdims=True)
            grad_scores = (attend * (grad_attend - mean)).astype(LOW)
            grad_q += jnp.dot(grad_scores, keys_one, preferred_element_type=FULL)
            grad_k += lax.dot_general(
                grad_scores, jnp.where(mask, queries, 0), LEAD_DIMS, preferred_element_type=FULL
            )
        grad_q = turn(grad_q * scale, cos_ref, up_ref, down_ref, -1.0)
        grad_k = turn(grad_k * scale, cos_ref, up_ref, down_ref, -1.0)
        for n, grad in enumerate((grad_q, grad_k, grad_v)):
            start = n * width + pair * 128
            grad_ref[0, :, start : start + 128] = grad.astype(LOW)
    grads_all[pl.ds(pl.multiple_of(step * rows, rows), rows)] = grad_ref[0]
    sum_ref[0:1, :] += jnp.sum(grad_ref[0].astype(FULL), axis=0, keepdims=True)

    @pl.when(step == last)
    def _():
        for copy in loads[1:]:
            copy.wait()

        for pair in range(width // 128):
            wo_grad[pair * 128 : pair * 128 + 128, :] = lax.dot_general(
                mix[:, pair * 128 : pair * 128 + 128],
                gao[...],
                LEAD_DIMS,
                preferred_element_type=FULL,
            ).astype(LOW)

        def store(index, slot):
            return pltpu.make_async_copy(stage.at[slot], attn_hbm.at[index], local.at[5 + slot])

        def one_shard(index, carry):
            slot = index % 2

            @pl.when(index >= 2)
            def _():
                store(index - 2, slot).wait()

            here = pl.ds(pl.multiple_of(index * 256, 256), 256)
            stage[slot, :, : 3 * width] = lax.dot_general(
                normed[:, here], grads_all[...], LEAD_DIMS, preferred_element_type=FULL
            ).astype(LOW)
            side = pl.ds(pl.multiple_of(index * 64, 64), 64)
            for part in range(N_DP):
                stage[slot, part * 64 : part * 64 + 64, 3 * width :] = wo_grad[
                    side, part * width : part * width + width
                ]
            store(index, slot).start()
            return carry

        lax.fori_loop(0, N_SH, one_shard, 0)
        for index in (N_SH - 2, N_SH - 1):
            store(index, index % 2).wait()
        total.finish()

        def body(here):
            block_ref[here] = to_places(resid_ref[here] + total.rows(here)).astype(LOW)

        in_chunks(rows, body)


def attn_backward(
    out_part, normed1, mixture, resid, gao, w_out, queries, keys, values, mask, tables, number
):
    groups, seq, cols = gao.shape
    width = queries.shape[-1]
    row_spec = pl.BlockSpec((seq, 128), lambda g: (g, 0))
    grad = jax.ShapeDtypeStruct((groups, seq, 3 * width), LOW)
    sums = jax.ShapeDtypeStruct((8, 3 * width), FULL)
    flat = groups * seq
    return pl.pallas_call(
        attn_backward_kernel,
        grid=(groups,),
        out_shape=[
            jax.ShapeDtypeStruct(resid.shape, LOW),
            grad,
            sums,
            jax.ShapeDtypeStruct((N_SH, D // N_SH, 4 * width), LOW),
        ],
        in_specs=[
            ANY,
            ANY,
            ANY,
            ANY,
            ANY,
            group_spec(gao),
            VMEM,
            group_spec(queries),
            group_spec(keys),
            group_spec(values),
            group_spec(mask),
            row_spec,
            row_spec,
            row_spec,
        ],
        out_specs=[VMEM, group_spec(grad), whole_spec(sums), ANY],
        scratch_shapes=[
            pltpu.VMEM((seq, width), LOW),
            pltpu.VMEM(gao.shape, LOW),
            pltpu.VMEM((flat, cols), LOW),
            pltpu.VMEM((flat, width), LOW),
            pltpu.VMEM((flat, cols), LOW),
            pltpu.VMEM(resid.shape, FULL),
            pltpu.VMEM((width, cols), LOW),
            pltpu.VMEM((2, D // N_SH, 4 * width), LOW),
            pltpu.VMEM((flat, 3 * width), LOW),
        ]
        + row_sum_scratch(seq, cols)
        + sems(6)
        + [pltpu.SemaphoreType.DMA((7,))],
        compiler_params=comm_params(number),
        cost_estimate=cost(55),
        name="attn_backward",
    )(
        out_part,
        normed1.reshape(flat, cols),
        mixture.reshape(flat, width),
        gao.reshape(flat, cols),
        resid,
        gao,
        w_out,
        queries,
        keys,
        values,
        mask,
        *tables,
    )


class RowSum:
    scratch = 3

    def __init__(self, parts, scratch, pair, base, pieces=1, column_base=0, source=None):
        self.parts, self.pair = parts, pair
        self.pieces, self.column_base = pieces, column_base
        self.out, self.diag, self.full = scratch
        self.half = parts.shape[1] // 2
        self.top, self.bottom = pl.ds(0, self.half), pl.ds(self.half, self.half)
        top, bottom = self.top, self.bottom
        parts = parts if source is None else source
        whole = [
            lambda: remote(parts.at[3, top], self.diag.at[0], pair, base + 0, to_dp(1)),
            lambda: remote(parts.at[3, bottom], self.diag.at[1], pair, base + 1, to_dp(2)),
        ]
        self.first = [make() if pieces == 1 else None for make in whole] + [
            remote(parts.at[1, top], self.full.at[0, top], pair, base + 2, to_dp(1)),
            remote(parts.at[2, bottom], self.full.at[1, bottom], pair, base + 3, to_dp(2)),
        ]
        self.second = [
            remote(self.out.at[0], self.full.at[0, bottom], pair, base + 4, to_dp(1)),
            remote(self.out.at[1], self.full.at[1, top], pair, base + 5, to_dp(2)),
        ]

    def send_columns(self, cols, index):
        for copy in self.column_copies(cols, index):
            copy.start()

    def column_copies(self, cols, index):
        here = pl.ds(cols.start, cols.stop - cols.start)
        return [
            remote(
                self.parts.at[3, rows, here],
                self.diag.at[side, rows_in, here],
                self.pair,
                self.column_base + 2 * index + side,
                to_dp(1 + side),
            )
            for side, rows, rows_in in (
                (0, self.top, pl.ds(0, self.half)),
                (1, self.bottom, pl.ds(0, self.half)),
            )
        ]

    def send(self, k):
        for copy in {3: self.first[:2], 1: self.first[2:3], 2: self.first[3:]}[k]:
            copy.start()

    def diag_wait(self, side):
        if self.pieces == 1:
            self.first[side].wait_recv()
            return
        size = self.parts.shape[2] // self.pieces
        for n in range(self.pieces):
            self.column_copies(slice(n * size, n * size + size), n)[side].wait_recv()

    def relay(self):
        self.diag_wait(1)
        self.out[0] = (
            self.parts[1, self.bottom].astype(FULL) + self.diag[1].astype(FULL)
        ).astype(LOW)
        self.second[0].start()
        self.diag_wait(0)
        self.out[1] = (self.parts[2, self.top].astype(FULL) + self.diag[0].astype(FULL)).astype(
            LOW
        )
        self.second[1].start()

    def finish(self):
        self.first[2].wait_recv()
        self.first[3].wait_recv()
        self.second[0].wait_recv()
        self.second[1].wait_recv()
        for copy in self.first[2:] + self.second:
            copy.wait_send()
        size = self.parts.shape[2] // self.pieces
        for n in range(self.pieces):
            if self.pieces > 1:
                for copy in self.column_copies(slice(n * size, n * size + size), n):
                    copy.wait_send()
        if self.pieces == 1:
            for copy in self.first[:2]:
                copy.wait_send()

    def rows(self, part):
        return (
            self.parts[0, part].astype(FULL)
            + self.full[0, part].astype(FULL)
            + self.full[1, part].astype(FULL)
        )


def row_sum_scratch(rows, cols):
    return [
        pltpu.VMEM((2, rows // 2, cols), LOW),
        pltpu.VMEM((2, rows // 2, cols), LOW),
        pltpu.VMEM((2, rows, cols), LOW),
    ]


def mid_forward_kernel(
    mix_ref, w_ref, tok_ref, norm_ref, resid_hbm, normed_all,
    resid_ref, parts, out, diag, full, own, send, recv, local,
):
    rows = tok_ref.shape[0]
    greet([to_dp(1), to_dp(2)])
    total = RowSum(parts, (out, diag, full), (send, recv), 0)
    for k in (3, 1, 2, 0):
        parts[k] = jnp.dot(mix_ref[k], w_ref[...], preferred_element_type=FULL).astype(LOW)
        if k:
            total.send(k)
    total.relay()
    total.finish()

    def body(here):
        resid = tok_ref[here].astype(FULL) + total.rows(here)
        resid_ref[here] = resid
        unit, _ = unit_rows(resid)
        own[here] = (unit * norm_ref[5:6, :] + norm_ref[6:7, :]).astype(LOW)

    in_chunks(rows, body)
    sent = spread(own, normed_all, (send, recv), 6)
    stores = [
        pltpu.make_async_copy(own, normed_all.at[0], local.at[0]),
        pltpu.make_async_copy(resid_ref, resid_hbm, local.at[1]),
    ]
    for copy in stores:
        copy.start()
    pass_on(*sent)
    spread_end(*sent)
    for copy in stores:
        copy.wait()


def mid_forward(mixture, w_out, tokens, norm_vals, number):
    rows, cols = tokens.shape
    group = (N_DP, rows, cols)
    return pl.pallas_call(
        mid_forward_kernel,
        out_shape=[
            jax.ShapeDtypeStruct(tokens.shape, FULL),
            jax.ShapeDtypeStruct(group, LOW),
        ],
        in_specs=[VMEM] * 4,
        out_specs=[ANY, ANY],
        scratch_shapes=[pltpu.VMEM((rows, cols), FULL), pltpu.VMEM(group, LOW)]
        + row_sum_scratch(rows, cols)
        + [pltpu.VMEM((rows, cols), LOW)]
        + sems(12)
        + [pltpu.SemaphoreType.DMA((2,))],
        compiler_params=comm_params(number),
        cost_estimate=cost(92),
        name="mid_forward",
    )(mixture, w_out, tokens, norm_vals)


def mid_backward_kernel(
    x_hbm, own_cot, near_hbm, far_hbm, wgu_hbm, wdown_hbm, gate_hbm, up_hbm, resid_hbm, norm_ref,
    grad_hbm, own_hbm, sum_ref, part_hbm,
    left, w_gu, w_down, gate_stage, up_stage, ggu, resid_ref, grad_ref, parts,
    out, diag, full, own, send, recv, local, loads, pair_send, pair_recv, pair_local, ready,
):
    rows, cols = resid_ref.shape
    width = w_down.shape[1]
    pieces = 4
    size = cols // pieces
    order = (3, 1, 2, 0)
    seqs = [pl.ds(k * rows, rows) for k in range(N_DP)]
    sources = (own_cot, near_hbm.at[0], near_hbm.at[1], far_hbm)

    def data(k):
        return pltpu.make_async_copy(sources[k], left.at[seqs[k]], local.at[k])

    def stage_loads(n):
        k = order[n]
        return [
            pltpu.make_async_copy(source.at[seqs[k]], stage.at[n % 2], loads.at[2 * (n % 2) + i])
            for i, (source, stage) in enumerate(((gate_hbm, gate_stage), (up_hbm, up_stage)))
        ]

    weights = [
        pltpu.make_async_copy(
            wgu_hbm.at[pl.ds(2 * n, 2)], w_gu.at[pl.ds(2 * n, 2)], local.at[4 + n]
        )
        for n in range(pieces)
    ]
    down_load = pltpu.make_async_copy(wdown_hbm, w_down, loads.at[4])
    later = [
        pltpu.make_async_copy(resid_hbm, resid_ref, local.at[8]),
        pltpu.make_async_copy(own_cot, own, local.at[9]),
    ]
    for copy in [data(3), down_load] + stage_loads(0) + weights[:2] + [data(1)] + stage_loads(1):
        copy.start()
    for copy in weights[2:] + [data(2), data(0)] + later:
        copy.start()
    greet([to_dp(1), to_dp(2), partner()])

    total = RowSum(parts, (out, diag, full), (send, recv), 0, pieces, 6)
    down_load.wait()
    for n, k in enumerate(order):
        data(k).wait()
        for copy in stage_loads(n):
            copy.wait()
        here = slice(k * rows, k * rows + rows)
        for begin, end in column_cuts(width):
            grad = jnp.dot(left[here], w_down[:, begin:end], preferred_element_type=FULL)
            gate, up = gate_stage[n % 2, :, begin:end], up_stage[n % 2, :, begin:end]
            sig = 1.0 / (1.0 + jnp.exp(-gate))
            ggu[here, begin:end] = (grad * up * sig * (1.0 + gate * (1.0 - sig))).astype(LOW)
            ggu[here, width + begin : width + end] = (grad * gate * sig).astype(LOW)
        if n + 2 < N_DP:
            for copy in stage_loads(n + 2):
                copy.start()
        for piece in range(pieces):
            if n == 0:
                weights[piece].wait()
            columns = slice(piece * size, piece * size + size)
            parts[k, :, columns] = lax.dot_general(
                ggu[here],
                w_gu[2 * piece : 2 * piece + 2].reshape(size, 2 * width),
                LAST_DIMS,
                preferred_element_type=FULL,
            ).astype(LOW)
            if n == 0:
                total.send_columns(columns, piece)
        if k and n:
            total.send(k)
    reload = pltpu.make_async_copy(x_hbm, left, local.at[10])
    reload.start()
    pl.semaphore_signal(ready, inc=1, device_id=partner(), device_id_type=MESH)
    sum_ref[...] = jnp.zeros_like(sum_ref)
    total.relay()
    reload.wait()
    pl.semaphore_wait(ready, 1)
    buffers = (w_gu.at[pl.ds(4, 2)], w_gu.at[pl.ds(0, 4)], w_gu.at[pl.ds(6, 2)])
    grad = PairGrad(left, ggu, part_hbm, buffers + (pair_send, pair_recv, pair_local))
    grad.run()
    for copy in later:
        copy.wait()
    total.finish()

    def body(here):
        grads = total.rows(here)
        unit, inverse = unit_rows(resid_ref[here])
        sum_ref[0:1, :] += jnp.sum(grads * unit, axis=0, keepdims=True)
        sum_ref[1:2, :] += jnp.sum(grads, axis=0, keepdims=True)
        grad = own[here].astype(FULL) + layer_back(grads, norm_ref[5:6, :], unit, inverse)
        grad_ref[here] = grad
        own[here] = grad.astype(LOW)

    in_chunks(rows, body)
    stores = [
        pltpu.make_async_copy(own, own_hbm, local.at[0]),
        pltpu.make_async_copy(grad_ref, grad_hbm, local.at[1]),
    ]
    for copy in stores:
        copy.start()
    grad.end()
    for copy in stores:
        copy.wait()


def mid_backward(
    normed2, cotangent, near, far, w_gu, w_down, gate, up, resid, norm_vals, number
):
    rows, cols = resid.shape
    total, width = gate.shape
    blocks = (N_SH, cols // N_SH, 2 * width)
    return pl.pallas_call(
        mid_backward_kernel,
        out_shape=[
            jax.ShapeDtypeStruct(resid.shape, FULL),
            jax.ShapeDtypeStruct(resid.shape, LOW),
            jax.ShapeDtypeStruct((8, cols), FULL),
            jax.ShapeDtypeStruct((N_SH // 2,) + blocks[1:], LOW),
        ],
        in_specs=[ANY] * 9 + [VMEM],
        out_specs=[ANY, ANY, VMEM, ANY],
        scratch_shapes=[
            pltpu.VMEM(normed2.shape, LOW),
            pltpu.VMEM(blocks, LOW),
            pltpu.VMEM(w_down.shape, LOW),
            pltpu.VMEM((2, rows, width), FULL),
            pltpu.VMEM((2, rows, width), FULL),
            pltpu.VMEM((total, 2 * width), LOW),
            pltpu.VMEM(resid.shape, FULL),
            pltpu.VMEM(resid.shape, FULL),
            pltpu.VMEM((N_DP, rows, cols), LOW),
        ]
        + row_sum_scratch(rows, cols)
        + [pltpu.VMEM((rows, cols), LOW)]
        + sems(14)
        + [pltpu.SemaphoreType.DMA((11,)), pltpu.SemaphoreType.DMA((6,))]
        + sems(N_SH // 2)
        + [pltpu.SemaphoreType.DMA((2,)), pltpu.SemaphoreType.REGULAR],
        compiler_params=comm_params(number),
        cost_estimate=cost(70),
        name="mid_backward",
    )(normed2, cotangent, near, far, w_gu.reshape(blocks), w_down, gate, up, resid, norm_vals)


def share_kernel(own_ref, hid_hbm, wdown_hbm, gao_all, part_hbm, hid, w_down, part_ref, send, recv, local):
    loads = [
        pltpu.make_async_copy(wdown_hbm, w_down, local.at[0]),
        pltpu.make_async_copy(hid_hbm, hid, local.at[1]),
    ]
    for copy in loads:
        copy.start()
    greet([to_dp(1), to_dp(2)])
    sent = spread(own_ref, gao_all, (send, recv), 0)
    stores = [pltpu.make_async_copy(own_ref, gao_all.at[0], local.at[2])]
    stores[0].start()
    for copy in loads:
        copy.wait()
    for k in range(N_DP):
        part_ref[k] = lax.dot_general(
            hid[k], w_down[...], LAST_DIMS, preferred_element_type=FULL
        ).astype(LOW)
        stores.append(pltpu.make_async_copy(part_ref.at[k], part_hbm.at[k], local.at[3 + k]))
        stores[-1].start()
    pass_on(*sent)
    spread_end(*sent)
    for copy in stores:
        copy.wait()


def share(own, hidden, w_down, number):
    group = jax.ShapeDtypeStruct((N_DP,) + own.shape, LOW)
    return pl.pallas_call(
        share_kernel,
        out_shape=[group, group],
        in_specs=[VMEM, ANY, ANY],
        out_specs=[ANY, ANY],
        scratch_shapes=[
            pltpu.VMEM(hidden.shape, LOW),
            pltpu.VMEM(w_down.shape, LOW),
            pltpu.VMEM(group.shape, LOW),
        ]
        + sems(6)
        + [pltpu.SemaphoreType.DMA((3 + N_DP,))],
        compiler_params=comm_params(number),
        cost_estimate=cost(48),
        name="share",
    )(own, hidden, w_down)


LINE = N_SH // 2
PIECES = 4


class LineSum:
    def __init__(self, terms_hbm, scratch, sem_refs):
        (self.terms, self.other, self.up_in, self.down_in, self.up_out, self.down_out) = scratch
        self.hbm = terms_hbm
        (core_s, core_r, up_s, up_r, down_s, down_r, self.local) = sem_refs
        self.core_sems, self.up_sems, self.down_sems = (core_s, core_r), (up_s, up_r), (down_s, down_r)
        mine, place = lax.axis_index("dp"), lax.axis_index("shard")
        self.line, self.core = place // 2, place % 2
        self.above, self.below = (mine, place + 2), (mine, place - 2)
        self.partner = (mine, place + 1 - 2 * self.core)
        self.size = self.terms.shape[1] // PIECES
        self.steps = (LINE - 1) * PIECES

    def at_end(self):
        return (self.line == 0) | (self.line == LINE - 1)

    def rows(self, piece):
        return pl.ds(pl.multiple_of(piece * self.size, self.size), self.size)

    def core_copy(self, target, piece):
        here = self.rows(piece)
        return remote(
            self.hbm.at[2 * target + 1 - self.core, here],
            self.other.at[target, here],
            self.core_sems,
            target * PIECES + piece,
            self.partner,
        )

    def load(self, target):
        return pltpu.make_async_copy(
            self.hbm.at[2 * target + self.core], self.terms.at[target], self.local.at[target]
        )

    def load_all(self):
        for target in (LINE - 1, 0, LINE - 2, 1):
            self.load(target).start()

    def start(self):
        for targets in ((LINE - 1, 0), (LINE - 2, 1)):
            for piece in range(PIECES):
                for target in targets:
                    self.core_copy(target, piece).start()

    def own(self, target, piece):
        @pl.when(piece == 0)
        def _():
            self.load(target).wait()

        self.core_copy(target, piece).wait_recv()
        here = self.rows(piece)
        return self.terms[target, here].astype(FULL) + self.other[target, here].astype(FULL)

    def up_copy(self, index):
        return remote(
            self.up_out.at[index], self.up_in.at[index], self.up_sems, index, self.above
        )

    def down_copy(self, index):
        return remote(
            self.down_out.at[index], self.down_in.at[index], self.down_sems, index, self.below
        )

    def up(self, index):
        target, piece = LINE - 1 - index // PIECES, index % PIECES

        @pl.when(target > self.line)
        def _():
            self.up_out[index] = self.own(target, piece).astype(LOW)

            @pl.when(self.line > 0)
            def _():
                self.up_copy(index).wait_recv()
                self.up_out[index] = (
                    self.up_out[index].astype(FULL) + self.up_in[index].astype(FULL)
                ).astype(LOW)

            self.up_copy(index).start()

    def down(self, index):
        target, piece = index // PIECES, index % PIECES

        @pl.when(target < self.line)
        def _():
            self.down_out[index] = self.own(target, piece).astype(LOW)

            @pl.when(self.line < LINE - 1)
            def _():
                self.down_copy(index).wait_recv()
                self.down_out[index] = (
                    self.down_out[index].astype(FULL) + self.down_in[index].astype(FULL)
                ).astype(LOW)

            self.down_copy(index).start()

    def run(self, begin, end):
        def step(index, carry):
            @pl.when(self.line < LINE // 2)
            def _():
                @pl.when(index < self.steps)
                def _():
                    self.up(index)

                @pl.when(index > 0)
                def _():
                    self.down(index - 1)

            @pl.when(self.line >= LINE // 2)
            def _():
                @pl.when(index < self.steps)
                def _():
                    self.down(index)

                @pl.when(index > 0)
                def _():
                    self.up(index - 1)

            return carry

        lax.fori_loop(begin, end, step, 0)

    def finish(self, piece, result):
        here = self.rows(piece)
        result[here] = self.own(self.line, piece)

        @pl.when(self.line > 0)
        def _():
            index = (LINE - 1 - self.line) * PIECES + piece
            self.up_copy(index).wait_recv()
            result[here] = result[here] + self.up_in[index].astype(FULL)

        @pl.when(self.line < LINE - 1)
        def _():
            index = self.line * PIECES + piece
            self.down_copy(index).wait_recv()
            result[here] = result[here] + self.down_in[index].astype(FULL)

    def drain(self):
        def step(index, carry):
            @pl.when(LINE - 1 - index // PIECES > self.line)
            def _():
                self.up_copy(index).wait_send()

            @pl.when(index // PIECES < self.line)
            def _():
                self.down_copy(index).wait_send()

            return carry

        lax.fori_loop(0, self.steps, step, 0)

        def step_core(index, carry):
            self.core_copy(index // PIECES, index % PIECES).wait_send()
            return carry

        lax.fori_loop(0, LINE * PIECES, step_core, 0)


def line_sum_scratch(rows, cols):
    steps = (LINE - 1) * PIECES
    return (
        [pltpu.VMEM((LINE, rows, cols), LOW)] * 2
        + [pltpu.VMEM((steps, rows // PIECES, cols), LOW)] * 4
        + sems(LINE * PIECES)
        + sems(steps)
        + sems(steps)
        + [pltpu.SemaphoreType.DMA((LINE,))]
    )


def fold(values, total):
    values = values * values
    for start in range(0, values.shape[1], 128):
        total = total + values[:, start : start + 128]
    return total


def last_kernel(
    attn_hbm, grad_qkv_hbm, w_hbm, gu_hbm, down_hbm, tok_hbm, grad_hbm, norm_ref, bias_ref, two_ref,
    input_hbm, norm_total_ref, gu_out, down_out, qkv_out, out_ref, total_ref,
    grad_qkv_ref, w_ref, tok_ref, grad_ref, gu_in, down_in_low,
    parts, out, diag, full, sum_ref, near, far, part, near_part, far_part, attn_sum, attn_low,
    terms, other, up_in, down_in, up_out, down_out_pieces,
    core_s, core_r, up_s, up_r, down_s, down_r, term_local,
    send, recv, send_a, recv_a, send_b, recv_b, send_c, recv_c, send_d, recv_d, local,
):
    rows = tok_ref.shape[0]
    mine, place = lax.axis_index("dp"), lax.axis_index("shard")
    loads = [
        pltpu.make_async_copy(source, target, local.at[3 + n])
        for n, (source, target) in enumerate(
            (
                (w_hbm, w_ref),
                (grad_qkv_hbm, grad_qkv_ref),
                (tok_hbm, tok_ref),
                (grad_hbm, grad_ref),
                (gu_hbm, gu_in),
                (down_hbm, down_in_low),
            )
        )
    ]
    line = LineSum(
        attn_hbm,
        (terms, other, up_in, down_in, up_out, down_out_pieces),
        (core_s, core_r, up_s, up_r, down_s, down_r, term_local),
    )
    line.load_all()
    for copy in loads:
        copy.start()
    greet([to_dp(k) for k in (1, 2, 3)] + [to_shard(j) for j in range(1, N_SH)])
    line.start()
    total = RowSum(parts, (out, diag, full), (send, recv), 0)
    blocks = []
    for n, (held, target) in enumerate(((gu_hbm, gu_out), (down_hbm, down_out))):
        for k in (3, 1, 2):
            blocks.append(
                remote(
                    held.at[dp_peer(k)], target.at[mine], (send_c, recv_c), 3 * n + k - 1, to_dp(k)
                )
            )
    keeps = [
        pltpu.make_async_copy(gu_in.at[mine], gu_out.at[mine], local.at[0]),
        pltpu.make_async_copy(down_in_low.at[mine], down_out.at[mine], local.at[1]),
    ]
    for copy in blocks[3:]:
        copy.start()
    middle = jnp.logical_not(line.at_end())
    line.run(0, 1)

    def norm1_part(k):
        parts[k] = lax.dot_general(
            grad_qkv_ref[k], w_ref[...], LAST_DIMS, preferred_element_type=FULL
        ).astype(LOW)
        if k:
            total.send(k)

    def middle_run(begin, end):
        @pl.when(middle)
        def _():
            line.run(begin, end)

    loads[0].wait()
    loads[1].wait()
    norm1_part(3)

    @pl.when(line.at_end())
    def _():
        line.run(1, line.steps + 1)

    middle_run(1, 2)
    norm1_part(1)
    middle_run(2, 3)
    norm1_part(2)
    middle_run(3, 4)
    norm1_part(0)
    sum_ref[...] = jnp.zeros_like(sum_ref)
    sum_ref[5:7, :] = two_ref[0:2, :]
    bias_width = bias_ref.shape[1] // 3
    for d in range(N_DP):

        @pl.when(mine == d)
        def _(d=d):
            for n in range(3):
                sum_ref[2 + n : 3 + n, d * bias_width : (d + 1) * bias_width] = bias_ref[
                    0:1, n * bias_width : (n + 1) * bias_width
                ]

    middle_run(4, 6)
    total.relay()
    for copy in blocks[:3]:
        copy.start()
    loads[4].wait()
    loads[5].wait()
    for copy in keeps:
        copy.start()

    def square_low(array, value):
        def step(index, value):
            here = pl.ds(pl.multiple_of(index * 16, 16), 16)
            for k in range(N_DP):
                rows16 = array[k, here].astype(FULL)
                value = fold(rows16[8:], fold(rows16[:8], value))
            return value

        return lax.fori_loop(0, array.shape[1] // 16, step, value)

    part[...] = square_low(down_in_low, square_low(gu_in, jnp.zeros(part.shape, FULL)))
    middle_run(6, 9)
    total.finish()
    loads[2].wait()
    loads[3].wait()

    def body(here):
        grads = total.rows(here)
        unit, inverse = unit_rows(tok_ref[here].astype(FULL))
        sum_ref[0:1, :] += jnp.sum(grads * unit, axis=0, keepdims=True)
        sum_ref[1:2, :] += jnp.sum(grads, axis=0, keepdims=True)
        grad_ref[here] = to_places(
            grad_ref[here] + layer_back(grads, norm_ref[0:1, :], unit, inverse)
        )

    in_chunks(rows, body)
    keeps.append(pltpu.make_async_copy(grad_ref, input_hbm, local.at[9]))
    keeps[-1].start()
    norm_near = [
        remote(sum_ref, near.at[k - 1], (send_a, recv_a), k - 1, to_dp(k)) for k in (1, 2, 3)
    ]
    for copy in norm_near:
        copy.start()
    for copy in norm_near:
        copy.wait()
    sum_ref[...] = sum_ref[...] + near[0] + near[1] + near[2]
    norm_far = [
        remote(sum_ref, far.at[j - 1], (send_b, recv_b), j - 1, to_shard(j))
        for j in range(1, N_SH)
    ]
    for copy in norm_far:
        copy.start()

    width = qkv_out.shape[-1]
    size = qkv_out.shape[1]

    def trade(sender, owner):
        return pltpu.make_async_remote_copy(
            src_ref=attn_low.at[owner],
            dst_ref=qkv_out.at[sender],
            send_sem=send_d.at[owner],
            recv_sem=recv_d.at[sender],
            device_id=(owner, place),
            device_id_type=MESH,
        )

    squares = part[...]
    for d in range(N_DP):
        line.finish(d, attn_sum)

        def square(index, value, d=d):
            here = pl.ds(pl.multiple_of(d * size + index * 8, 8), 8)
            return fold(attn_sum[here], value)

        squares = lax.fori_loop(0, size // 8, square, squares)
        if d == N_DP - 1:
            part[...] = squares
            small = [
                remote(part, near_part.at[k - 1], (send_a, recv_a), 2 + k, to_dp(k))
                for k in (1, 2, 3)
            ]
            for copy in small:
                copy.start()
        attn_low[d] = attn_sum[d * size : d * size + size, :width].astype(LOW)

        @pl.when(mine != d)
        def _(d=d):
            trade(mine, d).start()

    keep = pltpu.make_async_copy(attn_low.at[mine], qkv_out.at[mine], local.at[2])
    keep.start()
    for copy in small:
        copy.wait()
    part[...] = part[...] + near_part[0] + near_part[1] + near_part[2]
    small = [
        remote(part, far_part.at[j - 1], (send_b, recv_b), N_SH - 2 + j, to_shard(j))
        for j in range(1, N_SH)
    ]
    for copy in small:
        copy.start()
    out_ref[...] = to_places(
        jnp.concatenate(
            [attn_sum[d * size : d * size + size, width:] for d in range(N_DP)], axis=1
        )
    )
    for copy in norm_far:
        copy.wait()
    norm_total = sum_ref[...]
    for j in range(N_SH - 1):
        norm_total = norm_total + far[j]
    norm_total_ref[...] = norm_total
    squares = fold(norm_total, part[...])
    for copy in small:
        copy.wait()
    for j in range(N_SH - 1):
        squares = squares + far_part[j]
    total_ref[0, 0] = jnp.sum(squares)
    line.drain()
    for copy in blocks + keeps + [keep]:
        copy.wait()
    for d in range(N_DP):

        @pl.when(mine != d)
        def _(d=d):
            trade(mine, d).wait_send()
            trade(d, mine).wait_recv()


def last(
    part_attn, grad_qkv, w_qkv, gu_sum, down_sum, tokens, grad_resid, norm_vals, biases, sums, number
):
    rows, cols = tokens.shape
    rest = sums
    square_shape = (8, 128)
    block = part_attn.shape[1:]
    width = grad_qkv.shape[-1]
    size = block[0] // N_DP
    return pl.pallas_call(
        last_kernel,
        out_shape=[
            jax.ShapeDtypeStruct(tokens.shape, FULL),
            jax.ShapeDtypeStruct(rest.shape, FULL),
            jax.ShapeDtypeStruct(gu_sum.shape, gu_sum.dtype),
            jax.ShapeDtypeStruct(down_sum.shape, down_sum.dtype),
            jax.ShapeDtypeStruct((N_DP, size, width), LOW),
            jax.ShapeDtypeStruct((size, D), FULL),
            jax.ShapeDtypeStruct((1, 1), FULL),
        ],
        in_specs=[ANY] * 7 + [VMEM] * 3,
        out_specs=[ANY, VMEM, ANY, ANY, ANY, VMEM, pl.BlockSpec(memory_space=pltpu.SMEM)],
        scratch_shapes=[
            pltpu.VMEM(a.shape, a.dtype)
            for a in (grad_qkv, w_qkv, tokens, grad_resid, gu_sum, down_sum)
        ]
        + [pltpu.VMEM((N_DP, rows, cols), LOW)]
        + row_sum_scratch(rows, cols)
        + [
            pltpu.VMEM(rest.shape, FULL),
            pltpu.VMEM((N_DP - 1,) + rest.shape, FULL),
            pltpu.VMEM((N_SH - 1,) + rest.shape, FULL),
            pltpu.VMEM(square_shape, FULL),
            pltpu.VMEM((N_DP - 1,) + square_shape, FULL),
            pltpu.VMEM((N_SH - 1,) + square_shape, FULL),
            pltpu.VMEM(block, FULL),
            pltpu.VMEM((N_DP, size, width), LOW),
        ]
        + line_sum_scratch(*block)
        + sems(6)
        + sems(2 * (N_DP - 1))
        + sems(2 * (N_SH - 1))
        + sems(6)
        + sems(N_DP)
        + [pltpu.SemaphoreType.DMA((10,))],
        compiler_params=comm_params(number),
        cost_estimate=cost(90),
        name="last",
    )(
        part_attn,
        grad_qkv,
        w_qkv,
        gu_sum,
        down_sum,
        tokens,
        grad_resid,
        norm_vals,
        biases,
        sums,
    )


def column_cuts(cols):
    return [(c, min(c + 256, cols)) for c in range(0, cols, 256)]


class PairGrad:
    def __init__(self, left, right, target, scratch):
        self.left, self.right, self.target = left, right, target
        self.give, self.take, self.keep, send, recv, self.local = scratch
        self.pair = (send, recv)
        place = lax.axis_index("shard")
        self.core = place % 2
        self.partner = (lax.axis_index("dp"), place + 1 - 2 * self.core)
        self.size, self.count = self.give.shape[1], self.take.shape[0]

    def move(self, index):
        return remote(
            self.give.at[index % 2], self.take.at[index], self.pair, index, self.partner
        )

    def store(self, index):
        return pltpu.make_async_copy(
            self.keep.at[index % 2], self.target.at[index], self.local.at[index % 2]
        )

    def fill(self, target, index):
        here = pl.ds(pl.multiple_of(index * self.size, self.size), self.size)
        cols = self.right.shape[1]
        half = cols // 2 if cols > 2048 else cols
        for begin in range(0, cols, half):
            target[:, begin : begin + half] = lax.dot_general(
                self.left[:, here],
                self.right[:, begin : begin + half],
                LEAD_DIMS,
                preferred_element_type=FULL,
            ).astype(LOW)

    def add(self, index):
        self.move(index).wait_recv()
        slot = index % 2
        self.keep[slot] = (self.keep[slot].astype(FULL) + self.take[index].astype(FULL)).astype(LOW)
        self.store(index).start()

    def run(self):
        def step(index, carry):
            @pl.when(index >= 2)
            def _():
                self.move(index - 2).wait_send()
                self.store(index - 2).wait()

            self.fill(self.give.at[index % 2], 2 * index + 1 - self.core)
            self.move(index).start()
            self.fill(self.keep.at[index % 2], 2 * index + self.core)

            @pl.when(index >= 1)
            def _():
                self.add(index - 1)

            return carry

        lax.fori_loop(0, self.count, step, 0)
        self.add(self.count - 1)

    def end(self):
        for index in (self.count - 2, self.count - 1):
            self.move(index).wait_send()
            self.store(index).wait()


def pair_grad_scratch(rows, cols):
    size = rows // N_SH
    count = N_SH // 2
    return [
        pltpu.VMEM((2, size, cols), LOW),
        pltpu.VMEM((count, size, cols), LOW),
        pltpu.VMEM((2, size, cols), LOW),
        *sems(count),
        pltpu.SemaphoreType.DMA((2,)),
    ]


def partner():
    place = lax.axis_index("shard")
    return (lax.axis_index("dp"), place + 1 - 2 * (place % 2))


def mlp_one_kernel(
    x_hbm, own_hbm, near_hbm, wgu_hbm, hid_out, gate_out, up_out, part_out, far_out,
    x_ref, cot_ref, w_gu, hid, gate_stage, up_stage, local, loads, stores, send, recv,
    *grad_scratch,
):
    total = x_ref.shape[0]
    known = N_DP - 1
    seq = total // N_DP
    half = seq // 2
    greet([to_dp(1), to_dp(2), partner()])
    passed = [
        remote(
            near_hbm.at[0, pl.ds(0, half)],
            cot_ref.at[pl.ds(known * seq, half)],
            (send, recv),
            0,
            to_dp(2),
        ),
        remote(
            near_hbm.at[1, pl.ds(half, half)],
            cot_ref.at[pl.ds(known * seq + half, half)],
            (send, recv),
            1,
            to_dp(1),
        ),
    ]
    for copy in passed:
        copy.start()
    cols = hid.shape[1]
    cuts = column_cuts(cols)
    block = total // 2

    def weight_loads(n):
        begin, end = cuts[n]
        return [
            pltpu.make_async_copy(
                wgu_hbm.at[:, pl.ds(at, end - begin)],
                w_gu.at[:, pl.ds(at, end - begin)],
                loads.at[2 * n + i],
            )
            for i, at in enumerate((begin, cols + begin))
        ]

    def stage_stores(n):
        begin, end = cuts[n]
        return [
            pltpu.make_async_copy(
                stage.at[n % 2, :, pl.ds(0, end - begin)],
                target.at[:, pl.ds(begin, end - begin)],
                stores.at[2 * i + n % 2],
            )
            for i, (stage, target) in enumerate(((gate_stage, gate_out), (up_stage, up_out)))
        ]

    data = [pltpu.make_async_copy(x_hbm, x_ref, local.at[0])]
    for copy in weight_loads(0) + data:
        copy.start()
    for n in range(1, len(cuts)):
        for copy in weight_loads(n):
            copy.start()
    data += [
        pltpu.make_async_copy(source, cot_ref.at[pl.ds(k * seq, seq)], local.at[5 + k])
        for k, source in enumerate((own_hbm, near_hbm.at[0], near_hbm.at[1]))
    ]
    for copy in data[1:]:
        copy.start()
    data[0].wait()
    for n, (begin, end) in enumerate(cuts):
        for copy in weight_loads(n):
            copy.wait()
        if n >= 2:
            for copy in stage_stores(n - 2):
                copy.wait()

        def rows(index, carry, begin=begin, end=end, slot=n % 2):
            here = pl.ds(pl.multiple_of(index * block, block), block)
            gate = jnp.dot(x_ref[here], w_gu[:, begin:end], preferred_element_type=FULL)
            up = jnp.dot(
                x_ref[here], w_gu[:, cols + begin : cols + end], preferred_element_type=FULL
            )
            hid[here, begin:end] = (gate / (1.0 + jnp.exp(-gate)) * up).astype(LOW)
            gate_stage[slot, here, : end - begin] = gate
            up_stage[slot, here, : end - begin] = up
            return carry

        lax.fori_loop(0, total // block, rows, 0)
        for copy in stage_stores(n):
            copy.start()
    outs = [
        pltpu.make_async_copy(hid, hid_out, local.at[2]),
        pltpu.make_async_copy(cot_ref.at[pl.ds(known * seq, seq)], far_out, local.at[1]),
    ]
    outs[0].start()
    for copy in data[1:]:
        copy.wait()
    for copy in passed:
        copy.wait()
    outs[1].start()
    grad = PairGrad(cot_ref, hid, part_out, grad_scratch)
    grad.run()
    for n in (len(cuts) - 2, len(cuts) - 1):
        for copy in stage_stores(n):
            copy.wait()
    grad.end()
    for copy in outs:
        copy.wait()


def mlp_one(normed2, cotangent, near, w_gu, number):
    total, width = normed2.shape
    cols = w_gu.shape[1] // 2
    values = jax.ShapeDtypeStruct((total, cols), FULL)
    return pl.pallas_call(
        mlp_one_kernel,
        out_shape=[
            jax.ShapeDtypeStruct((total, cols), LOW),
            values,
            values,
            jax.ShapeDtypeStruct((N_SH // 2, width // N_SH, cols), LOW),
            jax.ShapeDtypeStruct(cotangent.shape, LOW),
        ],
        in_specs=[ANY] * 4,
        out_specs=[ANY] * 5,
        scratch_shapes=[
            pltpu.VMEM((total, width), LOW),
            pltpu.VMEM((total, width), LOW),
            pltpu.VMEM((width, 2 * cols), LOW),
            pltpu.VMEM((total, cols), LOW),
            pltpu.VMEM((2, total, 256), FULL),
            pltpu.VMEM((2, total, 256), FULL),
            pltpu.SemaphoreType.DMA((8,)),
            pltpu.SemaphoreType.DMA((2 * len(column_cuts(cols)),)),
            pltpu.SemaphoreType.DMA((4,)),
        ]
        + sems(2)
        + pair_grad_scratch(width, cols),
        compiler_params=comm_params(number),
        cost_estimate=cost(30),
        name="mlp_one",
    )(normed2, cotangent, near, w_gu)


FIRST_HAT = 1.0 / (1.0 - BETA_ONE**STEP)
SECOND_HAT = 1.0 / (1.0 - BETA_TWO**STEP)


def clip_factor(total_ref, width):
    total = jnp.full((1, width), total_ref[0, 0], FULL)
    return CLIP_NORM / jnp.maximum(jnp.sqrt(total), CLIP_NORM)


def adam_step(grads, factor, master, first, second):
    clipped = grads.astype(FULL) * factor
    first_new = BETA_ONE * first + (1.0 - BETA_ONE) * clipped
    second_new = BETA_TWO * second + (1.0 - BETA_TWO) * clipped * clipped
    ratio = first_new * (RATE_MATRIX * FIRST_HAT) / (jnp.sqrt(second_new * SECOND_HAT) + ADAM_EPS)
    return (master * (1.0 - RATE_MATRIX * DECAY_MATRIX) - ratio, first_new, second_new)


def adam_kernel(
    total_ref, norm_ref, master_ref, first_ref, second_ref, rows_ref, low_ref,
    qkv_ref, out_ref, gu_ref, down_ref, *refs,
):
    norm_outs, (rows_out, low_out), refs = refs[6:9], refs[9:11], refs[:6] + refs[11:]
    factor = clip_factor(total_ref, 128)[:, 0:1]
    rows_out[...] = rows_ref[...]
    low_out[...] = low_ref[...]

    @pl.when(pl.program_id(0) == 0)
    def _():
        size = master_ref.shape[1]
        mine, place = lax.axis_index("dp"), lax.axis_index("shard")
        grads = jnp.zeros((8, size), FULL)
        row = lax.broadcasted_iota(jnp.int32, (8, size), 0)
        bias = (row >= 2) & (row < 5)
        spot = jnp.where(bias, mine * N_SH + place, place * N_DP + mine)
        for n in range(N_DP * N_SH):
            grads = jnp.where(spot == n, norm_ref[:, n * size : n * size + size], grads)
        values = adam_update(
            master_ref[...], first_ref[...], second_ref[...], grads[:7], factor, RATE_VECTOR, 0.0
        )
        for ref, value in zip(norm_outs, values):
            ref[...] = value

    def update(begin, grads, states, results):
        here = slice(begin, begin + grads.shape[1])
        values = adam_step(grads, factor, *[ref[:, here] for ref in states])
        for ref, value in zip(results, values):
            ref[:, here] = value

    attn, mlp = (refs[0:3], refs[6:9]), (refs[3:6], refs[9:12])
    width, ff_width = qkv_ref.shape[-1] // 3, down_ref.shape[-1]
    for d in range(N_DP):
        for part in range(3):
            here = slice(part * width, part * width + width)
            update(part * D + d * width, qkv_ref[d, :, here], *attn)
        for part in range(2):
            here = slice(part * ff_width, part * ff_width + ff_width)
            update(part * FF + d * ff_width, gu_ref[d, :, here], *mlp)
        update(2 * FF + d * ff_width, down_ref[d], *mlp)
    update(3 * D, out_ref[...], *attn)


def adam(total, norm_sums, norm_states, row_outputs, grads, states):
    size = 16
    steps = states[0].shape[0] // size

    def block(array):
        if array.ndim == 3:
            return pl.BlockSpec((N_DP, size, array.shape[-1]), lambda j: (0, j, 0))
        return pl.BlockSpec((array.shape[0] // steps, array.shape[-1]), lambda j: (j, 0))

    def whole(array):
        return pl.BlockSpec(array.shape, lambda j: (0, 0))

    count = sum(array.size for array in states)
    outs = norm_states + row_outputs + states
    return pl.pallas_call(
        adam_kernel,
        grid=(steps,),
        out_shape=[jax.ShapeDtypeStruct(array.shape, array.dtype) for array in outs],
        in_specs=[pl.BlockSpec(memory_space=pltpu.SMEM)]
        + [whole(array) for array in [norm_sums] + norm_states]
        + [block(array) for array in row_outputs + grads + states],
        out_specs=[whole(array) for array in norm_states]
        + [block(array) for array in row_outputs + states],
        compiler_params=pltpu.CompilerParams(vmem_limit_bytes=BIG_VMEM),
        cost_estimate=pl.CostEstimate(
            flops=6 * count, bytes_accessed=9 * count, transcendentals=count // 3
        ),
        name="adam",
    )(total, norm_sums, *norm_states, *row_outputs, *grads, *states)


def per_device_fast(
    tokens,
    cotangent,
    segments,
    positions,
    attn_master,
    mlp_master,
    norm_master,
    attn_first,
    mlp_first,
    norm_first,
    attn_second,
    mlp_second,
    norm_second,
):
    seq = tokens.shape[0]
    rows = attn_master.shape[0]
    width = D // N_DP
    ff_width = FF // N_DP
    group = N_DP * seq
    my_dp = lax.axis_index("dp")
    my_shard = lax.axis_index("shard")

    started = start(
        attn_master, mlp_master, norm_master, tokens, cotangent, segments, positions, 0
    )
    w_qkv, w_out, norm_all, tok_all, gu_blocks, down_blocks = started[2 * N_DP : -2]
    tokens, cotangent = started[-2:]
    w_qkv = w_qkv.reshape(D, 3 * width)
    w_out = w_out.reshape(width, D)

    def gather_rows(blocks):
        return lax.all_gather(blocks.reshape(-1, blocks.shape[-1]), "shard", axis=0, tiled=True)

    rates = ROPE_BASE ** (-((np.arange(128) % (ROT // 2)) * 2.0 / ROT))
    rates = np.broadcast_to(rates.astype(np.float32), (8, 128))
    w_gu = gather_rows(gu_blocks)
    w_down = gather_rows(down_blocks)
    results = attn_forward(
        cotangent, tok_all, started[: 2 * N_DP], rates, norm_all, w_qkv, 2
    )
    cot_near, norm_vals, normed1, queries, keys, values, mixture = results[:7]
    *tables, mask = results[7:]
    resid, normed2 = mid_forward(mixture, w_out, tokens, norm_vals, 3)
    normed2 = normed2.reshape(group, D)

    hidden, gate, up, part_down, cot_far = mlp_one(normed2, cotangent, cot_near, w_gu, 1)
    groups = [[place for place in range(N_SH) if place % 2 == core] for core in range(2)]

    def sum_line(blocks):
        blocks = blocks.reshape(-1, blocks.shape[-1])
        return lax.psum_scatter(
            blocks, "shard", scatter_dimension=0, axis_index_groups=groups, tiled=True
        )

    down_sum = sum_line(part_down)
    grad_resid, own_gao, sums2, part_gu = mid_backward(
        normed2, cotangent, cot_near, cot_far, w_gu, w_down, gate, up, resid, norm_vals, 4
    )
    gu_sum = sum_line(part_gu)
    grad_attn_out, out_part = share(own_gao, hidden.reshape(N_DP, seq, ff_width), w_down, 6)
    grad_attn_out, down_sum = lax.optimization_barrier((grad_attn_out, down_sum))
    block_out, grad_qkv, bias_sums, part_attn = attn_backward(
        out_part,
        normed1,
        mixture,
        resid,
        grad_attn_out,
        w_out,
        queries,
        keys,
        values,
        mask,
        tables,
        9,
    )
    gu_blocks = gu_sum.reshape(N_DP, rows, 2 * ff_width)
    down_blocks = down_sum.reshape(N_DP, rows, ff_width)
    input_grad, norm_sums, gu_grad, down_grad, qkv_grad, out_grad, box = last(
        part_attn,
        grad_qkv,
        w_qkv,
        gu_blocks,
        down_blocks,
        tokens,
        grad_resid,
        norm_vals,
        bias_sums,
        sums2,
        5,
    )
    results = adam(
        box,
        norm_sums,
        [norm_master, norm_first, norm_second],
        [input_grad, block_out],
        [qkv_grad, out_grad, gu_grad, down_grad],
        [attn_master, attn_first, attn_second, mlp_master, mlp_first, mlp_second],
    )
    norm_new, norm_first_new, norm_second_new, input_grad, block_out = results[:5]
    attn_new, attn_first_new, attn_second_new, mlp_new, mlp_first_new, mlp_second_new = results[5:]
    grad_size = jnp.sqrt(box[0, 0])
    return (
        block_out,
        input_grad,
        grad_size,
        attn_new,
        mlp_new,
        norm_new,
        attn_first_new,
        mlp_first_new,
        norm_first_new,
        attn_second_new,
        mlp_second_new,
        norm_second_new,
    )


def solution(mesh):
    in_specs = (
        P(("dp", "shard"), None),
        P(("dp", "shard"), None),
        P(("dp", "shard")),
        P(("dp", "shard")),
        P(("dp", "shard"), None),
        P(("dp", "shard"), None),
        P(None, ("dp", "shard")),
        P(("dp", "shard"), None),
        P(("dp", "shard"), None),
        P(None, ("dp", "shard")),
        P(("dp", "shard"), None),
        P(("dp", "shard"), None),
        P(None, ("dp", "shard")),
    )
    out_specs = (
        P(("dp", "shard"), None),
        P(("dp", "shard"), None),
        P(),
        P(("dp", "shard"), None),
        P(("dp", "shard"), None),
        P(None, ("dp", "shard")),
        P(("dp", "shard"), None),
        P(("dp", "shard"), None),
        P(None, ("dp", "shard")),
        P(("dp", "shard"), None),
        P(("dp", "shard"), None),
        P(None, ("dp", "shard")),
    )
    fast = dict(mesh.shape) == dict(dp=4, shard=8)
    body = per_device_fast if fast else per_device_any
    return jax.shard_map(
        body, mesh=mesh, in_specs=in_specs, out_specs=out_specs, check_vma=False
    )
```

```python
import functools

import numpy as np
import jax
import jax.numpy as jnp
from jax import lax
from jax.experimental import pallas as pl
from jax.experimental.pallas import tpu as pltpu
from jax.sharding import PartitionSpec as P

D = 2048
HEADS = 32
HEAD = 64
FF = 5632
ROT = 16
STEP = 10


NORM_EPS = 1e-05
NEG_FILL = -1e30
ROPE_BASE = 10000.0
CLIP_NORM = 1.0
BETA_ONE = 0.9
BETA_TWO = 0.95
ADAM_EPS = 1e-08
RATE_MATRIX = 0.02
RATE_VECTOR = 0.2
DECAY_MATRIX = 0.1
LEAD_DIMS = (((0,), (0,)), ((), ()))
LAST_DIMS = (((1,), (1,)), ((), ()))


def layer_norm(values_in, gain_vec, shift_vec):
    average = jnp.mean(values_in, axis=-1, keepdims=True)
    centered = values_in - average
    variance = jnp.mean(centered * centered, axis=-1, keepdims=True)
    return centered * lax.rsqrt(variance + NORM_EPS) * gain_vec + shift_vec


def rotary_tables(position_ids):
    half_rot = ROT // 2
    inverse_freq = ROPE_BASE ** (-(jnp.arange(half_rot, dtype=jnp.float32) * 2.0 / ROT))
    angles = position_ids.astype(jnp.float32)[:, None] * inverse_freq[None, :]
    return (jnp.cos(angles)[:, None, :], jnp.sin(angles)[:, None, :])


def rotate(heads_in, cos_table, sin_table):
    half_rot = ROT // 2
    first_half = heads_in[..., :half_rot]
    second_half = heads_in[..., half_rot:ROT]
    rest_part = heads_in[..., ROT:]
    turned_one = first_half * cos_table - second_half * sin_table
    turned_two = second_half * cos_table + first_half * sin_table
    return jnp.concatenate([turned_one, turned_two, rest_part], -1)


def pad_last(array, size):
    missing = size - array.shape[-1]
    if missing == 0:
        return array
    return jnp.pad(array, [(0, 0)] * (array.ndim - 1) + [(0, missing)])


def activate(gate_part, up_part):
    return jax.nn.silu(gate_part) * up_part


def adam_update(master, first, second, grads, factor, rate, decay):
    clipped = grads * factor
    first_new = BETA_ONE * first + (1.0 - BETA_ONE) * clipped
    second_new = BETA_TWO * second + (1.0 - BETA_TWO) * clipped * clipped
    first_hat = first_new / (1.0 - BETA_ONE**STEP)
    second_hat = second_new / (1.0 - BETA_TWO**STEP)
    master_new = master - rate * (first_hat / (jnp.sqrt(second_hat) + ADAM_EPS) + decay * master)
    return (master_new, first_new, second_new)


def exchange_dp(blocks):
    return lax.all_to_all(blocks, "dp", 0, 0, tiled=True)


def gather_dp(rows):
    return lax.all_gather(rows, "dp", axis=0, tiled=True)


def scatter_sum_dp(parts):
    return lax.psum_scatter(parts, "dp", scatter_dimension=0, tiled=True)


def gather_shard(block):
    return lax.all_gather(block, "shard", axis=1)


def scatter_sum_shard(parts):
    return lax.psum_scatter(parts, "shard", scatter_dimension=1)


def layer_stats(values_in):
    average = jnp.mean(values_in, axis=-1, keepdims=True)
    centered = values_in - average
    variance = jnp.mean(centered * centered, axis=-1, keepdims=True)
    inverse = lax.rsqrt(variance + NORM_EPS)
    return centered * inverse, inverse


def layer_back(grads, gain_vec, unit, inverse):
    scaled = grads * gain_vec
    mean_one = jnp.mean(scaled, axis=-1, keepdims=True)
    mean_two = jnp.mean(scaled * unit, axis=-1, keepdims=True)
    return inverse * (scaled - mean_one - unit * mean_two)


def per_device_any(
    tokens,
    cotangent,
    segments,
    positions,
    attn_master,
    mlp_master,
    norm_master,
    attn_first,
    mlp_first,
    norm_first,
    attn_second,
    mlp_second,
    norm_second,
):
    low = jnp.bfloat16
    full = jnp.float32
    n_dp = lax.axis_size("dp")
    n_sh = lax.axis_size("shard")
    seq = tokens.shape[0]
    rows = attn_master.shape[0]
    heads = HEADS // n_dp
    width = D // n_dp
    ff_width = -(-FF // (128 * n_dp)) * 128
    ff_pad = ff_width * n_dp
    scale = HEAD ** (-0.5)

    qkv_send = attn_master[:, : 3 * D].astype(low).reshape(rows, 3, n_dp, width)
    qkv_send = qkv_send.transpose(2, 0, 1, 3).reshape(n_dp, rows, 3 * width)
    mlp_send = pad_last(mlp_master.astype(low).reshape(rows, 3, FF), ff_pad)
    mlp_send = mlp_send.reshape(rows, 3, n_dp, ff_width)
    mlp_send = mlp_send.transpose(2, 0, 1, 3).reshape(n_dp, rows, 3 * ff_width)
    norm_full = lax.all_gather(norm_master.astype(low), ("dp", "shard"), axis=1, tiled=True)
    norm_vals = norm_full.astype(full)
    w_qkv = gather_shard(exchange_dp(qkv_send)).reshape(D, 3 * width)
    w_out = gather_shard(attn_master[None, :, 3 * D :].astype(low)).reshape(width, D)
    tokens_all = gather_dp(tokens)
    places_all = gather_dp(jnp.stack([segments, positions], 0)[None])
    cot_all = gather_dp(cotangent)
    w_mlp = gather_shard(exchange_dp(mlp_send)).reshape(D, 3 * ff_width)
    w_gu = w_mlp[:, : 2 * ff_width]
    w_down = w_mlp[:, 2 * ff_width :]
    seg_all, pos_all = places_all[:, 0], places_all[:, 1]

    inputs_all = tokens_all.astype(full)
    unit1, _ = layer_stats(inputs_all)
    normed1 = (unit1 * norm_vals[0] + norm_vals[1]).astype(low)
    my_dp = lax.axis_index("dp")
    bias = lax.dynamic_slice(norm_vals[2:5], (0, my_dp * width), (3, width)).reshape(3 * width)
    qkv = jnp.dot(normed1, w_qkv, preferred_element_type=full) + bias
    qkv = qkv.reshape(n_dp * seq, 3 * heads, HEAD)
    cos_table, sin_table = rotary_tables(pos_all.reshape(-1))

    def split(array):
        return array.reshape(n_dp, seq, heads, HEAD)

    queries = split(rotate(qkv[:, :heads], cos_table, sin_table).astype(low))
    key_rows = split(rotate(qkv[:, heads : 2 * heads], cos_table, sin_table).astype(low))
    values = split(qkv[:, 2 * heads :].astype(low))
    places = jnp.arange(seq)
    allowed = (seg_all[:, :, None] == seg_all[:, None, :]) & (
        places[:, None] >= places[None, :]
    )[None]
    scores = (
        jnp.einsum("gshd,gthd->ghst", queries, key_rows, preferred_element_type=full) * scale
    )
    scores = jnp.where(allowed[:, None], scores, NEG_FILL)
    attend = jax.nn.softmax(scores, axis=-1)
    attend_low = attend.astype(low)
    mixture = (
        jnp.einsum("ghst,gthd->gshd", attend_low, values, preferred_element_type=full)
        .reshape(n_dp * seq, width)
        .astype(low)
    )
    attn_part = jnp.dot(mixture, w_out, preferred_element_type=full).astype(low)
    resid = tokens.astype(full) + scatter_sum_dp(attn_part).astype(full)
    unit2, inverse2 = layer_stats(resid)
    normed2 = gather_dp((unit2 * norm_vals[5] + norm_vals[6]).astype(low))
    gate_up = jnp.dot(normed2, w_gu, preferred_element_type=full)
    hidden_f, act_pull = jax.vjp(activate, gate_up[:, :ff_width], gate_up[:, ff_width:])
    hidden = hidden_f.astype(low)
    grad_hidden = jnp.dot(cot_all, w_down, preferred_element_type=full)
    grad_gate, grad_up = act_pull(grad_hidden)
    grad_gu = jnp.concatenate([grad_gate, grad_up], 1).astype(low)
    norm2_part = lax.dot_general(grad_gu, w_gu, LAST_DIMS, preferred_element_type=full)
    grad_norm2 = scatter_sum_dp(norm2_part.astype(low)).astype(full)
    out_part = lax.dot_general(hidden, w_down, LAST_DIMS, preferred_element_type=full)
    block_out = (resid + scatter_sum_dp(out_part.astype(low)).astype(full)).astype(low)
    part_gu = lax.dot_general(normed2, grad_gu, LEAD_DIMS, preferred_element_type=full)
    part_down = lax.dot_general(cot_all, hidden, LEAD_DIMS, preferred_element_type=full)
    part_mlp = jnp.concatenate([part_gu.astype(low), part_down.astype(low)], 1)
    mlp_sum = scatter_sum_shard(part_mlp.reshape(n_dp, n_sh, rows, 3 * ff_width))

    grad_gain2 = jnp.sum(grad_norm2 * unit2, axis=0)
    grad_shift2 = jnp.sum(grad_norm2, axis=0)
    grad_resid = cotangent.astype(full) + layer_back(grad_norm2, norm_vals[5], unit2, inverse2)
    grad_attn_out = gather_dp(grad_resid.astype(low))
    grad_mixture = lax.dot_general(grad_attn_out, w_out, LAST_DIMS, preferred_element_type=full)
    grad_mixture = split(grad_mixture.astype(low))
    grad_attend = jnp.einsum("gshd,gthd->ghst", grad_mixture, values, preferred_element_type=full)
    grad_values = jnp.einsum(
        "ghst,gshd->gthd", attend_low, grad_mixture, preferred_element_type=full
    )
    grad_scores = (
        attend * (grad_attend - jnp.sum(attend * grad_attend, axis=-1, keepdims=True))
    ).astype(low)
    grad_queries = (
        jnp.einsum("ghst,gthd->gshd", grad_scores, key_rows, preferred_element_type=full) * scale
    )
    grad_keys = (
        jnp.einsum("ghst,gshd->gthd", grad_scores, queries, preferred_element_type=full) * scale
    )

    def turn_back(grads):
        grads = grads.reshape(n_dp * seq, heads, HEAD)
        return rotate(grads, cos_table, -sin_table).reshape(n_dp * seq, width)

    grad_qkv = jnp.concatenate(
        [
            turn_back(grad_queries),
            turn_back(grad_keys),
            grad_values.reshape(n_dp * seq, width),
        ],
        1,
    ).astype(low)
    part_qkv = lax.dot_general(normed1, grad_qkv, LEAD_DIMS, preferred_element_type=full)
    part_out = lax.dot_general(mixture, grad_attn_out, LEAD_DIMS, preferred_element_type=full)
    qkv_sum = scatter_sum_shard(part_qkv.astype(low).reshape(n_dp, n_sh, rows, 3 * width))
    out_sum = scatter_sum_shard(part_out.astype(low).reshape(1, n_sh, rows, D))[0].astype(full)

    norm1_part = lax.dot_general(grad_qkv, w_qkv, LAST_DIMS, preferred_element_type=full)
    grad_gain1 = jnp.sum(norm1_part * unit1, axis=0)
    grad_shift1 = jnp.sum(norm1_part, axis=0)
    grad_bias = jnp.sum(grad_qkv, axis=0, dtype=full).reshape(3, width)
    grad_norm1 = scatter_sum_dp(norm1_part.astype(low)).astype(full)
    own_unit1, own_inverse1 = layer_stats(tokens.astype(full))
    input_grad = grad_resid + layer_back(grad_norm1, norm_vals[0], own_unit1, own_inverse1)
    norm_term = lax.dynamic_update_slice(
        jnp.zeros((3, D), full), grad_bias, (0, my_dp * width)
    )
    norm_term = jnp.concatenate(
        [grad_gain1[None], grad_shift1[None], norm_term, grad_gain2[None], grad_shift2[None]], 0
    )
    norm_grad = lax.psum_scatter(norm_term, ("dp", "shard"), scatter_dimension=1, tiled=True)

    def columns_back(summed, parts, part_width, keep):
        back = exchange_dp(summed).reshape(n_dp, rows, parts, part_width)
        back = back.transpose(1, 2, 0, 3).reshape(rows, parts, n_dp * part_width)
        return back[:, :, :keep].reshape(rows, parts * keep).astype(full)

    mlp_grad = columns_back(mlp_sum, 3, ff_width, FF)
    attn_grad = jnp.concatenate([columns_back(qkv_sum, 3, width, D), out_sum], 1)
    squares = (
        jnp.sum(attn_grad * attn_grad)
        + jnp.sum(mlp_grad * mlp_grad)
        + jnp.sum(norm_grad * norm_grad)
    )
    overall = lax.psum(squares, ("dp", "shard"))
    grad_size = jnp.sqrt(overall)
    factor = CLIP_NORM / jnp.maximum(grad_size, CLIP_NORM)
    attn_new, attn_first_new, attn_second_new = adam_update(
        attn_master, attn_first, attn_second, attn_grad, factor, RATE_MATRIX, DECAY_MATRIX
    )
    mlp_new, mlp_first_new, mlp_second_new = adam_update(
        mlp_master, mlp_first, mlp_second, mlp_grad, factor, RATE_MATRIX, DECAY_MATRIX
    )
    norm_new, norm_first_new, norm_second_new = adam_update(
        norm_master, norm_first, norm_second, norm_grad, factor, RATE_VECTOR, 0.0
    )
    return (
        block_out,
        input_grad,
        grad_size,
        attn_new,
        mlp_new,
        norm_new,
        attn_first_new,
        mlp_first_new,
        norm_first_new,
        attn_second_new,
        mlp_second_new,
        norm_second_new,
    )


MESH = pl.DeviceIdType.MESH
ANY = pl.BlockSpec(memory_space=pl.ANY)
VMEM = pl.BlockSpec(memory_space=pltpu.VMEM)
LOW = jnp.bfloat16
FULL = jnp.float32
N_DP = 4
N_SH = 8
BIG_VMEM = 60 * 1024 * 1024


def dp_peer(step):
    mine = lax.axis_index("dp")
    if step == 1:
        return mine + 1 - 2 * (mine % 2)
    if step == 2:
        return (mine + 2) % 4
    return 3 - mine


def to_dp(step):
    return (dp_peer(step), lax.axis_index("shard"))


def to_shard(step):
    return (lax.axis_index("dp"), (lax.axis_index("shard") + step) % N_SH)


def cost(micros):
    return pl.CostEstimate(flops=0, bytes_accessed=int(micros * 3.0e6), transcendentals=0)


def greet(peers):
    barrier = pltpu.get_barrier_semaphore()
    for peer in peers:
        pl.semaphore_signal(barrier, inc=1, device_id=peer, device_id_type=MESH)
    pl.semaphore_wait(barrier, len(peers))


def remote(source, target, sems, index, peer):
    return pltpu.make_async_remote_copy(
        src_ref=source,
        dst_ref=target,
        send_sem=sems[0].at[index],
        recv_sem=sems[1].at[index],
        device_id=peer,
        device_id_type=MESH,
    )


def sems(count):
    return [pltpu.SemaphoreType.DMA((count,)), pltpu.SemaphoreType.DMA((count,))]


def comm_params(number):
    return pltpu.CompilerParams(
        collective_id=number, has_side_effects=True, vmem_limit_bytes=BIG_VMEM
    )


def to_places(value):
    size = value.shape[1] // (N_DP * N_SH)
    starts = [(n * N_DP + d) * size for d in range(N_DP) for n in range(N_SH)]
    return jnp.concatenate([value[:, start : start + size] for start in starts], axis=1)


def to_shards(value):
    size = value.shape[1] // (N_DP * N_SH)
    starts = [(d * N_SH + n) * size for n in range(N_SH) for d in range(N_DP)]
    return jnp.concatenate([value[:, start : start + size] for start in starts], axis=1)


CHUNK = 32


def in_chunks(rows, body):
    def step(index, carry):
        body(pl.ds(pl.multiple_of(index * CHUNK, CHUNK), CHUNK))
        return carry

    lax.fori_loop(0, rows // CHUNK, step, 0)


def spread_plan(own, result, sem_pair, base):
    half = own.shape[0] // 2
    top, bottom = pl.ds(0, half), pl.ds(half, half)
    sent = [
        remote(own.at[top], result.at[1, top], sem_pair, base + 0, to_dp(1)),
        remote(own.at[bottom], result.at[2, bottom], sem_pair, base + 1, to_dp(2)),
        remote(own.at[bottom], result.at[1, bottom], sem_pair, base + 2, to_dp(1)),
        remote(own.at[top], result.at[2, top], sem_pair, base + 3, to_dp(2)),
    ]
    passed = [
        remote(result.at[1, top], result.at[3, top], sem_pair, base + 4, to_dp(2)),
        remote(result.at[2, bottom], result.at[3, bottom], sem_pair, base + 5, to_dp(1)),
    ]
    return sent, passed


def spread(own, result, sem_pair, base):
    sent, passed = spread_plan(own, result, sem_pair, base)
    for copy in sent:
        copy.start()
    return sent, passed


def pass_on(sent, passed):
    sent[0].wait_recv()
    passed[0].start()
    sent[1].wait_recv()
    passed[1].start()


def spread_end(sent, passed):
    sent[2].wait_recv()
    sent[3].wait_recv()
    passed[0].wait_recv()
    passed[1].wait_recv()
    for copy in sent + passed:
        copy.wait_send()


SLABS = 6


def start_kernel(
    attn_hbm, mlp_hbm, norm_ref, tok_hbm, cot_hbm, seg_ref, pos_ref,
    seg_0, seg_1, seg_2, seg_3, pos_0, pos_1, pos_2, pos_3,
    w_qkv, w_out, norm_all, tok_all, gu_out, down_out, tok_own, cot_own,
    attn_in, mlp_in, tok_in, cot_in, qkv_send, out_send, norm_send, gu_send, down_send,
    tok_low, cot_low,
    up_send, up_recv, down_s, down_recv, core_send, core_recv, send, recv, local,
):
    mine, place = lax.axis_index("dp"), lax.axis_index("shard")
    line, core = place // 2, place % 2
    width, ff_width = qkv_send.shape[-1] // 3, down_send.shape[-1]
    above, below = (mine, place + 2), (mine, place - 2)
    partner = (mine, place + 1 - 2 * core)
    has_above, has_below = line < N_SH // 2 - 1, line > 0
    pair = (send, recv)
    loads = [
        pltpu.make_async_copy(attn_hbm, attn_in, local.at[0]),
        pltpu.make_async_copy(tok_hbm, tok_in, local.at[1]),
        pltpu.make_async_copy(mlp_hbm, mlp_in, local.at[2]),
        pltpu.make_async_copy(cot_hbm, cot_in, local.at[3]),
    ]
    for copy in loads:
        copy.start()

    barrier = pltpu.get_barrier_semaphore()
    for peer in [to_dp(k) for k in (1, 2, 3)] + [partner]:
        pl.semaphore_signal(barrier, inc=1, device_id=peer, device_id_type=MESH)

    @pl.when(has_above)
    def _():
        pl.semaphore_signal(barrier, inc=1, device_id=above, device_id_type=MESH)

    @pl.when(has_below)
    def _():
        pl.semaphore_signal(barrier, inc=1, device_id=below, device_id_type=MESH)

    norm_send[...] = jnp.zeros_like(norm_send)
    norm_send[0:7, 0 : norm_ref.shape[1]] = norm_ref[...].astype(LOW).astype(FULL)
    loads[0].wait()
    for part in range(3):
        for d in range(N_DP):
            begin = part * D + d * width
            qkv_send[d, :, part * width : part * width + width] = attn_in[
                :, begin : begin + width
            ].astype(LOW)
    out_send[...] = to_shards(attn_in[:, 3 * D :]).astype(LOW)

    @pl.when(has_above & has_below)
    def _():
        pl.semaphore_wait(barrier, 6)

    @pl.when(jnp.logical_not(has_above & has_below))
    def _():
        pl.semaphore_wait(barrier, 5)

    def slab(n, shard):
        if n == 0:
            return w_qkv.at[shard, mine]
        if n == 1:
            return w_out.at[shard]
        if n == 2:
            return norm_all.at[shard]
        return w_qkv.at[shard, dp_peer(n - 2)]

    def source(n):
        return {0: qkv_send.at[mine], 1: out_send}.get(n, slab(n, place))

    def along(n, shard, hop, sem_pair, peer, held=None):
        start = slab(n, shard) if held is None else held
        return remote(start, slab(n, shard), sem_pair, hop * SLABS + n, peer)

    ups, downs, cores = (up_send, up_recv), (down_s, down_recv), (core_send, core_recv)

    def pass_block(n, origin, hop, held, upward, downward):
        shard = 2 * origin + core
        if upward:

            @pl.when(has_above)
            def _():
                along(n, shard, hop, ups, above, held).start()

        if downward:

            @pl.when(has_below)
            def _():
                along(n, shard, hop, downs, below, held).start()

        along(n, shard, origin, cores, partner, held).start()

    norms = [
        remote(norm_send, norm_all.at[place, mine], pair, 21 + k - 1, to_dp(k)) for k in (1, 2, 3)
    ]
    trade = [
        remote(qkv_send.at[dp_peer(k)], w_qkv.at[place, mine], pair, k - 1, to_dp(k))
        for k in (1, 2, 3)
    ]
    own = [
        pltpu.make_async_copy(qkv_send.at[mine], w_qkv.at[place, mine], local.at[4]),
        pltpu.make_async_copy(out_send, w_out.at[place], local.at[5]),
        pltpu.make_async_copy(norm_send, norm_all.at[place, mine], local.at[6]),
        pltpu.make_async_copy(seg_ref, seg_0, local.at[7]),
        pltpu.make_async_copy(pos_ref, pos_0, local.at[13]),
    ]
    for copy in norms + trade:
        copy.start()
    pass_block(0, line, 0, source(0), True, True)
    pass_block(1, line, 0, source(1), True, True)
    for copy in own:
        copy.start()

    loads[1].wait()

    def permute_tokens(here):
        tok_low[here] = to_shards(tok_in[here].astype(FULL)).astype(LOW)

    in_chunks(tok_in.shape[0], permute_tokens)
    places = [
        remote(source, target, pair, base + k, to_dp(k + 1))
        for source, targets, base in (
            (seg_ref, (seg_1, seg_2, seg_3), 9),
            (pos_ref, (pos_1, pos_2, pos_3), 24),
        )
        for k, target in enumerate(targets)
    ]
    for copy in places:
        copy.start()
    tok = spread(tok_low, tok_all, pair, 3)
    keep = [
        pltpu.make_async_copy(tok_low, tok_all.at[0], local.at[8]),
        pltpu.make_async_copy(tok_low, tok_own, local.at[9]),
    ]
    for copy in keep:
        copy.start()

    own[2].wait()
    for copy in norms:
        copy.wait_recv()
    pass_block(2, line, 0, None, True, True)
    for k in (1, 2, 3):
        trade[k - 1].wait_recv()
        pass_block(2 + k, line, 0, None, True, True)

    loads[2].wait()
    for d in range(N_DP):
        for part in range(2):
            begin = part * FF + d * ff_width
            gu_send[d, :, part * ff_width : part * ff_width + ff_width] = mlp_in[
                :, begin : begin + ff_width
            ].astype(LOW)
        begin = 2 * FF + d * ff_width
        down_send[d] = mlp_in[:, begin : begin + ff_width].astype(LOW)
    blocks = []
    for n, (held, target) in enumerate(((gu_send, gu_out), (down_send, down_out))):
        for k in (3, 1, 2):
            blocks.append(
                remote(held.at[dp_peer(k)], target.at[mine], pair, 12 + 3 * n + k - 1, to_dp(k))
            )
        blocks.append(pltpu.make_async_copy(held.at[mine], target.at[mine], local.at[10 + n]))

    loads[3].wait()

    def permute_cotangent(here):
        cot_low[here] = to_shards(cot_in[here].astype(FULL)).astype(LOW)

    in_chunks(cot_in.shape[0], permute_cotangent)
    keep.append(pltpu.make_async_copy(cot_low, cot_own, local.at[12]))
    keep[2].start()

    def hop_step(hop):
        for n in range(SLABS):

            @pl.when(line >= hop)
            def _():
                shard = place - 2 * hop
                along(n, shard, hop - 1, ups, above).wait_recv()
                pass_block(n, line - hop, hop, None, True, False)

            @pl.when(line + hop < N_SH // 2)
            def _():
                shard = place + 2 * hop
                along(n, shard, hop - 1, downs, below).wait_recv()
                pass_block(n, line + hop, hop, None, False, True)

    hop_step(1)
    pass_on(*tok)
    for copy in blocks:
        copy.start()
    hop_step(2)
    hop_step(3)

    spread_end(*tok)
    for copy in blocks + own[:2] + own[3:] + keep + places:
        copy.wait()
    for copy in norms + trade:
        copy.wait_send()
    for hop in range(N_SH // 2 - 1):
        for n in range(SLABS):

            @pl.when(has_above & (line >= hop))
            def _():
                along(n, place - 2 * hop, hop, ups, above).wait_send()

            @pl.when(has_below & (line + hop < N_SH // 2))
            def _():
                along(n, place + 2 * hop, hop, downs, below).wait_send()

    for origin in range(N_SH // 2):
        for n in range(SLABS):
            along(n, 2 * origin + core, origin, cores, partner).wait_send()
            along(n, 2 * origin + 1 - core, origin, cores, partner).wait_recv()


def start(attn_master, mlp_master, norm_master, tokens, cotangent, segments, positions, number):
    rows = attn_master.shape[0]
    width, ff_width = D // N_DP, FF // N_DP
    seq = tokens.shape[0]
    norm_shape = (8, 128)
    hops = (N_SH // 2 - 1) * SLABS
    return pl.pallas_call(
        start_kernel,
        out_shape=[jax.ShapeDtypeStruct(segments.shape, segments.dtype)] * N_DP
        + [jax.ShapeDtypeStruct(positions.shape, positions.dtype)] * N_DP
        + [
            jax.ShapeDtypeStruct((N_SH, N_DP, rows, 3 * width), LOW),
            jax.ShapeDtypeStruct((N_SH, rows, D), LOW),
            jax.ShapeDtypeStruct((N_SH, N_DP) + norm_shape, FULL),
            jax.ShapeDtypeStruct((N_DP, seq, D), LOW),
            jax.ShapeDtypeStruct((N_DP, rows, 2 * ff_width), LOW),
            jax.ShapeDtypeStruct((N_DP, rows, ff_width), LOW),
            jax.ShapeDtypeStruct((seq, D), LOW),
            jax.ShapeDtypeStruct((seq, D), LOW),
        ],
        in_specs=[ANY, ANY, VMEM, ANY, ANY, ANY, ANY],
        out_specs=[ANY] * 16,
        scratch_shapes=[
            pltpu.VMEM(attn_master.shape, FULL),
            pltpu.VMEM(mlp_master.shape, FULL),
            pltpu.VMEM(tokens.shape, LOW),
            pltpu.VMEM(tokens.shape, LOW),
            pltpu.VMEM((N_DP, rows, 3 * width), LOW),
            pltpu.VMEM((rows, D), LOW),
            pltpu.VMEM(norm_shape, FULL),
            pltpu.VMEM((N_DP, rows, 2 * ff_width), LOW),
            pltpu.VMEM((N_DP, rows, ff_width), LOW),
            pltpu.VMEM(tokens.shape, LOW),
            pltpu.VMEM(tokens.shape, LOW),
        ]
        + sems(hops)
        + sems(hops)
        + sems((N_SH // 2) * SLABS)
        + sems(27)
        + [pltpu.SemaphoreType.DMA((14,))],
        compiler_params=comm_params(number),
        cost_estimate=cost(90),
        name="start",
    )(attn_master, mlp_master, norm_master, tokens, cotangent, segments, positions)


def unit_rows(values):
    average = jnp.mean(values, axis=-1, keepdims=True)
    centered = values - average
    variance = jnp.mean(centered * centered, axis=-1, keepdims=True)
    inverse = lax.rsqrt(variance + NORM_EPS)
    return centered * inverse, inverse


def turn(value, cos_ref, up_ref, down_ref, sign):
    left = pltpu.roll(value, 128 - ROT // 2, 1)
    right = pltpu.roll(value, ROT // 2, 1)
    return value * cos_ref[...] + sign * (left * up_ref[...] + right * down_ref[...])


def head_masks():
    lane = lax.broadcasted_iota(jnp.int32, (1, 128), 1)
    return [lane < HEAD, lane >= HEAD]


def softmax_rows(queries, keys, bias):
    scores = lax.dot_general(queries, keys, LAST_DIMS, preferred_element_type=FULL)
    scores = scores * (HEAD ** (-0.5)) + bias
    top = jnp.max(scores, axis=-1, keepdims=True)
    weights = jnp.exp(scores - top)
    return weights / jnp.sum(weights, axis=-1, keepdims=True)


def fill_tables(row, spot_row, rate_ref, cos_ref, up_ref, down_ref, mask_ref):
    seq = row.shape[-1]
    half = ROT // 2
    columns = jnp.transpose(jnp.broadcast_to(row, (8, seq)))[:, 0:1]
    spots = jnp.transpose(jnp.broadcast_to(spot_row, (8, seq)))[:, 0:1]
    angles = spots * rate_ref[0:1, :]
    lane = lax.broadcasted_iota(jnp.int32, (1, 128), 1) % HEAD
    sines = jnp.sin(angles)
    cos_ref[...] = jnp.where(lane < ROT, jnp.cos(angles), 1.0)
    up_ref[...] = jnp.where(lane < half, -sines, 0.0)
    down_ref[...] = jnp.where((lane >= half) & (lane < ROT), sines, 0.0)
    later = lax.broadcasted_iota(jnp.int32, (seq, seq), 0) >= lax.broadcasted_iota(
        jnp.int32, (seq, seq), 1
    )
    mask_ref[0] = jnp.where((columns == row) & later, 0.0, NEG_FILL)


def attn_forward_kernel(
    cot_ref, tok_ref, seg_0, seg_1, seg_2, seg_3, pos_0, pos_1, pos_2, pos_3, rate_ref, norm_all, w_ref,
    cot_all, norm_ref, normed_ref, q_ref, k_ref, v_ref, mix_ref, cos_ref, up_ref, down_ref, mask_ref,
    qkv_ref, b_ref, place_ref, send, recv,
):
    width = q_ref.shape[-1]
    step, last = pl.program_id(0), pl.num_programs(0) - 1
    mine = lax.axis_index("dp")
    sent = [
        remote(cot_ref, cot_all.at[k - 1], (send, recv), k - 1, to_dp(k)) for k in (1, 2)
    ]

    @pl.when(step == 0)
    def _():
        greet([to_dp(1), to_dp(2)])
        for copy in sent:
            copy.start()
        places = (seg_0, seg_1, seg_2, seg_3, pos_0, pos_1, pos_2, pos_3)
        for n, array in enumerate(places):
            place_ref[n : n + 1, :] = array[...].astype(FULL).reshape(1, array.shape[0])
        size = w_ref.shape[0] // (N_DP * N_SH)
        norm_ref[...] = jnp.concatenate(
            [norm_all[n, d, :, :size] for n in range(N_SH) for d in range(N_DP)], axis=1
        )
        for part in range(3):
            b_ref[0:1, part * width : part * width + width] = jnp.concatenate(
                [norm_all[n, mine, 2 + part : 3 + part, :size] for n in range(N_SH)], axis=1
            )

    fill_tables(
        place_ref[pl.ds(step, 1)],
        place_ref[pl.ds(N_DP + step, 1)],
        rate_ref,
        cos_ref,
        up_ref,
        down_ref,
        mask_ref,
    )
    unit, _ = unit_rows(tok_ref[0].astype(FULL))
    normed_ref[0] = (unit * norm_ref[0:1, :] + norm_ref[1:2, :]).astype(LOW)
    qkv_ref[...] = jnp.dot(normed_ref[0], w_ref[...], preferred_element_type=FULL) + b_ref[0:1, :]
    masks = head_masks()
    for pair in range(width // 128):
        here = slice(pair * 128, pair * 128 + 128)
        queries = turn(qkv_ref[:, here], cos_ref, up_ref, down_ref, 1.0).astype(LOW)
        there = slice(width + pair * 128, width + pair * 128 + 128)
        keys = turn(qkv_ref[:, there], cos_ref, up_ref, down_ref, 1.0).astype(LOW)
        there = slice(2 * width + pair * 128, 2 * width + pair * 128 + 128)
        values = qkv_ref[:, there].astype(LOW)
        q_ref[0, :, here] = queries
        k_ref[0, :, here] = keys
        v_ref[0, :, here] = values
        total = None
        for mask in masks:
            attend = softmax_rows(queries, jnp.where(mask, keys, 0), mask_ref[0])
            part = jnp.dot(
                attend.astype(LOW), jnp.where(mask, values, 0), preferred_element_type=FULL
            )
            total = part if total is None else total + part
        mix_ref[0, :, here] = total.astype(LOW)

    @pl.when(step == last)
    def _():
        for copy in sent:
            copy.wait()


def group_spec(array):
    return pl.BlockSpec((1,) + array.shape[1:], lambda g: (g, 0, 0))


def whole_spec(array):
    return pl.BlockSpec(array.shape, lambda g: (0,) * len(array.shape))


def attn_forward(cotangent, tokens, places, rates, norm_all, w_qkv, number):
    groups, seq, _ = tokens.shape
    width = w_qkv.shape[1] // 3
    row_spec = pl.BlockSpec((seq, 128), lambda g: (g, 0))
    part = jax.ShapeDtypeStruct((groups, seq, width), LOW)
    normed = jax.ShapeDtypeStruct(tokens.shape, LOW)
    norms = jax.ShapeDtypeStruct((8, D), FULL)
    near = jax.ShapeDtypeStruct((2,) + tokens.shape[1:], LOW)
    table = jax.ShapeDtypeStruct((groups * seq, 128), FULL)
    mask = jax.ShapeDtypeStruct((groups, seq, seq), FULL)
    return pl.pallas_call(
        attn_forward_kernel,
        grid=(groups,),
        out_shape=[near, norms, normed, part, part, part, part, table, table, table, mask],
        in_specs=[
            ANY,
            group_spec(tokens),
            *[VMEM] * len(places),
            whole_spec(rates),
            whole_spec(norm_all),
            whole_spec(w_qkv),
        ],
        out_specs=[ANY, whole_spec(norms), group_spec(normed)]
        + [group_spec(part)] * 4
        + [row_spec] * 3
        + [group_spec(mask)],
        scratch_shapes=[
            pltpu.VMEM((seq, 3 * width), FULL),
            pltpu.VMEM((8, 3 * width), FULL),
            pltpu.VMEM((2 * N_DP, seq), FULL),
        ]
        + sems(2),
        compiler_params=comm_params(number),
        cost_estimate=pl.CostEstimate(
            flops=2 * groups * seq * (D * 3 * width + 2 * seq * width * 2),
            bytes_accessed=2 * (w_qkv.size + 3 * tokens.size),
            transcendentals=groups * seq * seq * (width // HEAD),
        ),
        name="attn_forward",
    )(cotangent, tokens, *places, rates, norm_all, w_qkv)


def attn_backward_kernel(
    part_hbm, normed_hbm, mix_hbm, gao_hbm, resid_hbm, gao_ref, w_ref, q_ref, k_ref, v_ref,
    mask_ref, cos_ref, up_ref, down_ref,
    block_ref, grad_ref, sum_ref, attn_hbm,
    gm_ref, parts, normed, mix, gao, resid_ref, wo_grad, grads_all, out, diag, full,
    send, recv, local, *grad_scratch,
):
    width = q_ref.shape[-1]
    rows = q_ref.shape[1]
    step, last = pl.program_id(0), pl.num_programs(0) - 1
    total = RowSum(parts, (out, diag, full), (send, recv), 0, source=part_hbm)
    loads = [
        pltpu.make_async_copy(part_hbm, parts, local.at[0]),
        pltpu.make_async_copy(mix_hbm, mix, local.at[1]),
        pltpu.make_async_copy(gao_hbm, gao, local.at[2]),
        pltpu.make_async_copy(normed_hbm, normed, local.at[3]),
        pltpu.make_async_copy(resid_hbm, resid_ref, local.at[4]),
    ]

    @pl.when(step == 0)
    def _():
        loads[0].start()
        greet([to_dp(1), to_dp(2), partner()])
        for k in (3, 1, 2):
            total.send(k)
        for copy in loads[1:]:
            copy.start()
        sum_ref[...] = jnp.zeros_like(sum_ref)

    @pl.when(step == 2)
    def _():
        loads[0].wait()
        total.relay()

    scale = HEAD ** (-0.5)
    gm_ref[...] = lax.dot_general(
        gao_ref[0], w_ref[...], LAST_DIMS, preferred_element_type=FULL
    ).astype(LOW)
    masks = head_masks()
    for pair in range(width // 128):
        here = slice(pair * 128, pair * 128 + 128)
        queries, keys, values = q_ref[0, :, here], k_ref[0, :, here], v_ref[0, :, here]
        grads = gm_ref[:, here]
        grad_q = grad_k = grad_v = 0.0
        for mask in masks:
            keys_one = jnp.where(mask, keys, 0)
            attend = softmax_rows(queries, keys_one, mask_ref[0])
            grad_attend = lax.dot_general(
                grads, jnp.where(mask, values, 0), LAST_DIMS, preferred_element_type=FULL
            )
            grad_v += lax.dot_general(
                attend.astype(LOW),
                jnp.where(mask, grads, 0),
                LEAD_DIMS,
                preferred_element_type=FULL,
            )
            mean = jnp.sum(attend * grad_attend, axis=-1, keepdims=True)
            grad_scores = (attend * (grad_attend - mean)).astype(LOW)
            grad_q += jnp.dot(grad_scores, keys_one, preferred_element_type=FULL)
            grad_k += lax.dot_general(
                grad_scores, jnp.where(mask, queries, 0), LEAD_DIMS, preferred_element_type=FULL
            )
        grad_q = turn(grad_q * scale, cos_ref, up_ref, down_ref, -1.0)
        grad_k = turn(grad_k * scale, cos_ref, up_ref, down_ref, -1.0)
        for n, grad in enumerate((grad_q, grad_k, grad_v)):
            start = n * width + pair * 128
            grad_ref[0, :, start : start + 128] = grad.astype(LOW)
    grads_all[pl.ds(pl.multiple_of(step * rows, rows), rows)] = grad_ref[0]
    sum_ref[0:1, :] += jnp.sum(grad_ref[0].astype(FULL), axis=0, keepdims=True)

    @pl.when(step == last)
    def _():
        for copy in loads[1:]:
            copy.wait()

        for pair in range(width // 128):
            wo_grad[pair * 128 : pair * 128 + 128, :] = lax.dot_general(
                mix[:, pair * 128 : pair * 128 + 128],
                gao[...],
                LEAD_DIMS,
                preferred_element_type=FULL,
            ).astype(LOW)

        def out_columns(target, index):
            side = pl.ds(pl.multiple_of(index * 64, 64), 64)
            for part in range(N_DP):
                target[part * 64 : part * 64 + 64, 3 * width :] = wo_grad[
                    side, part * width : part * width + width
                ]

        grad = PairGrad(normed, grads_all, attn_hbm, grad_scratch, out_columns)
        grad.run()
        total.finish()

        def body(here):
            block_ref[here] = to_places(resid_ref[here] + total.rows(here)).astype(LOW)

        in_chunks(rows, body)
        grad.end()


def attn_backward(
    out_part, normed1, mixture, resid, gao, w_out, queries, keys, values, mask, tables, number
):
    groups, seq, cols = gao.shape
    width = queries.shape[-1]
    row_spec = pl.BlockSpec((seq, 128), lambda g: (g, 0))
    grad = jax.ShapeDtypeStruct((groups, seq, 3 * width), LOW)
    sums = jax.ShapeDtypeStruct((8, 3 * width), FULL)
    flat = groups * seq
    return pl.pallas_call(
        attn_backward_kernel,
        grid=(groups,),
        out_shape=[
            jax.ShapeDtypeStruct(resid.shape, LOW),
            grad,
            sums,
            jax.ShapeDtypeStruct((N_SH // 2, D // N_SH, 4 * width), LOW),
        ],
        in_specs=[
            ANY,
            ANY,
            ANY,
            ANY,
            ANY,
            group_spec(gao),
            VMEM,
            group_spec(queries),
            group_spec(keys),
            group_spec(values),
            group_spec(mask),
            row_spec,
            row_spec,
            row_spec,
        ],
        out_specs=[VMEM, group_spec(grad), whole_spec(sums), ANY],
        scratch_shapes=[
            pltpu.VMEM((seq, width), LOW),
            pltpu.VMEM(gao.shape, LOW),
            pltpu.VMEM((flat, cols), LOW),
            pltpu.VMEM((flat, width), LOW),
            pltpu.VMEM((flat, cols), LOW),
            pltpu.VMEM(resid.shape, FULL),
            pltpu.VMEM((width, cols), LOW),
            pltpu.VMEM((flat, 3 * width), LOW),
        ]
        + row_sum_scratch(seq, cols)
        + sems(6)
        + [pltpu.SemaphoreType.DMA((5,))]
        + pair_grad_scratch(cols, 4 * width),
        compiler_params=comm_params(number),
        cost_estimate=cost(55),
        name="attn_backward",
    )(
        out_part,
        normed1.reshape(flat, cols),
        mixture.reshape(flat, width),
        gao.reshape(flat, cols),
        resid,
        gao,
        w_out,
        queries,
        keys,
        values,
        mask,
        *tables,
    )


class RowSum:
    scratch = 3

    def __init__(self, parts, scratch, pair, base, pieces=1, column_base=0, source=None):
        self.parts, self.pair = parts, pair
        self.pieces, self.column_base = pieces, column_base
        self.out, self.diag, self.full = scratch
        self.half = parts.shape[1] // 2
        self.top, self.bottom = pl.ds(0, self.half), pl.ds(self.half, self.half)
        top, bottom = self.top, self.bottom
        parts = parts if source is None else source
        whole = [
            lambda: remote(parts.at[3, top], self.diag.at[0], pair, base + 0, to_dp(1)),
            lambda: remote(parts.at[3, bottom], self.diag.at[1], pair, base + 1, to_dp(2)),
        ]
        self.first = [make() if pieces == 1 else None for make in whole] + [
            remote(parts.at[1, top], self.full.at[0, top], pair, base + 2, to_dp(1)),
            remote(parts.at[2, bottom], self.full.at[1, bottom], pair, base + 3, to_dp(2)),
        ]
        self.second = [
            remote(self.out.at[0], self.full.at[0, bottom], pair, base + 4, to_dp(1)),
            remote(self.out.at[1], self.full.at[1, top], pair, base + 5, to_dp(2)),
        ]

    def send_columns(self, cols, index):
        for copy in self.column_copies(cols, index):
            copy.start()

    def column_copies(self, cols, index):
        here = pl.ds(cols.start, cols.stop - cols.start)
        return [
            remote(
                self.parts.at[3, rows, here],
                self.diag.at[side, rows_in, here],
                self.pair,
                self.column_base + 2 * index + side,
                to_dp(1 + side),
            )
            for side, rows, rows_in in (
                (0, self.top, pl.ds(0, self.half)),
                (1, self.bottom, pl.ds(0, self.half)),
            )
        ]

    def send(self, k):
        for copy in {3: self.first[:2], 1: self.first[2:3], 2: self.first[3:]}[k]:
            copy.start()

    def diag_wait(self, side):
        if self.pieces == 1:
            self.first[side].wait_recv()
            return
        size = self.parts.shape[2] // self.pieces
        for n in range(self.pieces):
            self.column_copies(slice(n * size, n * size + size), n)[side].wait_recv()

    def relay(self):
        self.diag_wait(1)
        self.out[0] = (
            self.parts[1, self.bottom].astype(FULL) + self.diag[1].astype(FULL)
        ).astype(LOW)
        self.second[0].start()
        self.diag_wait(0)
        self.out[1] = (self.parts[2, self.top].astype(FULL) + self.diag[0].astype(FULL)).astype(
            LOW
        )
        self.second[1].start()

    def finish(self):
        self.first[2].wait_recv()
        self.first[3].wait_recv()
        self.second[0].wait_recv()
        self.second[1].wait_recv()
        for copy in self.first[2:] + self.second:
            copy.wait_send()
        size = self.parts.shape[2] // self.pieces
        for n in range(self.pieces):
            if self.pieces > 1:
                for copy in self.column_copies(slice(n * size, n * size + size), n):
                    copy.wait_send()
        if self.pieces == 1:
            for copy in self.first[:2]:
                copy.wait_send()

    def rows(self, part):
        return (
            self.parts[0, part].astype(FULL)
            + self.full[0, part].astype(FULL)
            + self.full[1, part].astype(FULL)
        )


def row_sum_scratch(rows, cols):
    return [
        pltpu.VMEM((2, rows // 2, cols), LOW),
        pltpu.VMEM((2, rows // 2, cols), LOW),
        pltpu.VMEM((2, rows, cols), LOW),
    ]


def mid_forward_kernel(
    mix_ref, w_ref, tok_ref, norm_ref, resid_hbm, normed_all,
    resid_ref, parts, out, diag, full, own, send, recv, local,
):
    rows = tok_ref.shape[0]
    greet([to_dp(1), to_dp(2)])
    total = RowSum(parts, (out, diag, full), (send, recv), 0)
    for k in (3, 1, 2, 0):
        parts[k] = jnp.dot(mix_ref[k], w_ref[...], preferred_element_type=FULL).astype(LOW)
        if k:
            total.send(k)
    total.relay()
    total.finish()

    def body(here):
        resid = tok_ref[here].astype(FULL) + total.rows(here)
        resid_ref[here] = resid
        unit, _ = unit_rows(resid)
        own[here] = (unit * norm_ref[5:6, :] + norm_ref[6:7, :]).astype(LOW)

    in_chunks(rows, body)
    sent = spread(own, normed_all, (send, recv), 6)
    stores = [
        pltpu.make_async_copy(own, normed_all.at[0], local.at[0]),
        pltpu.make_async_copy(resid_ref, resid_hbm, local.at[1]),
    ]
    for copy in stores:
        copy.start()
    pass_on(*sent)
    spread_end(*sent)
    for copy in stores:
        copy.wait()


def mid_forward(mixture, w_out, tokens, norm_vals, number):
    rows, cols = tokens.shape
    group = (N_DP, rows, cols)
    return pl.pallas_call(
        mid_forward_kernel,
        out_shape=[
            jax.ShapeDtypeStruct(tokens.shape, FULL),
            jax.ShapeDtypeStruct(group, LOW),
        ],
        in_specs=[VMEM] * 4,
        out_specs=[ANY, ANY],
        scratch_shapes=[pltpu.VMEM((rows, cols), FULL), pltpu.VMEM(group, LOW)]
        + row_sum_scratch(rows, cols)
        + [pltpu.VMEM((rows, cols), LOW)]
        + sems(12)
        + [pltpu.SemaphoreType.DMA((2,))],
        compiler_params=comm_params(number),
        cost_estimate=cost(92),
        name="mid_forward",
    )(mixture, w_out, tokens, norm_vals)


def mid_backward_kernel(
    x_hbm, own_cot, near_hbm, far_hbm, wgu_hbm, wdown_hbm, gate_hbm, up_hbm, resid_hbm, norm_ref,
    grad_hbm, own_hbm, sum_ref, part_hbm,
    left, w_gu, w_down, gate_stage, up_stage, ggu, resid_ref, grad_ref, parts,
    out, diag, full, own, send, recv, local, loads, pair_send, pair_recv, pair_local, ready,
):
    rows, cols = resid_ref.shape
    width = w_down.shape[1]
    pieces = 4
    size = cols // pieces
    order = (3, 1, 2, 0)
    seqs = [pl.ds(k * rows, rows) for k in range(N_DP)]
    sources = (own_cot, near_hbm.at[0], near_hbm.at[1], far_hbm)

    def data(k):
        return pltpu.make_async_copy(sources[k], left.at[seqs[k]], local.at[k])

    def stage_loads(n):
        k = order[n]
        return [
            pltpu.make_async_copy(source.at[seqs[k]], stage.at[n % 2], loads.at[2 * (n % 2) + i])
            for i, (source, stage) in enumerate(((gate_hbm, gate_stage), (up_hbm, up_stage)))
        ]

    weights = [
        pltpu.make_async_copy(
            wgu_hbm.at[pl.ds(2 * n, 2)], w_gu.at[pl.ds(2 * n, 2)], local.at[4 + n]
        )
        for n in range(pieces)
    ]
    down_load = pltpu.make_async_copy(wdown_hbm, w_down, loads.at[4])
    later = [
        pltpu.make_async_copy(resid_hbm, resid_ref, local.at[8]),
        pltpu.make_async_copy(own_cot, own, local.at[9]),
    ]
    for copy in [data(3), down_load] + stage_loads(0) + weights[:2] + [data(1)] + stage_loads(1):
        copy.start()
    for copy in weights[2:] + [data(2), data(0)] + later:
        copy.start()
    greet([to_dp(1), to_dp(2), partner()])

    total = RowSum(parts, (out, diag, full), (send, recv), 0, pieces, 6)
    down_load.wait()
    for n, k in enumerate(order):
        data(k).wait()
        for copy in stage_loads(n):
            copy.wait()
        here = slice(k * rows, k * rows + rows)
        for begin, end in column_cuts(width):
            grad = jnp.dot(left[here], w_down[:, begin:end], preferred_element_type=FULL)
            gate, up = gate_stage[n % 2, :, begin:end], up_stage[n % 2, :, begin:end]
            sig = 1.0 / (1.0 + jnp.exp(-gate))
            ggu[here, begin:end] = (grad * up * sig * (1.0 + gate * (1.0 - sig))).astype(LOW)
            ggu[here, width + begin : width + end] = (grad * gate * sig).astype(LOW)
        if n + 2 < N_DP:
            for copy in stage_loads(n + 2):
                copy.start()
        for piece in range(pieces):
            if n == 0:
                weights[piece].wait()
            columns = slice(piece * size, piece * size + size)
            parts[k, :, columns] = lax.dot_general(
                ggu[here],
                w_gu[2 * piece : 2 * piece + 2].reshape(size, 2 * width),
                LAST_DIMS,
                preferred_element_type=FULL,
            ).astype(LOW)
            if n == 0:
                total.send_columns(columns, piece)
        if k and n:
            total.send(k)
    reload = pltpu.make_async_copy(x_hbm, left, local.at[10])
    reload.start()
    pl.semaphore_signal(ready, inc=1, device_id=partner(), device_id_type=MESH)
    sum_ref[...] = jnp.zeros_like(sum_ref)
    total.relay()
    reload.wait()
    pl.semaphore_wait(ready, 1)
    buffers = (w_gu.at[pl.ds(4, 2)], w_gu.at[pl.ds(0, 4)], w_gu.at[pl.ds(6, 2)])
    grad = PairGrad(left, ggu, part_hbm, buffers + (pair_send, pair_recv, pair_local))
    grad.run()
    for copy in later:
        copy.wait()
    total.finish()

    def body(here):
        grads = total.rows(here)
        unit, inverse = unit_rows(resid_ref[here])
        sum_ref[0:1, :] += jnp.sum(grads * unit, axis=0, keepdims=True)
        sum_ref[1:2, :] += jnp.sum(grads, axis=0, keepdims=True)
        grad = own[here].astype(FULL) + layer_back(grads, norm_ref[5:6, :], unit, inverse)
        grad_ref[here] = grad
        own[here] = grad.astype(LOW)

    in_chunks(rows, body)
    stores = [
        pltpu.make_async_copy(own, own_hbm, local.at[0]),
        pltpu.make_async_copy(grad_ref, grad_hbm, local.at[1]),
    ]
    for copy in stores:
        copy.start()
    grad.end()
    for copy in stores:
        copy.wait()


def mid_backward(
    normed2, cotangent, near, far, w_gu, w_down, gate, up, resid, norm_vals, number
):
    rows, cols = resid.shape
    total, width = gate.shape
    blocks = (N_SH, cols // N_SH, 2 * width)
    return pl.pallas_call(
        mid_backward_kernel,
        out_shape=[
            jax.ShapeDtypeStruct(resid.shape, FULL),
            jax.ShapeDtypeStruct(resid.shape, LOW),
            jax.ShapeDtypeStruct((8, cols), FULL),
            jax.ShapeDtypeStruct((N_SH // 2,) + blocks[1:], LOW),
        ],
        in_specs=[ANY] * 9 + [VMEM],
        out_specs=[ANY, ANY, VMEM, ANY],
        scratch_shapes=[
            pltpu.VMEM(normed2.shape, LOW),
            pltpu.VMEM(blocks, LOW),
            pltpu.VMEM(w_down.shape, LOW),
            pltpu.VMEM((2, rows, width), FULL),
            pltpu.VMEM((2, rows, width), FULL),
            pltpu.VMEM((total, 2 * width), LOW),
            pltpu.VMEM(resid.shape, FULL),
            pltpu.VMEM(resid.shape, FULL),
            pltpu.VMEM((N_DP, rows, cols), LOW),
        ]
        + row_sum_scratch(rows, cols)
        + [pltpu.VMEM((rows, cols), LOW)]
        + sems(14)
        + [pltpu.SemaphoreType.DMA((11,)), pltpu.SemaphoreType.DMA((6,))]
        + sems(N_SH // 2)
        + [pltpu.SemaphoreType.DMA((2,)), pltpu.SemaphoreType.REGULAR],
        compiler_params=comm_params(number),
        cost_estimate=cost(70),
        name="mid_backward",
    )(normed2, cotangent, near, far, w_gu.reshape(blocks), w_down, gate, up, resid, norm_vals)


def share_kernel(own_ref, hid_hbm, wdown_hbm, gao_all, part_hbm, hid, w_down, part_ref, send, recv, local):
    loads = [
        pltpu.make_async_copy(wdown_hbm, w_down, local.at[0]),
        pltpu.make_async_copy(hid_hbm, hid, local.at[1]),
    ]
    for copy in loads:
        copy.start()
    greet([to_dp(1), to_dp(2)])
    sent = spread(own_ref, gao_all, (send, recv), 0)
    stores = [pltpu.make_async_copy(own_ref, gao_all.at[0], local.at[2])]
    stores[0].start()
    for copy in loads:
        copy.wait()
    for k in range(N_DP):
        part_ref[k] = lax.dot_general(
            hid[k], w_down[...], LAST_DIMS, preferred_element_type=FULL
        ).astype(LOW)
        stores.append(pltpu.make_async_copy(part_ref.at[k], part_hbm.at[k], local.at[3 + k]))
        stores[-1].start()
    pass_on(*sent)
    spread_end(*sent)
    for copy in stores:
        copy.wait()


def share(own, hidden, w_down, number):
    group = jax.ShapeDtypeStruct((N_DP,) + own.shape, LOW)
    return pl.pallas_call(
        share_kernel,
        out_shape=[group, group],
        in_specs=[VMEM, ANY, ANY],
        out_specs=[ANY, ANY],
        scratch_shapes=[
            pltpu.VMEM(hidden.shape, LOW),
            pltpu.VMEM(w_down.shape, LOW),
            pltpu.VMEM(group.shape, LOW),
        ]
        + sems(6)
        + [pltpu.SemaphoreType.DMA((3 + N_DP,))],
        compiler_params=comm_params(number),
        cost_estimate=cost(48),
        name="share",
    )(own, hidden, w_down)


LINE = N_SH // 2
PIECES = 4


class LineSum:
    def __init__(self, terms_hbm, scratch, sem_refs):
        (self.terms, self.up_in, self.down_in, self.up_out, self.down_out) = scratch
        self.hbm = terms_hbm
        (up_s, up_r, down_s, down_r, self.local) = sem_refs
        self.up_sems, self.down_sems = (up_s, up_r), (down_s, down_r)
        mine, place = lax.axis_index("dp"), lax.axis_index("shard")
        self.line = place // 2
        self.above, self.below = (mine, place + 2), (mine, place - 2)
        self.size = self.terms.shape[1] // PIECES
        self.steps = (LINE - 1) * PIECES

    def at_end(self):
        return (self.line == 0) | (self.line == LINE - 1)

    def rows(self, piece):
        return pl.ds(pl.multiple_of(piece * self.size, self.size), self.size)

    def load(self, target):
        return pltpu.make_async_copy(self.hbm.at[target], self.terms.at[target], self.local.at[target])

    def load_all(self):
        for target in (LINE - 1, 0, LINE - 2, 1):
            self.load(target).start()

    def own(self, target, piece):
        @pl.when(piece == 0)
        def _():
            self.load(target).wait()

        return self.terms[target, self.rows(piece)].astype(FULL)

    def up_copy(self, index):
        return remote(
            self.up_out.at[index], self.up_in.at[index], self.up_sems, index, self.above
        )

    def down_copy(self, index):
        return remote(
            self.down_out.at[index], self.down_in.at[index], self.down_sems, index, self.below
        )

    def up(self, index):
        target, piece = LINE - 1 - index // PIECES, index % PIECES

        @pl.when(target > self.line)
        def _():
            self.up_out[index] = self.own(target, piece).astype(LOW)

            @pl.when(self.line > 0)
            def _():
                self.up_copy(index).wait_recv()
                self.up_out[index] = (
                    self.up_out[index].astype(FULL) + self.up_in[index].astype(FULL)
                ).astype(LOW)

            self.up_copy(index).start()

    def down(self, index):
        target, piece = index // PIECES, index % PIECES

        @pl.when(target < self.line)
        def _():
            self.down_out[index] = self.own(target, piece).astype(LOW)

            @pl.when(self.line < LINE - 1)
            def _():
                self.down_copy(index).wait_recv()
                self.down_out[index] = (
                    self.down_out[index].astype(FULL) + self.down_in[index].astype(FULL)
                ).astype(LOW)

            self.down_copy(index).start()

    def run(self, begin, end):
        def step(index, carry):
            @pl.when(self.line < LINE // 2)
            def _():
                @pl.when(index < self.steps)
                def _():
                    self.up(index)

                @pl.when(index > 0)
                def _():
                    self.down(index - 1)

            @pl.when(self.line >= LINE // 2)
            def _():
                @pl.when(index < self.steps)
                def _():
                    self.down(index)

                @pl.when(index > 0)
                def _():
                    self.up(index - 1)

            return carry

        lax.fori_loop(begin, end, step, 0)

    def finish(self, piece, result):
        here = self.rows(piece)
        result[here] = self.own(self.line, piece)

        @pl.when(self.line > 0)
        def _():
            index = (LINE - 1 - self.line) * PIECES + piece
            self.up_copy(index).wait_recv()
            result[here] = result[here] + self.up_in[index].astype(FULL)

        @pl.when(self.line < LINE - 1)
        def _():
            index = self.line * PIECES + piece
            self.down_copy(index).wait_recv()
            result[here] = result[here] + self.down_in[index].astype(FULL)

    def drain(self):
        def step(index, carry):
            @pl.when(LINE - 1 - index // PIECES > self.line)
            def _():
                self.up_copy(index).wait_send()

            @pl.when(index // PIECES < self.line)
            def _():
                self.down_copy(index).wait_send()

            return carry

        lax.fori_loop(0, self.steps, step, 0)


def line_sum_scratch(rows, cols):
    steps = (LINE - 1) * PIECES
    return (
        [pltpu.VMEM((LINE, rows, cols), LOW)]
        + [pltpu.VMEM((steps, rows // PIECES, cols), LOW)] * 4
        + sems(steps)
        + sems(steps)
        + [pltpu.SemaphoreType.DMA((LINE,))]
    )


def fold(values, total):
    values = values * values
    for start in range(0, values.shape[1], 128):
        total = total + values[:, start : start + 128]
    return total


def last_kernel(
    attn_hbm, grad_qkv_hbm, w_hbm, gu_hbm, down_hbm, tok_hbm, grad_hbm, norm_ref, bias_ref, two_ref,
    input_hbm, norm_total_ref, gu_out, down_out, qkv_out, out_ref, total_ref,
    grad_qkv_ref, w_ref, tok_ref, grad_ref, gu_in, down_in_low,
    parts, out, diag, full, sum_ref, near, far, part, near_part, far_part, attn_sum, attn_low,
    terms, up_in, down_in, up_out, down_out_pieces,
    up_s, up_r, down_s, down_r, term_local,
    send, recv, send_a, recv_a, send_b, recv_b, send_c, recv_c, send_d, recv_d, local,
):
    rows = tok_ref.shape[0]
    mine, place = lax.axis_index("dp"), lax.axis_index("shard")
    loads = [
        pltpu.make_async_copy(source, target, local.at[3 + n])
        for n, (source, target) in enumerate(
            (
                (w_hbm.at[pl.ds(0, w_hbm.shape[0] // 4)], w_ref.at[pl.ds(0, w_hbm.shape[0] // 4)]),
                (grad_qkv_hbm, grad_qkv_ref),
                (tok_hbm, tok_ref),
                (grad_hbm, grad_ref),
                (gu_hbm, gu_in),
                (down_hbm, down_in_low),
            )
        )
    ]
    line = LineSum(
        attn_hbm,
        (terms, up_in, down_in, up_out, down_out_pieces),
        (up_s, up_r, down_s, down_r, term_local),
    )
    line.load_all()
    pieces = 4
    size_in = w_ref.shape[0] // pieces
    weights = [loads[0]] + [
        pltpu.make_async_copy(
            w_hbm.at[pl.ds(n * size_in, size_in)], w_ref.at[pl.ds(n * size_in, size_in)], local.at[9 + n]
        )
        for n in range(1, pieces)
    ]
    for copy in [loads[1]] + weights + loads[2:]:
        copy.start()
    greet([to_dp(k) for k in (1, 2, 3)] + [to_shard(j) for j in range(1, N_SH)])
    total = RowSum(parts, (out, diag, full), (send, recv), 0, pieces, 6)
    blocks = []
    for n, (held, target) in enumerate(((gu_hbm, gu_out), (down_hbm, down_out))):
        for k in (3, 1, 2):
            blocks.append(
                remote(
                    held.at[dp_peer(k)], target.at[mine], (send_c, recv_c), 3 * n + k - 1, to_dp(k)
                )
            )
    keeps = [
        pltpu.make_async_copy(gu_in.at[mine], gu_out.at[mine], local.at[0]),
        pltpu.make_async_copy(down_in_low.at[mine], down_out.at[mine], local.at[1]),
    ]
    for copy in blocks[3:]:
        copy.start()
    middle = jnp.logical_not(line.at_end())
    line.run(0, 1)

    def norm1_part(k):
        parts[k] = lax.dot_general(
            grad_qkv_ref[k], w_ref[...], LAST_DIMS, preferred_element_type=FULL
        ).astype(LOW)
        if k:
            total.send(k)

    def middle_run(begin, end):
        @pl.when(middle)
        def _():
            line.run(begin, end)

    loads[1].wait()
    for n in range(pieces):
        weights[n].wait()
        here = slice(n * size_in, n * size_in + size_in)
        parts[3, :, here] = lax.dot_general(
            grad_qkv_ref[3], w_ref[here, :], LAST_DIMS, preferred_element_type=FULL
        ).astype(LOW)
        total.send_columns(here, n)

    @pl.when(line.at_end())
    def _():
        line.run(1, line.steps + 1)

    middle_run(1, 2)
    norm1_part(1)
    middle_run(2, 3)
    norm1_part(2)
    middle_run(3, 4)
    norm1_part(0)
    sum_ref[...] = jnp.zeros_like(sum_ref)
    sum_ref[5:7, :] = two_ref[0:2, :]
    bias_width = bias_ref.shape[1] // 3
    for d in range(N_DP):

        @pl.when(mine == d)
        def _(d=d):
            for n in range(3):
                sum_ref[2 + n : 3 + n, d * bias_width : (d + 1) * bias_width] = bias_ref[
                    0:1, n * bias_width : (n + 1) * bias_width
                ]

    middle_run(4, 6)
    total.relay()
    for copy in blocks[:3]:
        copy.start()
    loads[4].wait()
    loads[5].wait()
    for copy in keeps:
        copy.start()

    def square_low(array, value):
        def step(index, value):
            here = pl.ds(pl.multiple_of(index * 16, 16), 16)
            for k in range(N_DP):
                rows16 = array[k, here].astype(FULL)
                value = fold(rows16[8:], fold(rows16[:8], value))
            return value

        return lax.fori_loop(0, array.shape[1] // 16, step, value)

    part[...] = square_low(down_in_low, square_low(gu_in, jnp.zeros(part.shape, FULL)))
    middle_run(6, 9)
    total.finish()
    loads[2].wait()
    loads[3].wait()

    def body(here):
        grads = total.rows(here)
        unit, inverse = unit_rows(tok_ref[here].astype(FULL))
        sum_ref[0:1, :] += jnp.sum(grads * unit, axis=0, keepdims=True)
        sum_ref[1:2, :] += jnp.sum(grads, axis=0, keepdims=True)
        grad_ref[here] = to_places(
            grad_ref[here] + layer_back(grads, norm_ref[0:1, :], unit, inverse)
        )

    in_chunks(rows, body)
    keeps.append(pltpu.make_async_copy(grad_ref, input_hbm, local.at[9]))
    keeps[-1].start()
    norm_near = [
        remote(sum_ref, near.at[k - 1], (send_a, recv_a), k - 1, to_dp(k)) for k in (1, 2, 3)
    ]
    for copy in norm_near:
        copy.start()
    for copy in norm_near:
        copy.wait()
    sum_ref[...] = sum_ref[...] + near[0] + near[1] + near[2]
    norm_far = [
        remote(sum_ref, far.at[j - 1], (send_b, recv_b), j - 1, to_shard(j))
        for j in range(1, N_SH)
    ]
    for copy in norm_far:
        copy.start()

    width = qkv_out.shape[-1]
    size = qkv_out.shape[1]

    def trade(sender, owner):
        return pltpu.make_async_remote_copy(
            src_ref=attn_low.at[owner],
            dst_ref=qkv_out.at[sender],
            send_sem=send_d.at[owner],
            recv_sem=recv_d.at[sender],
            device_id=(owner, place),
            device_id_type=MESH,
        )

    squares = part[...]
    for d in range(N_DP):
        line.finish(d, attn_sum)

        def square(index, value, d=d):
            here = pl.ds(pl.multiple_of(d * size + index * 8, 8), 8)
            return fold(attn_sum[here], value)

        squares = lax.fori_loop(0, size // 8, square, squares)
        if d == N_DP - 1:
            part[...] = squares
            small = [
                remote(part, near_part.at[k - 1], (send_a, recv_a), 2 + k, to_dp(k))
                for k in (1, 2, 3)
            ]
            for copy in small:
                copy.start()
        attn_low[d] = attn_sum[d * size : d * size + size, :width].astype(LOW)

        @pl.when(mine != d)
        def _(d=d):
            trade(mine, d).start()

    keep = pltpu.make_async_copy(attn_low.at[mine], qkv_out.at[mine], local.at[2])
    keep.start()
    for copy in small:
        copy.wait()
    part[...] = part[...] + near_part[0] + near_part[1] + near_part[2]
    small = [
        remote(part, far_part.at[j - 1], (send_b, recv_b), N_SH - 2 + j, to_shard(j))
        for j in range(1, N_SH)
    ]
    for copy in small:
        copy.start()
    out_ref[...] = to_places(
        jnp.concatenate(
            [attn_sum[d * size : d * size + size, width:] for d in range(N_DP)], axis=1
        )
    )
    for copy in norm_far:
        copy.wait()
    norm_total = sum_ref[...]
    for j in range(N_SH - 1):
        norm_total = norm_total + far[j]
    norm_total_ref[...] = norm_total
    squares = fold(norm_total, part[...])
    for copy in small:
        copy.wait()
    for j in range(N_SH - 1):
        squares = squares + far_part[j]
    total_ref[0, 0] = jnp.sum(squares)
    line.drain()
    for copy in blocks + keeps + [keep]:
        copy.wait()
    for d in range(N_DP):

        @pl.when(mine != d)
        def _(d=d):
            trade(mine, d).wait_send()
            trade(d, mine).wait_recv()


def last(
    part_attn, grad_qkv, w_qkv, gu_sum, down_sum, tokens, grad_resid, norm_vals, biases, sums, number
):
    rows, cols = tokens.shape
    rest = sums
    square_shape = (8, 128)
    block = part_attn.shape[1:]
    width = grad_qkv.shape[-1]
    size = block[0] // N_DP
    return pl.pallas_call(
        last_kernel,
        out_shape=[
            jax.ShapeDtypeStruct(tokens.shape, FULL),
            jax.ShapeDtypeStruct(rest.shape, FULL),
            jax.ShapeDtypeStruct(gu_sum.shape, gu_sum.dtype),
            jax.ShapeDtypeStruct(down_sum.shape, down_sum.dtype),
            jax.ShapeDtypeStruct((N_DP, size, width), LOW),
            jax.ShapeDtypeStruct((size, D), FULL),
            jax.ShapeDtypeStruct((1, 1), FULL),
        ],
        in_specs=[ANY] * 7 + [VMEM] * 3,
        out_specs=[ANY, VMEM, ANY, ANY, ANY, VMEM, pl.BlockSpec(memory_space=pltpu.SMEM)],
        scratch_shapes=[
            pltpu.VMEM(a.shape, a.dtype)
            for a in (grad_qkv, w_qkv, tokens, grad_resid, gu_sum, down_sum)
        ]
        + [pltpu.VMEM((N_DP, rows, cols), LOW)]
        + row_sum_scratch(rows, cols)
        + [
            pltpu.VMEM(rest.shape, FULL),
            pltpu.VMEM((N_DP - 1,) + rest.shape, FULL),
            pltpu.VMEM((N_SH - 1,) + rest.shape, FULL),
            pltpu.VMEM(square_shape, FULL),
            pltpu.VMEM((N_DP - 1,) + square_shape, FULL),
            pltpu.VMEM((N_SH - 1,) + square_shape, FULL),
            pltpu.VMEM(block, FULL),
            pltpu.VMEM((N_DP, size, width), LOW),
        ]
        + line_sum_scratch(*block)
        + sems(14)
        + sems(2 * (N_DP - 1))
        + sems(2 * (N_SH - 1))
        + sems(6)
        + sems(N_DP)
        + [pltpu.SemaphoreType.DMA((13,))],
        compiler_params=comm_params(number),
        cost_estimate=cost(90),
        name="last",
    )(
        part_attn,
        grad_qkv,
        w_qkv,
        gu_sum,
        down_sum,
        tokens,
        grad_resid,
        norm_vals,
        biases,
        sums,
    )


def column_cuts(cols):
    return [(c, min(c + 256, cols)) for c in range(0, cols, 256)]


class PairGrad:
    def __init__(self, left, right, target, scratch, extra=None):
        self.left, self.right, self.target, self.extra = left, right, target, extra
        self.give, self.take, self.keep, send, recv, self.local = scratch
        self.pair = (send, recv)
        place = lax.axis_index("shard")
        self.core = place % 2
        self.partner = (lax.axis_index("dp"), place + 1 - 2 * self.core)
        self.size, self.count = self.give.shape[1], self.take.shape[0]

    def move(self, index):
        return remote(
            self.give.at[index % 2], self.take.at[index], self.pair, index, self.partner
        )

    def store(self, index):
        return pltpu.make_async_copy(
            self.keep.at[index % 2], self.target.at[index], self.local.at[index % 2]
        )

    def fill(self, target, index):
        here = pl.ds(pl.multiple_of(index * self.size, self.size), self.size)
        cols = self.right.shape[1]
        half = cols // 2 if cols > 2048 else cols
        for begin in range(0, cols, half):
            target[:, begin : begin + half] = lax.dot_general(
                self.left[:, here],
                self.right[:, begin : begin + half],
                LEAD_DIMS,
                preferred_element_type=FULL,
            ).astype(LOW)
        if self.extra is not None:
            self.extra(target, index)

    def add(self, index):
        self.move(index).wait_recv()
        slot = index % 2
        self.keep[slot] = (self.keep[slot].astype(FULL) + self.take[index].astype(FULL)).astype(LOW)
        self.store(index).start()

    def run(self):
        def step(index, carry):
            @pl.when(index >= 2)
            def _():
                self.move(index - 2).wait_send()
                self.store(index - 2).wait()

            self.fill(self.give.at[index % 2], 2 * index + 1 - self.core)
            self.move(index).start()
            self.fill(self.keep.at[index % 2], 2 * index + self.core)

            @pl.when(index >= 1)
            def _():
                self.add(index - 1)

            return carry

        lax.fori_loop(0, self.count, step, 0)
        self.add(self.count - 1)

    def end(self):
        for index in (self.count - 2, self.count - 1):
            self.move(index).wait_send()
            self.store(index).wait()


def pair_grad_scratch(rows, cols):
    size = rows // N_SH
    count = N_SH // 2
    return [
        pltpu.VMEM((2, size, cols), LOW),
        pltpu.VMEM((count, size, cols), LOW),
        pltpu.VMEM((2, size, cols), LOW),
        *sems(count),
        pltpu.SemaphoreType.DMA((2,)),
    ]


def partner():
    place = lax.axis_index("shard")
    return (lax.axis_index("dp"), place + 1 - 2 * (place % 2))


def mlp_one_kernel(
    x_hbm, own_hbm, near_hbm, wgu_hbm, hid_out, gate_out, up_out, part_out, far_out,
    x_ref, cot_ref, w_gu, hid, gate_stage, up_stage, local, loads, stores, send, recv,
    *grad_scratch,
):
    total = x_ref.shape[0]
    known = N_DP - 1
    seq = total // N_DP
    half = seq // 2
    greet([to_dp(1), to_dp(2), partner()])
    passed = [
        remote(
            near_hbm.at[0, pl.ds(0, half)],
            cot_ref.at[pl.ds(known * seq, half)],
            (send, recv),
            0,
            to_dp(2),
        ),
        remote(
            near_hbm.at[1, pl.ds(half, half)],
            cot_ref.at[pl.ds(known * seq + half, half)],
            (send, recv),
            1,
            to_dp(1),
        ),
    ]
    for copy in passed:
        copy.start()
    cols = hid.shape[1]
    cuts = column_cuts(cols)
    block = total // 2

    def weight_loads(n):
        begin, end = cuts[n]
        return [
            pltpu.make_async_copy(
                wgu_hbm.at[:, pl.ds(at, end - begin)],
                w_gu.at[:, pl.ds(at, end - begin)],
                loads.at[2 * n + i],
            )
            for i, at in enumerate((begin, cols + begin))
        ]

    def stage_stores(n):
        begin, end = cuts[n]
        return [
            pltpu.make_async_copy(
                stage.at[n % 2, :, pl.ds(0, end - begin)],
                target.at[:, pl.ds(begin, end - begin)],
                stores.at[2 * i + n % 2],
            )
            for i, (stage, target) in enumerate(((gate_stage, gate_out), (up_stage, up_out)))
        ]

    data = [pltpu.make_async_copy(x_hbm, x_ref, local.at[0])]
    for copy in weight_loads(0) + data:
        copy.start()
    for n in range(1, len(cuts)):
        for copy in weight_loads(n):
            copy.start()
    data += [
        pltpu.make_async_copy(source, cot_ref.at[pl.ds(k * seq, seq)], local.at[5 + k])
        for k, source in enumerate((own_hbm, near_hbm.at[0], near_hbm.at[1]))
    ]
    for copy in data[1:]:
        copy.start()
    data[0].wait()
    for n, (begin, end) in enumerate(cuts):
        for copy in weight_loads(n):
            copy.wait()
        if n >= 2:
            for copy in stage_stores(n - 2):
                copy.wait()

        def rows(index, carry, begin=begin, end=end, slot=n % 2):
            here = pl.ds(pl.multiple_of(index * block, block), block)
            gate = jnp.dot(x_ref[here], w_gu[:, begin:end], preferred_element_type=FULL)
            up = jnp.dot(
                x_ref[here], w_gu[:, cols + begin : cols + end], preferred_element_type=FULL
            )
            hid[here, begin:end] = (gate / (1.0 + jnp.exp(-gate)) * up).astype(LOW)
            gate_stage[slot, here, : end - begin] = gate
            up_stage[slot, here, : end - begin] = up
            return carry

        lax.fori_loop(0, total // block, rows, 0)
        for copy in stage_stores(n):
            copy.start()
    outs = [
        pltpu.make_async_copy(hid, hid_out, local.at[2]),
        pltpu.make_async_copy(cot_ref.at[pl.ds(known * seq, seq)], far_out, local.at[1]),
    ]
    outs[0].start()
    for copy in data[1:]:
        copy.wait()
    for copy in passed:
        copy.wait()
    outs[1].start()
    grad = PairGrad(cot_ref, hid, part_out, grad_scratch)
    grad.run()
    for n in (len(cuts) - 2, len(cuts) - 1):
        for copy in stage_stores(n):
            copy.wait()
    grad.end()
    for copy in outs:
        copy.wait()


def mlp_one(normed2, cotangent, near, w_gu, number):
    total, width = normed2.shape
    cols = w_gu.shape[1] // 2
    values = jax.ShapeDtypeStruct((total, cols), FULL)
    return pl.pallas_call(
        mlp_one_kernel,
        out_shape=[
            jax.ShapeDtypeStruct((total, cols), LOW),
            values,
            values,
            jax.ShapeDtypeStruct((N_SH // 2, width // N_SH, cols), LOW),
            jax.ShapeDtypeStruct(cotangent.shape, LOW),
        ],
        in_specs=[ANY] * 4,
        out_specs=[ANY] * 5,
        scratch_shapes=[
            pltpu.VMEM((total, width), LOW),
            pltpu.VMEM((total, width), LOW),
            pltpu.VMEM((width, 2 * cols), LOW),
            pltpu.VMEM((total, cols), LOW),
            pltpu.VMEM((2, total, 256), FULL),
            pltpu.VMEM((2, total, 256), FULL),
            pltpu.SemaphoreType.DMA((8,)),
            pltpu.SemaphoreType.DMA((2 * len(column_cuts(cols)),)),
            pltpu.SemaphoreType.DMA((4,)),
        ]
        + sems(2)
        + pair_grad_scratch(width, cols),
        compiler_params=comm_params(number),
        cost_estimate=cost(30),
        name="mlp_one",
    )(normed2, cotangent, near, w_gu)


FIRST_HAT = 1.0 / (1.0 - BETA_ONE**STEP)
SECOND_HAT = 1.0 / (1.0 - BETA_TWO**STEP)


def clip_factor(total_ref, width):
    total = jnp.full((1, width), total_ref[0, 0], FULL)
    return CLIP_NORM / jnp.maximum(jnp.sqrt(total), CLIP_NORM)


def adam_step(grads, factor, master, first, second):
    clipped = grads.astype(FULL) * factor
    first_new = BETA_ONE * first + (1.0 - BETA_ONE) * clipped
    second_new = BETA_TWO * second + (1.0 - BETA_TWO) * clipped * clipped
    ratio = first_new * (RATE_MATRIX * FIRST_HAT) / (jnp.sqrt(second_new * SECOND_HAT) + ADAM_EPS)
    return (master * (1.0 - RATE_MATRIX * DECAY_MATRIX) - ratio, first_new, second_new)


def adam_kernel(
    total_ref, norm_ref, master_ref, first_ref, second_ref, rows_ref, low_ref,
    qkv_ref, out_ref, gu_ref, down_ref, *refs,
):
    norm_outs, (rows_out, low_out), refs = refs[6:9], refs[9:11], refs[:6] + refs[11:]
    factor = clip_factor(total_ref, 128)[:, 0:1]
    rows_out[...] = rows_ref[...]
    low_out[...] = low_ref[...]

    @pl.when(pl.program_id(0) == 0)
    def _():
        size = master_ref.shape[1]
        mine, place = lax.axis_index("dp"), lax.axis_index("shard")
        grads = jnp.zeros((8, size), FULL)
        row = lax.broadcasted_iota(jnp.int32, (8, size), 0)
        bias = (row >= 2) & (row < 5)
        spot = jnp.where(bias, mine * N_SH + place, place * N_DP + mine)
        for n in range(N_DP * N_SH):
            grads = jnp.where(spot == n, norm_ref[:, n * size : n * size + size], grads)
        values = adam_update(
            master_ref[...], first_ref[...], second_ref[...], grads[:7], factor, RATE_VECTOR, 0.0
        )
        for ref, value in zip(norm_outs, values):
            ref[...] = value

    def update(begin, grads, states, results):
        here = slice(begin, begin + grads.shape[1])
        values = adam_step(grads, factor, *[ref[:, here] for ref in states])
        for ref, value in zip(results, values):
            ref[:, here] = value

    attn, mlp = (refs[0:3], refs[6:9]), (refs[3:6], refs[9:12])
    width, ff_width = qkv_ref.shape[-1] // 3, down_ref.shape[-1]
    for d in range(N_DP):
        for part in range(3):
            here = slice(part * width, part * width + width)
            update(part * D + d * width, qkv_ref[d, :, here], *attn)
        for part in range(2):
            here = slice(part * ff_width, part * ff_width + ff_width)
            update(part * FF + d * ff_width, gu_ref[d, :, here], *mlp)
        update(2 * FF + d * ff_width, down_ref[d], *mlp)
    update(3 * D, out_ref[...], *attn)


def adam(total, norm_sums, norm_states, row_outputs, grads, states):
    size = 16
    steps = states[0].shape[0] // size

    def block(array):
        if array.ndim == 3:
            return pl.BlockSpec((N_DP, size, array.shape[-1]), lambda j: (0, j, 0))
        return pl.BlockSpec((array.shape[0] // steps, array.shape[-1]), lambda j: (j, 0))

    def whole(array):
        return pl.BlockSpec(array.shape, lambda j: (0, 0))

    count = sum(array.size for array in states)
    outs = norm_states + row_outputs + states
    return pl.pallas_call(
        adam_kernel,
        grid=(steps,),
        out_shape=[jax.ShapeDtypeStruct(array.shape, array.dtype) for array in outs],
        in_specs=[pl.BlockSpec(memory_space=pltpu.SMEM)]
        + [whole(array) for array in [norm_sums] + norm_states]
        + [block(array) for array in row_outputs + grads + states],
        out_specs=[whole(array) for array in norm_states]
        + [block(array) for array in row_outputs + states],
        compiler_params=pltpu.CompilerParams(vmem_limit_bytes=BIG_VMEM),
        cost_estimate=pl.CostEstimate(
            flops=6 * count, bytes_accessed=9 * count, transcendentals=count // 3
        ),
        name="adam",
    )(total, norm_sums, *norm_states, *row_outputs, *grads, *states)


def per_device_fast(
    tokens,
    cotangent,
    segments,
    positions,
    attn_master,
    mlp_master,
    norm_master,
    attn_first,
    mlp_first,
    norm_first,
    attn_second,
    mlp_second,
    norm_second,
):
    seq = tokens.shape[0]
    rows = attn_master.shape[0]
    width = D // N_DP
    ff_width = FF // N_DP
    group = N_DP * seq
    my_dp = lax.axis_index("dp")
    my_shard = lax.axis_index("shard")

    started = start(
        attn_master, mlp_master, norm_master, tokens, cotangent, segments, positions, 0
    )
    w_qkv, w_out, norm_all, tok_all, gu_blocks, down_blocks = started[2 * N_DP : -2]
    tokens, cotangent = started[-2:]
    w_qkv = w_qkv.reshape(D, 3 * width)
    w_out = w_out.reshape(width, D)

    def gather_rows(blocks):
        return lax.all_gather(blocks.reshape(-1, blocks.shape[-1]), "shard", axis=0, tiled=True)

    rates = ROPE_BASE ** (-((np.arange(128) % (ROT // 2)) * 2.0 / ROT))
    rates = np.broadcast_to(rates.astype(np.float32), (8, 128))
    w_gu = gather_rows(gu_blocks)
    w_down = gather_rows(down_blocks)
    results = attn_forward(
        cotangent, tok_all, started[: 2 * N_DP], rates, norm_all, w_qkv, 2
    )
    cot_near, norm_vals, normed1, queries, keys, values, mixture = results[:7]
    *tables, mask = results[7:]
    resid, normed2 = mid_forward(mixture, w_out, tokens, norm_vals, 3)
    normed2 = normed2.reshape(group, D)

    hidden, gate, up, part_down, cot_far = mlp_one(normed2, cotangent, cot_near, w_gu, 1)
    groups = [[place for place in range(N_SH) if place % 2 == core] for core in range(2)]

    def sum_line(blocks):
        blocks = blocks.reshape(-1, blocks.shape[-1])
        return lax.psum_scatter(
            blocks, "shard", scatter_dimension=0, axis_index_groups=groups, tiled=True
        )

    down_sum = sum_line(part_down)
    grad_resid, own_gao, sums2, part_gu = mid_backward(
        normed2, cotangent, cot_near, cot_far, w_gu, w_down, gate, up, resid, norm_vals, 4
    )
    gu_sum = sum_line(part_gu)
    grad_attn_out, out_part = share(own_gao, hidden.reshape(N_DP, seq, ff_width), w_down, 6)
    grad_attn_out, down_sum = lax.optimization_barrier((grad_attn_out, down_sum))
    block_out, grad_qkv, bias_sums, part_attn = attn_backward(
        out_part,
        normed1,
        mixture,
        resid,
        grad_attn_out,
        w_out,
        queries,
        keys,
        values,
        mask,
        tables,
        9,
    )
    gu_blocks = gu_sum.reshape(N_DP, rows, 2 * ff_width)
    down_blocks = down_sum.reshape(N_DP, rows, ff_width)
    input_grad, norm_sums, gu_grad, down_grad, qkv_grad, out_grad, box = last(
        part_attn,
        grad_qkv,
        w_qkv,
        gu_blocks,
        down_blocks,
        tokens,
        grad_resid,
        norm_vals,
        bias_sums,
        sums2,
        5,
    )
    results = adam(
        box,
        norm_sums,
        [norm_master, norm_first, norm_second],
        [input_grad, block_out],
        [qkv_grad, out_grad, gu_grad, down_grad],
        [attn_master, attn_first, attn_second, mlp_master, mlp_first, mlp_second],
    )
    norm_new, norm_first_new, norm_second_new, input_grad, block_out = results[:5]
    attn_new, attn_first_new, attn_second_new, mlp_new, mlp_first_new, mlp_second_new = results[5:]
    grad_size = jnp.sqrt(box[0, 0])
    return (
        block_out,
        input_grad,
        grad_size,
        attn_new,
        mlp_new,
        norm_new,
        attn_first_new,
        mlp_first_new,
        norm_first_new,
        attn_second_new,
        mlp_second_new,
        norm_second_new,
    )


def solution(mesh):
    in_specs = (
        P(("dp", "shard"), None),
        P(("dp", "shard"), None),
        P(("dp", "shard")),
        P(("dp", "shard")),
        P(("dp", "shard"), None),
        P(("dp", "shard"), None),
        P(None, ("dp", "shard")),
        P(("dp", "shard"), None),
        P(("dp", "shard"), None),
        P(None, ("dp", "shard")),
        P(("dp", "shard"), None),
        P(("dp", "shard"), None),
        P(None, ("dp", "shard")),
    )
    out_specs = (
        P(("dp", "shard"), None),
        P(("dp", "shard"), None),
        P(),
        P(("dp", "shard"), None),
        P(("dp", "shard"), None),
        P(None, ("dp", "shard")),
        P(("dp", "shard"), None),
        P(("dp", "shard"), None),
        P(None, ("dp", "shard")),
        P(("dp", "shard"), None),
        P(("dp", "shard"), None),
        P(None, ("dp", "shard")),
    )
    fast = dict(mesh.shape) == dict(dp=4, shard=8)
    body = per_device_fast if fast else per_device_any
    return jax.shard_map(
        body, mesh=mesh, in_specs=in_specs, out_specs=out_specs, check_vma=False
    )
```
